128 devices in a mesh: ctx: 16 (over y, z), tp: 8 (over x, core).
Axes of the slice: x: 4, y: 4, z: 4, core: 2. Of those that a mesh axis runs over, the one named last changes fastest.
Arguments:
- token_ids: int32 [4096], P('ctx'), may hold values from 0 to 31999
- target_ids: int32 [4096], P('ctx'), may hold values from 0 to 31999
- loss_mask: int32 [4096], P('ctx'), may hold values from 0 to 1, as said below
- segment_ids: int32 [4096], replicated, may hold values from 0 to 4, as said below
- span_pairs: int32 [16], replicated, may hold values from 0 to 15, each once
- attention_master: float32 [2, 2048, 2048], P(None, 'ctx', 'tp')
- feed_master: float32 [3, 2048, 5632], P(None, 'ctx', 'tp'), may hold values from -0.125 to 0.125
- vocab_master: float32 [2, 2048, 32000], P(None, 'ctx', 'tp')
- key_value_master: float32 [2048, 512], P(('ctx', 'tp')), may hold values from -0.125 to 0.125
- gain_master: float32 [2048, 3], P(('ctx', 'tp')), may hold values from 0.5 to 1.5
- attention_row_moment: float32 [2, 2048], P(None, 'ctx'), may hold values from 2.026558e-08 to 1.347065e-06
- attention_column_moment: float32 [2, 2048], P(None, 'tp'), may hold values from 1.1920929e-07 to 4.7683716e-07
- feed_row_moment: float32 [3, 2048], P(None, 'ctx'), may hold values from 2.026558e-08 to 1.347065e-06
- feed_column_moment: float32 [3, 5632], P(None, 'tp'), may hold values from 1.1920929e-07 to 4.7683716e-07
- vocab_row_moment: float32 [2, 2048], P(None, 'ctx'), may hold values from 1.2969971e-09 to 8.621216e-08
- vocab_column_moment: float32 [2, 32000], P(None, 'tp'), may hold values from 1.9073487e-09 to 3.051758e-08
- key_value_row_moment: float32 [2048], P(('ctx', 'tp')), may hold values from 2.026558e-08 to 1.347065e-06
- key_value_column_moment: float32 [512], replicated, may hold values from 1.1920929e-07 to 4.7683716e-07
- gain_moment: float32 [2048, 3], P(('ctx', 'tp')), may hold values from 2.026558e-08 to 1.347065e-06
Outputs:
- token_loss: float32 [], replicated
- update_rms: float32 [11], replicated
- attention_grad: float32 [2, 2048, 2048], P(None, 'ctx', 'tp')
- attention_row_new: float32 [2, 2048], P(None, 'ctx')
- attention_column_new: float32 [2, 2048], P(None, 'tp')
- attention_new: float32 [2, 2048, 2048], P(None, 'ctx', 'tp')
- feed_grad: float32 [3, 2048, 5632], P(None, 'ctx', 'tp')
- feed_row_new: float32 [3, 2048], P(None, 'ctx')
- feed_column_new: float32 [3, 5632], P(None, 'tp')
- feed_new: float32 [3, 2048, 5632], P(None, 'ctx', 'tp')
- vocab_grad: float32 [2, 2048, 32000], P(None, 'ctx', 'tp')
- vocab_row_new: float32 [2, 2048], P(None, 'ctx')
- vocab_column_new: float32 [32000], P('tp')
- embed_column_new: float32 [32000], P('tp')
- vocab_new: float32 [2, 2048, 32000], P(None, 'ctx', 'tp')
- key_value_grad: float32 [2048, 512], P(('ctx', 'tp'))
- key_value_row_new: float32 [2048], P(('ctx', 'tp'))
- key_value_column_new: float32 [512], replicated
- key_value_new: float32 [2048, 512], P(('ctx', 'tp'))
- gain_grad: float32 [2048, 3], P(('ctx', 'tp'))
- gain_moment_new: float32 [2048, 3], P(('ctx', 'tp'))
- gain_new: float32 [2048, 3], P(('ctx', 'tp'))
The draws below stay inside these ranges and needn't reach their ends.
Inputs may be any that keep to these rules, and one draw needn't show every extreme that they name: `loss_mask`: rises slot by slot: the share of ones grows from about a fifth in the first slots to about four fifths in the last. `segment_ids`: never falls, starts at 0 and grows by at most 1 from one position to the next; document 0 covers at least the first half of the row; the last document is number 16 // 4. `span_pairs`: each span pair index once.
All inputs are finite; a program needn't handle non-finite values.
Results may differ from the reference program's by a relative error of at most 0.017.
The reference program's roundings to bfloat16 on the way count: a program that leaves them out, or rounds other values in their place, can miss the bound.
Values may be sent and summed in bfloat16 or wider, within the bound.
No kernel may reach another device: no remote copies, remote signals or barrier semaphores. Data moves between devices by JAX's collectives and lax.ppermute only.
A program may use at most 256 MiB of HBM per device.

```python
import math
import jax
import jax.numpy as jnp
import numpy as np
from jax import lax

D = 2048
HEADS = 32
KV_HEADS = 4
HD = 64
FF = 5632
VOCAB = 32000
TOK_DEV = 256
ORIG_CTX = 2048
HQ = 2048
KVW = 512
TOKENS = 4096
N_CTX = 16


def draw_loss_mask(key, part):
    key = jax.random.fold_in(key, 11)
    places = jnp.arange(TOKENS, dtype=jnp.int32)
    slots = places // (TOK_DEV // 2)
    limit = 200 + 600 * slots // (2 * N_CTX)
    rolled = jax.random.randint(key, (TOKENS,), 0, 1000)
    return (rolled < limit).astype(jnp.int32)


def draw_segment_ids(key, part):
    key = jax.random.fold_in(key, 12)
    first_key, rest_key = jax.random.split(key)
    leading = TOKENS // 2 + jax.random.randint(first_key, (), 0, TOKENS // 4 + 1)
    places = jnp.arange(TOKENS, dtype=jnp.int32)
    scores = jax.random.randint(rest_key, (TOKENS,), 0, 65536) * TOKENS + places
    scores = jnp.where(places > leading, scores, -1)
    picked = lax.top_k(scores, N_CTX // 4 - 1)[1]
    starts = jnp.zeros((TOKENS,), jnp.int32).at[picked].set(1)
    starts = jnp.where(places == leading, 1, starts)
    return jnp.cumsum(starts).astype(jnp.int32)


def spread_values(key, shape):
    return jax.random.normal(key, shape, jnp.float32)


def draw_attention_master(key, part):
    key = jax.random.fold_in(key, 13)
    first_key, second_key = jax.random.split(key)
    query_part = spread_values(first_key, (D, HQ)) / math.sqrt(D)
    output_part = spread_values(second_key, (D, HQ)) * 12.0 / math.sqrt(HQ)
    return jnp.stack([query_part, output_part]).astype(jnp.float32)


def draw_vocab_master(key, part):
    key = jax.random.fold_in(key, 14)
    first_key, second_key = jax.random.split(key)
    columns = jnp.arange(VOCAB, dtype=jnp.float32) / VOCAB
    rising = 1.0 + 2.0 * columns
    head_part = spread_values(first_key, (D, VOCAB)) * rising[None, :] / math.sqrt(D)
    embed_part = spread_values(second_key, (D, VOCAB))
    return jnp.stack([head_part, embed_part]).astype(jnp.float32)


def falling_moment(key, stacks, base, steep):
    fraction = jnp.arange(D, dtype=jnp.float32) / D
    profile = 8.0 * jnp.exp(-steep * fraction)
    jitter = jnp.exp(jax.random.uniform(key, (stacks, D), jnp.float32, math.log(0.7), math.log(1.4)))
    return (profile[None, :] * jitter * base).astype(jnp.float32)


def draw_attention_row_moment(key, part):
    key = jax.random.fold_in(key, 21)
    steep = math.log(16.0)
    return falling_moment(key, 2, 1.0 / (TOKENS * D), steep)


def draw_feed_row_moment(key, part):
    key = jax.random.fold_in(key, 22)
    steep = math.log(16.0)
    return falling_moment(key, 3, 1.0 / (TOKENS * D), steep)


def draw_vocab_row_moment(key, part):
    key = jax.random.fold_in(key, 23)
    steep = math.log(16.0)
    return falling_moment(key, 2, 1.0 / (TOKENS * VOCAB), steep)


def draw_key_value_row_moment(key, part):
    key = jax.random.fold_in(key, 24)
    steep = math.log(16.0)
    return falling_moment(key, 1, 1.0 / (TOKENS * D), steep)[0]


def draw_gain_moment(key, part):
    key = jax.random.fold_in(key, 25)
    steep = math.log(16.0)
    return falling_moment(key, 3, 1.0 / (TOKENS * D), steep).T


def set_ends(result, own_key, smallest, top_value):
    spot = [jax.random.randint(jax.random.fold_in(own_key, axis), (), 0, length) for axis, length in enumerate(result.shape)]
    longest = result.shape.index(max(result.shape))
    neighbour = spot[:longest] + [(spot[longest] + 1) % result.shape[longest]] + spot[longest + 1:]
    return result.at[tuple(spot)].set(smallest).at[tuple(neighbour)].set(top_value)


def levels(own_key, extent, cuts, low, high):
    def one(dim, parts):
        draws = jax.random.uniform(jax.random.fold_in(jax.random.fold_in(own_key, 6), dim), (parts,), jnp.float32, low / len(cuts), high / len(cuts))
        return jnp.repeat(jnp.exp(draws), extent[dim] // parts).reshape((-1,) + (1,) * (len(extent) - dim - 1))

    level = one(*cuts[0])
    for cut in cuts[1:]:
        level = level * one(*cut)
    return level


def rank_table(amount, lean):
    loads = [(1 << 20) // math.isqrt(grade ** lean) + 1 for grade in range(1, amount + 1)]
    deviation = 1 + sum(loads) // (1 << 30)
    return np.cumsum(np.array([max(1, weight // deviation) for weight in loads]))


def ranked(own_key, dims, amount, skew):
    grid = rank_table(amount, skew)
    lot = jax.random.randint(jax.random.fold_in(own_key, 1), dims, 0, int(grid[amount - 1]))
    standing = jnp.searchsorted(jnp.asarray(grid, jnp.int32), lot, side="right")
    return jax.random.permutation(jax.random.fold_in(own_key, 2), amount)[standing].astype(jnp.int32)


def noise(rng, extent, scale, bound, cuts=(), held_as=jnp.bfloat16):
    result = scale * jax.random.normal(rng, extent, jnp.float32)
    if cuts:
        result = result * levels(rng, extent, cuts, -0.22, 0.18)
    return jnp.clip(result, -bound, bound).astype(held_as)


def setup_inputs(seed: int = 0) -> dict:
    key_list = jax.random.split(jax.random.key(seed), 20)
    token_ids = set_ends(ranked(key_list[0], (TOKENS,), VOCAB, 2), jax.random.fold_in(key_list[0], 3), 0, VOCAB - 1).astype(jnp.int32)
    target_ids = set_ends(ranked(key_list[1], (TOKENS,), VOCAB, 2), jax.random.fold_in(key_list[1], 3), 0, VOCAB - 1).astype(jnp.int32)
    loss_mask = draw_loss_mask(jax.random.fold_in(key_list[19], 71), 0)
    segment_ids = draw_segment_ids(jax.random.fold_in(key_list[19], 71), 0)
    span_pairs = jax.random.permutation(key_list[4], N_CTX).astype(jnp.int32)
    attention_master = draw_attention_master(jax.random.fold_in(key_list[19], 71), 0)
    feed_master = noise(key_list[6], (3, D, FF), D ** -0.5, 0.125, ((1, 16), (2, 8)), jnp.float32)
    vocab_master = draw_vocab_master(jax.random.fold_in(key_list[19], 71), 0)
    key_value_master = noise(key_list[8], (D, KVW), D ** -0.5, 0.125, ((0, 128),), jnp.float32)
    gain_master = jnp.clip(1.0 + 0.1 * jax.random.normal(key_list[9], (D, 3), jnp.float32), 0.5, 1.5)
    attention_row_moment = draw_attention_row_moment(jax.random.fold_in(key_list[19], 71), 0)
    attention_column_moment = jnp.clip(jnp.exp(math.log(4.76837158203125e-07) - 1.3862944 * jax.random.uniform(key_list[11], (2, HQ), jnp.float32) ** levels(key_list[11], (2, HQ), ((1, 8),), -0.2, 0.2)), 1.1920928955078125e-07, 4.76837158203125e-07)
    feed_row_moment = draw_feed_row_moment(jax.random.fold_in(key_list[19], 71), 0)
    feed_column_moment = jnp.clip(jnp.exp(math.log(4.76837158203125e-07) - 1.3862944 * jax.random.uniform(key_list[13], (3, FF), jnp.float32) ** levels(key_list[13], (3, FF), ((1, 8),), -0.2, 0.2)), 1.1920928955078125e-07, 4.76837158203125e-07)
    vocab_row_moment = draw_vocab_row_moment(jax.random.fold_in(key_list[19], 71), 0)
    vocab_column_moment = jnp.clip(jnp.exp(math.log(3.051757957450718e-08) - 2.7725887 * jax.random.uniform(key_list[15], (2, VOCAB), jnp.float32) ** levels(key_list[15], (2, VOCAB), ((1, 8),), -0.2, 0.2)), 1.907348723406699e-09, 3.051757957450718e-08)
    key_value_row_moment = draw_key_value_row_moment(jax.random.fold_in(key_list[19], 71), 0)
    key_value_column_moment = jnp.clip(jnp.exp(jax.random.uniform(key_list[17], (KVW,), jnp.float32, math.log(1.1920928955078125e-07), math.log(4.76837158203125e-07))), 1.1920928955078125e-07, 4.76837158203125e-07)
    gain_moment = draw_gain_moment(jax.random.fold_in(key_list[19], 71), 0)
    return dict(token_ids=token_ids, target_ids=target_ids, loss_mask=loss_mask, segment_ids=segment_ids, span_pairs=span_pairs, attention_master=attention_master, feed_master=feed_master, vocab_master=vocab_master, key_value_master=key_value_master, gain_master=gain_master, attention_row_moment=attention_row_moment, attention_column_moment=attention_column_moment, feed_row_moment=feed_row_moment, feed_column_moment=feed_column_moment, vocab_row_moment=vocab_row_moment, vocab_column_moment=vocab_column_moment, key_value_row_moment=key_value_row_moment, key_value_column_moment=key_value_column_moment, gain_moment=gain_moment)


@jax.custom_vjp
def low(v):
    return lax.optimization_barrier(v.astype(jnp.bfloat16)).astype(jnp.float32)

@jax.custom_vjp
def low_back(v):
    return v

def low_keep(v):
    return (low(v), None)

def low_pass(kept, grad):
    return (grad,)

def back_keep(v):
    return (v, None)

def back_low(kept, grad):
    return (low(grad),)
low.defvjp(low_keep, low_pass)
low_back.defvjp(back_keep, back_low)
PRECISE = lax.Precision.HIGHEST
NORM_EPS = 1e-05
MOMENT_DECAY = 0.5
MOMENT_EPS = 1e-30
CLIP_LIMIT = 0.5
STEP_SCALE = 1.0
ROPE_BASE = 10000.0
YARN_SCALE = 4.0
YARN_ALPHA = 1.0
YARN_BETA = 32.0

def layout(span_pairs, segment_ids):
    length = segment_ids.shape[0]
    groups = span_pairs.shape[0]
    width = length // (2 * groups)
    places = jnp.arange(length, dtype=jnp.int32)
    slots = places // width
    paired = span_pairs[slots // 2]
    span_of = jnp.where(slots % 2 == 0, paired, 2 * groups - 1 - paired)
    row_pos = (span_of * width + places % width).astype(jnp.int32)
    change = jnp.concatenate([jnp.ones((1,), jnp.int32), (segment_ids[1:] != segment_ids[:-1]).astype(jnp.int32)])
    starts = lax.cummax(places * change, axis=0)
    return (row_pos, segment_ids[row_pos], row_pos - starts[row_pos])

def rope_tables(positions):
    ladder = jnp.arange(HD // 2, dtype=jnp.float32)
    freqs = ROPE_BASE ** (-2.0 * ladder / HD)
    ratio = ORIG_CTX * freqs / (2.0 * math.pi)
    ramped = jnp.clip((ratio - YARN_ALPHA) / (YARN_BETA - YARN_ALPHA), 0.0, 1.0)
    inverse = freqs * (1.0 - ramped) / YARN_SCALE + freqs * ramped
    angles = positions.astype(jnp.float32)[:, None] * inverse[None, :]
    mscale = 0.1 * math.log(YARN_SCALE) + 1.0
    return (jnp.cos(angles) * mscale, jnp.sin(angles) * mscale)

def rotate(values, cosine, sine):
    halves = values.shape[-1] // 2
    first, second = (values[..., :halves], values[..., halves:])
    cos_b, sin_b = (cosine[:, None, :], sine[:, None, :])
    return jnp.concatenate([first * cos_b - second * sin_b, second * cos_b + first * sin_b], axis=-1)

def rms_norm(values, gain):
    return values * lax.rsqrt(lax.optimization_barrier(jnp.mean(values * values, axis=-1, keepdims=True)) + NORM_EPS) * gain

def one_head(queries, head_keys, head_values, seg_rows, pos_rows):
    scores = low_back(jnp.dot(queries, head_keys.T, precision=PRECISE) / math.sqrt(HD))
    visible = (seg_rows[:, None] == seg_rows[None, :]) & (pos_rows[None, :] <= pos_rows[:, None])
    scores = jnp.where(visible, scores, -1e+30)
    weights = low(jax.nn.softmax(scores, axis=-1))
    return low_back(jnp.dot(weights, head_values, precision=PRECISE))

def block_loss(final_rows, target_rows, keep_rows, head):
    logits = low_back(jnp.dot(final_rows, head, precision=PRECISE))
    highest = lax.optimization_barrier(jnp.max(logits, axis=-1, keepdims=True))
    total = highest[:, 0] + jnp.log(lax.optimization_barrier(jnp.sum(jnp.exp(logits - highest), axis=-1)))
    picked = jnp.take_along_axis(logits, target_rows[:, None], axis=1)[:, 0]
    return jnp.sum(keep_rows * (total - picked))

def forward(params, token_ids, target_ids, keep, seg_rows, pos_rows, rope_pos):
    attention, feed, vocab, key_value, gains = params
    count = token_ids.shape[0]
    stream_in = jnp.take(vocab[1], token_ids, axis=1).T
    normed = low(rms_norm(stream_in, gains[:, 0]))
    cosine, sine = rope_tables(rope_pos)
    query_linear = low_back(jnp.dot(normed, attention[0], precision=PRECISE)).reshape(count, HEADS, HD)
    queries = low(rotate(query_linear, cosine, sine))
    keyval_linear = jnp.dot(normed, key_value, precision=PRECISE)
    all_keys = low(rotate(keyval_linear[:, :KV_HEADS * HD].reshape(count, KV_HEADS, HD), cosine, sine))
    all_values = low(keyval_linear[:, KV_HEADS * HD:].reshape(count, KV_HEADS, HD))
    group = HEADS // KV_HEADS
    wide_keys = jnp.repeat(all_keys, group, axis=1).transpose(1, 0, 2)
    wide_values = jnp.repeat(all_values, group, axis=1).transpose(1, 0, 2)
    checked = jax.checkpoint(one_head)
    heads_out = lax.map(lambda triple: checked(triple[0], triple[1], triple[2], seg_rows, pos_rows), (queries.transpose(1, 0, 2), wide_keys, wide_values))
    attended = low(heads_out.transpose(1, 0, 2).reshape(count, HQ))
    stream_mid = stream_in + low_back(jnp.dot(attended, attention[1].T, precision=PRECISE))
    inner = low(rms_norm(stream_mid, gains[:, 1]))
    gate = low_back(jnp.dot(inner, feed[0], precision=PRECISE))
    upward = low_back(jnp.dot(inner, feed[1], precision=PRECISE))
    hidden = low(jax.nn.silu(gate) * upward)
    stream_out = stream_mid + low_back(jnp.dot(hidden, feed[2].T, precision=PRECISE))
    finals = low(rms_norm(stream_out, gains[:, 2]))
    block = math.gcd(count, 512)
    pieces = count // block
    checked_loss = jax.checkpoint(block_loss)
    sums = lax.map(lambda triple: checked_loss(triple[0], triple[1], triple[2], vocab[0]), (finals.reshape(pieces, block, D), target_ids.reshape(pieces, block), keep.reshape(pieces, block)))
    return jnp.sum(sums) / count

def factored(grad, master, row_old, column_old):
    squares = grad * grad + MOMENT_EPS
    row_new = MOMENT_DECAY * row_old + (1.0 - MOMENT_DECAY) * lax.optimization_barrier(jnp.mean(squares, axis=-1))
    column_new = MOMENT_DECAY * column_old + (1.0 - MOMENT_DECAY) * lax.optimization_barrier(jnp.mean(squares, axis=-2))
    row_mean = lax.optimization_barrier(jnp.mean(row_new, axis=-1))
    scale = row_new[..., :, None] * column_new[..., None, :] / row_mean[..., None, None]
    raw_step = grad * lax.rsqrt(scale)
    rms = jnp.sqrt(lax.optimization_barrier(jnp.mean(raw_step * raw_step, axis=(-2, -1))))
    weight_rms = jnp.sqrt(lax.optimization_barrier(jnp.mean(master * master, axis=(-2, -1))))
    factor = STEP_SCALE * weight_rms / jnp.maximum(1.0, rms / CLIP_LIMIT)
    return (row_new, column_new, master - factor[..., None, None] * raw_step, rms)

def reference(token_ids, target_ids, loss_mask, segment_ids, span_pairs, attention_master, feed_master, vocab_master, key_value_master, gain_master, attention_row_moment, attention_column_moment, feed_row_moment, feed_column_moment, vocab_row_moment, vocab_column_moment, key_value_row_moment, key_value_column_moment, gain_moment):
    row_pos, seg_rows, rope_pos = layout(span_pairs, segment_ids)
    keep = loss_mask.astype(jnp.float32)
    masters = (attention_master, feed_master, vocab_master, key_value_master, gain_master)
    params = tuple((master.astype(jnp.bfloat16).astype(jnp.float32) for master in masters))
    loss_value, pull = jax.vjp(lambda *weights: forward(weights, token_ids, target_ids, keep, seg_rows, row_pos, rope_pos), *params)
    grads = pull(jnp.ones_like(loss_value))
    attn_rows, attn_cols, attn_new, attn_rms = factored(grads[0], attention_master, attention_row_moment, attention_column_moment)
    feed_rows, feed_cols, feed_new, feed_rms = factored(grads[1], feed_master, feed_row_moment, feed_column_moment)
    voc_rows, voc_cols, voc_new, voc_rms = factored(grads[2], vocab_master, vocab_row_moment, vocab_column_moment)
    kv_rows, kv_cols, kv_new, kv_rms = factored(grads[3], key_value_master, key_value_row_moment, key_value_column_moment)
    gain_grad = grads[4]
    gain_second = MOMENT_DECAY * gain_moment + (1.0 - MOMENT_DECAY) * (gain_grad * gain_grad + MOMENT_EPS)
    gain_step = gain_grad * lax.rsqrt(gain_second)
    gain_rms = jnp.sqrt(lax.optimization_barrier(jnp.mean(gain_step * gain_step, axis=0)))
    gain_scale = jnp.sqrt(lax.optimization_barrier(jnp.mean(gain_master * gain_master, axis=0)))
    gain_new = gain_master - (STEP_SCALE * gain_scale / jnp.maximum(1.0, gain_rms / CLIP_LIMIT))[None, :] * gain_step
    update_rms = jnp.concatenate([attn_rms, feed_rms, voc_rms, kv_rms[None], gain_rms])
    return (loss_value, update_rms, grads[0], attn_rows, attn_cols, attn_new, grads[1], feed_rows, feed_cols, feed_new, grads[2], voc_rows, voc_cols[0], voc_cols[1], voc_new, grads[3], kv_rows, kv_cols, kv_new, gain_grad, gain_second, gain_new)
```

```python
import functools
import math

import jax
import jax.numpy as jnp
from jax import lax
from jax.experimental import pallas as pl
from jax.experimental.pallas import tpu as pltpu
from jax.sharding import Mesh
from jax.sharding import PartitionSpec as P

D = 2048
HEADS = 32
KV_HEADS = 4
HD = 64
FF = 5632
VOCAB = 32000
ORIG_CTX = 2048
HQ = 2048
KVW = 512
TOKENS = 4096
TP = ("tp_0", "tp_1")
CTX = ("ctx_0", "ctx_1")
CTX_TP = ("ctx_0", "ctx_1", "tp_0", "tp_1")
N_CTX = 16
N_X = 4
N_TP = 8
SHARD = 32
LINES = 128
DOCS = 5

NORM_EPS = 1e-05
MOMENT_DECAY = 0.5
MOMENT_EPS = 1e-30
CLIP_LIMIT = 0.5
STEP_SCALE = 1.0
ROPE_BASE = 10000.0
YARN_SCALE = 4.0
YARN_ALPHA = 1.0
YARN_BETA = 32.0

bf16 = jnp.bfloat16
f32 = jnp.float32


def x_from(values, step):
    return lax.ppermute(values, "tp_0", [((i + step) % N_X, i) for i in range(N_X)])


def x_to(values, step):
    return lax.ppermute(values, "tp_0", [(i, (i + step) % N_X) for i in range(N_X)])


def core_swap(values):
    return lax.ppermute(values, "tp_1", [(0, 1), (1, 0)])


def turned(stack, start):
    return lax.dynamic_slice_in_dim(jnp.concatenate([stack, stack]), start, N_X, 0)


def to_absolute(stack, xs):
    return turned(stack, (N_X - xs) % N_X)


def gather_tp(shard):
    column = jnp.concatenate([shard] + [x_from(shard, d) for d in range(1, N_X)])
    return jnp.concatenate([column, core_swap(column)])


def scatter_tp(partial):
    half = partial[0] + core_swap(partial[1].astype(bf16)).astype(f32)
    low = half.astype(bf16)
    total = half[0]
    for d in range(1, N_X):
        total = total + x_to(low[d], d).astype(f32)
    return total


def both_cores(column, cs):
    other = core_swap(column)
    both = jnp.where(
        cs == 0, jnp.stack([column, other], axis=1), jnp.stack([other, column], axis=1)
    )
    return both.reshape(-1, *column.shape[2:])


def swapped_x(blocks, xs):
    ours = turned(blocks, xs)
    came = [ours[0]] + [x_to(ours[d], d) for d in range(1, N_X)]
    return to_absolute(jnp.stack([came[0], came[3], came[2], came[1]]), xs)


def sum_tp(values, xs):
    pair = values + core_swap(values)
    parts = to_absolute(jnp.stack([pair] + [x_from(pair, d) for d in range(1, N_X)]), xs)
    return (parts[0] + parts[1]) + (parts[2] + parts[3])


def own_order(values, xs, cs):
    blocks = turned(values.reshape(N_X, 2, SHARD), xs)
    blocks = jnp.where(cs == 0, blocks, blocks[:, ::-1])
    return blocks.transpose(1, 0, 2)


def sent_to_all(array, axis):
    copies = jnp.broadcast_to(array, (lax.axis_size(axis), *array.shape))
    return lax.all_to_all(copies, axis, split_axis=0, concat_axis=0, tiled=True)


def rope_tables(positions):
    ladder = jnp.arange(HD // 2, dtype=f32)
    freqs = ROPE_BASE ** (-2.0 * ladder / HD)
    ratio = ORIG_CTX * freqs / (2.0 * math.pi)
    ramped = jnp.clip((ratio - YARN_ALPHA) / (YARN_BETA - YARN_ALPHA), 0.0, 1.0)
    inverse = freqs * (1.0 - ramped) / YARN_SCALE + freqs * ramped
    angles = inverse[:, None] * positions.astype(f32)[None, :]
    mscale = 0.1 * math.log(YARN_SCALE) + 1.0
    return (jnp.cos(angles) * mscale, jnp.sin(angles) * mscale)


def rotate_rows(values, cosine, sine):
    half = values.shape[0] // 2
    first, second = (values[:half], values[half:])
    return jnp.concatenate([first * cosine - second * sine, second * cosine + first * sine])


def rotate_lanes(values, cosine, sine):
    half = values.shape[1] // 2
    first, second = (values[:, :half], values[:, half:])
    return jnp.concatenate([first * cosine - second * sine, second * cosine + first * sine], axis=1)


def rms_norm(values, gain):
    return values * lax.rsqrt(jnp.mean(values * values, axis=-1, keepdims=True) + NORM_EPS) * gain


def contract_last(left, right):
    return lax.dot_general(left, right, (((1,), (1,)), ((), ())), preferred_element_type=f32)


def contract_first(left, right):
    return lax.dot_general(left, right, (((0,), (0,)), ((), ())), preferred_element_type=f32)


def contract(left, right):
    return jnp.dot(left, right, preferred_element_type=f32)


def combine_stats(former, latter):
    highest = jnp.maximum(former[0], latter[0])
    summed = former[1] * jnp.exp(former[0] - highest) + latter[1] * jnp.exp(latter[0] - highest)
    return jnp.stack([highest, summed, former[2] + latter[2]])


def contract_ft(weights, places):
    return lax.dot_general(weights, places, (((0,), (1,)), ((), ())), preferred_element_type=f32)


def contract_tf(features, weights):
    return lax.dot_general(features, weights, (((0,), (1,)), ((), ())), preferred_element_type=f32)


def heads_on_lanes(features):
    return jnp.concatenate([features[h * HD : (h + 1) * HD] for h in range(4)], axis=1)


def heads_on_rows(features):
    return jnp.concatenate(jnp.split(features, 4, axis=1))


VMEM_LIMIT = 50 * 1024 * 1024


def products_kernel(count, offsets, *refs):
    lefts, rights, out_ref = (refs[:count], refs[count : 2 * count], refs[2 * count])
    for left, right, (at, width) in zip(lefts, rights, offsets):
        out_ref[:, at : at + width] = contract_first(left[...], right[...]).astype(bf16)


def row_products(lefts, rights):
    places, rows = lefts[0].shape
    step = 256
    offsets, at = ([], 0)
    for right in rights:
        offsets.append((at, right.shape[1]))
        at += right.shape[1]
    return pl.pallas_call(
        functools.partial(products_kernel, len(lefts), tuple(offsets)),
        grid=(rows // step,),
        in_specs=[pl.BlockSpec((places, step), lambda i: (0, i)) for _ in lefts]
        + [pl.BlockSpec(right.shape, lambda i: (0, 0)) for right in rights],
        out_specs=pl.BlockSpec((step, at), lambda i: (i, 0)),
        out_shape=jax.ShapeDtypeStruct((rows, at), bf16),
        compiler_params=pltpu.CompilerParams(vmem_limit_bytes=VMEM_LIMIT),
        cost_estimate=pl.CostEstimate(
            flops=2 * places * rows * at, bytes_accessed=2 * rows * at, transcendentals=0
        ),
    )(*lefts, *rights)


GROUP = 4
KEYS = 128 * GROUP
STEPS = TOKENS // KEYS


def key_places(core_bit, spans):
    line = lax.broadcasted_iota(jnp.int32, (128, 1), 0)
    x = (spans[N_CTX] + line // SHARD) % N_X
    place = (x * 2 + (spans[N_CTX + 1] ^ core_bit)) * SHARD + line % SHARD
    return place >= 128, place % 128


def visible_keys(spans, places, step, own, start):
    lines = []
    for block in range(step * GROUP, (step + 1) * GROUP):
        span = spans[block % N_CTX]
        second, within = places[block // N_CTX]
        lines.append(jnp.where(second, (2 * N_CTX - 1 - span) * 128, span * 128) + within)
    at = jnp.concatenate(lines, axis=0)
    return (at >= start) & (at <= own)


def key_columns(kv_ref, step, at):
    return jnp.concatenate(
        [kv_ref[step * GROUP + i, at : at + HD] for i in range(GROUP)], axis=1
    )


def attend_kernel(spans, own_ref, q_ref, kv_ref, o_ref, total_ref, s_ref):
    q = q_ref[...]
    own, start = (own_ref[0:1], own_ref[1:2])
    places = [key_places(core_bit, spans) for core_bit in range(2)]
    top = None
    for step in range(STEPS):
        scores = contract_first(key_columns(kv_ref, step, 0), q)
        scores = jnp.where(visible_keys(spans, places, step, own, start), scores, -1e30)
        s_ref[step * KEYS : (step + 1) * KEYS] = scores
        highest = jnp.max(scores, axis=0, keepdims=True)
        top = highest if top is None else jnp.maximum(top, highest)
    total = jnp.zeros(top.shape, f32)
    for step in range(STEPS):
        powers = jnp.exp(s_ref[step * KEYS : (step + 1) * KEYS] - top)
        s_ref[step * KEYS : (step + 1) * KEYS] = powers
        total = total + jnp.sum(powers, axis=0, keepdims=True)
    share = 1.0 / total
    out = jnp.zeros(q.shape, f32)
    for step in range(STEPS):
        weights = (s_ref[step * KEYS : (step + 1) * KEYS] * share).astype(bf16)
        out = out + contract(key_columns(kv_ref, step, HD), weights)
    o_ref[...] = out.astype(bf16)
    total_ref[...] = top + jnp.log(total)


SPLIT = 2


def attend(spans, own, q, kv):
    lanes = q.shape[1] // SPLIT
    column = lambda rows: pl.BlockSpec((rows, lanes), lambda i: (0, i))
    return pl.pallas_call(
        attend_kernel,
        grid=(SPLIT,),
        in_specs=[
            pl.BlockSpec(memory_space=pltpu.SMEM),
            column(2),
            column(HD),
            pl.BlockSpec(kv.shape, lambda i: (0, 0, 0)),
        ],
        out_specs=[column(HD), column(1)],
        out_shape=[
            jax.ShapeDtypeStruct(q.shape, bf16),
            jax.ShapeDtypeStruct((1, q.shape[1]), f32),
        ],
        scratch_shapes=[pltpu.VMEM((TOKENS, lanes), f32)],
        compiler_params=pltpu.CompilerParams(vmem_limit_bytes=VMEM_LIMIT),
        cost_estimate=pl.CostEstimate(
            flops=16 * TOKENS * q.shape[1] * HD, bytes_accessed=2 << 20, transcendentals=0
        ),
    )(spans, own, q, kv)


def attend_back_kernel(
    spans, own_ref, q_ref, do_ref, total_ref, kv_ref, dq_ref, dkv_ref, p_ref, dp_ref
):
    q, do = (q_ref[...], do_ref[...])
    own, start = (own_ref[0:1], own_ref[1:2])
    total = total_ref[...]
    places = [key_places(core_bit, spans) for core_bit in range(2)]
    rowsum = jnp.zeros(total.shape, f32)
    for step in range(STEPS):
        scores = contract_first(key_columns(kv_ref, step, 0), q)
        scores = jnp.where(visible_keys(spans, places, step, own, start), scores, -1e30)
        probs = jnp.exp(scores - total)
        probs_grad = contract_first(key_columns(kv_ref, step, HD), do)
        p_ref[step * KEYS : (step + 1) * KEYS] = probs
        dp_ref[step * KEYS : (step + 1) * KEYS] = probs_grad
        rowsum = rowsum + jnp.sum(probs * probs_grad, axis=0, keepdims=True)

    @pl.when(pl.program_id(0) == 0)
    def _():
        dkv_ref[...] = jnp.zeros(dkv_ref.shape, f32)

    dq = jnp.zeros(q.shape, f32)
    for step in range(STEPS):
        rows = slice(step * KEYS, (step + 1) * KEYS)
        probs = p_ref[rows]
        score_grad = (probs * (dp_ref[rows] - rowsum)).astype(bf16)
        dkv_ref[rows] += jnp.concatenate(
            [contract_last(score_grad, q), contract_last(probs.astype(bf16), do)], axis=1
        )
        dq = dq + contract(key_columns(kv_ref, step, 0), score_grad)
    dq_ref[...] = dq * (1.0 / math.sqrt(HD))


def attend_back(spans, own, q, do, total, kv):
    lanes = q.shape[1] // SPLIT
    column = lambda rows: pl.BlockSpec((rows, lanes), lambda i: (0, i))
    return pl.pallas_call(
        attend_back_kernel,
        grid=(SPLIT,),
        in_specs=[
            pl.BlockSpec(memory_space=pltpu.SMEM),
            column(2),
            column(HD),
            column(HD),
            column(1),
            pl.BlockSpec(kv.shape, lambda i: (0, 0, 0)),
        ],
        out_specs=[column(HD), pl.BlockSpec((TOKENS, 2 * HD), lambda i: (0, 0))],
        out_shape=[
            jax.ShapeDtypeStruct(q.shape, f32),
            jax.ShapeDtypeStruct((TOKENS, 2 * HD), f32),
        ],
        scratch_shapes=[pltpu.VMEM((TOKENS, lanes), f32), pltpu.VMEM((TOKENS, lanes), f32)],
        compiler_params=pltpu.CompilerParams(vmem_limit_bytes=VMEM_LIMIT),
        cost_estimate=pl.CostEstimate(
            flops=40 * TOKENS * q.shape[1] * HD, bytes_accessed=4 << 20, transcendentals=0
        ),
    )(spans, own, q, do, total, kv)


def moments(old, sums, count):
    return MOMENT_DECAY * old + (1.0 - MOMENT_DECAY) * (sums / count + MOMENT_EPS)


def weighted_squares(grad, row_new, column_new):
    inner = jnp.sum(grad * grad * (1.0 / column_new)[..., None, :], axis=-1)
    return jnp.sum(inner / row_new, axis=-1)


def apply_step(master, grad, row_new, column_new, factor):
    wide = (factor[..., None] * lax.rsqrt(row_new))[..., None]
    return master - grad * wide * lax.rsqrt(column_new)[..., None, :]


def body(
    token_ids,
    target_ids,
    loss_mask,
    segment_ids,
    span_pairs,
    attention_master,
    feed_master,
    vocab_master,
    key_value_master,
    gain_master,
    attention_row_moment,
    attention_column_moment,
    feed_row_moment,
    feed_column_moment,
    vocab_row_moment,
    vocab_column_moment,
    key_value_row_moment,
    key_value_column_moment,
    gain_moment,
):
    ctx_index = lax.axis_index(CTX)
    xs = lax.axis_index("tp_0")
    cs = lax.axis_index("tp_1")
    tp_index = xs * 2 + cs
    vocab_here = vocab_master.shape[2]
    ff_here = feed_master.shape[2]
    first_id = tp_index * vocab_here

    kv_low = key_value_master.astype(bf16).reshape(16, 2, KV_HEADS, HD).transpose(2, 0, 1, 3)
    gain_low = jnp.pad(gain_master.astype(bf16), ((0, 0), (0, 125)))
    blocks = jnp.concatenate(
        [
            kv_low.reshape(KV_HEADS, 16, 2 * HD),
            jnp.broadcast_to(gain_low, (KV_HEADS, *gain_low.shape)),
        ],
        axis=2,
    )
    line_block = both_cores(swapped_x(blocks, xs), cs)

    attention_low = attention_master.astype(bf16)
    feed_low = feed_master.astype(bf16)
    first_block = jnp.concatenate(
        [attention_low[0], attention_low[1], line_block, feed_low[0], feed_low[1], feed_low[2]],
        axis=1,
    )
    first_all = lax.all_gather(first_block, CTX, axis=0, tiled=True)
    head = lax.all_gather(vocab_master[0].astype(bf16), CTX, axis=0, tiled=True)
    gate_up = first_all[:, 768:2176]
    down = first_all[:, 2176:]
    w_query = first_all[:, :256]
    w_out = first_all[:, 256:512]
    w_pair = first_all[:, 512:640]
    gains = first_all[:, 640:643].astype(f32).T

    order = (
        ((xs + jnp.arange(N_X, dtype=jnp.int32)) % N_X * 2)[None, :]
        + (cs ^ jnp.arange(2, dtype=jnp.int32))[:, None]
    )[:, :, None] * SHARD + jnp.arange(SHARD, dtype=jnp.int32)
    second_span = order >= 128
    within = order % 128
    own_pair = lax.dynamic_slice_in_dim(span_pairs, ctx_index, 1)[0]
    last_span = 2 * N_CTX - 1
    own_pos = (jnp.where(second_span, last_span - own_pair, own_pair) * 128 + within).reshape(-1)
    doc_start = jnp.zeros_like(own_pos)
    for k in range(1, DOCS):
        start = jnp.sum((segment_ids < k).astype(jnp.int32))
        doc_start = jnp.where(own_pos >= start, start, doc_start)
    cosine, sine = rope_tables(own_pos - doc_start)
    cosine_4, sine_4 = (jnp.tile(cosine, (1, 4)), jnp.tile(sine, (1, 4)))
    own_places = jnp.tile(jnp.stack([own_pos, doc_start]), (1, 4))
    spans = jnp.concatenate([span_pairs, jnp.stack([xs, cs]).astype(jnp.int32)])

    ids_here = own_order(token_ids, xs, cs).reshape(8, SHARD)
    all_ids = sent_to_all(ids_here, CTX).transpose(1, 0, 2).reshape(TOKENS)
    columns = jnp.arange(vocab_here, dtype=jnp.int32)
    onehot_ids = ((all_ids - first_id)[:, None] == columns[None, :]).astype(bf16)
    looked = contract_last(onehot_ids, vocab_master[1].astype(bf16))
    mine = scatter_tp(looked.reshape(2, N_X, N_CTX, SHARD, LINES))
    rows_in = lax.all_to_all(mine.astype(bf16), CTX, 0, 0, tiled=True)
    stream_in = rows_in.transpose(1, 0, 2).reshape(SHARD, D).astype(f32)

    normed_low = gather_tp(rms_norm(stream_in, gains[0]).astype(bf16))
    normed_half = normed_low[:128]
    keyval_linear = contract_ft(w_pair, normed_half)
    own_keyvals = jnp.concatenate(
        [rotate_rows(keyval_linear[:HD], cosine[:, :128], sine[:, :128]), keyval_linear[HD:]]
    ).astype(bf16)
    half_keyvals = sent_to_all(own_keyvals, CTX)
    row_keyvals = jnp.concatenate([half_keyvals, core_swap(half_keyvals)])
    query_linear = heads_on_lanes(contract_ft(w_query, normed_low))
    queries = rotate_rows(query_linear, cosine_4, sine_4).astype(bf16) * jnp.asarray(
        1.0 / math.sqrt(HD), bf16
    )
    attended, log_total = attend(spans, own_places, queries, row_keyvals)
    attended_rows = heads_on_rows(attended)
    stream_mid = stream_in + scatter_tp(
        contract_tf(attended_rows, w_out).reshape(2, N_X, SHARD, D)
    )

    inner_low = gather_tp(rms_norm(stream_mid, gains[1]).astype(bf16))
    both = contract(inner_low, gate_up)
    gate, upward = (both[:, :ff_here], both[:, ff_here:])
    sigmoid_gate = jax.nn.sigmoid(gate)
    silu_gate = gate * sigmoid_gate
    hidden_low = (silu_gate * upward).astype(bf16)
    stream_out = stream_mid + scatter_tp(
        contract_last(hidden_low, down).reshape(2, N_X, SHARD, D)
    )

    finals_low = gather_tp(rms_norm(stream_out, gains[2]).astype(bf16))
    logits = contract(finals_low, head)
    local_targets = own_order(target_ids, xs, cs).reshape(-1) - first_id
    onehot = columns[None, :] == local_targets[:, None]
    local_top = jnp.max(logits, axis=-1)
    local_sum = jnp.sum(jnp.exp(logits - local_top[:, None]), axis=-1)
    picked = jnp.sum(jnp.where(onehot, logits, 0.0), axis=-1)
    stats = jnp.stack([local_top, local_sum, picked]).reshape(3, 2, N_X, SHARD)
    stats = combine_stats(stats, core_swap(stats)[:, ::-1])
    others = [jnp.roll(x_from(stats, d), d, axis=2) for d in range(1, N_X)]
    stats = combine_stats(combine_stats(stats, others[0]), combine_stats(others[1], others[2]))
    stats = stats.reshape(3, -1)
    vocab_total = stats[0] + jnp.log(stats[1])
    keep = own_order(loss_mask, xs, cs).reshape(-1).astype(f32)
    loss_part = jnp.sum((keep * (vocab_total - stats[2]))[:SHARD]) / TOKENS

    dlogits_low = (
        (keep / TOKENS)[:, None]
        * (jnp.exp(logits - vocab_total[:, None]) - onehot.astype(f32))
    ).astype(bf16)
    final_grad = scatter_tp(contract_last(dlogits_low, head).reshape(2, N_X, SHARD, D))
    head_low = row_products([finals_low], [dlogits_low])
    final_grad, head_low = lax.optimization_barrier((final_grad, head_low))
    head_low = lax.psum_scatter(head_low, CTX, scatter_dimension=0, tiled=True)
    out_grad, final_gain_grad = jax.vjp(rms_norm, stream_out, gains[2])[1](final_grad)
    branch_low = gather_tp(out_grad.astype(bf16))
    hidden_grad = contract(branch_low, down)
    gate_grad_low = (
        hidden_grad * upward * sigmoid_gate * (1.0 + gate * (1.0 - sigmoid_gate))
    ).astype(bf16)
    upward_grad_low = (hidden_grad * silu_gate).astype(bf16)
    both_grad_low = jnp.concatenate([gate_grad_low, upward_grad_low], axis=1)
    inner_grad = scatter_tp(contract_last(both_grad_low, gate_up).reshape(2, N_X, SHARD, D))
    mid_part, middle_gain_grad = jax.vjp(rms_norm, stream_mid, gains[1])[1](inner_grad)
    mid_grad = out_grad + mid_part
    attend_low = gather_tp(mid_grad.astype(bf16))
    attended_grad = heads_on_lanes(contract_ft(w_out, attend_low).astype(bf16))
    dq, pair_grads = attend_back(
        spans, own_places, queries, attended_grad, log_total, row_keyvals
    )
    pair_grads = pair_grads.reshape(2, N_CTX, 128, 2 * HD)
    half_grads = pair_grads[0] + core_swap(pair_grads[1].astype(bf16)).astype(f32)
    came = lax.all_to_all(half_grads.astype(bf16), CTX, 0, 0, tiled=True)
    layer_low = row_products(
        [inner_low, attend_low, branch_low], [both_grad_low, attended_rows.T, hidden_low]
    )
    came, layer_low, head_low = lax.optimization_barrier((came, layer_low, head_low))
    layer_grad = lax.psum_scatter(layer_low, CTX, scatter_dimension=0, tiled=True).astype(f32)
    own_grads = jnp.sum(came.astype(f32), axis=0)
    keyval_low = jnp.concatenate(
        [
            rotate_lanes(own_grads[:, :HD], cosine[:, :128].T, -sine[:, :128].T),
            own_grads[:, HD:],
        ],
        axis=1,
    ).astype(bf16)
    query_linear_low = heads_on_rows(rotate_rows(dq, cosine_4, -sine_4).astype(bf16))
    normed_part = contract_tf(query_linear_low, w_query).reshape(2, 128, D)
    normed_part = jnp.stack([normed_part[0] + contract_last(keyval_low, w_pair), normed_part[1]])
    normed_grad = scatter_tp(normed_part.reshape(2, N_X, SHARD, D))
    late_grads = jnp.concatenate(
        [
            lax.dot_general(
                normed_low,
                query_linear_low,
                (((0,), (1,)), ((), ())),
                preferred_element_type=f32,
            ).astype(bf16),
            contract_first(normed_half, keyval_low).astype(bf16),
        ],
        axis=1,
    ).reshape(N_CTX, LINES, 384)
    late_sum = jnp.sum(
        lax.all_to_all(late_grads, CTX, 0, 0, tiled=True).astype(f32), axis=0
    )
    first_part, first_gain_grad = jax.vjp(rms_norm, stream_in, gains[0])[1](normed_grad)
    input_low = (mid_grad + first_part).astype(bf16)

    gain_parts = jnp.stack([first_gain_grad, middle_gain_grad, final_gain_grad]).astype(bf16)
    sent = jnp.concatenate(
        [
            input_low.reshape(SHARD, N_CTX, LINES).transpose(1, 0, 2),
            jnp.pad(gain_parts.reshape(3, N_CTX, LINES).transpose(1, 0, 2), ((0, 0), (0, 13), (0, 0))),
        ],
        axis=1,
    )
    arrived = lax.all_to_all(sent, CTX, 0, 0, tiled=True)
    gain_sums = jnp.sum(arrived[:, SHARD : SHARD + 3].astype(f32), axis=0)
    place_grads = gather_tp(arrived[:, :SHARD].reshape(N_CTX * SHARD, LINES))
    embed_grad = contract_first(place_grads, onehot_ids)

    attention_grad = jnp.stack([late_sum[:, :256], layer_grad[:, 1408:1664]])
    feed_grad = jnp.stack(
        [layer_grad[:, :ff_here], layer_grad[:, ff_here:1408], layer_grad[:, 1664:]]
    )
    vocab_grad = jnp.stack([head_low.astype(f32), embed_grad])
    kv_part = late_sum[:, 256:]
    kv_full = kv_part + core_swap(kv_part)
    kv_split = kv_full.reshape(N_X, 2, 16, 2 * HD)
    kv_owned = swapped_x(jnp.where(cs == 0, kv_split[:, 0], kv_split[:, 1]), xs)
    key_value_grad = (
        kv_owned.reshape(KV_HEADS, 16, 2, HD).transpose(1, 2, 0, 3).reshape(16, KVW)
    )

    stacks = (
        (attention_grad, attention_master, attention_row_moment, attention_column_moment, HQ),
        (feed_grad, feed_master, feed_row_moment, feed_column_moment, FF),
        (vocab_grad, vocab_master, vocab_row_moment, vocab_column_moment, VOCAB),
    )
    row_parts = [jnp.sum(s[0] * s[0], axis=2) for s in stacks]
    column_parts = [jnp.sum(s[0] * s[0], axis=1) for s in stacks]
    kv_squares = kv_full * kv_full
    row_parts.append(0.5 * jnp.sum(kv_squares, axis=1)[None])
    column_parts.append(jnp.sum(kv_squares, axis=0)[None])
    kv_old_line = lax.dynamic_update_slice_in_dim(
        jnp.zeros((1, LINES), f32), key_value_row_moment[None], tp_index * 16, 1
    )
    row_lines = jnp.concatenate(row_parts + [gain_sums, kv_old_line])
    row_sums = sum_tp(row_lines, xs)
    flat = jnp.concatenate([c.reshape(-1) for c in column_parts])
    column_sums = jnp.sum(sent_to_all(flat.reshape(-1, LINES), CTX), axis=0).reshape(-1)
    row_news, column_news, at, line = ([], [], 0, 0)
    for grad, master, row_old, column_old, width in stacks:
        count, here = column_old.shape
        row_news.append(moments(row_old, row_sums[line : line + count], width))
        column_news.append(
            moments(column_old, column_sums[at : at + count * here].reshape(count, here), D)
        )
        line += count
        at += count * here
    kv_row_all = moments(row_sums[line + 4], row_sums[line], KVW)
    kv_old_columns = lax.dynamic_index_in_dim(
        key_value_column_moment.reshape(2, KV_HEADS, HD), xs, 1, keepdims=False
    ).reshape(-1)
    kv_columns_here = moments(kv_old_columns, column_sums[at:], D)
    gain_grad = lax.dynamic_slice_in_dim(
        row_sums[line + 1 : line + 4], tp_index * 16, 16, 1
    ).T
    gain_second = MOMENT_DECAY * gain_moment + (1.0 - MOMENT_DECAY) * (
        gain_grad * gain_grad + MOMENT_EPS
    )
    gain_step = gain_grad * lax.rsqrt(gain_second)

    scalars = [loss_part[None]]
    for number, (grad, master, row_old, column_old, width) in enumerate(stacks):
        scalars.append(weighted_squares(grad, row_news[number], column_news[number]))
    scalars.append(0.5 * weighted_squares(kv_full, kv_row_all, kv_columns_here)[None])
    scalars.extend(jnp.sum(r, axis=1) for r in row_parts)
    scalars.extend(jnp.sum(s[2], axis=1) / N_TP for s in stacks)
    scalars.append(jnp.sum(key_value_row_moment)[None])
    scalars.extend(jnp.sum(s[1] * s[1], axis=(1, 2)) for s in stacks)
    scalars.append(jnp.sum(key_value_master * key_value_master)[None])
    scalars.append(jnp.sum(gain_master * gain_master, axis=0))
    scalars.append(jnp.sum(gain_step * gain_step, axis=0))
    packed = jnp.concatenate(scalars)
    summed = jnp.sum(sent_to_all(packed[None], CTX_TP)[:, 0], axis=0)
    token_loss = summed[0]
    counts = jnp.array(
        [D * HQ] * 2 + [D * FF] * 3 + [D * VOCAB] * 2 + [D * KVW], dtype=f32
    )
    row_mean = MOMENT_DECAY * summed[17:25] / D + (1.0 - MOMENT_DECAY) * (
        summed[9:17] / counts + MOMENT_EPS
    )
    rms = jnp.sqrt(row_mean * summed[1:9] / counts)
    factor = (
        STEP_SCALE
        * jnp.sqrt(summed[25:33] / counts)
        / jnp.maximum(1.0, rms / CLIP_LIMIT)
        * jnp.sqrt(row_mean)
    )
    gain_rms = jnp.sqrt(summed[36:39] / D)
    gain_factor = STEP_SCALE * jnp.sqrt(summed[33:36] / D) / jnp.maximum(1.0, gain_rms / CLIP_LIMIT)
    gain_new = gain_master - gain_factor[None, :] * gain_step
    update_rms = jnp.concatenate([rms, gain_rms])
    bounds = ((0, 2), (2, 5), (5, 7))
    new_masters = [
        apply_step(s[1], s[0], row_news[n], column_news[n], factor[lo:hi])
        for n, (s, (lo, hi)) in enumerate(zip(stacks, bounds))
    ]
    kv_row_new = lax.dynamic_slice_in_dim(kv_row_all, tp_index * 16, 16, 0)
    kv_column_new = (
        to_absolute(
            jnp.stack([kv_columns_here] + [x_from(kv_columns_here, d) for d in range(1, N_X)]), xs
        )
        .reshape(KV_HEADS, 2, HD)
        .transpose(1, 0, 2)
        .reshape(KVW)
    )
    kv_new = apply_step(key_value_master, key_value_grad, kv_row_new, kv_column_new, factor[7])
    return (
        token_loss,
        update_rms,
        attention_grad,
        row_news[0],
        column_news[0],
        new_masters[0],
        feed_grad,
        row_news[1],
        column_news[1],
        new_masters[1],
        vocab_grad,
        row_news[2],
        column_news[2][0],
        column_news[2][1],
        new_masters[2],
        key_value_grad,
        kv_row_new,
        kv_column_new,
        kv_new,
        gain_grad,
        gain_second,
        gain_new,
    )


def solution(mesh):
    finer = Mesh(mesh.devices.reshape(4, 4, 4, 2), ("ctx_0", "ctx_1", "tp_0", "tp_1"))
    in_specs = (
        P(CTX),
        P(CTX),
        P(CTX),
        P(),
        P(),
        P(None, CTX, TP),
        P(None, CTX, TP),
        P(None, CTX, TP),
        P(CTX_TP, None),
        P(CTX_TP, None),
        P(None, CTX),
        P(None, TP),
        P(None, CTX),
        P(None, TP),
        P(None, CTX),
        P(None, TP),
        P(CTX_TP),
        P(),
        P(CTX_TP, None),
    )
    out_specs = (
        P(),
        P(),
        P(None, CTX, TP),
        P(None, CTX),
        P(None, TP),
        P(None, CTX, TP),
        P(None, CTX, TP),
        P(None, CTX),
        P(None, TP),
        P(None, CTX, TP),
        P(None, CTX, TP),
        P(None, CTX),
        P(TP),
        P(TP),
        P(None, CTX, TP),
        P(CTX_TP, None),
        P(CTX_TP),
        P(),
        P(CTX_TP, None),
        P(CTX_TP, None),
        P(CTX_TP, None),
        P(CTX_TP, None),
    )
    return jax.shard_map(body, mesh=finer, in_specs=in_specs, out_specs=out_specs, check_vma=False)
```

```python
import functools
import math

import jax
import jax.numpy as jnp
from jax import lax
from jax.experimental import pallas as pl
from jax.experimental.pallas import tpu as pltpu
from jax.sharding import Mesh
from jax.sharding import PartitionSpec as P

D = 2048
HEADS = 32
KV_HEADS = 4
HD = 64
FF = 5632
VOCAB = 32000
ORIG_CTX = 2048
HQ = 2048
KVW = 512
TOKENS = 4096
TP = ("tp_0", "tp_1")
CTX = ("ctx_0", "ctx_1")
CTX_TP = ("ctx_0", "ctx_1", "tp_0", "tp_1")
N_CTX = 16
N_X = 4
N_TP = 8
SHARD = 32
LINES = 128
DOCS = 5

NORM_EPS = 1e-05
MOMENT_DECAY = 0.5
MOMENT_EPS = 1e-30
CLIP_LIMIT = 0.5
STEP_SCALE = 1.0
ROPE_BASE = 10000.0
YARN_SCALE = 4.0
YARN_ALPHA = 1.0
YARN_BETA = 32.0

bf16 = jnp.bfloat16
f32 = jnp.float32


def x_from(values, step):
    return lax.ppermute(values, "tp_0", [((i + step) % N_X, i) for i in range(N_X)])


def x_to(values, step):
    return lax.ppermute(values, "tp_0", [(i, (i + step) % N_X) for i in range(N_X)])


def core_swap(values):
    return lax.ppermute(values, "tp_1", [(0, 1), (1, 0)])


def turned(stack, start):
    return lax.dynamic_slice_in_dim(jnp.concatenate([stack, stack]), start, N_X, 0)


def to_absolute(stack, xs):
    return turned(stack, (N_X - xs) % N_X)


def gather_tp(shard):
    column = jnp.concatenate([shard] + [x_from(shard, d) for d in range(1, N_X)])
    return jnp.concatenate([column, core_swap(column)])


def scatter_tp(partial):
    half = partial[0] + core_swap(partial[1].astype(bf16)).astype(f32)
    low = half.astype(bf16)
    total = half[0]
    for d in range(1, N_X):
        total = total + x_to(low[d], d).astype(f32)
    return total


def both_cores(column, cs):
    other = core_swap(column)
    both = jnp.where(
        cs == 0, jnp.stack([column, other], axis=1), jnp.stack([other, column], axis=1)
    )
    return both.reshape(-1, *column.shape[2:])


def swapped_x(blocks, xs):
    ours = turned(blocks, xs)
    came = [ours[0]] + [x_to(ours[d], d) for d in range(1, N_X)]
    return to_absolute(jnp.stack([came[0], came[3], came[2], came[1]]), xs)


def partner(values, axis, mask):
    size = 2 if axis == "tp_1" else 4
    return lax.ppermute(values, axis, [(i, i ^ mask) for i in range(size)])


def sum_over_four(values, axis):
    return (values + partner(values, axis, 1)) + (
        partner(values, axis, 2) + partner(values, axis, 3)
    )


def sum_tp(values):
    return sum_over_four(values + partner(values, "tp_1", 1), "tp_0")


def sum_ctx(values):
    return sum_over_four(sum_over_four(values, "ctx_1"), "ctx_0")


def own_order(values, xs, cs):
    blocks = turned(values.reshape(N_X, 2, SHARD), xs)
    blocks = jnp.where(cs == 0, blocks, blocks[:, ::-1])
    return blocks.transpose(1, 0, 2)


def sent_to_all(array, axis):
    copies = jnp.broadcast_to(array, (lax.axis_size(axis), *array.shape))
    return lax.all_to_all(copies, axis, split_axis=0, concat_axis=0, tiled=True)


def rope_tables(positions):
    ladder = jnp.arange(HD // 2, dtype=f32)
    freqs = ROPE_BASE ** (-2.0 * ladder / HD)
    ratio = ORIG_CTX * freqs / (2.0 * math.pi)
    ramped = jnp.clip((ratio - YARN_ALPHA) / (YARN_BETA - YARN_ALPHA), 0.0, 1.0)
    inverse = freqs * (1.0 - ramped) / YARN_SCALE + freqs * ramped
    angles = inverse[:, None] * positions.astype(f32)[None, :]
    mscale = 0.1 * math.log(YARN_SCALE) + 1.0
    return (jnp.cos(angles) * mscale, jnp.sin(angles) * mscale)


def rotate_rows(values, cosine, sine):
    half = values.shape[0] // 2
    first, second = (values[:half], values[half:])
    return jnp.concatenate([first * cosine - second * sine, second * cosine + first * sine])


def rotate_lanes(values, cosine, sine):
    half = values.shape[1] // 2
    first, second = (values[:, :half], values[:, half:])
    return jnp.concatenate([first * cosine - second * sine, second * cosine + first * sine], axis=1)


def rms_norm(values, gain):
    return values * lax.rsqrt(jnp.mean(values * values, axis=-1, keepdims=True) + NORM_EPS) * gain


def contract_last(left, right):
    return lax.dot_general(left, right, (((1,), (1,)), ((), ())), preferred_element_type=f32)


def contract_first(left, right):
    return lax.dot_general(left, right, (((0,), (0,)), ((), ())), preferred_element_type=f32)


def contract(left, right):
    return jnp.dot(left, right, preferred_element_type=f32)


def combine_stats(former, latter):
    highest = jnp.maximum(former[0], latter[0])
    summed = former[1] * jnp.exp(former[0] - highest) + latter[1] * jnp.exp(latter[0] - highest)
    return jnp.stack([highest, summed, former[2] + latter[2]])


def contract_ft(weights, places):
    return lax.dot_general(weights, places, (((0,), (1,)), ((), ())), preferred_element_type=f32)


def contract_tf(features, weights):
    return lax.dot_general(features, weights, (((0,), (1,)), ((), ())), preferred_element_type=f32)


def heads_on_lanes(features):
    return jnp.concatenate([features[h * HD : (h + 1) * HD] for h in range(4)], axis=1)


def heads_on_rows(features):
    return jnp.concatenate(jnp.split(features, 4, axis=1))


VMEM_LIMIT = 50 * 1024 * 1024


GROUP = 4
KEYS = 128 * GROUP
STEPS = TOKENS // KEYS


def key_places(core_bit, spans):
    line = lax.broadcasted_iota(jnp.int32, (128, 1), 0)
    x = (spans[N_CTX] + line // SHARD) % N_X
    place = (x * 2 + (spans[N_CTX + 1] ^ core_bit)) * SHARD + line % SHARD
    return place >= 128, place % 128


def visible_keys(spans, places, step, own, start):
    lines = []
    for block in range(step * GROUP, (step + 1) * GROUP):
        span = spans[block % N_CTX]
        second, within = places[block // N_CTX]
        lines.append(jnp.where(second, (2 * N_CTX - 1 - span) * 128, span * 128) + within)
    at = jnp.concatenate(lines, axis=0)
    return (at >= start) & (at <= own)


def key_columns(kv_ref, step, at):
    return jnp.concatenate(
        [kv_ref[step * GROUP + i, at : at + HD] for i in range(GROUP)], axis=1
    )


def attend_kernel(spans, own_ref, q_ref, kv_ref, o_ref, total_ref, s_ref):
    q = q_ref[...]
    own, start = (own_ref[0:1], own_ref[1:2])
    places = [key_places(core_bit, spans) for core_bit in range(2)]
    top = None
    for step in range(STEPS):
        scores = contract_first(key_columns(kv_ref, step, 0), q)
        scores = jnp.where(visible_keys(spans, places, step, own, start), scores, -1e30)
        s_ref[step * KEYS : (step + 1) * KEYS] = scores
        highest = jnp.max(scores, axis=0, keepdims=True)
        top = highest if top is None else jnp.maximum(top, highest)
    total = jnp.zeros(top.shape, f32)
    for step in range(STEPS):
        powers = jnp.exp(s_ref[step * KEYS : (step + 1) * KEYS] - top)
        s_ref[step * KEYS : (step + 1) * KEYS] = powers
        total = total + jnp.sum(powers, axis=0, keepdims=True)
    share = 1.0 / total
    out = jnp.zeros(q.shape, f32)
    for step in range(STEPS):
        weights = (s_ref[step * KEYS : (step + 1) * KEYS] * share).astype(bf16)
        out = out + contract(key_columns(kv_ref, step, HD), weights)
    o_ref[...] = out.astype(bf16)
    total_ref[...] = top + jnp.log(total)


SPLIT = 2


def attend(spans, own, q, kv):
    lanes = q.shape[1] // SPLIT
    column = lambda rows: pl.BlockSpec((rows, lanes), lambda i: (0, i))
    return pl.pallas_call(
        attend_kernel,
        grid=(SPLIT,),
        in_specs=[
            pl.BlockSpec(memory_space=pltpu.SMEM),
            column(2),
            column(HD),
            pl.BlockSpec(kv.shape, lambda i: (0, 0, 0)),
        ],
        out_specs=[column(HD), column(1)],
        out_shape=[
            jax.ShapeDtypeStruct(q.shape, bf16),
            jax.ShapeDtypeStruct((1, q.shape[1]), f32),
        ],
        scratch_shapes=[pltpu.VMEM((TOKENS, lanes), f32)],
        compiler_params=pltpu.CompilerParams(vmem_limit_bytes=VMEM_LIMIT),
        cost_estimate=pl.CostEstimate(
            flops=16 * TOKENS * q.shape[1] * HD, bytes_accessed=2 << 20, transcendentals=0
        ),
    )(spans, own, q, kv)


def attend_back_kernel(
    spans, own_ref, q_ref, do_ref, total_ref, kv_ref, dq_ref, dkv_ref, p_ref, dp_ref
):
    q, do = (q_ref[...], do_ref[...])
    own, start = (own_ref[0:1], own_ref[1:2])
    total = total_ref[...]
    places = [key_places(core_bit, spans) for core_bit in range(2)]
    rowsum = jnp.zeros(total.shape, f32)
    for step in range(STEPS):
        scores = contract_first(key_columns(kv_ref, step, 0), q)
        scores = jnp.where(visible_keys(spans, places, step, own, start), scores, -1e30)
        probs = jnp.exp(scores - total)
        probs_grad = contract_first(key_columns(kv_ref, step, HD), do)
        p_ref[step * KEYS : (step + 1) * KEYS] = probs
        dp_ref[step * KEYS : (step + 1) * KEYS] = probs_grad
        rowsum = rowsum + jnp.sum(probs * probs_grad, axis=0, keepdims=True)

    @pl.when(pl.program_id(0) == 0)
    def _():
        dkv_ref[...] = jnp.zeros(dkv_ref.shape, f32)

    dq = jnp.zeros(q.shape, f32)
    for step in range(STEPS):
        rows = slice(step * KEYS, (step + 1) * KEYS)
        probs = p_ref[rows]
        score_grad = (probs * (dp_ref[rows] - rowsum)).astype(bf16)
        dkv_ref[rows] += jnp.concatenate(
            [contract_last(score_grad, q), contract_last(probs.astype(bf16), do)], axis=1
        )
        dq = dq + contract(key_columns(kv_ref, step, 0), score_grad)
    dq_ref[...] = dq * (1.0 / math.sqrt(HD))


def attend_back(spans, own, q, do, total, kv):
    lanes = q.shape[1] // SPLIT
    column = lambda rows: pl.BlockSpec((rows, lanes), lambda i: (0, i))
    return pl.pallas_call(
        attend_back_kernel,
        grid=(SPLIT,),
        in_specs=[
            pl.BlockSpec(memory_space=pltpu.SMEM),
            column(2),
            column(HD),
            column(HD),
            column(1),
            pl.BlockSpec(kv.shape, lambda i: (0, 0, 0)),
        ],
        out_specs=[column(HD), pl.BlockSpec((TOKENS, 2 * HD), lambda i: (0, 0))],
        out_shape=[
            jax.ShapeDtypeStruct(q.shape, f32),
            jax.ShapeDtypeStruct((TOKENS, 2 * HD), f32),
        ],
        scratch_shapes=[pltpu.VMEM((TOKENS, lanes), f32), pltpu.VMEM((TOKENS, lanes), f32)],
        compiler_params=pltpu.CompilerParams(vmem_limit_bytes=VMEM_LIMIT),
        cost_estimate=pl.CostEstimate(
            flops=40 * TOKENS * q.shape[1] * HD, bytes_accessed=4 << 20, transcendentals=0
        ),
    )(spans, own, q, do, total, kv)


def moments(old, sums, count):
    return MOMENT_DECAY * old + (1.0 - MOMENT_DECAY) * (sums / count + MOMENT_EPS)


def params():
    return pltpu.CompilerParams(vmem_limit_bytes=VMEM_LIMIT)


def whole(array):
    zeros = (0,) * array.ndim
    return pl.BlockSpec(array.shape, lambda *i: zeros)


def cost(flops, moved):
    return pl.CostEstimate(flops=flops, bytes_accessed=moved, transcendentals=0)


ID_STEP = 1024


def look_kernel(ids_ref, table_ref, out_ref, low_ref):
    @pl.when(pl.program_id(0) == 0)
    def _():
        low_ref[...] = table_ref[0].astype(bf16)

    width = low_ref.shape[0]
    ids = jnp.transpose(jnp.broadcast_to(ids_ref[...], (8, ID_STEP)))[:, :1]
    hits = ids == lax.broadcasted_iota(jnp.int32, (ID_STEP, width), 1)
    out_ref[...] = contract(jnp.where(hits, 1.0, 0.0).astype(bf16), low_ref[...]).astype(bf16)


def look_up(ids, tables):
    width, lines = tables.shape[1:]
    count = ids.shape[1]
    return pl.pallas_call(
        look_kernel,
        grid=(count // ID_STEP,),
        in_specs=[
            pl.BlockSpec((1, ID_STEP), lambda i: (0, i)),
            pl.BlockSpec((1, width, lines), lambda i: (1, 0, 0)),
        ],
        out_specs=pl.BlockSpec((ID_STEP, lines), lambda i: (i, 0)),
        out_shape=jax.ShapeDtypeStruct((count, lines), bf16),
        scratch_shapes=[pltpu.VMEM((width, lines), bf16)],
        compiler_params=params(),
        cost_estimate=cost(4 * count * width * lines, 4 * lines * width),
    )(ids, tables)


def add_kernel(ids_ref, grads_ref, out_ref):
    hits = lax.broadcasted_iota(jnp.int32, (out_ref.shape[0], ID_STEP), 0) == ids_ref[...]
    added = contract(jnp.where(hits, 1.0, 0.0).astype(bf16), grads_ref[...])

    @pl.when(pl.program_id(0) == 0)
    def _():
        out_ref[...] = added

    @pl.when(pl.program_id(0) > 0)
    def _():
        out_ref[...] += added


def add_up(ids, grads, width):
    count, lines = grads.shape
    return pl.pallas_call(
        add_kernel,
        grid=(count // ID_STEP,),
        in_specs=[
            pl.BlockSpec((1, ID_STEP), lambda i: (0, i)),
            pl.BlockSpec((ID_STEP, lines), lambda i: (i, 0)),
        ],
        out_specs=pl.BlockSpec((width, lines), lambda i: (0, 0)),
        out_shape=jax.ShapeDtypeStruct((width, lines), f32),
        compiler_params=params(),
        cost_estimate=cost(4 * count * width * lines, 4 * lines * width),
    )(ids, grads)


LOGIT_STEP = 800


def logits_kernel(c_ref, w_ref, target_ref, out_ref, stats_ref):
    step = pl.program_id(0)
    logits = contract_last(w_ref[...], c_ref[...])
    out_ref[...] = logits
    row = lax.broadcasted_iota(jnp.int32, logits.shape, 0) + step * LOGIT_STEP
    here = jnp.max(logits, axis=0, keepdims=True)
    pick = jnp.sum(jnp.where(row == target_ref[...], logits, 0.0), axis=0, keepdims=True)

    @pl.when(step == 0)
    def _():
        stats_ref[...] = jnp.zeros(stats_ref.shape, f32)
        stats_ref[0:1] = here

    old = stats_ref[0:1]
    top = jnp.maximum(old, here)
    powers = jnp.sum(jnp.exp(logits - top), axis=0, keepdims=True)
    stats_ref[1:2] = stats_ref[1:2] * jnp.exp(old - top) + powers
    stats_ref[2:3] += pick
    stats_ref[0:1] = top


def logits_and_stats(c, head, targets):
    places, rows = c.shape
    width = head.shape[0]
    return pl.pallas_call(
        logits_kernel,
        grid=(width // LOGIT_STEP,),
        in_specs=[whole(c), pl.BlockSpec((LOGIT_STEP, rows), lambda i: (i, 0)), whole(targets)],
        out_specs=[
            pl.BlockSpec((LOGIT_STEP, places), lambda i: (i, 0)),
            pl.BlockSpec((8, places), lambda i: (0, 0)),
        ],
        out_shape=[
            jax.ShapeDtypeStruct((width, places), f32),
            jax.ShapeDtypeStruct((8, places), f32),
        ],
        compiler_params=params(),
        cost_estimate=cost(2 * places * rows * width, 2 * rows * width),
    )(c, head, targets)


def logit_grads_kernel(logits_ref, c_ref, w_ref, place_ref, target_ref, dw_ref, dc_ref):
    step = pl.program_id(0)
    logits = logits_ref[...]
    row = lax.broadcasted_iota(jnp.int32, logits.shape, 0) + step * LOGIT_STEP
    hit = row == target_ref[...]
    shares = jnp.exp(logits - place_ref[0:1]) - jnp.where(hit, 1.0, 0.0)
    low = (place_ref[1:2] * shares).astype(bf16)
    grad = contract(low, c_ref[...]).astype(bf16)
    for k in range(N_CTX):
        dw_ref[k] = grad[:, k * 128 : (k + 1) * 128]
    part = contract_first(low, w_ref[...])

    @pl.when(step == 0)
    def _():
        dc_ref[...] = part

    @pl.when(step > 0)
    def _():
        dc_ref[...] += part


def logit_grads(logits, c, head, place, targets):
    places, rows = c.shape
    width = head.shape[0]
    return pl.pallas_call(
        logit_grads_kernel,
        grid=(width // LOGIT_STEP,),
        in_specs=[
            pl.BlockSpec((LOGIT_STEP, places), lambda i: (i, 0)),
            whole(c),
            pl.BlockSpec((LOGIT_STEP, rows), lambda i: (i, 0)),
            whole(place),
            whole(targets),
        ],
        out_specs=[
            pl.BlockSpec((N_CTX, LOGIT_STEP, 128), lambda i: (0, i, 0)),
            pl.BlockSpec((places, rows), lambda i: (0, 0)),
        ],
        out_shape=[
            jax.ShapeDtypeStruct((N_CTX, width, 128), bf16),
            jax.ShapeDtypeStruct((places, rows), f32),
        ],
        compiler_params=params(),
        cost_estimate=cost(4 * places * rows * width, 4 * rows * width),
    )(logits, c, head, place, targets)


def products_kernel(count, offsets, *refs):
    lefts, rights = (refs[:count], refs[count : 2 * count])
    out_ref, turned_ref = refs[2 * count :]

    @pl.when(pl.program_id(0) == 0)
    def _():
        for right, (at, width) in zip(rights, offsets):
            turned_ref[at : at + width] = jnp.transpose(right[...])

    for left, (at, width) in zip(lefts, offsets):
        grad = contract(turned_ref[at : at + width], left[...]).astype(bf16)
        for k in range(2):
            out_ref[k, at : at + width] = grad[:, k * 128 : (k + 1) * 128]


def row_products(lefts, rights):
    places, rows = lefts[0].shape
    offsets, at = ([], 0)
    for right in rights:
        offsets.append((at, right.shape[1]))
        at += right.shape[1]
    return pl.pallas_call(
        functools.partial(products_kernel, len(lefts), tuple(offsets)),
        grid=(N_CTX // 2,),
        in_specs=[pl.BlockSpec((places, 256), lambda i: (0, i)) for _ in lefts]
        + [whole(right) for right in rights],
        out_specs=pl.BlockSpec((2, at, 128), lambda i: (i, 0, 0)),
        out_shape=jax.ShapeDtypeStruct((N_CTX, at, rows // N_CTX), bf16),
        scratch_shapes=[pltpu.VMEM((at, places), bf16)],
        compiler_params=params(),
        cost_estimate=cost(2 * places * rows * at, 2 * rows * at),
    )(*lefts, *rights)


MATRICES = 8
WIDTHS = (HQ, HQ, FF, FF, FF, VOCAB, VOCAB, KVW)
COLUMN_LANES = 4096
COLUMN_AT = {0: (2, 2432, 256), 1: (2, 1408, 256), 2: (2, 0, 704), 3: (2, 704, 704)}
COLUMN_AT.update({4: (2, 1664, 704), 5: (0, 0, 4000), 6: (1, 0, 4000), 7: (2, 2688, 128)})
S_LANE, T_LANE, OLD_LANE, W_LANE, WG_LANE, UG_LANE, LOSS_LANE = (0, 8, 16, 24, 32, 35, 38)


def lane_is(shape, lane):
    return lax.broadcasted_iota(jnp.int32, shape, 1) == lane


def line_sum(values):
    return jnp.sum(values, axis=0, keepdims=True)


def total_of(values):
    return jnp.sum(line_sum(values), axis=1, keepdims=True)


def column_sums(squares):
    ones = jnp.ones((8, squares.shape[1]), f32)
    return lax.dot_general(
        ones,
        squares,
        (((1,), (1,)), ((), ())),
        precision=lax.Precision.HIGHEST,
        preferred_element_type=f32,
    )


def vocab_kernel(head_ref, embed_ref, master_ref, grad_ref, lines_ref, columns_ref, scalars_ref):
    columns_ref[...] = jnp.zeros(columns_ref.shape, f32)
    scalars = jnp.zeros(scalars_ref.shape, f32)
    for k, ref in enumerate((head_ref, embed_ref)):
        grad = ref[...].astype(f32)
        grad_ref[k] = grad
        squares = grad * grad
        lines_ref[k : k + 1] = line_sum(squares)
        columns_ref[k : k + 1, : grad.shape[0]] = column_sums(squares)[:1]
        weights = master_ref[k]
        scalars += jnp.where(lane_is(scalars.shape, W_LANE + 5 + k), total_of(weights * weights), 0.0)
    scalars_ref[...] = scalars


def vocab_figures(head_low, embed, masters):
    shapes = (masters.shape, (2, 128), (2, COLUMN_LANES), (1, 128))
    return pl.pallas_call(
        vocab_kernel,
        out_shape=[jax.ShapeDtypeStruct(shape, f32) for shape in shapes],
        compiler_params=params(),
        cost_estimate=cost(0, 12 << 20),
    )(head_low, embed, masters)


def layer_kernel(
    layer_ref, late_ref, kv_ref, gains_ref, kv_old_ref, vocab_lines_ref, vocab_columns_ref,
    vocab_scalars_ref, feed_ref, attention_ref, kv_master_ref, gain_ref, loss_ref,
    feed_grad_ref, attention_grad_ref, lines_ref, columns_ref, scalars_ref,
):
    scalars = vocab_scalars_ref[...]
    columns_ref[0:2] = vocab_columns_ref[...]
    columns_ref[2:3] = jnp.zeros((1, COLUMN_LANES), f32)
    lines_ref[...] = jnp.zeros(lines_ref.shape, f32)
    lines_ref[5:7] = vocab_lines_ref[...]
    lines_ref[8:11] = gains_ref[...]
    lines_ref[11:12] = kv_old_ref[...]
    layer = layer_ref[...].astype(f32)
    late = late_ref[...]
    kv = kv_ref[...]
    attention_grad_ref[0] = jnp.transpose(late)
    attention_grad_ref[1] = jnp.transpose(layer[1408:1664])
    feed_grad_ref[0] = layer[0:704]
    feed_grad_ref[1] = layer[704:1408]
    feed_grad_ref[2] = layer[1664:2368]
    squares = layer * layer
    columns_ref[2:3, 0:2368] = column_sums(squares)[:1]
    for number, at, end in ((2, 0, 704), (3, 704, 1408), (1, 1408, 1664), (4, 1664, 2368)):
        lines_ref[number : number + 1] = line_sum(squares[at:end])
    squares = late * late
    columns_ref[2:3, 2432:2688] = column_sums(squares)[:1]
    lines_ref[0:1] = line_sum(squares)
    squares = kv * kv
    columns_ref[2:3, 2688:2816] = column_sums(squares)[:1]
    lines_ref[7:8] = 0.5 * line_sum(squares)
    for number, weights in (
        (0, attention_ref[0]),
        (1, attention_ref[1]),
        (2, feed_ref[0]),
        (3, feed_ref[1]),
        (4, feed_ref[2]),
        (7, kv_master_ref[...]),
        (8, gain_ref[0:1]),
        (9, gain_ref[1:2]),
        (10, gain_ref[2:3]),
    ):
        scalars += jnp.where(
            lane_is(scalars.shape, W_LANE + number), total_of(weights * weights), 0.0
        )
    scalars_ref[...] = scalars + jnp.where(lane_is(scalars.shape, LOSS_LANE), loss_ref[...], 0.0)


def layer_figures(layer, late, kv, gains, kv_old, vocab_parts, feed, attention, kv_master, gain, loss):
    shapes = (feed.shape, attention.shape, (16, 128), (3, COLUMN_LANES), (1, 128))
    return pl.pallas_call(
        layer_kernel,
        out_shape=[jax.ShapeDtypeStruct(shape, f32) for shape in shapes],
        compiler_params=params(),
        cost_estimate=cost(0, 8 << 20),
    )(layer, late, kv, gains, kv_old, *vocab_parts, feed, attention, kv_master, gain, loss)


def per_column(figures, number):
    line, at, width = COLUMN_AT[number]
    return figures[at : at + width, line : line + 1]


def on_rows(columns):
    return jnp.transpose(
        jnp.concatenate([columns, jnp.ones((5, columns.shape[1]), f32)], axis=0)
    )


def squares_kernel(
    vocab_ref, feed_ref, attention_ref, kv_ref, lines_ref, columns_ref, old_ref,
    old_columns_ref, base_ref, row_ref, column_ref, scalars_ref,
):
    lines = lines_ref[...]
    number = lax.broadcasted_iota(jnp.int32, lines.shape, 0)
    old = jnp.where(number == 7, lines_ref[11:12], old_ref[...])
    widths = jnp.full(lines.shape, 1.0, f32)
    for k, width in enumerate(WIDTHS):
        widths = jnp.where(number == k, float(width), widths)
    row_new = moments(old, lines / widths, 1.0)
    row_ref[...] = row_new
    column_new = moments(old_columns_ref[...], columns_ref[...], float(D))
    column_ref[...] = column_new
    weights = on_rows(1.0 / column_new)
    scalars = base_ref[...]
    had = jnp.sum(old, axis=1, keepdims=True) * (1.0 / N_TP)
    got = jnp.sum(lines, axis=1, keepdims=True) * (1.0 / N_TP)
    sources = (
        (0, jnp.transpose(attention_ref[0])),
        (1, jnp.transpose(attention_ref[1])),
        (2, feed_ref[0]),
        (3, feed_ref[1]),
        (4, feed_ref[2]),
        (5, vocab_ref[0]),
        (6, vocab_ref[1]),
        (7, kv_ref[...]),
    )
    for k, grad in sources:
        inner = line_sum(grad * grad * per_column(weights, k)) / row_new[k : k + 1]
        part = jnp.sum(inner, axis=1, keepdims=True) * (0.5 if k == 7 else 1.0)
        scalars += jnp.where(lane_is(scalars.shape, S_LANE + k), part, 0.0)
        scalars += jnp.where(lane_is(scalars.shape, T_LANE + k), got[k : k + 1], 0.0)
        scalars += jnp.where(lane_is(scalars.shape, OLD_LANE + k), had[k : k + 1], 0.0)
    scalars_ref[...] = scalars


def step_squares(vocab, feed, attention, kv, lines, columns, old, old_columns, base):
    return pl.pallas_call(
        squares_kernel,
        out_shape=[jax.ShapeDtypeStruct(a.shape, f32) for a in (lines, columns, base)],
        compiler_params=params(),
        cost_estimate=cost(0, 8 << 20),
    )(vocab, feed, attention, kv, lines, columns, old, old_columns, base)


UPDATE_STEP = 800


def update_kernel(
    all_ref, vocab_ref, vocab_grad_ref, feed_ref, feed_grad_ref, attention_ref,
    attention_grad_ref, row_ref, column_ref,
    vocab_new_ref, feed_new_ref, attention_new_ref, figures_ref, scale_ref,
):
    sums = jnp.sum(all_ref[...], axis=0, keepdims=True)
    sums = jnp.broadcast_to(sums, (8, 128))

    def lanes_from(at):
        return pltpu.roll(sums, (128 - at) % 128, 1)[0:1]

    lane = lax.broadcasted_iota(jnp.int32, (1, 128), 1)
    counts = jnp.full((1, 128), float(D), f32)
    for k, width in enumerate(WIDTHS):
        counts = jnp.where(lane == k, float(D * width), counts)
    mean = MOMENT_DECAY * lanes_from(OLD_LANE) / D + (1.0 - MOMENT_DECAY) * (
        lanes_from(T_LANE) / counts + MOMENT_EPS
    )
    mean = jnp.where(lane < MATRICES, mean, 1.0)
    rms = jnp.sqrt(mean * lanes_from(S_LANE) / counts)
    factor = (
        STEP_SCALE
        * jnp.sqrt(lanes_from(W_LANE) / counts)
        / jnp.maximum(1.0, rms / CLIP_LIMIT)
        * jnp.sqrt(mean)
    )
    row_scale = lax.rsqrt(row_ref[...])
    first = pl.program_id(0) == 0

    def stepped(master, grad, number, scale):
        tall = row_scale[number : number + 1] * factor[:, number : number + 1]
        return master - grad * tall * scale

    @pl.when(first)
    def _():
        scale = on_rows(lax.rsqrt(column_ref[...]))
        scale_ref[...] = scale
        for k in range(2):
            grad = jnp.transpose(attention_grad_ref[k])
            master = jnp.transpose(attention_ref[k])
            attention_new_ref[k] = jnp.transpose(stepped(master, grad, k, per_column(scale, k)))
        for k in range(3):
            feed_new_ref[k] = stepped(
                feed_ref[k], feed_grad_ref[k], 2 + k, per_column(scale, 2 + k)
            )
        gain_rms = jnp.sqrt(lanes_from(UG_LANE) / D)
        gain_factor = (
            STEP_SCALE
            * jnp.sqrt(lanes_from(WG_LANE) / D)
            / jnp.maximum(1.0, gain_rms / CLIP_LIMIT)
        )
        figures_ref[0:1] = rms
        figures_ref[1:2] = factor
        figures_ref[2:3] = gain_rms
        figures_ref[3:4] = gain_factor
        figures_ref[4:5] = lanes_from(LOSS_LANE)
        figures_ref[5:8] = jnp.zeros((3, 128), f32)

    rows = pl.ds(pl.multiple_of(pl.program_id(0) * UPDATE_STEP, UPDATE_STEP), UPDATE_STEP)
    scale = scale_ref[rows]
    for k in range(2):
        vocab_new_ref[k] = stepped(vocab_ref[k], vocab_grad_ref[k], 5 + k, scale[:, k : k + 1])


def update(gathered, vocab, vocab_grad, feed, feed_grad, attention, attention_grad, row_new, column_new):
    stack = pl.BlockSpec((2, UPDATE_STEP, vocab.shape[2]), lambda i: (0, i, 0))
    others = (feed, feed_grad, attention, attention_grad, row_new, column_new)
    figures = jax.ShapeDtypeStruct((8, 128), f32)
    return pl.pallas_call(
        update_kernel,
        grid=(vocab.shape[1] // UPDATE_STEP,),
        in_specs=[whole(gathered), stack, stack] + [whole(a) for a in others],
        out_specs=[stack, whole(feed), whole(attention), whole(figures)],
        out_shape=[jax.ShapeDtypeStruct(a.shape, f32) for a in (vocab, feed, attention)]
        + [figures],
        scratch_shapes=[pltpu.VMEM((COLUMN_LANES, 8), f32)],
        compiler_params=params(),
        cost_estimate=cost(0, 24 << 20),
    )(gathered, vocab, vocab_grad, *others)


def body(
    token_ids,
    target_ids,
    loss_mask,
    segment_ids,
    span_pairs,
    attention_master,
    feed_master,
    vocab_master,
    key_value_master,
    gain_master,
    attention_row_moment,
    attention_column_moment,
    feed_row_moment,
    feed_column_moment,
    vocab_row_moment,
    vocab_column_moment,
    key_value_row_moment,
    key_value_column_moment,
    gain_moment,
):
    ctx_index = lax.axis_index(CTX)
    xs = lax.axis_index("tp_0")
    cs = lax.axis_index("tp_1")
    tp_index = xs * 2 + cs
    vocab_here = vocab_master.shape[2]
    ff_here = feed_master.shape[2]
    first_id = tp_index * vocab_here

    attention_low = attention_master.astype(bf16)
    feed_low = feed_master.astype(bf16)
    layer_all = lax.all_gather(
        jnp.concatenate(
            [attention_low[0], attention_low[1], feed_low[0], feed_low[1], feed_low[2]], axis=1
        ),
        CTX,
        axis=0,
        tiled=True,
    )
    head = lax.all_gather(vocab_master[0].astype(bf16), CTX, axis=0, tiled=True)
    w_query = layer_all[:, :256]
    w_out = layer_all[:, 256:512]
    gate_up = layer_all[:, 512:1920]
    down = layer_all[:, 1920:]

    kv_low = key_value_master.astype(bf16).reshape(16, 2, KV_HEADS, HD).transpose(2, 0, 1, 3)
    gain_low = jnp.pad(gain_master.astype(bf16), ((0, 0), (0, 125)))
    blocks = jnp.concatenate(
        [
            kv_low.reshape(KV_HEADS, 16, 2 * HD),
            jnp.broadcast_to(gain_low, (KV_HEADS, *gain_low.shape)),
        ],
        axis=2,
    )
    ids_here = own_order(token_ids, xs, cs).reshape(1, 256)
    early = sent_to_all(
        jnp.concatenate(
            [
                both_cores(swapped_x(blocks, xs), cs),
                (ids_here // 256).astype(bf16),
                (ids_here % 256).astype(bf16),
                jnp.zeros((14, 256), bf16),
            ]
        ),
        CTX,
    )
    w_pair = early[:, :LINES, : 2 * HD].reshape(D, 2 * HD)
    gains = early[:, :LINES, 128:131].reshape(D, 3).astype(f32).T
    all_ids = (
        early[:, LINES].astype(jnp.int32) * 256 + early[:, LINES + 1].astype(jnp.int32)
    )
    all_ids = all_ids.reshape(N_CTX, 8, SHARD).transpose(1, 0, 2).reshape(1, TOKENS) - first_id

    order = (
        ((xs + jnp.arange(N_X, dtype=jnp.int32)) % N_X * 2)[None, :]
        + (cs ^ jnp.arange(2, dtype=jnp.int32))[:, None]
    )[:, :, None] * SHARD + jnp.arange(SHARD, dtype=jnp.int32)
    second_span = order >= 128
    within = order % 128
    own_pair = lax.dynamic_slice_in_dim(span_pairs, ctx_index, 1)[0]
    last_span = 2 * N_CTX - 1
    own_pos = (jnp.where(second_span, last_span - own_pair, own_pair) * 128 + within).reshape(-1)
    doc_start = jnp.zeros_like(own_pos)
    for k in range(1, DOCS):
        start = jnp.sum((segment_ids < k).astype(jnp.int32))
        doc_start = jnp.where(own_pos >= start, start, doc_start)
    cosine, sine = rope_tables(own_pos - doc_start)
    cosine_4, sine_4 = (jnp.tile(cosine, (1, 4)), jnp.tile(sine, (1, 4)))
    own_places = jnp.tile(jnp.stack([own_pos, doc_start]), (1, 4))
    spans = jnp.concatenate([span_pairs, jnp.stack([xs, cs]).astype(jnp.int32)])

    tables = vocab_master.transpose(0, 2, 1)
    looked = look_up(all_ids, tables).reshape(2, N_X, N_CTX, SHARD, LINES)
    half = looked[0] + core_swap(looked[1])
    mine = half[0]
    for d in range(1, N_X):
        mine = mine + x_to(half[d], d)
    rows_in = lax.all_to_all(mine, CTX, 0, 0, tiled=True)
    stream_in = rows_in.transpose(1, 0, 2).reshape(SHARD, D).astype(f32)

    normed_low = gather_tp(rms_norm(stream_in, gains[0]).astype(bf16))
    normed_half = normed_low[:128]
    keyval_linear = contract_ft(w_pair, normed_half)
    own_keyvals = jnp.concatenate(
        [rotate_rows(keyval_linear[:HD], cosine[:, :128], sine[:, :128]), keyval_linear[HD:]]
    ).astype(bf16)
    half_keyvals = sent_to_all(own_keyvals, CTX)
    row_keyvals = jnp.concatenate([half_keyvals, core_swap(half_keyvals)])
    query_linear = heads_on_lanes(contract_ft(w_query, normed_low))
    queries = rotate_rows(query_linear, cosine_4, sine_4).astype(bf16) * jnp.asarray(
        1.0 / math.sqrt(HD), bf16
    )
    attended, log_total = attend(spans, own_places, queries, row_keyvals)
    attended_rows = heads_on_rows(attended)
    stream_mid = stream_in + scatter_tp(
        contract_tf(attended_rows, w_out).reshape(2, N_X, SHARD, D)
    )

    inner_low = gather_tp(rms_norm(stream_mid, gains[1]).astype(bf16))
    both = contract(inner_low, gate_up)
    gate, upward = (both[:, :ff_here], both[:, ff_here:])
    sigmoid_gate = jax.nn.sigmoid(gate)
    silu_gate = gate * sigmoid_gate
    hidden_low = (silu_gate * upward).astype(bf16)
    stream_out = stream_mid + scatter_tp(
        contract_last(hidden_low, down).reshape(2, N_X, SHARD, D)
    )

    finals_low = gather_tp(rms_norm(stream_out, gains[2]).astype(bf16))
    local_targets = own_order(target_ids, xs, cs).reshape(1, -1) - first_id
    logits, stats = logits_and_stats(finals_low, head.T, local_targets)
    stats = stats[:3].reshape(3, 2, N_X, SHARD)
    stats = combine_stats(stats, core_swap(stats)[:, ::-1])
    others = [jnp.roll(x_from(stats, d), d, axis=2) for d in range(1, N_X)]
    stats = combine_stats(combine_stats(stats, others[0]), combine_stats(others[1], others[2]))
    stats = stats.reshape(3, -1)
    vocab_total = stats[0] + jnp.log(stats[1])
    keep = own_order(loss_mask, xs, cs).reshape(-1).astype(f32)
    loss_part = jnp.sum((keep * (vocab_total - stats[2]))[:SHARD]) / TOKENS

    place = jnp.stack([vocab_total, keep / TOKENS])
    head_low, final_part = logit_grads(logits, finals_low, head.T, place, local_targets)
    head_low = lax.psum_scatter(head_low, CTX, scatter_dimension=0, tiled=True)[0]
    final_grad = scatter_tp(final_part.reshape(2, N_X, SHARD, D))
    out_grad, final_gain_grad = jax.vjp(rms_norm, stream_out, gains[2])[1](final_grad)
    branch_low = gather_tp(out_grad.astype(bf16))
    hidden_grad = contract(branch_low, down)
    gate_grad_low = (
        hidden_grad * upward * sigmoid_gate * (1.0 + gate * (1.0 - sigmoid_gate))
    ).astype(bf16)
    upward_grad_low = (hidden_grad * silu_gate).astype(bf16)
    both_grad_low = jnp.concatenate([gate_grad_low, upward_grad_low], axis=1)
    inner_grad = scatter_tp(contract_last(both_grad_low, gate_up).reshape(2, N_X, SHARD, D))
    mid_part, middle_gain_grad = jax.vjp(rms_norm, stream_mid, gains[1])[1](inner_grad)
    mid_grad = out_grad + mid_part
    attend_low = gather_tp(mid_grad.astype(bf16))
    attended_grad = heads_on_lanes(contract_ft(w_out, attend_low).astype(bf16))
    dq, pair_grads = attend_back(
        spans, own_places, queries, attended_grad, log_total, row_keyvals
    )
    pair_grads = pair_grads.reshape(2, N_CTX, 128, 2 * HD)
    half_grads = pair_grads[0] + core_swap(pair_grads[1].astype(bf16)).astype(f32)
    came = lax.all_to_all(half_grads.astype(bf16), CTX, 0, 0, tiled=True)
    layer_low = row_products(
        [inner_low, attend_low, branch_low], [both_grad_low, attended_rows.T, hidden_low]
    )
    layer_low, head_low = lax.optimization_barrier((layer_low, head_low))
    layer_low = lax.psum_scatter(layer_low, CTX, scatter_dimension=0, tiled=True)[0]
    own_grads = jnp.sum(came.astype(f32), axis=0)
    keyval_low = jnp.concatenate(
        [
            rotate_lanes(own_grads[:, :HD], cosine[:, :128].T, -sine[:, :128].T),
            own_grads[:, HD:],
        ],
        axis=1,
    ).astype(bf16)
    query_linear_low = heads_on_rows(rotate_rows(dq, cosine_4, -sine_4).astype(bf16))
    normed_part = contract_tf(query_linear_low, w_query).reshape(2, 128, D)
    normed_part = jnp.stack([normed_part[0] + contract_last(keyval_low, w_pair), normed_part[1]])
    normed_grad = scatter_tp(normed_part.reshape(2, N_X, SHARD, D))
    late_grads = jnp.concatenate(
        [contract(query_linear_low, normed_low), contract_first(keyval_low, normed_half)]
    ).astype(bf16)
    late_grads = late_grads.reshape(384, N_CTX, LINES).transpose(1, 0, 2)
    late_sum = jnp.sum(
        lax.all_to_all(late_grads, CTX, 0, 0, tiled=True).astype(f32), axis=0
    )
    first_part, first_gain_grad = jax.vjp(rms_norm, stream_in, gains[0])[1](normed_grad)
    input_low = (mid_grad + first_part).astype(bf16)

    gain_parts = jnp.stack([first_gain_grad, middle_gain_grad, final_gain_grad]).astype(bf16)
    sent = jnp.concatenate(
        [
            input_low.reshape(SHARD, N_CTX, LINES).transpose(1, 0, 2),
            jnp.pad(gain_parts.reshape(3, N_CTX, LINES).transpose(1, 0, 2), ((0, 0), (0, 13), (0, 0))),
        ],
        axis=1,
    )
    arrived = lax.all_to_all(sent, CTX, 0, 0, tiled=True)
    gain_sums = jnp.sum(arrived[:, SHARD : SHARD + 3].astype(f32), axis=0)
    place_grads = gather_tp(arrived[:, :SHARD].reshape(N_CTX * SHARD, LINES))
    embed_grad = add_up(all_ids, place_grads, vocab_here)

    kv_part = late_sum[256:]
    kv_full = kv_part + core_swap(kv_part)
    kv_split = kv_full.T.reshape(N_X, 2, 16, 2 * HD)
    kv_owned = swapped_x(jnp.where(cs == 0, kv_split[:, 0], kv_split[:, 1]), xs)
    key_value_grad = (
        kv_owned.reshape(KV_HEADS, 16, 2, HD).transpose(1, 2, 0, 3).reshape(16, KVW)
    )

    old_rows = jnp.concatenate(
        [attention_row_moment, feed_row_moment, vocab_row_moment, jnp.ones((9, LINES), f32)]
    )
    kv_old_columns = lax.dynamic_index_in_dim(
        key_value_column_moment.reshape(2, KV_HEADS, HD), xs, 1, keepdims=False
    ).reshape(-1)
    layer_old = jnp.concatenate(
        [
            feed_column_moment[0],
            feed_column_moment[1],
            attention_column_moment[1],
            feed_column_moment[2],
            jnp.ones((64,), f32),
            attention_column_moment[0],
            kv_old_columns,
            jnp.ones((COLUMN_LANES - 2816,), f32),
        ]
    )
    old_columns = jnp.concatenate(
        [
            jnp.pad(vocab_column_moment, ((0, 0), (0, COLUMN_LANES - vocab_here)), constant_values=1.0),
            layer_old[None],
        ]
    )
    kv_old_line = lax.dynamic_update_slice_in_dim(
        jnp.zeros((1, LINES), f32), key_value_row_moment[None], tp_index * 16, 1
    )
    feed_tables = feed_master.transpose(0, 2, 1)
    vocab_grad, *vocab_parts = vocab_figures(head_low, embed_grad, tables)
    feed_grad, attention_grad, line_parts, column_parts, base = layer_figures(
        layer_low,
        late_sum[:256],
        kv_full,
        gain_sums,
        kv_old_line,
        vocab_parts,
        feed_tables,
        attention_master,
        key_value_master,
        gain_master.T,
        loss_part.reshape(1, 1),
    )
    lines = sum_tp(line_parts)
    columns = sum_ctx(column_parts)
    gain_grad = lax.dynamic_slice_in_dim(lines[8:11], tp_index * 16, 16, 1)
    gain_second = moments(gain_moment.T, gain_grad * gain_grad, 1.0)
    gain_step = gain_grad * lax.rsqrt(gain_second)
    gain_squares = jnp.sum(gain_step * gain_step, axis=1)[None]
    base = base + jnp.pad(gain_squares, ((0, 0), (UG_LANE, 128 - UG_LANE - 3)))
    row_new, column_new, scalars = step_squares(
        vocab_grad, feed_grad, attention_grad, kv_full, lines, columns, old_rows, old_columns, base
    )
    gathered = sent_to_all(scalars, CTX_TP).reshape(-1, 128)
    vocab_new, feed_new, attention_new, figures = update(
        gathered,
        tables,
        vocab_grad,
        feed_tables,
        feed_grad,
        attention_master,
        attention_grad,
        row_new,
        column_new,
    )
    token_loss = figures[4, 0]
    update_rms = jnp.concatenate([figures[0, :8], figures[2, :3]])
    kv_row_new = lax.dynamic_slice_in_dim(row_new[7], tp_index * 16, 16, 0)
    kv_columns_here = column_new[2, 2688:2816]
    kv_column_new = (
        to_absolute(
            jnp.stack([kv_columns_here] + [x_from(kv_columns_here, d) for d in range(1, N_X)]), xs
        )
        .reshape(KV_HEADS, 2, HD)
        .transpose(1, 0, 2)
        .reshape(KVW)
    )
    kv_tall = figures[1, 7] * lax.rsqrt(kv_row_new)
    kv_new = key_value_master - key_value_grad * kv_tall[:, None] * lax.rsqrt(kv_column_new)[None]
    gain_new = gain_master - figures[3, :3][None] * gain_step.T
    attention_columns = jnp.stack([column_new[2, 2432:2688], column_new[2, 1408:1664]])
    feed_columns = jnp.stack(
        [column_new[2, :704], column_new[2, 704:1408], column_new[2, 1664:2368]]
    )
    return (
        token_loss,
        update_rms,
        attention_grad,
        row_new[0:2],
        attention_columns,
        attention_new,
        feed_grad.transpose(0, 2, 1),
        row_new[2:5],
        feed_columns,
        feed_new.transpose(0, 2, 1),
        vocab_grad.transpose(0, 2, 1),
        row_new[5:7],
        column_new[0, :vocab_here],
        column_new[1, :vocab_here],
        vocab_new.transpose(0, 2, 1),
        key_value_grad,
        kv_row_new,
        kv_column_new,
        kv_new,
        gain_grad.T,
        gain_second.T,
        gain_new,
    )


def solution(mesh):
    finer = Mesh(mesh.devices.reshape(4, 4, 4, 2), ("ctx_0", "ctx_1", "tp_0", "tp_1"))
    in_specs = (
        P(CTX),
        P(CTX),
        P(CTX),
        P(),
        P(),
        P(None, CTX, TP),
        P(None, CTX, TP),
        P(None, CTX, TP),
        P(CTX_TP, None),
        P(CTX_TP, None),
        P(None, CTX),
        P(None, TP),
        P(None, CTX),
        P(None, TP),
        P(None, CTX),
        P(None, TP),
        P(CTX_TP),
        P(),
        P(CTX_TP, None),
    )
    out_specs = (
        P(),
        P(),
        P(None, CTX, TP),
        P(None, CTX),
        P(None, TP),
        P(None, CTX, TP),
        P(None, CTX, TP),
        P(None, CTX),
        P(None, TP),
        P(None, CTX, TP),
        P(None, CTX, TP),
        P(None, CTX),
        P(TP),
        P(TP),
        P(None, CTX, TP),
        P(CTX_TP, None),
        P(CTX_TP),
        P(),
        P(CTX_TP, None),
        P(CTX_TP, None),
        P(CTX_TP, None),
        P(CTX_TP, None),
    )
    return jax.shard_map(body, mesh=finer, in_specs=in_specs, out_specs=out_specs, check_vma=False)
```

```python
import functools
import math

import jax
import jax.numpy as jnp
from jax import lax
from jax.experimental import pallas as pl
from jax.experimental.pallas import tpu as pltpu
from jax.sharding import Mesh
from jax.sharding import PartitionSpec as P

D = 2048
HEADS = 32
KV_HEADS = 4
HD = 64
FF = 5632
VOCAB = 32000
ORIG_CTX = 2048
HQ = 2048
KVW = 512
TOKENS = 4096
TP = ("tp_0", "tp_1")
CTX = ("ctx_0", "ctx_1")
CTX_TP = ("ctx_0", "ctx_1", "tp_0", "tp_1")
N_CTX = 16
N_X = 4
N_TP = 8
SHARD = 32
LINES = 128
DOCS = 5

NORM_EPS = 1e-05
MOMENT_DECAY = 0.5
MOMENT_EPS = 1e-30
CLIP_LIMIT = 0.5
STEP_SCALE = 1.0
ROPE_BASE = 10000.0
YARN_SCALE = 4.0
YARN_ALPHA = 1.0
YARN_BETA = 32.0

bf16 = jnp.bfloat16
f32 = jnp.float32


def x_from(values, step):
    return lax.ppermute(values, "tp_0", [((i + step) % N_X, i) for i in range(N_X)])


def x_to(values, step):
    return lax.ppermute(values, "tp_0", [(i, (i + step) % N_X) for i in range(N_X)])


def core_swap(values):
    return lax.ppermute(values, "tp_1", [(0, 1), (1, 0)])


def turned(stack, start):
    return lax.dynamic_slice_in_dim(jnp.concatenate([stack, stack]), start, N_X, 0)


def to_absolute(stack, xs):
    return turned(stack, (N_X - xs) % N_X)


def gather_tp(shard):
    column = jnp.concatenate([shard] + [x_from(shard, d) for d in range(1, N_X)])
    return jnp.concatenate([column, core_swap(column)])


def scatter_tp(partial):
    half = partial[0] + core_swap(partial[1].astype(bf16)).astype(f32)
    low = half.astype(bf16)
    total = half[0]
    for d in range(1, N_X):
        total = total + x_to(low[d], d).astype(f32)
    return total


def both_cores(column, cs):
    other = core_swap(column)
    both = jnp.where(
        cs == 0, jnp.stack([column, other], axis=1), jnp.stack([other, column], axis=1)
    )
    return both.reshape(-1, *column.shape[2:])


def swapped_x(blocks, xs):
    ours = turned(blocks, xs)
    came = [ours[0]] + [x_to(ours[d], d) for d in range(1, N_X)]
    return to_absolute(jnp.stack([came[0], came[3], came[2], came[1]]), xs)


def partner(values, axis, mask):
    size = 2 if axis == "tp_1" else 4
    return lax.ppermute(values, axis, [(i, i ^ mask) for i in range(size)])


def sum_over_four(values, axis):
    return (values + partner(values, axis, 1)) + (
        partner(values, axis, 2) + partner(values, axis, 3)
    )


def sum_tp(values):
    return sum_over_four(values + partner(values, "tp_1", 1), "tp_0")


def sum_ctx(values):
    return sum_over_four(sum_over_four(values, "ctx_1"), "ctx_0")


def own_order(values, xs, cs):
    blocks = turned(values.reshape(N_X, 2, SHARD), xs)
    blocks = jnp.where(cs == 0, blocks, blocks[:, ::-1])
    return blocks.transpose(1, 0, 2)


def sent_to_all(array, axis):
    copies = jnp.broadcast_to(array, (lax.axis_size(axis), *array.shape))
    return lax.all_to_all(copies, axis, split_axis=0, concat_axis=0, tiled=True)


def rope_tables(positions):
    ladder = jnp.arange(HD // 2, dtype=f32)
    freqs = ROPE_BASE ** (-2.0 * ladder / HD)
    ratio = ORIG_CTX * freqs / (2.0 * math.pi)
    ramped = jnp.clip((ratio - YARN_ALPHA) / (YARN_BETA - YARN_ALPHA), 0.0, 1.0)
    inverse = freqs * (1.0 - ramped) / YARN_SCALE + freqs * ramped
    angles = inverse[:, None] * positions.astype(f32)[None, :]
    mscale = 0.1 * math.log(YARN_SCALE) + 1.0
    return (jnp.cos(angles) * mscale, jnp.sin(angles) * mscale)


def rotate_rows(values, cosine, sine):
    half = values.shape[0] // 2
    first, second = (values[:half], values[half:])
    return jnp.concatenate([first * cosine - second * sine, second * cosine + first * sine])


def rotate_lanes(values, cosine, sine):
    half = values.shape[1] // 2
    first, second = (values[:, :half], values[:, half:])
    return jnp.concatenate([first * cosine - second * sine, second * cosine + first * sine], axis=1)


def rms_norm(values, gain):
    return values * lax.rsqrt(jnp.mean(values * values, axis=-1, keepdims=True) + NORM_EPS) * gain


def contract_last(left, right):
    return lax.dot_general(left, right, (((1,), (1,)), ((), ())), preferred_element_type=f32)


def contract_first(left, right):
    return lax.dot_general(left, right, (((0,), (0,)), ((), ())), preferred_element_type=f32)


def contract(left, right):
    return jnp.dot(left, right, preferred_element_type=f32)


def combine_stats(former, latter):
    highest = jnp.maximum(former[0], latter[0])
    summed = former[1] * jnp.exp(former[0] - highest) + latter[1] * jnp.exp(latter[0] - highest)
    return jnp.stack([highest, summed, former[2] + latter[2]])


def contract_ft(weights, places):
    return lax.dot_general(weights, places, (((0,), (1,)), ((), ())), preferred_element_type=f32)


def contract_tf(features, weights):
    return lax.dot_general(features, weights, (((0,), (1,)), ((), ())), preferred_element_type=f32)


def heads_on_lanes(features):
    return jnp.concatenate([features[h * HD : (h + 1) * HD] for h in range(4)], axis=1)


def heads_on_rows(features):
    return jnp.concatenate(jnp.split(features, 4, axis=1))


VMEM_LIMIT = 50 * 1024 * 1024


GROUP = 4
KEYS = 128 * GROUP
STEPS = TOKENS // KEYS


def key_places(core_bit, spans):
    line = lax.broadcasted_iota(jnp.int32, (128, 1), 0)
    x = (spans[N_CTX] + line // SHARD) % N_X
    place = (x * 2 + (spans[N_CTX + 1] ^ core_bit)) * SHARD + line % SHARD
    return place >= 128, place % 128


def visible_keys(spans, places, step, own, start):
    lines = []
    for block in range(step * GROUP, (step + 1) * GROUP):
        span = spans[block % N_CTX]
        second, within = places[block // N_CTX]
        lines.append(jnp.where(second, (2 * N_CTX - 1 - span) * 128, span * 128) + within)
    at = jnp.concatenate(lines, axis=0)
    return (at >= start) & (at <= own)


def key_columns(kv_ref, step, at):
    return jnp.concatenate(
        [kv_ref[step * GROUP + i, at : at + HD] for i in range(GROUP)], axis=1
    )


def attend_kernel(spans, own_ref, q_ref, kv_ref, o_ref, total_ref, s_ref):
    q = q_ref[...]
    own, start = (own_ref[0:1], own_ref[1:2])
    places = [key_places(core_bit, spans) for core_bit in range(2)]
    top = None
    for step in range(STEPS):
        scores = contract_first(key_columns(kv_ref, step, 0), q)
        scores = jnp.where(visible_keys(spans, places, step, own, start), scores, -1e30)
        s_ref[step * KEYS : (step + 1) * KEYS] = scores
        highest = jnp.max(scores, axis=0, keepdims=True)
        top = highest if top is None else jnp.maximum(top, highest)
    total = jnp.zeros(top.shape, f32)
    for step in range(STEPS):
        powers = jnp.exp(s_ref[step * KEYS : (step + 1) * KEYS] - top)
        s_ref[step * KEYS : (step + 1) * KEYS] = powers
        total = total + jnp.sum(powers, axis=0, keepdims=True)
    share = 1.0 / total
    out = jnp.zeros(q.shape, f32)
    for step in range(STEPS):
        weights = (s_ref[step * KEYS : (step + 1) * KEYS] * share).astype(bf16)
        out = out + contract(key_columns(kv_ref, step, HD), weights)
    o_ref[...] = out.astype(bf16)
    total_ref[...] = top + jnp.log(total)


SPLIT = 2


def attend(spans, own, q, kv):
    lanes = q.shape[1] // SPLIT
    column = lambda rows: pl.BlockSpec((rows, lanes), lambda i: (0, i))
    return pl.pallas_call(
        attend_kernel,
        grid=(SPLIT,),
        in_specs=[
            pl.BlockSpec(memory_space=pltpu.SMEM),
            column(2),
            column(HD),
            pl.BlockSpec(kv.shape, lambda i: (0, 0, 0)),
        ],
        out_specs=[column(HD), column(1)],
        out_shape=[
            jax.ShapeDtypeStruct(q.shape, bf16),
            jax.ShapeDtypeStruct((1, q.shape[1]), f32),
        ],
        scratch_shapes=[pltpu.VMEM((TOKENS, lanes), f32)],
        compiler_params=pltpu.CompilerParams(vmem_limit_bytes=VMEM_LIMIT),
        cost_estimate=pl.CostEstimate(
            flops=16 * TOKENS * q.shape[1] * HD, bytes_accessed=2 << 20, transcendentals=0
        ),
    )(spans, own, q, kv)


def attend_back_kernel(
    spans, own_ref, q_ref, do_ref, total_ref, kv_ref, dq_ref, dkv_ref, p_ref, dp_ref
):
    q, do = (q_ref[...], do_ref[...])
    own, start = (own_ref[0:1], own_ref[1:2])
    total = total_ref[...]
    places = [key_places(core_bit, spans) for core_bit in range(2)]
    rowsum = jnp.zeros(total.shape, f32)
    for step in range(STEPS):
        scores = contract_first(key_columns(kv_ref, step, 0), q)
        scores = jnp.where(visible_keys(spans, places, step, own, start), scores, -1e30)
        probs = jnp.exp(scores - total)
        probs_grad = contract_first(key_columns(kv_ref, step, HD), do)
        p_ref[step * KEYS : (step + 1) * KEYS] = probs
        dp_ref[step * KEYS : (step + 1) * KEYS] = probs_grad
        rowsum = rowsum + jnp.sum(probs * probs_grad, axis=0, keepdims=True)

    @pl.when(pl.program_id(0) == 0)
    def _():
        dkv_ref[...] = jnp.zeros(dkv_ref.shape, f32)

    dq = jnp.zeros(q.shape, f32)
    for step in range(STEPS):
        rows = slice(step * KEYS, (step + 1) * KEYS)
        probs = p_ref[rows]
        score_grad = (probs * (dp_ref[rows] - rowsum)).astype(bf16)
        dkv_ref[rows] += jnp.concatenate(
            [contract_last(score_grad, q), contract_last(probs.astype(bf16), do)], axis=1
        )
        dq = dq + contract(key_columns(kv_ref, step, 0), score_grad)
    dq_ref[...] = dq * (1.0 / math.sqrt(HD))


def attend_back(spans, own, q, do, total, kv):
    lanes = q.shape[1] // SPLIT
    column = lambda rows: pl.BlockSpec((rows, lanes), lambda i: (0, i))
    return pl.pallas_call(
        attend_back_kernel,
        grid=(SPLIT,),
        in_specs=[
            pl.BlockSpec(memory_space=pltpu.SMEM),
            column(2),
            column(HD),
            column(HD),
            column(1),
            pl.BlockSpec(kv.shape, lambda i: (0, 0, 0)),
        ],
        out_specs=[column(HD), pl.BlockSpec((TOKENS, 2 * HD), lambda i: (0, 0))],
        out_shape=[
            jax.ShapeDtypeStruct(q.shape, f32),
            jax.ShapeDtypeStruct((TOKENS, 2 * HD), f32),
        ],
        scratch_shapes=[pltpu.VMEM((TOKENS, lanes), f32), pltpu.VMEM((TOKENS, lanes), f32)],
        compiler_params=pltpu.CompilerParams(vmem_limit_bytes=VMEM_LIMIT),
        cost_estimate=pl.CostEstimate(
            flops=40 * TOKENS * q.shape[1] * HD, bytes_accessed=4 << 20, transcendentals=0
        ),
    )(spans, own, q, do, total, kv)


def moments(old, sums, count):
    return MOMENT_DECAY * old + (1.0 - MOMENT_DECAY) * (sums / count + MOMENT_EPS)


def params():
    return pltpu.CompilerParams(vmem_limit_bytes=VMEM_LIMIT)


def whole(array):
    zeros = (0,) * array.ndim
    return pl.BlockSpec(array.shape, lambda *i: zeros)


def cost(flops, moved):
    return pl.CostEstimate(flops=flops, bytes_accessed=moved, transcendentals=0)


ID_STEP = 1024


def look_kernel(ids_ref, table_ref, out_ref, low_ref):
    @pl.when(pl.program_id(0) == 0)
    def _():
        low_ref[...] = table_ref[0].astype(bf16)

    width = low_ref.shape[0]
    ids = jnp.transpose(jnp.broadcast_to(ids_ref[...], (8, ID_STEP)))[:, :1]
    hits = ids == lax.broadcasted_iota(jnp.int32, (ID_STEP, width), 1)
    out_ref[...] = contract(jnp.where(hits, 1.0, 0.0).astype(bf16), low_ref[...]).astype(bf16)


def look_up(ids, tables):
    width, lines = tables.shape[1:]
    count = ids.shape[1]
    return pl.pallas_call(
        look_kernel,
        grid=(count // ID_STEP,),
        in_specs=[
            pl.BlockSpec((1, ID_STEP), lambda i: (0, i)),
            pl.BlockSpec((1, width, lines), lambda i: (1, 0, 0)),
        ],
        out_specs=pl.BlockSpec((ID_STEP, lines), lambda i: (i, 0)),
        out_shape=jax.ShapeDtypeStruct((count, lines), bf16),
        scratch_shapes=[pltpu.VMEM((width, lines), bf16)],
        compiler_params=params(),
        cost_estimate=cost(4 * count * width * lines, 4 * lines * width),
    )(ids, tables)


def add_kernel(ids_ref, grads_ref, out_ref):
    hits = lax.broadcasted_iota(jnp.int32, (out_ref.shape[0], ID_STEP), 0) == ids_ref[...]
    added = contract(jnp.where(hits, 1.0, 0.0).astype(bf16), grads_ref[...])

    @pl.when(pl.program_id(0) == 0)
    def _():
        out_ref[...] = added

    @pl.when(pl.program_id(0) > 0)
    def _():
        out_ref[...] += added


def add_up(ids, grads, width):
    count, lines = grads.shape
    return pl.pallas_call(
        add_kernel,
        grid=(count // ID_STEP,),
        in_specs=[
            pl.BlockSpec((1, ID_STEP), lambda i: (0, i)),
            pl.BlockSpec((ID_STEP, lines), lambda i: (i, 0)),
        ],
        out_specs=pl.BlockSpec((width, lines), lambda i: (0, 0)),
        out_shape=jax.ShapeDtypeStruct((width, lines), f32),
        compiler_params=params(),
        cost_estimate=cost(4 * count * width * lines, 4 * lines * width),
    )(ids, grads)


LOGIT_STEP = 800


def logits_kernel(c_ref, w_ref, target_ref, out_ref, stats_ref):
    step = pl.program_id(0)
    logits = contract_last(w_ref[...], c_ref[...])
    out_ref[...] = logits
    row = lax.broadcasted_iota(jnp.int32, logits.shape, 0) + step * LOGIT_STEP
    here = jnp.max(logits, axis=0, keepdims=True)
    pick = jnp.sum(jnp.where(row == target_ref[...], logits, 0.0), axis=0, keepdims=True)

    @pl.when(step == 0)
    def _():
        stats_ref[...] = jnp.zeros(stats_ref.shape, f32)
        stats_ref[0:1] = here

    old = stats_ref[0:1]
    top = jnp.maximum(old, here)
    powers = jnp.sum(jnp.exp(logits - top), axis=0, keepdims=True)
    stats_ref[1:2] = stats_ref[1:2] * jnp.exp(old - top) + powers
    stats_ref[2:3] += pick
    stats_ref[0:1] = top


def logits_and_stats(c, head, targets):
    places, rows = c.shape
    width = head.shape[0]
    return pl.pallas_call(
        logits_kernel,
        grid=(width // LOGIT_STEP,),
        in_specs=[whole(c), pl.BlockSpec((LOGIT_STEP, rows), lambda i: (i, 0)), whole(targets)],
        out_specs=[
            pl.BlockSpec((LOGIT_STEP, places), lambda i: (i, 0)),
            pl.BlockSpec((8, places), lambda i: (0, 0)),
        ],
        out_shape=[
            jax.ShapeDtypeStruct((width, places), f32),
            jax.ShapeDtypeStruct((8, places), f32),
        ],
        compiler_params=params(),
        cost_estimate=cost(2 * places * rows * width, 2 * rows * width),
    )(c, head, targets)


def head_grad_kernel(logits_ref, c_ref, place_ref, target_ref, dw_ref, low_ref):
    step = pl.program_id(0)
    logits = logits_ref[...]
    row = lax.broadcasted_iota(jnp.int32, logits.shape, 0) + step * LOGIT_STEP
    hit = row == target_ref[...]
    shares = jnp.exp(logits - place_ref[0:1]) - jnp.where(hit, 1.0, 0.0)
    low = (place_ref[1:2] * shares).astype(bf16)
    low_ref[...] = low
    grad = contract(low, c_ref[...]).astype(bf16)
    for k in range(N_CTX):
        dw_ref[k] = grad[:, k * 128 : (k + 1) * 128]


def head_grads(logits, c, place, targets):
    places, rows = c.shape
    width = logits.shape[0]
    block = pl.BlockSpec((LOGIT_STEP, places), lambda i: (i, 0))
    return pl.pallas_call(
        head_grad_kernel,
        grid=(width // LOGIT_STEP,),
        in_specs=[block, whole(c), whole(place), whole(targets)],
        out_specs=[pl.BlockSpec((N_CTX, LOGIT_STEP, 128), lambda i: (0, i, 0)), block],
        out_shape=[
            jax.ShapeDtypeStruct((N_CTX, width, 128), bf16),
            jax.ShapeDtypeStruct((width, places), bf16),
        ],
        compiler_params=params(),
        cost_estimate=cost(2 * places * rows * width, 2 * rows * width),
    )(logits, c, place, targets)


def products_kernel(count, offsets, *refs):
    lefts, rights = (refs[:count], refs[count : 2 * count])
    out_ref, turned_ref = refs[2 * count :]

    @pl.when(pl.program_id(0) == 0)
    def _():
        for right, (at, width) in zip(rights, offsets):
            turned_ref[at : at + width] = jnp.transpose(right[...])

    for left, (at, width) in zip(lefts, offsets):
        grad = contract(turned_ref[at : at + width], left[...]).astype(bf16)
        for k in range(2):
            out_ref[k, at : at + width] = grad[:, k * 128 : (k + 1) * 128]


def row_products(lefts, rights):
    places, rows = lefts[0].shape
    offsets, at = ([], 0)
    for right in rights:
        offsets.append((at, right.shape[1]))
        at += right.shape[1]
    return pl.pallas_call(
        functools.partial(products_kernel, len(lefts), tuple(offsets)),
        grid=(N_CTX // 2,),
        in_specs=[pl.BlockSpec((places, 256), lambda i: (0, i)) for _ in lefts]
        + [whole(right) for right in rights],
        out_specs=pl.BlockSpec((2, at, 128), lambda i: (i, 0, 0)),
        out_shape=jax.ShapeDtypeStruct((N_CTX, at, rows // N_CTX), bf16),
        scratch_shapes=[pltpu.VMEM((at, places), bf16)],
        compiler_params=params(),
        cost_estimate=cost(2 * places * rows * at, 2 * rows * at),
    )(*lefts, *rights)


MATRICES = 8
WIDTHS = (HQ, HQ, FF, FF, FF, VOCAB, VOCAB, KVW)
EARLY_LANES = 4096
LATE_LANES = 2432
COLUMN_AT = {0: (2, 0, 256), 7: (2, 256, 128), 5: (0, 0, 4000), 6: (1, 0, 4000)}
COLUMN_AT.update({2: (0, 0, 704), 3: (0, 704, 704), 1: (0, 1408, 256), 4: (0, 1664, 704)})
S_LANE, T_LANE, OLD_LANE, W_LANE, WG_LANE, UG_LANE, LOSS_LANE = (0, 8, 16, 24, 32, 35, 38)


def lane_is(shape, lane):
    return lax.broadcasted_iota(jnp.int32, shape, 1) == lane


def line_sum(values):
    return jnp.sum(values, axis=0, keepdims=True)


def total_of(values):
    return jnp.sum(line_sum(values), axis=1, keepdims=True)


def column_sums(squares):
    ones = jnp.ones((8, squares.shape[1]), f32)
    return lax.dot_general(
        ones,
        squares,
        (((1,), (1,)), ((), ())),
        precision=lax.Precision.HIGHEST,
        preferred_element_type=f32,
    )


def early_kernel(
    head_ref, embed_ref, late_ref, kv_ref, gains_ref, kv_old_ref, tables_ref, feed_ref,
    attention_ref, kv_master_ref, gain_ref, loss_ref,
    vocab_grad_ref, lines_ref, columns_ref, scalars_ref,
):
    columns_ref[...] = jnp.zeros(columns_ref.shape, f32)
    lines_ref[...] = jnp.zeros(lines_ref.shape, f32)
    lines_ref[8:11] = gains_ref[...]
    lines_ref[11:12] = kv_old_ref[...]
    for number, ref in ((5, head_ref), (6, embed_ref), (0, late_ref), (7, kv_ref)):
        grad = ref[...].astype(f32)
        if number in (5, 6):
            vocab_grad_ref[number - 5] = grad
        squares = grad * grad
        lines_ref[number : number + 1] = (0.5 if number == 7 else 1.0) * line_sum(squares)
        line, at, width = COLUMN_AT[number]
        columns_ref[line : line + 1, at : at + width] = column_sums(squares)[:1]
    scalars = jnp.where(lane_is(scalars_ref.shape, LOSS_LANE), loss_ref[...], 0.0)
    for number, weights in (
        (0, attention_ref[0]),
        (1, attention_ref[1]),
        (2, feed_ref[0]),
        (3, feed_ref[1]),
        (4, feed_ref[2]),
        (5, tables_ref[0]),
        (6, tables_ref[1]),
        (7, kv_master_ref[...]),
        (8, gain_ref[0:1]),
        (9, gain_ref[1:2]),
        (10, gain_ref[2:3]),
    ):
        scalars += jnp.where(
            lane_is(scalars.shape, W_LANE + number), total_of(weights * weights), 0.0
        )
    scalars_ref[...] = scalars


def early_figures(*arrays):
    tables = arrays[6]
    shapes = (tables.shape, (16, 128), (3, EARLY_LANES), (1, 128))
    return pl.pallas_call(
        early_kernel,
        out_shape=[jax.ShapeDtypeStruct(shape, f32) for shape in shapes],
        compiler_params=params(),
        cost_estimate=cost(0, 16 << 20),
    )(*arrays)


def late_kernel(layer_ref, q_ref, feed_grad_ref, attention_grad_ref, lines_ref, columns_ref):
    layer = layer_ref[...].astype(f32)
    squares = layer * layer
    lines_ref[...] = jnp.zeros(lines_ref.shape, f32)
    columns_ref[...] = jnp.zeros(columns_ref.shape, f32)
    columns_ref[:, : layer.shape[0]] = column_sums(squares)[:1]
    for number in range(1, 5):
        line, at, width = COLUMN_AT[number]
        lines_ref[number : number + 1] = line_sum(squares[at : at + width])
        if number > 1:
            feed_grad_ref[number - 2] = layer[at : at + width]
    attention_grad_ref[0] = jnp.transpose(q_ref[...])
    attention_grad_ref[1] = jnp.transpose(layer[1408:1664])


def late_figures(layer, q):
    shapes = ((3, 704, 128), (2, 128, 256), (8, 128), (1, LATE_LANES))
    return pl.pallas_call(
        late_kernel,
        out_shape=[jax.ShapeDtypeStruct(shape, f32) for shape in shapes],
        compiler_params=params(),
        cost_estimate=cost(0, 4 << 20),
    )(layer, q)


def per_column(figures, number):
    line, at, width = COLUMN_AT[number]
    return figures[at : at + width, line : line + 1]


def on_rows(columns):
    spare = 8 - columns.shape[0]
    return jnp.transpose(
        jnp.concatenate([columns, jnp.ones((spare, columns.shape[1]), f32)], axis=0)
    )


def squares_of(sources, lines, old, columns, old_columns, base, row_ref, column_ref, scalars_ref):
    number = lax.broadcasted_iota(jnp.int32, lines.shape, 0)
    widths = jnp.full(lines.shape, 1.0, f32)
    for k, width in enumerate(WIDTHS):
        widths = jnp.where(number == k, float(width), widths)
    row_new = moments(old, lines / widths, 1.0)
    row_ref[...] = row_new
    column_new = moments(old_columns, columns, float(D))
    column_ref[...] = column_new
    weights = on_rows(1.0 / column_new)
    scalars = base
    had = jnp.sum(old, axis=1, keepdims=True) * (1.0 / N_TP)
    got = jnp.sum(lines, axis=1, keepdims=True) * (1.0 / N_TP)
    for k, grad in sources:
        inner = line_sum(grad * grad * per_column(weights, k)) / row_new[k : k + 1]
        part = jnp.sum(inner, axis=1, keepdims=True) * (0.5 if k == 7 else 1.0)
        scalars += jnp.where(lane_is(scalars.shape, S_LANE + k), part, 0.0)
        scalars += jnp.where(lane_is(scalars.shape, T_LANE + k), got[k : k + 1], 0.0)
        scalars += jnp.where(lane_is(scalars.shape, OLD_LANE + k), had[k : k + 1], 0.0)
    scalars_ref[...] = scalars


def early_squares_kernel(
    vocab_ref, q_ref, kv_ref, lines_ref, columns_ref, old_ref, old_columns_ref, base_ref,
    row_ref, column_ref, scalars_ref,
):
    lines = lines_ref[...]
    number = lax.broadcasted_iota(jnp.int32, lines.shape, 0)
    old = jnp.where(number == 7, lines_ref[11:12], old_ref[...])
    sources = ((0, q_ref[...]), (5, vocab_ref[0]), (6, vocab_ref[1]), (7, kv_ref[...]))
    squares_of(
        sources, lines, old, columns_ref[...], old_columns_ref[...], base_ref[...],
        row_ref, column_ref, scalars_ref,
    )


def late_squares_kernel(
    layer_ref, lines_ref, columns_ref, old_ref, old_columns_ref, base_ref,
    row_ref, column_ref, scalars_ref,
):
    layer = layer_ref[...].astype(f32)
    sources = []
    for number in range(1, 5):
        line, at, width = COLUMN_AT[number]
        sources.append((number, layer[at : at + width]))
    columns = jnp.sum(columns_ref[...], axis=0)
    squares_of(
        sources, lines_ref[...], old_ref[0:8], columns, old_columns_ref[...], base_ref[...],
        row_ref, column_ref, scalars_ref,
    )


def step_squares(kernel, grads, lines, columns, old, old_columns, base):
    return pl.pallas_call(
        kernel,
        out_shape=[jax.ShapeDtypeStruct(a.shape, f32) for a in (lines, old_columns, base)],
        compiler_params=params(),
        cost_estimate=cost(0, 8 << 20),
    )(*grads, lines, columns, old, old_columns, base)


UPDATE_STEP = 800


def update_kernel(
    all_ref, vocab_ref, vocab_grad_ref, feed_ref, feed_grad_ref, attention_ref,
    attention_grad_ref, early_row_ref, late_row_ref, early_column_ref, late_column_ref, gain_ref,
    gain_step_ref,
    vocab_new_ref, feed_new_ref, attention_new_ref, gain_new_ref, figures_ref, scale_ref,
):
    sums = jnp.sum(all_ref[...], axis=0, keepdims=True)
    sums = jnp.broadcast_to(sums, (8, 128))

    def lanes_from(at):
        return pltpu.roll(sums, (128 - at) % 128, 1)[0:1]

    lane = lax.broadcasted_iota(jnp.int32, (1, 128), 1)
    counts = jnp.full((1, 128), float(D), f32)
    for k, width in enumerate(WIDTHS):
        counts = jnp.where(lane == k, float(D * width), counts)
    mean = MOMENT_DECAY * lanes_from(OLD_LANE) / D + (1.0 - MOMENT_DECAY) * (
        lanes_from(T_LANE) / counts + MOMENT_EPS
    )
    mean = jnp.where(lane < MATRICES, mean, 1.0)
    rms = jnp.sqrt(mean * lanes_from(S_LANE) / counts)
    factor = (
        STEP_SCALE
        * jnp.sqrt(lanes_from(W_LANE) / counts)
        / jnp.maximum(1.0, rms / CLIP_LIMIT)
        * jnp.sqrt(mean)
    )
    early_scale = lax.rsqrt(early_row_ref[...])
    late_scale = lax.rsqrt(late_row_ref[...])

    def stepped(master, grad, number, scale):
        row_scale = late_scale if 0 < number < 5 else early_scale
        tall = row_scale[number : number + 1] * factor[:, number : number + 1]
        return master - grad * tall * scale

    @pl.when(pl.program_id(0) == 0)
    def _():
        early = on_rows(lax.rsqrt(early_column_ref[...]))
        late = on_rows(lax.rsqrt(late_column_ref[...]))
        scale_ref[...] = early
        for k in range(2):
            grad = jnp.transpose(attention_grad_ref[k])
            master = jnp.transpose(attention_ref[k])
            scale = per_column(late if k else early, k)
            attention_new_ref[k] = jnp.transpose(stepped(master, grad, k, scale))
        for k in range(3):
            feed_new_ref[k] = stepped(feed_ref[k], feed_grad_ref[k], 2 + k, per_column(late, 2 + k))
        gain_rms = jnp.sqrt(lanes_from(UG_LANE) / D)
        gain_factor = (
            STEP_SCALE
            * jnp.sqrt(lanes_from(WG_LANE) / D)
            / jnp.maximum(1.0, gain_rms / CLIP_LIMIT)
        )
        for k in range(3):
            gain_new_ref[k : k + 1] = (
                gain_ref[k : k + 1] - gain_factor[:, k : k + 1] * gain_step_ref[k : k + 1]
            )
        after = pltpu.roll(jnp.broadcast_to(gain_rms, (8, 128)), MATRICES, 1)[0:1]
        figures_ref[0:1] = jnp.where(lane < MATRICES, rms, after)
        figures_ref[1:2] = factor
        figures_ref[2:3] = lanes_from(LOSS_LANE)
        figures_ref[3:8] = jnp.zeros((5, 128), f32)

    rows = pl.ds(pl.multiple_of(pl.program_id(0) * UPDATE_STEP, UPDATE_STEP), UPDATE_STEP)
    scale = scale_ref[rows]
    for k in range(2):
        vocab_new_ref[k] = stepped(vocab_ref[k], vocab_grad_ref[k], 5 + k, scale[:, k : k + 1])


def update(gathered, vocab, vocab_grad, feed, *others):
    stack = pl.BlockSpec((2, UPDATE_STEP, vocab.shape[2]), lambda i: (0, i, 0))
    attention, gain = (others[1], others[7])
    outs = (vocab, feed, attention, gain)
    return pl.pallas_call(
        update_kernel,
        grid=(vocab.shape[1] // UPDATE_STEP,),
        in_specs=[whole(gathered), stack, stack, whole(feed)] + [whole(a) for a in others],
        out_specs=[stack]
        + [whole(a) for a in outs[1:]]
        + [pl.BlockSpec((8, 128), lambda i: (0, 0))],
        out_shape=[jax.ShapeDtypeStruct(a.shape, f32) for a in outs]
        + [jax.ShapeDtypeStruct((8, 128), f32)],
        scratch_shapes=[pltpu.VMEM((EARLY_LANES, 8), f32)],
        compiler_params=params(),
        cost_estimate=cost(0, 24 << 20),
    )(gathered, vocab, vocab_grad, feed, *others)


def body(
    token_ids,
    target_ids,
    loss_mask,
    segment_ids,
    span_pairs,
    attention_master,
    feed_master,
    vocab_master,
    key_value_master,
    gain_master,
    attention_row_moment,
    attention_column_moment,
    feed_row_moment,
    feed_column_moment,
    vocab_row_moment,
    vocab_column_moment,
    key_value_row_moment,
    key_value_column_moment,
    gain_moment,
):
    ctx_index = lax.axis_index(CTX)
    xs = lax.axis_index("tp_0")
    cs = lax.axis_index("tp_1")
    tp_index = xs * 2 + cs
    vocab_here = vocab_master.shape[2]
    ff_here = feed_master.shape[2]
    first_id = tp_index * vocab_here

    attention_low = attention_master.astype(bf16)
    feed_low = feed_master.astype(bf16)
    layer_all = lax.all_gather(
        jnp.concatenate(
            [attention_low[0], attention_low[1], feed_low[0], feed_low[1], feed_low[2]], axis=1
        ),
        CTX,
        axis=0,
        tiled=True,
    )
    head = lax.all_gather(vocab_master[0].astype(bf16), CTX, axis=0, tiled=True)
    w_query = layer_all[:, :256]
    w_out = layer_all[:, 256:512]
    gate_up = layer_all[:, 512:1920]
    down = layer_all[:, 1920:]

    kv_low = key_value_master.astype(bf16).reshape(16, 2, KV_HEADS, HD).transpose(2, 0, 1, 3)
    gain_low = jnp.pad(gain_master.astype(bf16), ((0, 0), (0, 125)))
    blocks = jnp.concatenate(
        [
            kv_low.reshape(KV_HEADS, 16, 2 * HD),
            jnp.broadcast_to(gain_low, (KV_HEADS, *gain_low.shape)),
        ],
        axis=2,
    )
    ids_here = own_order(token_ids, xs, cs).reshape(1, 256)
    line_block = both_cores(swapped_x(blocks, xs), cs)
    early = sent_to_all(
        jnp.concatenate(
            [
                line_block[:, : 2 * HD],
                line_block[:, 2 * HD : 2 * HD + 3].T,
                (ids_here // 256).astype(bf16).reshape(2, 128),
                (ids_here % 256).astype(bf16).reshape(2, 128),
                jnp.zeros((9, 128), bf16),
            ]
        ),
        CTX,
    )
    w_pair = early[:, :LINES].reshape(D, 2 * HD)
    gains = early[:, LINES : LINES + 3].astype(f32).transpose(1, 0, 2).reshape(3, D)
    parts = early[:, LINES + 3 : LINES + 7].astype(jnp.int32).reshape(N_CTX, 2, 256)
    all_ids = parts[:, 0] * 256 + parts[:, 1]
    all_ids = all_ids.reshape(N_CTX, 8, SHARD).transpose(1, 0, 2).reshape(1, TOKENS) - first_id

    order = (
        ((xs + jnp.arange(N_X, dtype=jnp.int32)) % N_X * 2)[None, :]
        + (cs ^ jnp.arange(2, dtype=jnp.int32))[:, None]
    )[:, :, None] * SHARD + jnp.arange(SHARD, dtype=jnp.int32)
    second_span = order >= 128
    within = order % 128
    own_pair = lax.dynamic_slice_in_dim(span_pairs, ctx_index, 1)[0]
    last_span = 2 * N_CTX - 1
    own_pos = (jnp.where(second_span, last_span - own_pair, own_pair) * 128 + within).reshape(-1)
    doc_start = jnp.zeros_like(own_pos)
    for k in range(1, DOCS):
        start = jnp.sum((segment_ids < k).astype(jnp.int32))
        doc_start = jnp.where(own_pos >= start, start, doc_start)
    cosine, sine = rope_tables(own_pos - doc_start)
    cosine_4, sine_4 = (jnp.tile(cosine, (1, 4)), jnp.tile(sine, (1, 4)))
    own_places = jnp.tile(jnp.stack([own_pos, doc_start]), (1, 4))
    spans = jnp.concatenate([span_pairs, jnp.stack([xs, cs]).astype(jnp.int32)])

    tables = vocab_master.transpose(0, 2, 1)
    looked = look_up(all_ids, tables).reshape(2, N_X, N_CTX, SHARD, LINES)
    half = looked[0] + core_swap(looked[1])
    mine = half[0]
    for d in range(1, N_X):
        mine = mine + x_to(half[d], d)
    rows_in = lax.all_to_all(mine, CTX, 0, 0, tiled=True)
    stream_in = rows_in.transpose(1, 0, 2).reshape(SHARD, D).astype(f32)

    normed_low = gather_tp(rms_norm(stream_in, gains[0]).astype(bf16))
    normed_half = normed_low[:128]
    keyval_linear = contract_ft(w_pair, normed_half)
    own_keyvals = jnp.concatenate(
        [rotate_rows(keyval_linear[:HD], cosine[:, :128], sine[:, :128]), keyval_linear[HD:]]
    ).astype(bf16)
    half_keyvals = sent_to_all(own_keyvals, CTX)
    row_keyvals = jnp.concatenate([half_keyvals, core_swap(half_keyvals)])
    query_linear = heads_on_lanes(contract_ft(w_query, normed_low))
    queries = rotate_rows(query_linear, cosine_4, sine_4).astype(bf16) * jnp.asarray(
        1.0 / math.sqrt(HD), bf16
    )
    attended, log_total = attend(spans, own_places, queries, row_keyvals)
    attended_rows = heads_on_rows(attended)
    stream_mid = stream_in + scatter_tp(
        contract_tf(attended_rows, w_out).reshape(2, N_X, SHARD, D)
    )

    inner_low = gather_tp(rms_norm(stream_mid, gains[1]).astype(bf16))
    both = contract(inner_low, gate_up)
    gate, upward = (both[:, :ff_here], both[:, ff_here:])
    sigmoid_gate = jax.nn.sigmoid(gate)
    silu_gate = gate * sigmoid_gate
    hidden_low = (silu_gate * upward).astype(bf16)
    stream_out = stream_mid + scatter_tp(
        contract_last(hidden_low, down).reshape(2, N_X, SHARD, D)
    )

    finals_low = gather_tp(rms_norm(stream_out, gains[2]).astype(bf16))
    local_targets = own_order(target_ids, xs, cs).reshape(1, -1) - first_id
    logits, stats = logits_and_stats(finals_low, head.T, local_targets)
    stats = stats[:3].reshape(3, 2, N_X, SHARD)
    stats = combine_stats(stats, core_swap(stats)[:, ::-1])
    others = [jnp.roll(x_from(stats, d), d, axis=2) for d in range(1, N_X)]
    stats = combine_stats(combine_stats(stats, others[0]), combine_stats(others[1], others[2]))
    stats = stats.reshape(3, -1)
    vocab_total = stats[0] + jnp.log(stats[1])
    keep = own_order(loss_mask, xs, cs).reshape(-1).astype(f32)
    loss_part = jnp.sum((keep * (vocab_total - stats[2]))[:SHARD]) / TOKENS

    place = jnp.stack([vocab_total, keep / TOKENS])
    head_low, dlogits_low = head_grads(logits, finals_low, place, local_targets)
    head_low = lax.psum_scatter(head_low, CTX, scatter_dimension=0, tiled=True)[0]
    final_part = contract_first(dlogits_low, head.T)
    final_grad = scatter_tp(final_part.reshape(2, N_X, SHARD, D))
    out_grad, final_gain_grad = jax.vjp(rms_norm, stream_out, gains[2])[1](final_grad)
    branch_low = gather_tp(out_grad.astype(bf16))
    hidden_grad = contract(branch_low, down)
    gate_grad_low = (
        hidden_grad * upward * sigmoid_gate * (1.0 + gate * (1.0 - sigmoid_gate))
    ).astype(bf16)
    upward_grad_low = (hidden_grad * silu_gate).astype(bf16)
    both_grad_low = jnp.concatenate([gate_grad_low, upward_grad_low], axis=1)
    inner_grad = scatter_tp(contract_last(both_grad_low, gate_up).reshape(2, N_X, SHARD, D))
    mid_part, middle_gain_grad = jax.vjp(rms_norm, stream_mid, gains[1])[1](inner_grad)
    mid_grad = out_grad + mid_part
    attend_low = gather_tp(mid_grad.astype(bf16))
    attended_grad = heads_on_lanes(contract_ft(w_out, attend_low).astype(bf16))
    dq, pair_grads = attend_back(
        spans, own_places, queries, attended_grad, log_total, row_keyvals
    )
    pair_grads = pair_grads.reshape(2, N_CTX, 128, 2 * HD)
    half_grads = pair_grads[0] + core_swap(pair_grads[1].astype(bf16)).astype(f32)
    came = lax.all_to_all(half_grads.astype(bf16), CTX, 0, 0, tiled=True)
    layer_low = row_products(
        [inner_low, attend_low, branch_low], [both_grad_low, attended_rows.T, hidden_low]
    )
    own_grads = jnp.sum(came.astype(f32), axis=0)
    keyval_low = jnp.concatenate(
        [
            rotate_lanes(own_grads[:, :HD], cosine[:, :128].T, -sine[:, :128].T),
            own_grads[:, HD:],
        ],
        axis=1,
    ).astype(bf16)
    query_linear_low = heads_on_rows(rotate_rows(dq, cosine_4, -sine_4).astype(bf16))
    normed_part = contract_tf(query_linear_low, w_query).reshape(2, 128, D)
    normed_part = jnp.stack([normed_part[0] + contract_last(keyval_low, w_pair), normed_part[1]])
    layer_low, head_low, normed_part = lax.optimization_barrier((layer_low, head_low, normed_part))
    layer_low = lax.psum_scatter(layer_low, CTX, scatter_dimension=0, tiled=True)[0]
    normed_grad = scatter_tp(normed_part.reshape(2, N_X, SHARD, D))
    late_grads = jnp.concatenate(
        [contract(query_linear_low, normed_low), contract_first(keyval_low, normed_half)]
    ).astype(bf16)
    late_grads = late_grads.reshape(384, N_CTX, LINES).transpose(1, 0, 2)
    late_sum = jnp.sum(
        lax.all_to_all(late_grads, CTX, 0, 0, tiled=True).astype(f32), axis=0
    )
    first_part, first_gain_grad = jax.vjp(rms_norm, stream_in, gains[0])[1](normed_grad)
    input_low = (mid_grad + first_part).astype(bf16)

    gain_parts = jnp.stack([first_gain_grad, middle_gain_grad, final_gain_grad]).astype(bf16)
    sent = jnp.concatenate(
        [
            input_low.reshape(SHARD, N_CTX, LINES).transpose(1, 0, 2),
            jnp.pad(gain_parts.reshape(3, N_CTX, LINES).transpose(1, 0, 2), ((0, 0), (0, 13), (0, 0))),
        ],
        axis=1,
    )
    arrived = lax.all_to_all(sent, CTX, 0, 0, tiled=True)
    gain_sums = jnp.sum(arrived[:, SHARD : SHARD + 3].astype(f32), axis=0)
    place_grads = gather_tp(arrived[:, :SHARD].reshape(N_CTX * SHARD, LINES))
    embed_grad = add_up(all_ids, place_grads, vocab_here)

    kv_part = late_sum[256:]
    kv_full = kv_part + core_swap(kv_part)
    kv_split = kv_full.T.reshape(N_X, 2, 16, 2 * HD)
    kv_owned = swapped_x(jnp.where(cs == 0, kv_split[:, 0], kv_split[:, 1]), xs)
    key_value_grad = (
        kv_owned.reshape(KV_HEADS, 16, 2, HD).transpose(1, 2, 0, 3).reshape(16, KVW)
    )

    old_rows = jnp.concatenate(
        [attention_row_moment, feed_row_moment, vocab_row_moment, jnp.ones((9, LINES), f32)]
    )
    kv_old_columns = lax.dynamic_index_in_dim(
        key_value_column_moment.reshape(2, KV_HEADS, HD), xs, 1, keepdims=False
    ).reshape(-1)
    early_old = jnp.concatenate(
        [
            jnp.pad(vocab_column_moment, ((0, 0), (0, EARLY_LANES - vocab_here)), constant_values=1.0),
            jnp.concatenate(
                [attention_column_moment[0], kv_old_columns, jnp.ones((EARLY_LANES - 384,), f32)]
            )[None],
        ]
    )
    late_old = jnp.concatenate(
        [
            feed_column_moment[0],
            feed_column_moment[1],
            attention_column_moment[1],
            feed_column_moment[2],
            jnp.ones((64,), f32),
        ]
    )[None]
    kv_old_line = lax.dynamic_update_slice_in_dim(
        jnp.zeros((1, LINES), f32), key_value_row_moment[None], tp_index * 16, 1
    )
    feed_tables = feed_master.transpose(0, 2, 1)
    vocab_grad, line_parts, column_parts, base = early_figures(
        head_low,
        embed_grad,
        late_sum[:256],
        kv_full,
        gain_sums,
        kv_old_line,
        tables,
        feed_tables,
        attention_master,
        key_value_master,
        gain_master.T,
        loss_part.reshape(1, 1),
    )
    lines = sum_tp(line_parts)
    columns = sum_ctx(column_parts)
    gain_grad = lax.dynamic_slice_in_dim(lines[8:11], tp_index * 16, 16, 1)
    gain_second = moments(gain_moment.T, gain_grad * gain_grad, 1.0)
    gain_step = gain_grad * lax.rsqrt(gain_second)
    gain_squares = jnp.sum(gain_step * gain_step, axis=1)[None]
    base = base + jnp.pad(gain_squares, ((0, 0), (UG_LANE, 128 - UG_LANE - 3)))
    early_rows, early_columns, base = step_squares(
        early_squares_kernel,
        (vocab_grad, late_sum[:256], kv_full),
        lines,
        columns,
        old_rows,
        early_old,
        base,
    )
    feed_grad, attention_grad, late_line_parts, late_column_parts = late_figures(
        layer_low, late_sum[:256]
    )
    late_rows, late_columns, scalars = step_squares(
        late_squares_kernel,
        (layer_low,),
        sum_tp(late_line_parts),
        sent_to_all(late_column_parts, CTX),
        old_rows,
        late_old,
        base,
    )
    kv_columns_here = early_columns[2:3, 256:384]
    gathered = sent_to_all(jnp.concatenate([scalars, kv_columns_here]), CTX_TP)
    vocab_new, feed_new, attention_new, gain_new, figures = update(
        gathered[:, 0],
        tables,
        vocab_grad,
        feed_tables,
        feed_grad,
        attention_master,
        attention_grad,
        early_rows,
        late_rows,
        early_columns,
        late_columns,
        gain_master.T,
        gain_step,
    )
    token_loss = figures[2, 0]
    update_rms = figures[0, :11]
    kv_row_new = lax.dynamic_slice_in_dim(early_rows[7], tp_index * 16, 16, 0)
    kv_column_new = (
        gathered[0:8:2, 1].reshape(KV_HEADS, 2, HD).transpose(1, 0, 2).reshape(KVW)
    )
    kv_step = key_value_grad * lax.rsqrt(kv_row_new)[:, None] * lax.rsqrt(kv_column_new)[None]
    kv_new = key_value_master - figures[1, 7] * kv_step
    attention_columns = jnp.stack([early_columns[2, :256], late_columns[0, 1408:1664]])
    feed_columns = jnp.stack(
        [late_columns[0, :704], late_columns[0, 704:1408], late_columns[0, 1664:2368]]
    )
    return (
        token_loss,
        update_rms,
        attention_grad,
        jnp.stack([early_rows[0], late_rows[1]]),
        attention_columns,
        attention_new,
        feed_grad.transpose(0, 2, 1),
        late_rows[2:5],
        feed_columns,
        feed_new.transpose(0, 2, 1),
        vocab_grad.transpose(0, 2, 1),
        early_rows[5:7],
        early_columns[0, :vocab_here],
        early_columns[1, :vocab_here],
        vocab_new.transpose(0, 2, 1),
        key_value_grad,
        kv_row_new,
        kv_column_new,
        kv_new,
        gain_grad.T,
        gain_second.T,
        gain_new.T,
    )


def solution(mesh):
    finer = Mesh(mesh.devices.reshape(4, 4, 4, 2), ("ctx_0", "ctx_1", "tp_0", "tp_1"))
    in_specs = (
        P(CTX),
        P(CTX),
        P(CTX),
        P(),
        P(),
        P(None, CTX, TP),
        P(None, CTX, TP),
        P(None, CTX, TP),
        P(CTX_TP, None),
        P(CTX_TP, None),
        P(None, CTX),
        P(None, TP),
        P(None, CTX),
        P(None, TP),
        P(None, CTX),
        P(None, TP),
        P(CTX_TP),
        P(),
        P(CTX_TP, None),
    )
    out_specs = (
        P(),
        P(),
        P(None, CTX, TP),
        P(None, CTX),
        P(None, TP),
        P(None, CTX, TP),
        P(None, CTX, TP),
        P(None, CTX),
        P(None, TP),
        P(None, CTX, TP),
        P(None, CTX, TP),
        P(None, CTX),
        P(TP),
        P(TP),
        P(None, CTX, TP),
        P(CTX_TP, None),
        P(CTX_TP),
        P(),
        P(CTX_TP, None),
        P(CTX_TP, None),
        P(CTX_TP, None),
        P(CTX_TP, None),
    )
    return jax.shard_map(body, mesh=finer, in_specs=in_specs, out_specs=out_specs, check_vma=False)
```

```python
import functools
import math

import jax
import jax.numpy as jnp
from jax import lax
from jax.experimental import pallas as pl
from jax.experimental.pallas import tpu as pltpu
from jax.sharding import Mesh
from jax.sharding import PartitionSpec as P

D = 2048
HEADS = 32
KV_HEADS = 4
HD = 64
FF = 5632
VOCAB = 32000
ORIG_CTX = 2048
HQ = 2048
KVW = 512
TOKENS = 4096
TP = ("tp_0", "tp_1")
CTX = ("ctx_0", "ctx_1")
CTX_TP = ("ctx_0", "ctx_1", "tp_0", "tp_1")
N_CTX = 16
N_X = 4
N_TP = 8
SHARD = 32
LINES = 128
DOCS = 5

NORM_EPS = 1e-05
MOMENT_DECAY = 0.5
MOMENT_EPS = 1e-30
CLIP_LIMIT = 0.5
STEP_SCALE = 1.0
ROPE_BASE = 10000.0
YARN_SCALE = 4.0
YARN_ALPHA = 1.0
YARN_BETA = 32.0

bf16 = jnp.bfloat16
f32 = jnp.float32


def x_from(values, step):
    return lax.ppermute(values, "tp_0", [((i + step) % N_X, i) for i in range(N_X)])


def x_to(values, step):
    return lax.ppermute(values, "tp_0", [(i, (i + step) % N_X) for i in range(N_X)])


def core_swap(values):
    return lax.ppermute(values, "tp_1", [(0, 1), (1, 0)])


def turned(stack, start):
    return lax.dynamic_slice_in_dim(jnp.concatenate([stack, stack]), start, N_X, 0)


def to_absolute(stack, xs):
    return turned(stack, (N_X - xs) % N_X)


def gather_tp(shard):
    column = jnp.concatenate([shard] + [x_from(shard, d) for d in range(1, N_X)])
    return jnp.concatenate([column, core_swap(column)])


def scatter_tp(partial):
    half = partial[0] + core_swap(partial[1].astype(bf16)).astype(f32)
    low = half.astype(bf16)
    total = half[0]
    for d in range(1, N_X):
        total = total + x_to(low[d], d).astype(f32)
    return total


def both_cores(column, cs):
    other = core_swap(column)
    both = jnp.where(
        cs == 0, jnp.stack([column, other], axis=1), jnp.stack([other, column], axis=1)
    )
    return both.reshape(-1, *column.shape[2:])


def swapped_x(blocks, xs):
    ours = turned(blocks, xs)
    came = [ours[0]] + [x_to(ours[d], d) for d in range(1, N_X)]
    return to_absolute(jnp.stack([came[0], came[3], came[2], came[1]]), xs)


def partner(values, axis, mask):
    size = 2 if axis == "tp_1" else 4
    return lax.ppermute(values, axis, [(i, i ^ mask) for i in range(size)])


def sum_over_four(values, axis):
    return (values + partner(values, axis, 1)) + (
        partner(values, axis, 2) + partner(values, axis, 3)
    )


def sum_tp(values):
    return sum_over_four(values + partner(values, "tp_1", 1), "tp_0")


def sum_ctx(values):
    return sum_over_four(sum_over_four(values, "ctx_1"), "ctx_0")


def own_order(values, xs, cs):
    blocks = turned(values.reshape(N_X, 2, SHARD), xs)
    blocks = jnp.where(cs == 0, blocks, blocks[:, ::-1])
    return blocks.transpose(1, 0, 2)


def sent_to_all(array, axis):
    copies = jnp.broadcast_to(array, (lax.axis_size(axis), *array.shape))
    return lax.all_to_all(copies, axis, split_axis=0, concat_axis=0, tiled=True)


def rope_tables(positions):
    ladder = jnp.arange(HD // 2, dtype=f32)
    freqs = ROPE_BASE ** (-2.0 * ladder / HD)
    ratio = ORIG_CTX * freqs / (2.0 * math.pi)
    ramped = jnp.clip((ratio - YARN_ALPHA) / (YARN_BETA - YARN_ALPHA), 0.0, 1.0)
    inverse = freqs * (1.0 - ramped) / YARN_SCALE + freqs * ramped
    angles = inverse[:, None] * positions.astype(f32)[None, :]
    mscale = 0.1 * math.log(YARN_SCALE) + 1.0
    return (jnp.cos(angles) * mscale, jnp.sin(angles) * mscale)


def rotate_rows(values, cosine, sine):
    half = values.shape[0] // 2
    first, second = (values[:half], values[half:])
    return jnp.concatenate([first * cosine - second * sine, second * cosine + first * sine])


def rotate_lanes(values, cosine, sine):
    half = values.shape[1] // 2
    first, second = (values[:, :half], values[:, half:])
    return jnp.concatenate([first * cosine - second * sine, second * cosine + first * sine], axis=1)


def rms_norm(values, gain):
    return values * lax.rsqrt(jnp.mean(values * values, axis=-1, keepdims=True) + NORM_EPS) * gain


def contract_last(left, right):
    return lax.dot_general(left, right, (((1,), (1,)), ((), ())), preferred_element_type=f32)


def contract_first(left, right):
    return lax.dot_general(left, right, (((0,), (0,)), ((), ())), preferred_element_type=f32)


def contract(left, right):
    return jnp.dot(left, right, preferred_element_type=f32)


def combine_stats(former, latter):
    highest = jnp.maximum(former[0], latter[0])
    summed = former[1] * jnp.exp(former[0] - highest) + latter[1] * jnp.exp(latter[0] - highest)
    return jnp.stack([highest, summed, former[2] + latter[2]])


def contract_ft(weights, places):
    return lax.dot_general(weights, places, (((0,), (1,)), ((), ())), preferred_element_type=f32)


def contract_tf(features, weights):
    return lax.dot_general(features, weights, (((0,), (1,)), ((), ())), preferred_element_type=f32)


def heads_on_lanes(features):
    return jnp.concatenate([features[h * HD : (h + 1) * HD] for h in range(4)], axis=1)


def heads_on_rows(features):
    return jnp.concatenate(jnp.split(features, 4, axis=1))


VMEM_LIMIT = 50 * 1024 * 1024


GROUP = 4
KEYS = 128 * GROUP
STEPS = TOKENS // KEYS


def key_places(core_bit, spans):
    line = lax.broadcasted_iota(jnp.int32, (128, 1), 0)
    x = (spans[N_CTX] + line // SHARD) % N_X
    place = (x * 2 + (spans[N_CTX + 1] ^ core_bit)) * SHARD + line % SHARD
    return place >= 128, place % 128


def visible_keys(spans, places, step, own, start):
    lines = []
    for block in range(step * GROUP, (step + 1) * GROUP):
        span = spans[block % N_CTX]
        second, within = places[block // N_CTX]
        lines.append(jnp.where(second, (2 * N_CTX - 1 - span) * 128, span * 128) + within)
    at = jnp.concatenate(lines, axis=0)
    return (at >= start) & (at <= own)


def key_columns(kv_ref, step, at):
    return jnp.concatenate(
        [kv_ref[step * GROUP + i, at : at + HD] for i in range(GROUP)], axis=1
    )


def attend_kernel(spans, own_ref, q_ref, kv_ref, o_ref, total_ref, s_ref):
    q = q_ref[...]
    own, start = (own_ref[0:1], own_ref[1:2])
    places = [key_places(core_bit, spans) for core_bit in range(2)]
    top = None
    for step in range(STEPS):
        scores = contract_first(key_columns(kv_ref, step, 0), q)
        scores = jnp.where(visible_keys(spans, places, step, own, start), scores, -1e30)
        s_ref[step * KEYS : (step + 1) * KEYS] = scores
        highest = jnp.max(scores, axis=0, keepdims=True)
        top = highest if top is None else jnp.maximum(top, highest)
    total = jnp.zeros(top.shape, f32)
    for step in range(STEPS):
        powers = jnp.exp(s_ref[step * KEYS : (step + 1) * KEYS] - top)
        s_ref[step * KEYS : (step + 1) * KEYS] = powers
        total = total + jnp.sum(powers, axis=0, keepdims=True)
    share = 1.0 / total
    out = jnp.zeros(q.shape, f32)
    for step in range(STEPS):
        weights = (s_ref[step * KEYS : (step + 1) * KEYS] * share).astype(bf16)
        out = out + contract(key_columns(kv_ref, step, HD), weights)
    o_ref[...] = out.astype(bf16)
    total_ref[...] = top + jnp.log(total)


SPLIT = 2


def attend(spans, own, q, kv):
    lanes = q.shape[1] // SPLIT
    column = lambda rows: pl.BlockSpec((rows, lanes), lambda i: (0, i))
    return pl.pallas_call(
        attend_kernel,
        grid=(SPLIT,),
        in_specs=[
            pl.BlockSpec(memory_space=pltpu.SMEM),
            column(2),
            column(HD),
            pl.BlockSpec(kv.shape, lambda i: (0, 0, 0)),
        ],
        out_specs=[column(HD), column(1)],
        out_shape=[
            jax.ShapeDtypeStruct(q.shape, bf16),
            jax.ShapeDtypeStruct((1, q.shape[1]), f32),
        ],
        scratch_shapes=[pltpu.VMEM((TOKENS, lanes), f32)],
        compiler_params=pltpu.CompilerParams(vmem_limit_bytes=VMEM_LIMIT),
        cost_estimate=pl.CostEstimate(
            flops=16 * TOKENS * q.shape[1] * HD, bytes_accessed=2 << 20, transcendentals=0
        ),
    )(spans, own, q, kv)


def attend_back_kernel(
    spans, own_ref, q_ref, do_ref, total_ref, kv_ref, dq_ref, dkv_ref, p_ref, dp_ref
):
    q, do = (q_ref[...], do_ref[...])
    own, start = (own_ref[0:1], own_ref[1:2])
    total = total_ref[...]
    places = [key_places(core_bit, spans) for core_bit in range(2)]
    rowsum = jnp.zeros(total.shape, f32)
    for step in range(STEPS):
        scores = contract_first(key_columns(kv_ref, step, 0), q)
        scores = jnp.where(visible_keys(spans, places, step, own, start), scores, -1e30)
        probs = jnp.exp(scores - total)
        probs_grad = contract_first(key_columns(kv_ref, step, HD), do)
        p_ref[step * KEYS : (step + 1) * KEYS] = probs
        dp_ref[step * KEYS : (step + 1) * KEYS] = probs_grad
        rowsum = rowsum + jnp.sum(probs * probs_grad, axis=0, keepdims=True)

    @pl.when(pl.program_id(0) == 0)
    def _():
        dkv_ref[...] = jnp.zeros(dkv_ref.shape, f32)

    dq = jnp.zeros(q.shape, f32)
    for step in range(STEPS):
        rows = slice(step * KEYS, (step + 1) * KEYS)
        probs = p_ref[rows]
        score_grad = (probs * (dp_ref[rows] - rowsum)).astype(bf16)
        dkv_ref[rows] += jnp.concatenate(
            [contract_last(score_grad, q), contract_last(probs.astype(bf16), do)], axis=1
        )
        dq = dq + contract(key_columns(kv_ref, step, 0), score_grad)
    dq_ref[...] = dq * (1.0 / math.sqrt(HD))


def attend_back(spans, own, q, do, total, kv):
    lanes = q.shape[1] // SPLIT
    column = lambda rows: pl.BlockSpec((rows, lanes), lambda i: (0, i))
    return pl.pallas_call(
        attend_back_kernel,
        grid=(SPLIT,),
        in_specs=[
            pl.BlockSpec(memory_space=pltpu.SMEM),
            column(2),
            column(HD),
            column(HD),
            column(1),
            pl.BlockSpec(kv.shape, lambda i: (0, 0, 0)),
        ],
        out_specs=[column(HD), pl.BlockSpec((TOKENS, 2 * HD), lambda i: (0, 0))],
        out_shape=[
            jax.ShapeDtypeStruct(q.shape, f32),
            jax.ShapeDtypeStruct((TOKENS, 2 * HD), f32),
        ],
        scratch_shapes=[pltpu.VMEM((TOKENS, lanes), f32), pltpu.VMEM((TOKENS, lanes), f32)],
        compiler_params=pltpu.CompilerParams(vmem_limit_bytes=VMEM_LIMIT),
        cost_estimate=pl.CostEstimate(
            flops=40 * TOKENS * q.shape[1] * HD, bytes_accessed=4 << 20, transcendentals=0
        ),
    )(spans, own, q, do, total, kv)


def moments(old, sums, count):
    return MOMENT_DECAY * old + (1.0 - MOMENT_DECAY) * (sums / count + MOMENT_EPS)


def params():
    return pltpu.CompilerParams(vmem_limit_bytes=VMEM_LIMIT)


def whole(array):
    zeros = (0,) * array.ndim
    return pl.BlockSpec(array.shape, lambda *i: zeros)


def cost(flops, moved):
    return pl.CostEstimate(flops=flops, bytes_accessed=moved, transcendentals=0)


ID_STEP = 1024


def look_kernel(ids_ref, table_ref, out_ref, low_ref):
    @pl.when(pl.program_id(0) == 0)
    def _():
        low_ref[...] = table_ref[0].astype(bf16)

    width = low_ref.shape[0]
    ids = jnp.transpose(jnp.broadcast_to(ids_ref[...], (8, ID_STEP)))[:, :1]
    hits = ids == lax.broadcasted_iota(jnp.int32, (ID_STEP, width), 1)
    out_ref[...] = contract(jnp.where(hits, 1.0, 0.0).astype(bf16), low_ref[...]).astype(bf16)


def look_up(ids, tables):
    width, lines = tables.shape[1:]
    count = ids.shape[1]
    return pl.pallas_call(
        look_kernel,
        grid=(count // ID_STEP,),
        in_specs=[
            pl.BlockSpec((1, ID_STEP), lambda i: (0, i)),
            pl.BlockSpec((1, width, lines), lambda i: (1, 0, 0)),
        ],
        out_specs=pl.BlockSpec((ID_STEP, lines), lambda i: (i, 0)),
        out_shape=jax.ShapeDtypeStruct((count, lines), bf16),
        scratch_shapes=[pltpu.VMEM((width, lines), bf16)],
        compiler_params=params(),
        cost_estimate=cost(4 * count * width * lines, 4 * lines * width),
    )(ids, tables)


def add_kernel(ids_ref, grads_ref, out_ref):
    hits = lax.broadcasted_iota(jnp.int32, (out_ref.shape[0], ID_STEP), 0) == ids_ref[...]
    added = contract(jnp.where(hits, 1.0, 0.0).astype(bf16), grads_ref[...])

    @pl.when(pl.program_id(0) == 0)
    def _():
        out_ref[...] = added

    @pl.when(pl.program_id(0) > 0)
    def _():
        out_ref[...] += added


def add_up(ids, grads, width):
    count, lines = grads.shape
    return pl.pallas_call(
        add_kernel,
        grid=(count // ID_STEP,),
        in_specs=[
            pl.BlockSpec((1, ID_STEP), lambda i: (0, i)),
            pl.BlockSpec((ID_STEP, lines), lambda i: (i, 0)),
        ],
        out_specs=pl.BlockSpec((width, lines), lambda i: (0, 0)),
        out_shape=jax.ShapeDtypeStruct((width, lines), f32),
        compiler_params=params(),
        cost_estimate=cost(4 * count * width * lines, 4 * lines * width),
    )(ids, grads)


LOGIT_STEP = 800


def logits_kernel(c_ref, w_ref, target_ref, out_ref, stats_ref):
    step = pl.program_id(0)
    logits = contract_last(w_ref[...], c_ref[...])
    out_ref[...] = logits
    row = lax.broadcasted_iota(jnp.int32, logits.shape, 0) + step * LOGIT_STEP
    here = jnp.max(logits, axis=0, keepdims=True)
    pick = jnp.sum(jnp.where(row == target_ref[...], logits, 0.0), axis=0, keepdims=True)

    @pl.when(step == 0)
    def _():
        stats_ref[...] = jnp.zeros(stats_ref.shape, f32)
        stats_ref[0:1] = here

    old = stats_ref[0:1]
    top = jnp.maximum(old, here)
    powers = jnp.sum(jnp.exp(logits - top), axis=0, keepdims=True)
    stats_ref[1:2] = stats_ref[1:2] * jnp.exp(old - top) + powers
    stats_ref[2:3] += pick
    stats_ref[0:1] = top


def logits_and_stats(c, head, width, targets):
    places, rows = c.shape
    return pl.pallas_call(
        logits_kernel,
        grid=(width // LOGIT_STEP,),
        in_specs=[whole(c), pl.BlockSpec((LOGIT_STEP, rows), lambda i: (i, 0)), whole(targets)],
        out_specs=[
            pl.BlockSpec((LOGIT_STEP, places), lambda i: (i, 0)),
            pl.BlockSpec((8, places), lambda i: (0, 0)),
        ],
        out_shape=[
            jax.ShapeDtypeStruct((width, places), f32),
            jax.ShapeDtypeStruct((8, places), f32),
        ],
        compiler_params=params(),
        cost_estimate=cost(2 * places * rows * width, 2 * rows * width),
    )(c, head, targets)


def head_grad_kernel(logits_ref, c_ref, place_ref, target_ref, dw_ref, low_ref):
    step = pl.program_id(0)
    logits = logits_ref[...]
    row = lax.broadcasted_iota(jnp.int32, logits.shape, 0) + step * LOGIT_STEP
    hit = row == target_ref[...]
    shares = jnp.exp(logits - place_ref[0:1]) - jnp.where(hit, 1.0, 0.0)
    low = (place_ref[1:2] * shares).astype(bf16)
    low_ref[...] = low
    grad = contract(low, c_ref[...]).astype(bf16)
    for k in range(N_CTX):
        dw_ref[k] = grad[:, k * 128 : (k + 1) * 128]


def head_grads(logits, c, place, targets):
    places, rows = c.shape
    width = logits.shape[0]
    block = pl.BlockSpec((LOGIT_STEP, places), lambda i: (i, 0))
    return pl.pallas_call(
        head_grad_kernel,
        grid=(width // LOGIT_STEP,),
        in_specs=[block, whole(c), whole(place), whole(targets)],
        out_specs=[pl.BlockSpec((N_CTX, LOGIT_STEP, 128), lambda i: (0, i, 0)), block],
        out_shape=[
            jax.ShapeDtypeStruct((N_CTX, width, 128), bf16),
            jax.ShapeDtypeStruct((width, places), bf16),
        ],
        compiler_params=params(),
        cost_estimate=cost(2 * places * rows * width, 2 * rows * width),
    )(logits, c, place, targets)


TURNED = (1, 3)


def products_kernel(count, offsets, *refs):
    lefts, rights = (refs[:count], refs[count : 2 * count])
    out_ref, turned_ref = refs[2 * count :]

    @pl.when(pl.program_id(0) == 0)
    def _():
        for k, (right, (at, width)) in enumerate(zip(rights, offsets)):
            values = right[...]
            turned_ref[at : at + width] = values if k in TURNED else jnp.transpose(values)

    for left, (at, width) in zip(lefts, offsets):
        grad = contract(turned_ref[at : at + width], left[...]).astype(bf16)
        for k in range(2):
            out_ref[k, at : at + width] = grad[:, k * 128 : (k + 1) * 128]


def row_products(lefts, rights):
    places, rows = lefts[0].shape
    offsets, at = ([], 0)
    for k, right in enumerate(rights):
        width = right.shape[0 if k in TURNED else 1]
        offsets.append((at, width))
        at += width
    return pl.pallas_call(
        functools.partial(products_kernel, len(lefts), tuple(offsets)),
        grid=(N_CTX // 2,),
        in_specs=[pl.BlockSpec((places, 256), lambda i: (0, i)) for _ in lefts]
        + [whole(right) for right in rights],
        out_specs=pl.BlockSpec((2, at, 128), lambda i: (i, 0, 0)),
        out_shape=jax.ShapeDtypeStruct((N_CTX, at, rows // N_CTX), bf16),
        scratch_shapes=[pltpu.VMEM((at, places), bf16)],
        compiler_params=params(),
        cost_estimate=cost(2 * places * rows * at, 2 * rows * at),
    )(*lefts, *rights)


MATRICES = 8
WIDTHS = (HQ, HQ, FF, FF, FF, VOCAB, VOCAB, KVW)
EARLY_LANES = 4096
LATE_LANES = 2688
COLUMN_AT = {0: (0, 2368, 256), 7: (2, 0, 128), 5: (0, 0, 4000), 6: (1, 0, 4000)}
COLUMN_AT.update({2: (0, 0, 704), 3: (0, 704, 704), 1: (0, 1408, 256), 4: (0, 1664, 704)})
S_LANE, T_LANE, OLD_LANE, W_LANE, WG_LANE, UG_LANE, LOSS_LANE = (0, 8, 16, 24, 32, 35, 38)


def lane_is(shape, lane):
    return lax.broadcasted_iota(jnp.int32, shape, 1) == lane


def line_sum(values):
    return jnp.sum(values, axis=0, keepdims=True)


def total_of(values):
    return jnp.sum(line_sum(values), axis=1, keepdims=True)


def column_sums(squares):
    ones = jnp.ones((8, squares.shape[1]), f32)
    return lax.dot_general(
        ones,
        squares,
        (((1,), (1,)), ((), ())),
        precision=lax.Precision.HIGHEST,
        preferred_element_type=f32,
    )


def early_kernel(
    head_ref, embed_ref, kv_ref, gains_ref, kv_old_ref, tables_ref, feed_ref,
    attention_ref, kv_master_ref, gain_ref, loss_ref,
    vocab_grad_ref, lines_ref, columns_ref, scalars_ref,
):
    columns_ref[...] = jnp.zeros(columns_ref.shape, f32)
    lines_ref[...] = jnp.zeros(lines_ref.shape, f32)
    lines_ref[8:11] = gains_ref[...]
    lines_ref[11:12] = kv_old_ref[...]
    for number, ref in ((5, head_ref), (6, embed_ref), (7, kv_ref)):
        grad = ref[...].astype(f32)
        if number in (5, 6):
            vocab_grad_ref[number - 5] = grad
        squares = grad * grad
        lines_ref[number : number + 1] = (0.5 if number == 7 else 1.0) * line_sum(squares)
        line, at, width = COLUMN_AT[number]
        columns_ref[line : line + 1, at : at + width] = column_sums(squares)[:1]
    scalars = jnp.where(lane_is(scalars_ref.shape, LOSS_LANE), loss_ref[...], 0.0)
    for number, weights in (
        (0, attention_ref[0]),
        (1, attention_ref[1]),
        (2, feed_ref[0]),
        (3, feed_ref[1]),
        (4, feed_ref[2]),
        (5, tables_ref[0]),
        (6, tables_ref[1]),
        (7, kv_master_ref[...]),
        (8, gain_ref[0:1]),
        (9, gain_ref[1:2]),
        (10, gain_ref[2:3]),
    ):
        scalars += jnp.where(
            lane_is(scalars.shape, W_LANE + number), total_of(weights * weights), 0.0
        )
    scalars_ref[...] = scalars


def early_figures(*arrays):
    tables = arrays[5]
    shapes = (tables.shape, (16, 128), (3, EARLY_LANES), (1, 128))
    return pl.pallas_call(
        early_kernel,
        out_shape=[jax.ShapeDtypeStruct(shape, f32) for shape in shapes],
        compiler_params=params(),
        cost_estimate=cost(0, 16 << 20),
    )(*arrays)


def late_kernel(layer_ref, feed_grad_ref, attention_grad_ref, lines_ref, columns_ref):
    layer = layer_ref[...].astype(f32)
    squares = layer * layer
    lines_ref[...] = jnp.zeros(lines_ref.shape, f32)
    columns_ref[...] = jnp.zeros(columns_ref.shape, f32)
    columns_ref[:, : layer.shape[0]] = column_sums(squares)[:1]
    for number in range(5):
        line, at, width = COLUMN_AT[number]
        lines_ref[number : number + 1] = line_sum(squares[at : at + width])
        if number > 1:
            feed_grad_ref[number - 2] = layer[at : at + width]
    attention_grad_ref[0] = jnp.transpose(layer[2368:2624])
    attention_grad_ref[1] = jnp.transpose(layer[1408:1664])


def late_figures(layer):
    shapes = ((3, 704, 128), (2, 128, 256), (8, 128), (1, LATE_LANES))
    return pl.pallas_call(
        late_kernel,
        out_shape=[jax.ShapeDtypeStruct(shape, f32) for shape in shapes],
        compiler_params=params(),
        cost_estimate=cost(0, 4 << 20),
    )(layer)


def per_column(figures, number):
    line, at, width = COLUMN_AT[number]
    return figures[at : at + width, line : line + 1]


def on_rows(columns):
    spare = 8 - columns.shape[0]
    return jnp.transpose(
        jnp.concatenate([columns, jnp.ones((spare, columns.shape[1]), f32)], axis=0)
    )


def squares_of(sources, lines, old, columns, old_columns, base, row_ref, column_ref, scalars_ref):
    number = lax.broadcasted_iota(jnp.int32, lines.shape, 0)
    widths = jnp.full(lines.shape, 1.0, f32)
    for k, width in enumerate(WIDTHS):
        widths = jnp.where(number == k, float(width), widths)
    row_new = moments(old, lines / widths, 1.0)
    row_ref[...] = row_new
    column_new = moments(old_columns, columns, float(D))
    column_ref[...] = column_new
    weights = on_rows(1.0 / column_new)
    scalars = base
    had = jnp.sum(old, axis=1, keepdims=True) * (1.0 / N_TP)
    got = jnp.sum(lines, axis=1, keepdims=True) * (1.0 / N_TP)
    for k, grad in sources:
        inner = line_sum(grad * grad * per_column(weights, k)) / row_new[k : k + 1]
        part = jnp.sum(inner, axis=1, keepdims=True) * (0.5 if k == 7 else 1.0)
        scalars += jnp.where(lane_is(scalars.shape, S_LANE + k), part, 0.0)
        scalars += jnp.where(lane_is(scalars.shape, T_LANE + k), got[k : k + 1], 0.0)
        scalars += jnp.where(lane_is(scalars.shape, OLD_LANE + k), had[k : k + 1], 0.0)
    scalars_ref[...] = scalars


def early_squares_kernel(
    vocab_ref, kv_ref, lines_ref, columns_ref, old_ref, old_columns_ref, base_ref,
    row_ref, column_ref, scalars_ref,
):
    lines = lines_ref[...]
    number = lax.broadcasted_iota(jnp.int32, lines.shape, 0)
    old = jnp.where(number == 7, lines_ref[11:12], old_ref[...])
    sources = ((5, vocab_ref[0]), (6, vocab_ref[1]), (7, kv_ref[...]))
    squares_of(
        sources, lines, old, columns_ref[...], old_columns_ref[...], base_ref[...],
        row_ref, column_ref, scalars_ref,
    )


def late_squares_kernel(
    layer_ref, lines_ref, columns_ref, old_ref, old_columns_ref, base_ref,
    row_ref, column_ref, scalars_ref,
):
    layer = layer_ref[...].astype(f32)
    sources = []
    for number in range(5):
        line, at, width = COLUMN_AT[number]
        sources.append((number, layer[at : at + width]))
    columns = jnp.sum(columns_ref[...], axis=0)
    squares_of(
        sources, lines_ref[...], old_ref[0:8], columns, old_columns_ref[...], base_ref[...],
        row_ref, column_ref, scalars_ref,
    )


def step_squares(kernel, grads, lines, columns, old, old_columns, base):
    return pl.pallas_call(
        kernel,
        out_shape=[jax.ShapeDtypeStruct(a.shape, f32) for a in (lines, old_columns, base)],
        compiler_params=params(),
        cost_estimate=cost(0, 8 << 20),
    )(*grads, lines, columns, old, old_columns, base)


UPDATE_STEP = 800


def update_kernel(
    all_ref, vocab_ref, vocab_grad_ref, feed_ref, feed_grad_ref, attention_ref,
    attention_grad_ref, early_row_ref, late_row_ref, early_column_ref, late_column_ref, gain_ref,
    gain_step_ref,
    vocab_new_ref, feed_new_ref, attention_new_ref, gain_new_ref, figures_ref, scale_ref,
):
    sums = jnp.sum(all_ref[...], axis=0, keepdims=True)
    sums = jnp.broadcast_to(sums, (8, 128))

    def lanes_from(at):
        return pltpu.roll(sums, (128 - at) % 128, 1)[0:1]

    lane = lax.broadcasted_iota(jnp.int32, (1, 128), 1)
    counts = jnp.full((1, 128), float(D), f32)
    for k, width in enumerate(WIDTHS):
        counts = jnp.where(lane == k, float(D * width), counts)
    mean = MOMENT_DECAY * lanes_from(OLD_LANE) / D + (1.0 - MOMENT_DECAY) * (
        lanes_from(T_LANE) / counts + MOMENT_EPS
    )
    mean = jnp.where(lane < MATRICES, mean, 1.0)
    rms = jnp.sqrt(mean * lanes_from(S_LANE) / counts)
    factor = (
        STEP_SCALE
        * jnp.sqrt(lanes_from(W_LANE) / counts)
        / jnp.maximum(1.0, rms / CLIP_LIMIT)
        * jnp.sqrt(mean)
    )
    early_scale = lax.rsqrt(early_row_ref[...])
    late_scale = lax.rsqrt(late_row_ref[...])

    def stepped(master, grad, number, scale):
        row_scale = late_scale if number < 5 else early_scale
        tall = row_scale[number : number + 1] * factor[:, number : number + 1]
        return master - grad * tall * scale

    @pl.when(pl.program_id(0) == 0)
    def _():
        early = on_rows(lax.rsqrt(early_column_ref[...]))
        late = on_rows(lax.rsqrt(late_column_ref[...]))
        scale_ref[...] = early
        for k in range(2):
            grad = jnp.transpose(attention_grad_ref[k])
            master = jnp.transpose(attention_ref[k])
            step = stepped(master, grad, k, per_column(late, k))
            attention_new_ref[k] = jnp.transpose(step)
        for k in range(3):
            feed_new_ref[k] = stepped(feed_ref[k], feed_grad_ref[k], 2 + k, per_column(late, 2 + k))
        gain_rms = jnp.sqrt(lanes_from(UG_LANE) / D)
        gain_factor = (
            STEP_SCALE
            * jnp.sqrt(lanes_from(WG_LANE) / D)
            / jnp.maximum(1.0, gain_rms / CLIP_LIMIT)
        )
        for k in range(3):
            gain_new_ref[k : k + 1] = (
                gain_ref[k : k + 1] - gain_factor[:, k : k + 1] * gain_step_ref[k : k + 1]
            )
        after = pltpu.roll(jnp.broadcast_to(gain_rms, (8, 128)), MATRICES, 1)[0:1]
        figures_ref[0:1] = jnp.where(lane < MATRICES, rms, after)
        figures_ref[1:2] = factor
        figures_ref[2:3] = lanes_from(LOSS_LANE)
        figures_ref[3:8] = jnp.zeros((5, 128), f32)

    rows = pl.ds(pl.multiple_of(pl.program_id(0) * UPDATE_STEP, UPDATE_STEP), UPDATE_STEP)
    scale = scale_ref[rows]
    for k in range(2):
        vocab_new_ref[k] = stepped(vocab_ref[k], vocab_grad_ref[k], 5 + k, scale[:, k : k + 1])


def update(gathered, vocab, vocab_grad, feed, *others):
    stack = pl.BlockSpec((2, UPDATE_STEP, vocab.shape[2]), lambda i: (0, i, 0))
    attention, gain = (others[1], others[7])
    outs = (vocab, feed, attention, gain)
    return pl.pallas_call(
        update_kernel,
        grid=(vocab.shape[1] // UPDATE_STEP,),
        in_specs=[whole(gathered), stack, stack, whole(feed)] + [whole(a) for a in others],
        out_specs=[stack]
        + [whole(a) for a in outs[1:]]
        + [pl.BlockSpec((8, 128), lambda i: (0, 0))],
        out_shape=[jax.ShapeDtypeStruct(a.shape, f32) for a in outs]
        + [jax.ShapeDtypeStruct((8, 128), f32)],
        scratch_shapes=[pltpu.VMEM((EARLY_LANES, 8), f32)],
        compiler_params=params(),
        cost_estimate=cost(0, 24 << 20),
    )(gathered, vocab, vocab_grad, feed, *others)


def body(
    token_ids,
    target_ids,
    loss_mask,
    segment_ids,
    span_pairs,
    attention_master,
    feed_master,
    vocab_master,
    key_value_master,
    gain_master,
    attention_row_moment,
    attention_column_moment,
    feed_row_moment,
    feed_column_moment,
    vocab_row_moment,
    vocab_column_moment,
    key_value_row_moment,
    key_value_column_moment,
    gain_moment,
):
    ctx_index = lax.axis_index(CTX)
    xs = lax.axis_index("tp_0")
    cs = lax.axis_index("tp_1")
    tp_index = xs * 2 + cs
    vocab_here = vocab_master.shape[2]
    ff_here = feed_master.shape[2]
    first_id = tp_index * vocab_here

    attention_low = attention_master.astype(bf16)
    feed_low = feed_master.astype(bf16)
    gathered_all = lax.all_gather(
        jnp.concatenate(
            [vocab_master[0].astype(bf16), feed_low[0], feed_low[1], feed_low[2]], axis=1
        ),
        CTX,
        axis=0,
        tiled=True,
    ).T
    head = gathered_all[:vocab_here]
    gate_up = gathered_all[vocab_here : vocab_here + 2 * ff_here]
    down = gathered_all[vocab_here + 2 * ff_here :]

    kv_low = key_value_master.astype(bf16).reshape(16, 2, KV_HEADS, HD).transpose(2, 0, 1, 3)
    gain_low = jnp.pad(gain_master.astype(bf16), ((0, 0), (0, 125)))
    blocks = jnp.concatenate(
        [
            kv_low.reshape(KV_HEADS, 16, 2 * HD),
            jnp.broadcast_to(gain_low, (KV_HEADS, *gain_low.shape)),
        ],
        axis=2,
    )
    ids_here = own_order(token_ids, xs, cs).reshape(1, 256)
    line_block = both_cores(swapped_x(blocks, xs), cs)
    early = sent_to_all(
        jnp.concatenate(
            [
                line_block[:, : 2 * HD],
                line_block[:, 2 * HD : 2 * HD + 3].T,
                (ids_here // 256).astype(bf16).reshape(2, 128),
                (ids_here % 256).astype(bf16).reshape(2, 128),
                jnp.zeros((9, 128), bf16),
                attention_low[0].T,
                attention_low[1].T,
            ]
        ),
        CTX,
    )
    w_pair = early[:, :LINES].reshape(D, 2 * HD)
    w_query = early[:, 144:400].transpose(1, 0, 2).reshape(256, D)
    w_out = early[:, 400:656].transpose(1, 0, 2).reshape(256, D)
    gains = early[:, LINES : LINES + 3].astype(f32).transpose(1, 0, 2).reshape(3, D)
    parts = early[:, LINES + 3 : LINES + 7].astype(jnp.int32).reshape(N_CTX, 2, 256)
    all_ids = parts[:, 0] * 256 + parts[:, 1]
    all_ids = all_ids.reshape(N_CTX, 8, SHARD).transpose(1, 0, 2).reshape(1, TOKENS) - first_id

    order = (
        ((xs + jnp.arange(N_X, dtype=jnp.int32)) % N_X * 2)[None, :]
        + (cs ^ jnp.arange(2, dtype=jnp.int32))[:, None]
    )[:, :, None] * SHARD + jnp.arange(SHARD, dtype=jnp.int32)
    second_span = order >= 128
    within = order % 128
    own_pair = lax.dynamic_slice_in_dim(span_pairs, ctx_index, 1)[0]
    last_span = 2 * N_CTX - 1
    own_pos = (jnp.where(second_span, last_span - own_pair, own_pair) * 128 + within).reshape(-1)
    doc_start = jnp.zeros_like(own_pos)
    for k in range(1, DOCS):
        start = jnp.sum((segment_ids < k).astype(jnp.int32))
        doc_start = jnp.where(own_pos >= start, start, doc_start)
    cosine, sine = rope_tables(own_pos - doc_start)
    cosine_4, sine_4 = (jnp.tile(cosine, (1, 4)), jnp.tile(sine, (1, 4)))
    own_places = jnp.tile(jnp.stack([own_pos, doc_start]), (1, 4))
    spans = jnp.concatenate([span_pairs, jnp.stack([xs, cs]).astype(jnp.int32)])

    tables = vocab_master.transpose(0, 2, 1)
    looked = look_up(all_ids, tables).reshape(2, N_X, N_CTX, SHARD, LINES)
    half = looked[0] + core_swap(looked[1])
    mine = half[0]
    for d in range(1, N_X):
        mine = mine + x_to(half[d], d)
    rows_in = lax.all_to_all(mine, CTX, 0, 0, tiled=True)
    stream_in = rows_in.transpose(1, 0, 2).reshape(SHARD, D).astype(f32)

    normed_low = gather_tp(rms_norm(stream_in, gains[0]).astype(bf16))
    normed_half = normed_low[:128]
    keyval_linear = contract_ft(w_pair, normed_half)
    own_keyvals = jnp.concatenate(
        [rotate_rows(keyval_linear[:HD], cosine[:, :128], sine[:, :128]), keyval_linear[HD:]]
    ).astype(bf16)
    half_keyvals = sent_to_all(own_keyvals, CTX)
    row_keyvals = jnp.concatenate([half_keyvals, core_swap(half_keyvals)])
    query_linear = heads_on_lanes(contract_last(w_query, normed_low))
    queries = rotate_rows(query_linear, cosine_4, sine_4).astype(bf16) * jnp.asarray(
        1.0 / math.sqrt(HD), bf16
    )
    attended, log_total = attend(spans, own_places, queries, row_keyvals)
    attended_rows = heads_on_rows(attended)
    stream_mid = stream_in + scatter_tp(
        contract_first(attended_rows, w_out).reshape(2, N_X, SHARD, D)
    )

    inner_low = gather_tp(rms_norm(stream_mid, gains[1]).astype(bf16))
    both = contract_last(inner_low, gate_up)
    gate, upward = (both[:, :ff_here], both[:, ff_here:])
    sigmoid_gate = jax.nn.sigmoid(gate)
    silu_gate = gate * sigmoid_gate
    hidden_low = (silu_gate * upward).astype(bf16)
    stream_out = stream_mid + scatter_tp(
        contract(hidden_low, down).reshape(2, N_X, SHARD, D)
    )

    finals_low = gather_tp(rms_norm(stream_out, gains[2]).astype(bf16))
    local_targets = own_order(target_ids, xs, cs).reshape(1, -1) - first_id
    logits, stats = logits_and_stats(finals_low, gathered_all, vocab_here, local_targets)
    stats = stats[:3].reshape(3, 2, N_X, SHARD)
    stats = combine_stats(stats, core_swap(stats)[:, ::-1])
    others = [jnp.roll(x_from(stats, d), d, axis=2) for d in range(1, N_X)]
    stats = combine_stats(combine_stats(stats, others[0]), combine_stats(others[1], others[2]))
    stats = stats.reshape(3, -1)
    vocab_total = stats[0] + jnp.log(stats[1])
    keep = own_order(loss_mask, xs, cs).reshape(-1).astype(f32)
    loss_part = jnp.sum((keep * (vocab_total - stats[2]))[:SHARD]) / TOKENS

    place = jnp.stack([vocab_total, keep / TOKENS])
    head_low, dlogits_low = head_grads(logits, finals_low, place, local_targets)
    head_low = lax.psum_scatter(head_low, CTX, scatter_dimension=0, tiled=True)[0]
    final_part = contract_first(dlogits_low, head)
    final_grad = scatter_tp(final_part.reshape(2, N_X, SHARD, D))
    out_grad, final_gain_grad = jax.vjp(rms_norm, stream_out, gains[2])[1](final_grad)
    branch_low = gather_tp(out_grad.astype(bf16))
    hidden_grad = contract_last(branch_low, down)
    gate_grad_low = (
        hidden_grad * upward * sigmoid_gate * (1.0 + gate * (1.0 - sigmoid_gate))
    ).astype(bf16)
    upward_grad_low = (hidden_grad * silu_gate).astype(bf16)
    both_grad_low = jnp.concatenate([gate_grad_low, upward_grad_low], axis=1)
    inner_grad = scatter_tp(contract(both_grad_low, gate_up).reshape(2, N_X, SHARD, D))
    mid_part, middle_gain_grad = jax.vjp(rms_norm, stream_mid, gains[1])[1](inner_grad)
    mid_grad = out_grad + mid_part
    attend_low = gather_tp(mid_grad.astype(bf16))
    attended_grad = heads_on_lanes(contract_last(w_out, attend_low).astype(bf16))
    dq, pair_grads = attend_back(
        spans, own_places, queries, attended_grad, log_total, row_keyvals
    )
    pair_grads = pair_grads.reshape(2, N_CTX, 128, 2 * HD)
    half_grads = (pair_grads[0] + core_swap(pair_grads[1].astype(bf16)).astype(f32)).astype(bf16)
    query_linear_low = heads_on_rows(rotate_rows(dq, cosine_4, -sine_4).astype(bf16))
    half_grads, both_low = lax.optimization_barrier((half_grads, both_grad_low))
    came = lax.all_to_all(half_grads, CTX, 0, 0, tiled=True)
    layer_low = row_products(
        [inner_low, attend_low, branch_low, normed_low],
        [both_low, attended_rows, hidden_low, query_linear_low],
    )
    own_grads = jnp.sum(came.astype(f32), axis=0)
    keyval_low = jnp.concatenate(
        [
            rotate_lanes(own_grads[:, :HD], cosine[:, :128].T, -sine[:, :128].T),
            own_grads[:, HD:],
        ],
        axis=1,
    ).astype(bf16)
    normed_part = contract_first(query_linear_low, w_query).reshape(2, 128, D)
    normed_part = jnp.stack([normed_part[0] + contract_last(keyval_low, w_pair), normed_part[1]])
    layer_low, head_low, normed_part = lax.optimization_barrier((layer_low, head_low, normed_part))
    layer_low = lax.psum_scatter(layer_low, CTX, scatter_dimension=0, tiled=True)[0]
    normed_grad = scatter_tp(normed_part.reshape(2, N_X, SHARD, D))
    pair_low = contract_first(keyval_low, normed_half).astype(bf16)
    pair_low = pair_low.reshape(2 * HD, N_CTX, LINES).transpose(1, 0, 2)
    first_part, first_gain_grad = jax.vjp(rms_norm, stream_in, gains[0])[1](normed_grad)
    input_low = (mid_grad + first_part).astype(bf16)

    gain_parts = jnp.stack([first_gain_grad, middle_gain_grad, final_gain_grad]).astype(bf16)
    sent = jnp.concatenate(
        [
            input_low.reshape(SHARD, N_CTX, LINES).transpose(1, 0, 2),
            jnp.pad(gain_parts.reshape(3, N_CTX, LINES).transpose(1, 0, 2), ((0, 0), (0, 13), (0, 0))),
        ],
        axis=1,
    )
    arrived = lax.all_to_all(sent, CTX, 0, 0, tiled=True)
    pair_low, arrived = lax.optimization_barrier((pair_low, arrived))
    kv_part = jnp.sum(lax.all_to_all(pair_low, CTX, 0, 0, tiled=True).astype(f32), axis=0)
    gain_sums = jnp.sum(arrived[:, SHARD : SHARD + 3].astype(f32), axis=0)
    place_grads = gather_tp(arrived[:, :SHARD].reshape(N_CTX * SHARD, LINES))
    embed_grad = add_up(all_ids, place_grads, vocab_here)

    kv_full = kv_part + core_swap(kv_part)
    kv_split = kv_full.T.reshape(N_X, 2, 16, 2 * HD)
    kv_owned = swapped_x(jnp.where(cs == 0, kv_split[:, 0], kv_split[:, 1]), xs)
    key_value_grad = (
        kv_owned.reshape(KV_HEADS, 16, 2, HD).transpose(1, 2, 0, 3).reshape(16, KVW)
    )

    old_rows = jnp.concatenate(
        [attention_row_moment, feed_row_moment, vocab_row_moment, jnp.ones((9, LINES), f32)]
    )
    kv_old_columns = lax.dynamic_index_in_dim(
        key_value_column_moment.reshape(2, KV_HEADS, HD), xs, 1, keepdims=False
    ).reshape(-1)
    early_old = jnp.concatenate(
        [
            jnp.pad(vocab_column_moment, ((0, 0), (0, EARLY_LANES - vocab_here)), constant_values=1.0),
            jnp.concatenate(
                [kv_old_columns, jnp.ones((EARLY_LANES - 128,), f32)]
            )[None],
        ]
    )
    late_old = jnp.concatenate(
        [
            feed_column_moment[0],
            feed_column_moment[1],
            attention_column_moment[1],
            feed_column_moment[2],
            attention_column_moment[0],
            jnp.ones((64,), f32),
        ]
    )[None]
    kv_old_line = lax.dynamic_update_slice_in_dim(
        jnp.zeros((1, LINES), f32), key_value_row_moment[None], tp_index * 16, 1
    )
    feed_tables = feed_master.transpose(0, 2, 1)
    vocab_grad, line_parts, column_parts, base = early_figures(
        head_low,
        embed_grad,
        kv_full,
        gain_sums,
        kv_old_line,
        tables,
        feed_tables,
        attention_master,
        key_value_master,
        gain_master.T,
        loss_part.reshape(1, 1),
    )
    lines = sum_tp(line_parts)
    columns = sum_ctx(column_parts)
    gain_grad = lax.dynamic_slice_in_dim(lines[8:11], tp_index * 16, 16, 1)
    gain_second = moments(gain_moment.T, gain_grad * gain_grad, 1.0)
    gain_step = gain_grad * lax.rsqrt(gain_second)
    gain_squares = jnp.sum(gain_step * gain_step, axis=1)[None]
    base = base + jnp.pad(gain_squares, ((0, 0), (UG_LANE, 128 - UG_LANE - 3)))
    early_rows, early_columns, base = step_squares(
        early_squares_kernel,
        (vocab_grad, kv_full),
        lines,
        columns,
        old_rows,
        early_old,
        base,
    )
    feed_grad, attention_grad, late_line_parts, late_column_parts = late_figures(layer_low)
    late_rows, late_columns, scalars = step_squares(
        late_squares_kernel,
        (layer_low,),
        sum_tp(late_line_parts),
        sent_to_all(late_column_parts, CTX),
        old_rows,
        late_old,
        base,
    )
    kv_columns_here = early_columns[2:3, :128]
    gathered = sent_to_all(jnp.concatenate([scalars, kv_columns_here]), CTX_TP)
    vocab_new, feed_new, attention_new, gain_new, figures = update(
        gathered[:, 0],
        tables,
        vocab_grad,
        feed_tables,
        feed_grad,
        attention_master,
        attention_grad,
        early_rows,
        late_rows,
        early_columns,
        late_columns,
        gain_master.T,
        gain_step,
    )
    token_loss = figures[2, 0]
    update_rms = figures[0, :11]
    kv_row_new = lax.dynamic_slice_in_dim(early_rows[7], tp_index * 16, 16, 0)
    kv_column_new = (
        gathered[0:8:2, 1].reshape(KV_HEADS, 2, HD).transpose(1, 0, 2).reshape(KVW)
    )
    kv_step = key_value_grad * lax.rsqrt(kv_row_new)[:, None] * lax.rsqrt(kv_column_new)[None]
    kv_new = key_value_master - figures[1, 7] * kv_step
    attention_columns = jnp.stack([late_columns[0, 2368:2624], late_columns[0, 1408:1664]])
    feed_columns = jnp.stack(
        [late_columns[0, :704], late_columns[0, 704:1408], late_columns[0, 1664:2368]]
    )
    return (
        token_loss,
        update_rms,
        attention_grad,
        late_rows[0:2],
        attention_columns,
        attention_new,
        feed_grad.transpose(0, 2, 1),
        late_rows[2:5],
        feed_columns,
        feed_new.transpose(0, 2, 1),
        vocab_grad.transpose(0, 2, 1),
        early_rows[5:7],
        early_columns[0, :vocab_here],
        early_columns[1, :vocab_here],
        vocab_new.transpose(0, 2, 1),
        key_value_grad,
        kv_row_new,
        kv_column_new,
        kv_new,
        gain_grad.T,
        gain_second.T,
        gain_new.T,
    )


def solution(mesh):
    finer = Mesh(mesh.devices.reshape(4, 4, 4, 2), ("ctx_0", "ctx_1", "tp_0", "tp_1"))
    in_specs = (
        P(CTX),
        P(CTX),
        P(CTX),
        P(),
        P(),
        P(None, CTX, TP),
        P(None, CTX, TP),
        P(None, CTX, TP),
        P(CTX_TP, None),
        P(CTX_TP, None),
        P(None, CTX),
        P(None, TP),
        P(None, CTX),
        P(None, TP),
        P(None, CTX),
        P(None, TP),
        P(CTX_TP),
        P(),
        P(CTX_TP, None),
    )
    out_specs = (
        P(),
        P(),
        P(None, CTX, TP),
        P(None, CTX),
        P(None, TP),
        P(None, CTX, TP),
        P(None, CTX, TP),
        P(None, CTX),
        P(None, TP),
        P(None, CTX, TP),
        P(None, CTX, TP),
        P(None, CTX),
        P(TP),
        P(TP),
        P(None, CTX, TP),
        P(CTX_TP, None),
        P(CTX_TP),
        P(),
        P(CTX_TP, None),
        P(CTX_TP, None),
        P(CTX_TP, None),
        P(CTX_TP, None),
    )
    return jax.shard_map(body, mesh=finer, in_specs=in_specs, out_specs=out_specs, check_vma=False)
```

```python
import functools
import math

import jax
import jax.numpy as jnp
from jax import lax
from jax.experimental import pallas as pl
from jax.experimental.pallas import tpu as pltpu
from jax.sharding import Mesh
from jax.sharding import PartitionSpec as P

D = 2048
HEADS = 32
KV_HEADS = 4
HD = 64
FF = 5632
VOCAB = 32000
ORIG_CTX = 2048
HQ = 2048
KVW = 512
TOKENS = 4096
TP = ("tp_0", "tp_1")
CTX = ("ctx_0", "ctx_1")
CTX_TP = ("ctx_0", "ctx_1", "tp_0", "tp_1")
N_CTX = 16
N_X = 4
N_TP = 8
SHARD = 32
LINES = 128
DOCS = 5

NORM_EPS = 1e-05
MOMENT_DECAY = 0.5
MOMENT_EPS = 1e-30
CLIP_LIMIT = 0.5
STEP_SCALE = 1.0
ROPE_BASE = 10000.0
YARN_SCALE = 4.0
YARN_ALPHA = 1.0
YARN_BETA = 32.0

bf16 = jnp.bfloat16
f32 = jnp.float32


def x_from(values, step):
    return lax.ppermute(values, "tp_0", [((i + step) % N_X, i) for i in range(N_X)])


def x_to(values, step):
    return lax.ppermute(values, "tp_0", [(i, (i + step) % N_X) for i in range(N_X)])


def core_swap(values):
    return lax.ppermute(values, "tp_1", [(0, 1), (1, 0)])


def turned(stack, start):
    return lax.dynamic_slice_in_dim(jnp.concatenate([stack, stack]), start, N_X, 0)


def to_absolute(stack, xs):
    return turned(stack, (N_X - xs) % N_X)


def gather_tp(shard):
    column = jnp.concatenate([shard] + [x_from(shard, d) for d in range(1, N_X)])
    return jnp.concatenate([column, core_swap(column)])


def scatter_tp(partial):
    half = partial[0] + core_swap(partial[1].astype(bf16)).astype(f32)
    low = half.astype(bf16)
    total = half[0]
    for d in range(1, N_X):
        total = total + x_to(low[d], d).astype(f32)
    return total


def both_cores(column, cs):
    other = core_swap(column)
    both = jnp.where(
        cs == 0, jnp.stack([column, other], axis=1), jnp.stack([other, column], axis=1)
    )
    return both.reshape(-1, *column.shape[2:])


def swapped_x(blocks, xs):
    ours = turned(blocks, xs)
    came = [ours[0]] + [x_to(ours[d], d) for d in range(1, N_X)]
    return to_absolute(jnp.stack([came[0], came[3], came[2], came[1]]), xs)


def partner(values, axis, mask):
    size = 2 if axis == "tp_1" else 4
    return lax.ppermute(values, axis, [(i, i ^ mask) for i in range(size)])


def sum_over_four(values, axis):
    return (values + partner(values, axis, 1)) + (
        partner(values, axis, 2) + partner(values, axis, 3)
    )


def sum_tp(values):
    return sum_over_four(values + partner(values, "tp_1", 1), "tp_0")


def sum_ctx(values):
    return sum_over_four(sum_over_four(values, "ctx_1"), "ctx_0")


def own_order(values, xs, cs):
    blocks = turned(values.reshape(N_X, 2, SHARD), xs)
    blocks = jnp.where(cs == 0, blocks, blocks[:, ::-1])
    return blocks.transpose(1, 0, 2)


def sent_to_all(array, axis):
    copies = jnp.broadcast_to(array, (lax.axis_size(axis), *array.shape))
    return lax.all_to_all(copies, axis, split_axis=0, concat_axis=0, tiled=True)


def rope_tables(positions):
    ladder = jnp.arange(HD // 2, dtype=f32)
    freqs = ROPE_BASE ** (-2.0 * ladder / HD)
    ratio = ORIG_CTX * freqs / (2.0 * math.pi)
    ramped = jnp.clip((ratio - YARN_ALPHA) / (YARN_BETA - YARN_ALPHA), 0.0, 1.0)
    inverse = freqs * (1.0 - ramped) / YARN_SCALE + freqs * ramped
    angles = inverse[:, None] * positions.astype(f32)[None, :]
    mscale = 0.1 * math.log(YARN_SCALE) + 1.0
    return (jnp.cos(angles) * mscale, jnp.sin(angles) * mscale)


def rotate_rows(values, cosine, sine):
    half = values.shape[0] // 2
    first, second = (values[:half], values[half:])
    return jnp.concatenate([first * cosine - second * sine, second * cosine + first * sine])


def rotate_lanes(values, cosine, sine):
    half = values.shape[1] // 2
    first, second = (values[:, :half], values[:, half:])
    return jnp.concatenate([first * cosine - second * sine, second * cosine + first * sine], axis=1)


def rms_norm(values, gain):
    return values * lax.rsqrt(jnp.mean(values * values, axis=-1, keepdims=True) + NORM_EPS) * gain


def contract_last(left, right):
    return lax.dot_general(left, right, (((1,), (1,)), ((), ())), preferred_element_type=f32)


def contract_first(left, right):
    return lax.dot_general(left, right, (((0,), (0,)), ((), ())), preferred_element_type=f32)


def contract(left, right):
    return jnp.dot(left, right, preferred_element_type=f32)


def combine_stats(former, latter):
    highest = jnp.maximum(former[0], latter[0])
    summed = former[1] * jnp.exp(former[0] - highest) + latter[1] * jnp.exp(latter[0] - highest)
    return jnp.stack([highest, summed, former[2] + latter[2]])


def contract_ft(weights, places):
    return lax.dot_general(weights, places, (((0,), (1,)), ((), ())), preferred_element_type=f32)


def contract_tf(features, weights):
    return lax.dot_general(features, weights, (((0,), (1,)), ((), ())), preferred_element_type=f32)


def heads_on_lanes(features):
    return jnp.concatenate([features[h * HD : (h + 1) * HD] for h in range(4)], axis=1)


def heads_on_rows(features):
    return jnp.concatenate(jnp.split(features, 4, axis=1))


VMEM_LIMIT = 50 * 1024 * 1024


GROUP = 4
KEYS = 128 * GROUP
STEPS = TOKENS // KEYS


def key_places(core_bit, spans):
    line = lax.broadcasted_iota(jnp.int32, (128, 1), 0)
    x = (spans[N_CTX] + line // SHARD) % N_X
    place = (x * 2 + (spans[N_CTX + 1] ^ core_bit)) * SHARD + line % SHARD
    return place >= 128, place % 128


def visible_keys(spans, places, step, own, start):
    lines = []
    for block in range(step * GROUP, (step + 1) * GROUP):
        span = spans[block % N_CTX]
        second, within = places[block // N_CTX]
        lines.append(jnp.where(second, (2 * N_CTX - 1 - span) * 128, span * 128) + within)
    at = jnp.concatenate(lines, axis=0)
    return (at >= start) & (at <= own)


def key_columns(kv_ref, step, at):
    return jnp.concatenate(
        [kv_ref[step * GROUP + i, at : at + HD] for i in range(GROUP)], axis=1
    )


def attend_kernel(spans, own_ref, q_ref, kv_ref, o_ref, total_ref, s_ref):
    q = q_ref[...]
    own, start = (own_ref[0:1], own_ref[1:2])
    places = [key_places(core_bit, spans) for core_bit in range(2)]
    top = None
    for step in range(STEPS):
        scores = contract_first(key_columns(kv_ref, step, 0), q)
        scores = jnp.where(visible_keys(spans, places, step, own, start), scores, -1e30)
        s_ref[step * KEYS : (step + 1) * KEYS] = scores
        highest = jnp.max(scores, axis=0, keepdims=True)
        top = highest if top is None else jnp.maximum(top, highest)
    total = jnp.zeros(top.shape, f32)
    for step in range(STEPS):
        powers = jnp.exp(s_ref[step * KEYS : (step + 1) * KEYS] - top)
        s_ref[step * KEYS : (step + 1) * KEYS] = powers
        total = total + jnp.sum(powers, axis=0, keepdims=True)
    share = 1.0 / total
    out = jnp.zeros(q.shape, f32)
    for step in range(STEPS):
        weights = (s_ref[step * KEYS : (step + 1) * KEYS] * share).astype(bf16)
        out = out + contract(key_columns(kv_ref, step, HD), weights)
    o_ref[...] = out.astype(bf16)
    total_ref[...] = top + jnp.log(total)


SPLIT = 2


def attend(spans, own, q, kv):
    lanes = q.shape[1] // SPLIT
    column = lambda rows: pl.BlockSpec((rows, lanes), lambda i: (0, i))
    return pl.pallas_call(
        attend_kernel,
        grid=(SPLIT,),
        in_specs=[
            pl.BlockSpec(memory_space=pltpu.SMEM),
            column(2),
            column(HD),
            pl.BlockSpec(kv.shape, lambda i: (0, 0, 0)),
        ],
        out_specs=[column(HD), column(1)],
        out_shape=[
            jax.ShapeDtypeStruct(q.shape, bf16),
            jax.ShapeDtypeStruct((1, q.shape[1]), f32),
        ],
        scratch_shapes=[pltpu.VMEM((TOKENS, lanes), f32)],
        compiler_params=pltpu.CompilerParams(vmem_limit_bytes=VMEM_LIMIT),
        cost_estimate=pl.CostEstimate(
            flops=16 * TOKENS * q.shape[1] * HD, bytes_accessed=2 << 20, transcendentals=0
        ),
    )(spans, own, q, kv)


def attend_back_kernel(
    spans, own_ref, q_ref, do_ref, total_ref, kv_ref, dq_ref, dkv_ref, p_ref, dp_ref
):
    q, do = (q_ref[...], do_ref[...])
    own, start = (own_ref[0:1], own_ref[1:2])
    total = total_ref[...]
    places = [key_places(core_bit, spans) for core_bit in range(2)]
    rowsum = jnp.zeros(total.shape, f32)
    for step in range(STEPS):
        scores = contract_first(key_columns(kv_ref, step, 0), q)
        scores = jnp.where(visible_keys(spans, places, step, own, start), scores, -1e30)
        probs = jnp.exp(scores - total)
        probs_grad = contract_first(key_columns(kv_ref, step, HD), do)
        p_ref[step * KEYS : (step + 1) * KEYS] = probs
        dp_ref[step * KEYS : (step + 1) * KEYS] = probs_grad
        rowsum = rowsum + jnp.sum(probs * probs_grad, axis=0, keepdims=True)

    @pl.when(pl.program_id(0) == 0)
    def _():
        dkv_ref[...] = jnp.zeros(dkv_ref.shape, f32)

    dq = jnp.zeros(q.shape, f32)
    for step in range(STEPS):
        rows = slice(step * KEYS, (step + 1) * KEYS)
        probs = p_ref[rows]
        score_grad = (probs * (dp_ref[rows] - rowsum)).astype(bf16)
        dkv_ref[rows] += jnp.concatenate(
            [contract_last(score_grad, q), contract_last(probs.astype(bf16), do)], axis=1
        )
        dq = dq + contract(key_columns(kv_ref, step, 0), score_grad)
    dq_ref[...] = dq * (1.0 / math.sqrt(HD))


def attend_back(spans, own, q, do, total, kv):
    lanes = q.shape[1] // SPLIT
    column = lambda rows: pl.BlockSpec((rows, lanes), lambda i: (0, i))
    return pl.pallas_call(
        attend_back_kernel,
        grid=(SPLIT,),
        in_specs=[
            pl.BlockSpec(memory_space=pltpu.SMEM),
            column(2),
            column(HD),
            column(HD),
            column(1),
            pl.BlockSpec(kv.shape, lambda i: (0, 0, 0)),
        ],
        out_specs=[column(HD), pl.BlockSpec((TOKENS, 2 * HD), lambda i: (0, 0))],
        out_shape=[
            jax.ShapeDtypeStruct(q.shape, f32),
            jax.ShapeDtypeStruct((TOKENS, 2 * HD), f32),
        ],
        scratch_shapes=[pltpu.VMEM((TOKENS, lanes), f32), pltpu.VMEM((TOKENS, lanes), f32)],
        compiler_params=pltpu.CompilerParams(vmem_limit_bytes=VMEM_LIMIT),
        cost_estimate=pl.CostEstimate(
            flops=40 * TOKENS * q.shape[1] * HD, bytes_accessed=4 << 20, transcendentals=0
        ),
    )(spans, own, q, do, total, kv)


def moments(old, sums, count):
    return MOMENT_DECAY * old + (1.0 - MOMENT_DECAY) * (sums / count + MOMENT_EPS)


def params():
    return pltpu.CompilerParams(vmem_limit_bytes=VMEM_LIMIT)


def whole(array):
    zeros = (0,) * array.ndim
    return pl.BlockSpec(array.shape, lambda *i: zeros)


def cost(flops, moved):
    return pl.CostEstimate(flops=flops, bytes_accessed=moved, transcendentals=0)


ID_STEP = 2048


def look_kernel(ids_ref, table_ref, out_ref, low_ref):
    @pl.when(pl.program_id(0) == 0)
    def _():
        low_ref[...] = table_ref[0].astype(bf16)

    width = low_ref.shape[0]
    ids = jnp.transpose(jnp.broadcast_to(ids_ref[...], (8, ID_STEP)))[:, :1]
    hits = ids == lax.broadcasted_iota(jnp.int32, (ID_STEP, width), 1)
    out_ref[...] = contract(jnp.where(hits, 1.0, 0.0).astype(bf16), low_ref[...]).astype(bf16)


def look_up(ids, tables):
    width, lines = tables.shape[1:]
    count = ids.shape[1]
    return pl.pallas_call(
        look_kernel,
        grid=(count // ID_STEP,),
        in_specs=[
            pl.BlockSpec((1, ID_STEP), lambda i: (0, i)),
            pl.BlockSpec((1, width, lines), lambda i: (1, 0, 0)),
        ],
        out_specs=pl.BlockSpec((ID_STEP, lines), lambda i: (i, 0)),
        out_shape=jax.ShapeDtypeStruct((count, lines), bf16),
        scratch_shapes=[pltpu.VMEM((width, lines), bf16)],
        compiler_params=params(),
        cost_estimate=cost(4 * count * width * lines, 4 * lines * width),
    )(ids, tables)


def add_kernel(ids_ref, grads_ref, out_ref):
    hits = lax.broadcasted_iota(jnp.int32, (out_ref.shape[0], ID_STEP), 0) == ids_ref[...]
    added = contract(jnp.where(hits, 1.0, 0.0).astype(bf16), grads_ref[...])

    @pl.when(pl.program_id(0) == 0)
    def _():
        out_ref[...] = added

    @pl.when(pl.program_id(0) > 0)
    def _():
        out_ref[...] += added


def add_up(ids, grads, width):
    count, lines = grads.shape
    return pl.pallas_call(
        add_kernel,
        grid=(count // ID_STEP,),
        in_specs=[
            pl.BlockSpec((1, ID_STEP), lambda i: (0, i)),
            pl.BlockSpec((ID_STEP, lines), lambda i: (i, 0)),
        ],
        out_specs=pl.BlockSpec((width, lines), lambda i: (0, 0)),
        out_shape=jax.ShapeDtypeStruct((width, lines), f32),
        compiler_params=params(),
        cost_estimate=cost(4 * count * width * lines, 4 * lines * width),
    )(ids, grads)


LOGIT_STEP = 800


def logits_kernel(c_ref, w_ref, target_ref, out_ref, stats_ref):
    step = pl.program_id(0)
    logits = contract_last(w_ref[...], c_ref[...])
    out_ref[...] = logits
    row = lax.broadcasted_iota(jnp.int32, logits.shape, 0) + step * LOGIT_STEP
    here = jnp.max(logits, axis=0, keepdims=True)
    pick = jnp.sum(jnp.where(row == target_ref[...], logits, 0.0), axis=0, keepdims=True)

    @pl.when(step == 0)
    def _():
        stats_ref[...] = jnp.zeros(stats_ref.shape, f32)
        stats_ref[0:1] = here

    old = stats_ref[0:1]
    top = jnp.maximum(old, here)
    powers = jnp.sum(jnp.exp(logits - top), axis=0, keepdims=True)
    stats_ref[1:2] = stats_ref[1:2] * jnp.exp(old - top) + powers
    stats_ref[2:3] += pick
    stats_ref[0:1] = top


def logits_and_stats(c, head, width, targets):
    places, rows = c.shape
    return pl.pallas_call(
        logits_kernel,
        grid=(width // LOGIT_STEP,),
        in_specs=[whole(c), pl.BlockSpec((LOGIT_STEP, rows), lambda i: (i, 0)), whole(targets)],
        out_specs=[
            pl.BlockSpec((LOGIT_STEP, places), lambda i: (i, 0)),
            pl.BlockSpec((8, places), lambda i: (0, 0)),
        ],
        out_shape=[
            jax.ShapeDtypeStruct((width, places), f32),
            jax.ShapeDtypeStruct((8, places), f32),
        ],
        compiler_params=params(),
        cost_estimate=cost(2 * places * rows * width, 2 * rows * width),
    )(c, head, targets)


def head_grad_kernel(logits_ref, c_ref, place_ref, target_ref, dw_ref, low_ref):
    step = pl.program_id(0)
    logits = logits_ref[...]
    row = lax.broadcasted_iota(jnp.int32, logits.shape, 0) + step * LOGIT_STEP
    hit = row == target_ref[...]
    shares = jnp.exp(logits - place_ref[0:1]) - jnp.where(hit, 1.0, 0.0)
    low = (place_ref[1:2] * shares).astype(bf16)
    low_ref[...] = low
    grad = contract(low, c_ref[...]).astype(bf16)
    for k in range(N_CTX):
        dw_ref[k] = grad[:, k * 128 : (k + 1) * 128]


def head_grads(logits, c, place, targets):
    places, rows = c.shape
    width = logits.shape[0]
    block = pl.BlockSpec((LOGIT_STEP, places), lambda i: (i, 0))
    return pl.pallas_call(
        head_grad_kernel,
        grid=(width // LOGIT_STEP,),
        in_specs=[block, whole(c), whole(place), whole(targets)],
        out_specs=[pl.BlockSpec((N_CTX, LOGIT_STEP, 128), lambda i: (0, i, 0)), block],
        out_shape=[
            jax.ShapeDtypeStruct((N_CTX, width, 128), bf16),
            jax.ShapeDtypeStruct((width, places), bf16),
        ],
        compiler_params=params(),
        cost_estimate=cost(2 * places * rows * width, 2 * rows * width),
    )(logits, c, place, targets)


TURNED = (1, 3)


def products_kernel(count, offsets, *refs):
    lefts, rights = (refs[:count], refs[count : 2 * count])
    out_ref, turned_ref = refs[2 * count :]

    @pl.when(pl.program_id(0) == 0)
    def _():
        for k, (right, (at, width)) in enumerate(zip(rights, offsets)):
            values = right[...]
            turned_ref[at : at + width] = values if k in TURNED else jnp.transpose(values)

    for left, (at, width) in zip(lefts, offsets):
        grad = contract(turned_ref[at : at + width], left[...]).astype(bf16)
        for k in range(2):
            out_ref[k, at : at + width] = grad[:, k * 128 : (k + 1) * 128]


def row_products(lefts, rights):
    places, rows = lefts[0].shape
    offsets, at = ([], 0)
    for k, right in enumerate(rights):
        width = right.shape[0 if k in TURNED else 1]
        offsets.append((at, width))
        at += width
    return pl.pallas_call(
        functools.partial(products_kernel, len(lefts), tuple(offsets)),
        grid=(N_CTX // 2,),
        in_specs=[pl.BlockSpec((places, 256), lambda i: (0, i)) for _ in lefts]
        + [whole(right) for right in rights],
        out_specs=pl.BlockSpec((2, at, 128), lambda i: (i, 0, 0)),
        out_shape=jax.ShapeDtypeStruct((N_CTX, at, rows // N_CTX), bf16),
        scratch_shapes=[pltpu.VMEM((at, places), bf16)],
        compiler_params=params(),
        cost_estimate=cost(2 * places * rows * at, 2 * rows * at),
    )(*lefts, *rights)


MATRICES = 8
WIDTHS = (HQ, HQ, FF, FF, FF, VOCAB, VOCAB, KVW)
EARLY_LANES = 4096
LATE_LANES = 2688
COLUMN_AT = {0: (0, 2368, 256), 7: (2, 0, 128), 5: (0, 0, 4000), 6: (1, 0, 4000)}
COLUMN_AT.update({2: (0, 0, 704), 3: (0, 704, 704), 1: (0, 1408, 256), 4: (0, 1664, 704)})
S_LANE, T_LANE, OLD_LANE, W_LANE, WG_LANE, UG_LANE, LOSS_LANE = (0, 8, 16, 24, 32, 35, 38)


def lane_is(shape, lane):
    return lax.broadcasted_iota(jnp.int32, shape, 1) == lane


def line_sum(values):
    return jnp.sum(values, axis=0, keepdims=True)


def total_of(values):
    return jnp.sum(line_sum(values), axis=1, keepdims=True)


def column_sums(squares):
    ones = jnp.ones((8, squares.shape[1]), f32)
    return lax.dot_general(
        ones,
        squares,
        (((1,), (1,)), ((), ())),
        precision=lax.Precision.HIGHEST,
        preferred_element_type=f32,
    )


def weights_kernel(tables_ref, feed_ref, attention_ref, kv_master_ref, gain_ref, scalars_ref):
    scalars = jnp.zeros(scalars_ref.shape, f32)
    for number, weights in (
        (0, attention_ref[0]),
        (1, attention_ref[1]),
        (2, feed_ref[0]),
        (3, feed_ref[1]),
        (4, feed_ref[2]),
        (5, tables_ref[0]),
        (6, tables_ref[1]),
        (7, kv_master_ref[...]),
        (8, gain_ref[0:1]),
        (9, gain_ref[1:2]),
        (10, gain_ref[2:3]),
    ):
        scalars += jnp.where(
            lane_is(scalars.shape, W_LANE + number), total_of(weights * weights), 0.0
        )
    scalars_ref[...] = scalars


def weight_squares(*masters):
    return pl.pallas_call(
        weights_kernel,
        out_shape=jax.ShapeDtypeStruct((1, 128), f32),
        compiler_params=params(),
        cost_estimate=cost(0, 6 << 20),
    )(*masters)


def early_kernel(
    head_ref, embed_ref, kv_ref, gains_ref, kv_old_ref, vocab_grad_ref, lines_ref, columns_ref
):
    columns_ref[...] = jnp.zeros(columns_ref.shape, f32)
    lines_ref[...] = jnp.zeros(lines_ref.shape, f32)
    lines_ref[8:11] = gains_ref[...]
    lines_ref[11:12] = kv_old_ref[...]
    for number, ref in ((5, head_ref), (6, embed_ref), (7, kv_ref)):
        grad = ref[...].astype(f32)
        if number in (5, 6):
            vocab_grad_ref[number - 5] = grad
        squares = grad * grad
        lines_ref[number : number + 1] = (0.5 if number == 7 else 1.0) * line_sum(squares)
        line, at, width = COLUMN_AT[number]
        columns_ref[line : line + 1, at : at + width] = column_sums(squares)[:1]


def early_figures(*arrays):
    shapes = ((2, *arrays[1].shape), (16, 128), (3, EARLY_LANES))
    return pl.pallas_call(
        early_kernel,
        out_shape=[jax.ShapeDtypeStruct(shape, f32) for shape in shapes],
        compiler_params=params(),
        cost_estimate=cost(0, 12 << 20),
    )(*arrays)


def late_kernel(layer_ref, feed_grad_ref, attention_grad_ref, lines_ref, columns_ref):
    layer = layer_ref[...].astype(f32)
    squares = layer * layer
    lines_ref[...] = jnp.zeros(lines_ref.shape, f32)
    columns_ref[...] = jnp.zeros(columns_ref.shape, f32)
    columns_ref[:, : layer.shape[0]] = column_sums(squares)[:1]
    for number in range(5):
        line, at, width = COLUMN_AT[number]
        lines_ref[number : number + 1] = line_sum(squares[at : at + width])
        if number > 1:
            feed_grad_ref[number - 2] = layer[at : at + width]
    attention_grad_ref[0] = jnp.transpose(layer[2368:2624])
    attention_grad_ref[1] = jnp.transpose(layer[1408:1664])


def late_figures(layer):
    shapes = ((3, 704, 128), (2, 128, 256), (8, 128), (1, LATE_LANES))
    return pl.pallas_call(
        late_kernel,
        out_shape=[jax.ShapeDtypeStruct(shape, f32) for shape in shapes],
        compiler_params=params(),
        cost_estimate=cost(0, 4 << 20),
    )(layer)


def per_column(figures, number):
    line, at, width = COLUMN_AT[number]
    return figures[at : at + width, line : line + 1]


def on_rows(columns):
    spare = 8 - columns.shape[0]
    return jnp.transpose(
        jnp.concatenate([columns, jnp.ones((spare, columns.shape[1]), f32)], axis=0)
    )


def squares_of(sources, lines, old, columns, old_columns, base, row_ref, column_ref, scalars_ref):
    number = lax.broadcasted_iota(jnp.int32, lines.shape, 0)
    widths = jnp.full(lines.shape, 1.0, f32)
    for k, width in enumerate(WIDTHS):
        widths = jnp.where(number == k, float(width), widths)
    row_new = moments(old, lines / widths, 1.0)
    row_ref[...] = row_new
    column_new = moments(old_columns, columns, float(D))
    column_ref[...] = column_new
    row_scale = lax.rsqrt(row_new)
    column_scale = on_rows(lax.rsqrt(column_new))
    scalars = base
    had = jnp.sum(old, axis=1, keepdims=True) * (1.0 / N_TP)
    got = jnp.sum(lines, axis=1, keepdims=True) * (1.0 / N_TP)
    for k, grad, keep in sources:
        unit = grad * row_scale[k : k + 1] * per_column(column_scale, k)
        if keep is not None:
            keep[0][keep[1]] = jnp.transpose(unit) if k < 2 else unit
        part = total_of(unit * unit) * (0.5 if k == 7 else 1.0)
        scalars += jnp.where(lane_is(scalars.shape, S_LANE + k), part, 0.0)
        scalars += jnp.where(lane_is(scalars.shape, T_LANE + k), got[k : k + 1], 0.0)
        scalars += jnp.where(lane_is(scalars.shape, OLD_LANE + k), had[k : k + 1], 0.0)
    scalars_ref[...] = scalars


def early_squares_kernel(
    vocab_ref, kv_ref, lines_ref, columns_ref, old_ref, old_columns_ref, base_ref,
    row_ref, column_ref, scalars_ref, unit_ref,
):
    lines = lines_ref[...]
    number = lax.broadcasted_iota(jnp.int32, lines.shape, 0)
    old = jnp.where(number == 7, lines_ref[11:12], old_ref[...])
    sources = (
        (5, vocab_ref[0], (unit_ref, 0)),
        (6, vocab_ref[1], (unit_ref, 1)),
        (7, kv_ref[...], None),
    )
    squares_of(
        sources, lines, old, columns_ref[...], old_columns_ref[...], base_ref[...],
        row_ref, column_ref, scalars_ref,
    )


def late_squares_kernel(
    layer_ref, lines_ref, columns_ref, old_ref, old_columns_ref, base_ref,
    row_ref, column_ref, scalars_ref, feed_unit_ref, attention_unit_ref,
):
    layer = layer_ref[...].astype(f32)
    sources = []
    for number in range(5):
        line, at, width = COLUMN_AT[number]
        keep = (attention_unit_ref, number) if number < 2 else (feed_unit_ref, number - 2)
        sources.append((number, layer[at : at + width], keep))
    columns = jnp.sum(columns_ref[...], axis=0)
    squares_of(
        sources, lines_ref[...], old_ref[0:8], columns, old_columns_ref[...], base_ref[...],
        row_ref, column_ref, scalars_ref,
    )


def step_squares(kernel, grads, lines, columns, old, old_columns, base, units):
    shapes = [a.shape for a in (lines, old_columns, base)] + list(units)
    return pl.pallas_call(
        kernel,
        out_shape=[jax.ShapeDtypeStruct(shape, f32) for shape in shapes],
        compiler_params=params(),
        cost_estimate=cost(0, 16 << 20),
    )(*grads, lines, columns, old, old_columns, base)


UPDATE_STEP = 800


def update_kernel(
    all_ref, vocab_ref, vocab_unit_ref, feed_ref, feed_unit_ref, attention_ref,
    attention_unit_ref, gain_ref, gain_step_ref,
    vocab_new_ref, feed_new_ref, attention_new_ref, gain_new_ref, figures_ref,
):
    sums = jnp.sum(all_ref[...], axis=0, keepdims=True)
    sums = jnp.broadcast_to(sums, (8, 128))

    def lanes_from(at):
        return pltpu.roll(sums, (128 - at) % 128, 1)[0:1]

    lane = lax.broadcasted_iota(jnp.int32, (1, 128), 1)
    counts = jnp.full((1, 128), float(D), f32)
    for k, width in enumerate(WIDTHS):
        counts = jnp.where(lane == k, float(D * width), counts)
    mean = MOMENT_DECAY * lanes_from(OLD_LANE) / D + (1.0 - MOMENT_DECAY) * (
        lanes_from(T_LANE) / counts + MOMENT_EPS
    )
    mean = jnp.where(lane < MATRICES, mean, 1.0)
    rms = jnp.sqrt(mean * lanes_from(S_LANE) / counts)
    factor = (
        STEP_SCALE
        * jnp.sqrt(lanes_from(W_LANE) / counts)
        / jnp.maximum(1.0, rms / CLIP_LIMIT)
        * jnp.sqrt(mean)
    )

    @pl.when(pl.program_id(0) == 0)
    def _():
        for k in range(2):
            attention_new_ref[k] = attention_ref[k] - attention_unit_ref[k] * factor[:, k : k + 1]
        for k in range(3):
            feed_new_ref[k] = feed_ref[k] - feed_unit_ref[k] * factor[:, 2 + k : 3 + k]
        gain_rms = jnp.sqrt(lanes_from(UG_LANE) / D)
        gain_factor = (
            STEP_SCALE
            * jnp.sqrt(lanes_from(WG_LANE) / D)
            / jnp.maximum(1.0, gain_rms / CLIP_LIMIT)
        )
        for k in range(3):
            gain_new_ref[k : k + 1] = (
                gain_ref[k : k + 1] - gain_factor[:, k : k + 1] * gain_step_ref[k : k + 1]
            )
        after = pltpu.roll(jnp.broadcast_to(gain_rms, (8, 128)), MATRICES, 1)[0:1]
        figures_ref[0:1] = jnp.where(lane < MATRICES, rms, after)
        figures_ref[1:2] = factor
        figures_ref[2:3] = lanes_from(LOSS_LANE)
        figures_ref[3:8] = jnp.zeros((5, 128), f32)

    for k in range(2):
        vocab_new_ref[k] = vocab_ref[k] - vocab_unit_ref[k] * factor[:, 5 + k : 6 + k]


def update(gathered, vocab, vocab_unit, feed, feed_unit, attention, attention_unit, gain, gain_step):
    stack = pl.BlockSpec((2, UPDATE_STEP, vocab.shape[2]), lambda i: (0, i, 0))
    others = (feed, feed_unit, attention, attention_unit, gain, gain_step)
    outs = (vocab, feed, attention, gain)
    return pl.pallas_call(
        update_kernel,
        grid=(vocab.shape[1] // UPDATE_STEP,),
        in_specs=[whole(gathered), stack, stack] + [whole(a) for a in others],
        out_specs=[stack]
        + [whole(a) for a in outs[1:]]
        + [pl.BlockSpec((8, 128), lambda i: (0, 0))],
        out_shape=[jax.ShapeDtypeStruct(a.shape, f32) for a in outs]
        + [jax.ShapeDtypeStruct((8, 128), f32)],
        compiler_params=params(),
        cost_estimate=cost(0, 24 << 20),
    )(gathered, vocab, vocab_unit, *others)


def body(
    token_ids,
    target_ids,
    loss_mask,
    segment_ids,
    span_pairs,
    attention_master,
    feed_master,
    vocab_master,
    key_value_master,
    gain_master,
    attention_row_moment,
    attention_column_moment,
    feed_row_moment,
    feed_column_moment,
    vocab_row_moment,
    vocab_column_moment,
    key_value_row_moment,
    key_value_column_moment,
    gain_moment,
):
    ctx_index = lax.axis_index(CTX)
    xs = lax.axis_index("tp_0")
    cs = lax.axis_index("tp_1")
    tp_index = xs * 2 + cs
    vocab_here = vocab_master.shape[2]
    ff_here = feed_master.shape[2]
    first_id = tp_index * vocab_here

    attention_low = attention_master.astype(bf16)
    feed_low = feed_master.astype(bf16)
    layer_all = lax.all_gather(
        jnp.concatenate(
            [attention_low[0], attention_low[1], feed_low[0], feed_low[1], feed_low[2]], axis=1
        ),
        CTX,
        axis=0,
        tiled=True,
    ).T
    head = lax.all_gather(vocab_master[0].astype(bf16), CTX, axis=0, tiled=True).T
    w_query = layer_all[:256]
    w_out = layer_all[256:512]
    gate_up = layer_all[512 : 512 + 2 * ff_here]
    down = layer_all[512 + 2 * ff_here :]

    kv_low = key_value_master.astype(bf16).reshape(16, 2, KV_HEADS, HD).transpose(2, 0, 1, 3)
    gain_low = jnp.pad(gain_master.astype(bf16), ((0, 0), (0, 125)))
    blocks = jnp.concatenate(
        [
            kv_low.reshape(KV_HEADS, 16, 2 * HD),
            jnp.broadcast_to(gain_low, (KV_HEADS, *gain_low.shape)),
        ],
        axis=2,
    )
    ids_here = own_order(token_ids, xs, cs).reshape(1, 256)
    line_block = both_cores(swapped_x(blocks, xs), cs)
    early = sent_to_all(
        jnp.concatenate(
            [
                line_block[:, : 2 * HD],
                line_block[:, 2 * HD : 2 * HD + 3].T,
                (ids_here // 256).astype(bf16).reshape(2, 128),
                (ids_here % 256).astype(bf16).reshape(2, 128),
                jnp.zeros((9, 128), bf16),
            ]
        ),
        CTX,
    )
    w_pair = early[:, :LINES].reshape(D, 2 * HD)
    gains = early[:, LINES : LINES + 3].astype(f32).transpose(1, 0, 2).reshape(3, D)
    parts = early[:, LINES + 3 : LINES + 7].astype(jnp.int32).reshape(N_CTX, 2, 256)
    all_ids = parts[:, 0] * 256 + parts[:, 1]
    all_ids = all_ids.reshape(N_CTX, 8, SHARD).transpose(1, 0, 2).reshape(1, TOKENS) - first_id

    order = (
        ((xs + jnp.arange(N_X, dtype=jnp.int32)) % N_X * 2)[None, :]
        + (cs ^ jnp.arange(2, dtype=jnp.int32))[:, None]
    )[:, :, None] * SHARD + jnp.arange(SHARD, dtype=jnp.int32)
    second_span = order >= 128
    within = order % 128
    own_pair = lax.dynamic_slice_in_dim(span_pairs, ctx_index, 1)[0]
    last_span = 2 * N_CTX - 1
    own_pos = (jnp.where(second_span, last_span - own_pair, own_pair) * 128 + within).reshape(-1)
    doc_start = jnp.zeros_like(own_pos)
    for k in range(1, DOCS):
        start = jnp.sum((segment_ids < k).astype(jnp.int32))
        doc_start = jnp.where(own_pos >= start, start, doc_start)
    cosine, sine = rope_tables(own_pos - doc_start)
    cosine_4, sine_4 = (jnp.tile(cosine, (1, 4)), jnp.tile(sine, (1, 4)))
    own_places = jnp.tile(jnp.stack([own_pos, doc_start]), (1, 4))
    spans = jnp.concatenate([span_pairs, jnp.stack([xs, cs]).astype(jnp.int32)])

    tables = vocab_master.transpose(0, 2, 1)
    looked = look_up(all_ids, tables).reshape(2, N_X, N_CTX, SHARD, LINES)
    half = looked[0] + core_swap(looked[1])
    mine = half[0]
    for d in range(1, N_X):
        mine = mine + x_to(half[d], d)
    rows_in = lax.all_to_all(mine, CTX, 0, 0, tiled=True)
    stream_in = rows_in.transpose(1, 0, 2).reshape(SHARD, D).astype(f32)

    normed_low = gather_tp(rms_norm(stream_in, gains[0]).astype(bf16))
    normed_half = normed_low[:128]
    keyval_linear = contract_ft(w_pair, normed_half)
    own_keyvals = jnp.concatenate(
        [rotate_rows(keyval_linear[:HD], cosine[:, :128], sine[:, :128]), keyval_linear[HD:]]
    ).astype(bf16)
    half_keyvals = sent_to_all(own_keyvals, CTX)
    row_keyvals = jnp.concatenate([half_keyvals, core_swap(half_keyvals)])
    query_linear = heads_on_lanes(contract_last(w_query, normed_low))
    queries = rotate_rows(query_linear, cosine_4, sine_4).astype(bf16) * jnp.asarray(
        1.0 / math.sqrt(HD), bf16
    )
    attended, log_total = attend(spans, own_places, queries, row_keyvals)
    attended_rows = heads_on_rows(attended)
    stream_mid = stream_in + scatter_tp(
        contract_first(attended_rows, w_out).reshape(2, N_X, SHARD, D)
    )

    inner_low = gather_tp(rms_norm(stream_mid, gains[1]).astype(bf16))
    both = contract_last(inner_low, gate_up)
    gate, upward = (both[:, :ff_here], both[:, ff_here:])
    sigmoid_gate = jax.nn.sigmoid(gate)
    silu_gate = gate * sigmoid_gate
    hidden_low = (silu_gate * upward).astype(bf16)
    stream_out = stream_mid + scatter_tp(
        contract(hidden_low, down).reshape(2, N_X, SHARD, D)
    )

    feed_tables = feed_master.transpose(0, 2, 1)
    masters = (tables, feed_tables, attention_master, key_value_master, gain_master.T)
    masters, inner_low = lax.optimization_barrier((masters, inner_low))
    weight_sums = weight_squares(*masters)
    finals_low = gather_tp(rms_norm(stream_out, gains[2]).astype(bf16))
    weight_sums, finals_low = lax.optimization_barrier((weight_sums, finals_low))
    local_targets = own_order(target_ids, xs, cs).reshape(1, -1) - first_id
    logits, stats = logits_and_stats(finals_low, head, vocab_here, local_targets)
    stats = stats[:3].reshape(3, 2, N_X, SHARD)
    stats = combine_stats(stats, core_swap(stats)[:, ::-1])
    others = [jnp.roll(x_from(stats, d), d, axis=2) for d in range(1, N_X)]
    stats = combine_stats(combine_stats(stats, others[0]), combine_stats(others[1], others[2]))
    stats = stats.reshape(3, -1)
    vocab_total = stats[0] + jnp.log(stats[1])
    keep = own_order(loss_mask, xs, cs).reshape(-1).astype(f32)
    loss_part = jnp.sum((keep * (vocab_total - stats[2]))[:SHARD]) / TOKENS

    place = jnp.stack([vocab_total, keep / TOKENS])
    head_low, dlogits_low = head_grads(logits, finals_low, place, local_targets)
    head_low = lax.psum_scatter(head_low, CTX, scatter_dimension=0, tiled=True)[0]
    final_part = contract_first(dlogits_low, head)
    final_grad = scatter_tp(final_part.reshape(2, N_X, SHARD, D))
    out_grad, final_gain_grad = jax.vjp(rms_norm, stream_out, gains[2])[1](final_grad)
    branch_low = gather_tp(out_grad.astype(bf16))
    hidden_grad = contract_last(branch_low, down)
    gate_grad_low = (
        hidden_grad * upward * sigmoid_gate * (1.0 + gate * (1.0 - sigmoid_gate))
    ).astype(bf16)
    upward_grad_low = (hidden_grad * silu_gate).astype(bf16)
    both_grad_low = jnp.concatenate([gate_grad_low, upward_grad_low], axis=1)
    inner_grad = scatter_tp(contract(both_grad_low, gate_up).reshape(2, N_X, SHARD, D))
    mid_part, middle_gain_grad = jax.vjp(rms_norm, stream_mid, gains[1])[1](inner_grad)
    mid_grad = out_grad + mid_part
    attend_low = gather_tp(mid_grad.astype(bf16))
    attended_grad = heads_on_lanes(contract_last(w_out, attend_low).astype(bf16))
    dq, pair_grads = attend_back(
        spans, own_places, queries, attended_grad, log_total, row_keyvals
    )
    pair_grads = pair_grads.reshape(2, N_CTX, 128, 2 * HD)
    half_grads = (pair_grads[0] + core_swap(pair_grads[1].astype(bf16)).astype(f32)).astype(bf16)
    query_linear_low = heads_on_rows(rotate_rows(dq, cosine_4, -sine_4).astype(bf16))
    half_grads, both_low = lax.optimization_barrier((half_grads, both_grad_low))
    came = lax.all_to_all(half_grads, CTX, 0, 0, tiled=True)
    layer_low = row_products(
        [inner_low, attend_low, branch_low, normed_low],
        [both_low, attended_rows, hidden_low, query_linear_low],
    )
    own_grads = jnp.sum(came.astype(f32), axis=0)
    keyval_low = jnp.concatenate(
        [
            rotate_lanes(own_grads[:, :HD], cosine[:, :128].T, -sine[:, :128].T),
            own_grads[:, HD:],
        ],
        axis=1,
    ).astype(bf16)
    normed_part = contract_first(query_linear_low, w_query).reshape(2, 128, D)
    normed_part = jnp.stack([normed_part[0] + contract_last(keyval_low, w_pair), normed_part[1]])
    layer_low, head_low, normed_part = lax.optimization_barrier((layer_low, head_low, normed_part))
    layer_low = lax.psum_scatter(layer_low, CTX, scatter_dimension=0, tiled=True)[0]
    normed_grad = scatter_tp(normed_part.reshape(2, N_X, SHARD, D))
    pair_low = contract_first(keyval_low, normed_half).astype(bf16)
    pair_low = pair_low.reshape(2 * HD, N_CTX, LINES).transpose(1, 0, 2)
    first_part, first_gain_grad = jax.vjp(rms_norm, stream_in, gains[0])[1](normed_grad)
    input_low = (mid_grad + first_part).astype(bf16)

    gain_parts = jnp.stack([first_gain_grad, middle_gain_grad, final_gain_grad]).astype(bf16)
    sent = jnp.concatenate(
        [
            input_low.reshape(SHARD, N_CTX, LINES).transpose(1, 0, 2),
            jnp.pad(gain_parts.reshape(3, N_CTX, LINES).transpose(1, 0, 2), ((0, 0), (0, 13), (0, 0))),
            pair_low,
        ],
        axis=1,
    )
    arrived = lax.all_to_all(sent, CTX, 0, 0, tiled=True)
    kv_part = jnp.sum(arrived[:, 48:].astype(f32), axis=0)
    gain_sums = jnp.sum(arrived[:, SHARD : SHARD + 3].astype(f32), axis=0)
    place_grads = gather_tp(arrived[:, :SHARD].reshape(N_CTX * SHARD, LINES))
    embed_grad = add_up(all_ids, place_grads, vocab_here)

    kv_full = kv_part + core_swap(kv_part)
    kv_split = kv_full.T.reshape(N_X, 2, 16, 2 * HD)
    kv_owned = swapped_x(jnp.where(cs == 0, kv_split[:, 0], kv_split[:, 1]), xs)
    key_value_grad = (
        kv_owned.reshape(KV_HEADS, 16, 2, HD).transpose(1, 2, 0, 3).reshape(16, KVW)
    )

    old_rows = jnp.concatenate(
        [attention_row_moment, feed_row_moment, vocab_row_moment, jnp.ones((9, LINES), f32)]
    )
    kv_old_columns = lax.dynamic_index_in_dim(
        key_value_column_moment.reshape(2, KV_HEADS, HD), xs, 1, keepdims=False
    ).reshape(-1)
    early_old = jnp.concatenate(
        [
            jnp.pad(vocab_column_moment, ((0, 0), (0, EARLY_LANES - vocab_here)), constant_values=1.0),
            jnp.concatenate(
                [kv_old_columns, jnp.ones((EARLY_LANES - 128,), f32)]
            )[None],
        ]
    )
    late_old = jnp.concatenate(
        [
            feed_column_moment[0],
            feed_column_moment[1],
            attention_column_moment[1],
            feed_column_moment[2],
            attention_column_moment[0],
            jnp.ones((64,), f32),
        ]
    )[None]
    kv_old_line = lax.dynamic_update_slice_in_dim(
        jnp.zeros((1, LINES), f32), key_value_row_moment[None], tp_index * 16, 1
    )
    vocab_grad, line_parts, column_parts = early_figures(
        head_low, embed_grad, kv_full, gain_sums, kv_old_line
    )
    lines = sum_tp(line_parts)
    columns = sum_ctx(column_parts)
    gain_grad = lax.dynamic_slice_in_dim(lines[8:11], tp_index * 16, 16, 1)
    gain_second = moments(gain_moment.T, gain_grad * gain_grad, 1.0)
    gain_step = gain_grad * lax.rsqrt(gain_second)
    gain_squares = jnp.sum(gain_step * gain_step, axis=1)
    base = weight_sums + jnp.concatenate(
        [
            jnp.zeros((UG_LANE,), f32),
            gain_squares,
            loss_part.reshape(1),
            jnp.zeros((127 - LOSS_LANE,), f32),
        ]
    )
    early_rows, early_columns, base, vocab_unit = step_squares(
        early_squares_kernel,
        (vocab_grad, kv_full),
        lines,
        columns,
        old_rows,
        early_old,
        base,
        [vocab_grad.shape],
    )
    feed_grad, attention_grad, late_line_parts, late_column_parts = late_figures(layer_low)
    late_rows, late_columns, scalars, feed_unit, attention_unit = step_squares(
        late_squares_kernel,
        (layer_low,),
        sum_tp(late_line_parts),
        sent_to_all(late_column_parts, CTX),
        old_rows,
        late_old,
        base,
        [feed_grad.shape, attention_grad.shape],
    )
    kv_columns_here = early_columns[2:3, :128]
    gathered = sent_to_all(jnp.concatenate([scalars, kv_columns_here]), CTX_TP)
    vocab_new, feed_new, attention_new, gain_new, figures = update(
        gathered[:, 0],
        tables,
        vocab_unit,
        feed_tables,
        feed_unit,
        attention_master,
        attention_unit,
        gain_master.T,
        gain_step,
    )
    token_loss = figures[2, 0]
    update_rms = figures[0, :11]
    kv_row_new = lax.dynamic_slice_in_dim(early_rows[7], tp_index * 16, 16, 0)
    kv_column_new = (
        gathered[0:8:2, 1].reshape(KV_HEADS, 2, HD).transpose(1, 0, 2).reshape(KVW)
    )
    kv_step = key_value_grad * lax.rsqrt(kv_row_new)[:, None] * lax.rsqrt(kv_column_new)[None]
    kv_new = key_value_master - figures[1, 7] * kv_step
    attention_columns = jnp.stack([late_columns[0, 2368:2624], late_columns[0, 1408:1664]])
    feed_columns = jnp.stack(
        [late_columns[0, :704], late_columns[0, 704:1408], late_columns[0, 1664:2368]]
    )
    return (
        token_loss,
        update_rms,
        attention_grad,
        late_rows[0:2],
        attention_columns,
        attention_new,
        feed_grad.transpose(0, 2, 1),
        late_rows[2:5],
        feed_columns,
        feed_new.transpose(0, 2, 1),
        vocab_grad.transpose(0, 2, 1),
        early_rows[5:7],
        early_columns[0, :vocab_here],
        early_columns[1, :vocab_here],
        vocab_new.transpose(0, 2, 1),
        key_value_grad,
        kv_row_new,
        kv_column_new,
        kv_new,
        gain_grad.T,
        gain_second.T,
        gain_new.T,
    )


def solution(mesh):
    finer = Mesh(mesh.devices.reshape(4, 4, 4, 2), ("ctx_0", "ctx_1", "tp_0", "tp_1"))
    in_specs = (
        P(CTX),
        P(CTX),
        P(CTX),
        P(),
        P(),
        P(None, CTX, TP),
        P(None, CTX, TP),
        P(None, CTX, TP),
        P(CTX_TP, None),
        P(CTX_TP, None),
        P(None, CTX),
        P(None, TP),
        P(None, CTX),
        P(None, TP),
        P(None, CTX),
        P(None, TP),
        P(CTX_TP),
        P(),
        P(CTX_TP, None),
    )
    out_specs = (
        P(),
        P(),
        P(None, CTX, TP),
        P(None, CTX),
        P(None, TP),
        P(None, CTX, TP),
        P(None, CTX, TP),
        P(None, CTX),
        P(None, TP),
        P(None, CTX, TP),
        P(None, CTX, TP),
        P(None, CTX),
        P(TP),
        P(TP),
        P(None, CTX, TP),
        P(CTX_TP, None),
        P(CTX_TP),
        P(),
        P(CTX_TP, None),
        P(CTX_TP, None),
        P(CTX_TP, None),
        P(CTX_TP, None),
    )
    return jax.shard_map(body, mesh=finer, in_specs=in_specs, out_specs=out_specs, check_vma=False)
```

```python
import functools
import math

import jax
import jax.numpy as jnp
from jax import lax
from jax.experimental import pallas as pl
from jax.experimental.pallas import tpu as pltpu
from jax.sharding import Mesh
from jax.sharding import PartitionSpec as P

D = 2048
HEADS = 32
KV_HEADS = 4
HD = 64
FF = 5632
VOCAB = 32000
ORIG_CTX = 2048
HQ = 2048
KVW = 512
TOKENS = 4096
TP = ("tp_0", "tp_1")
CTX = ("ctx_0", "ctx_1")
CTX_TP = ("ctx_0", "ctx_1", "tp_0", "tp_1")
N_CTX = 16
N_X = 4
N_TP = 8
SHARD = 32
LINES = 128
DOCS = 5

NORM_EPS = 1e-05
MOMENT_DECAY = 0.5
MOMENT_EPS = 1e-30
CLIP_LIMIT = 0.5
STEP_SCALE = 1.0
ROPE_BASE = 10000.0
YARN_SCALE = 4.0
YARN_ALPHA = 1.0
YARN_BETA = 32.0

bf16 = jnp.bfloat16
f32 = jnp.float32


def x_from(values, step):
    return lax.ppermute(values, "tp_0", [((i + step) % N_X, i) for i in range(N_X)])


def x_to(values, step):
    return lax.ppermute(values, "tp_0", [(i, (i + step) % N_X) for i in range(N_X)])


def core_swap(values):
    return lax.ppermute(values, "tp_1", [(0, 1), (1, 0)])


def turned(stack, start):
    return lax.dynamic_slice_in_dim(jnp.concatenate([stack, stack]), start, N_X, 0)


def to_absolute(stack, xs):
    return turned(stack, (N_X - xs) % N_X)


def gather_tp(shard):
    column = jnp.concatenate([shard] + [x_from(shard, d) for d in range(1, N_X)])
    return jnp.concatenate([column, core_swap(column)])


def scatter_tp(partial):
    half = partial[0] + core_swap(partial[1].astype(bf16)).astype(f32)
    low = half.astype(bf16)
    total = half[0]
    for d in range(1, N_X):
        total = total + x_to(low[d], d).astype(f32)
    return total


def both_cores(column, cs):
    other = core_swap(column)
    both = jnp.where(
        cs == 0, jnp.stack([column, other], axis=1), jnp.stack([other, column], axis=1)
    )
    return both.reshape(-1, *column.shape[2:])


def swapped_x(blocks, xs):
    ours = turned(blocks, xs)
    came = [ours[0]] + [x_to(ours[d], d) for d in range(1, N_X)]
    return to_absolute(jnp.stack([came[0], came[3], came[2], came[1]]), xs)


def partner(values, axis, mask):
    size = 2 if axis == "tp_1" else 4
    return lax.ppermute(values, axis, [(i, i ^ mask) for i in range(size)])


def sum_over_four(values, axis):
    return (values + partner(values, axis, 1)) + (
        partner(values, axis, 2) + partner(values, axis, 3)
    )


def sum_tp(values):
    return sum_over_four(values + partner(values, "tp_1", 1), "tp_0")


def sum_ctx(values):
    return sum_over_four(sum_over_four(values, "ctx_1"), "ctx_0")


def own_order(values, xs, cs):
    blocks = turned(values.reshape(N_X, 2, SHARD), xs)
    blocks = jnp.where(cs == 0, blocks, blocks[:, ::-1])
    return blocks.transpose(1, 0, 2)


def sent_to_all(array, axis):
    copies = jnp.broadcast_to(array, (lax.axis_size(axis), *array.shape))
    return lax.all_to_all(copies, axis, split_axis=0, concat_axis=0, tiled=True)


def rope_tables(positions):
    ladder = jnp.arange(HD // 2, dtype=f32)
    freqs = ROPE_BASE ** (-2.0 * ladder / HD)
    ratio = ORIG_CTX * freqs / (2.0 * math.pi)
    ramped = jnp.clip((ratio - YARN_ALPHA) / (YARN_BETA - YARN_ALPHA), 0.0, 1.0)
    inverse = freqs * (1.0 - ramped) / YARN_SCALE + freqs * ramped
    angles = inverse[:, None] * positions.astype(f32)[None, :]
    mscale = 0.1 * math.log(YARN_SCALE) + 1.0
    return (jnp.cos(angles) * mscale, jnp.sin(angles) * mscale)


def rotate_rows(values, cosine, sine):
    half = values.shape[0] // 2
    first, second = (values[:half], values[half:])
    return jnp.concatenate([first * cosine - second * sine, second * cosine + first * sine])


def rotate_lanes(values, cosine, sine):
    half = values.shape[1] // 2
    first, second = (values[:, :half], values[:, half:])
    return jnp.concatenate([first * cosine - second * sine, second * cosine + first * sine], axis=1)


def rms_norm(values, gain):
    return values * lax.rsqrt(jnp.mean(values * values, axis=-1, keepdims=True) + NORM_EPS) * gain


def contract_last(left, right):
    return lax.dot_general(left, right, (((1,), (1,)), ((), ())), preferred_element_type=f32)


def contract_first(left, right):
    return lax.dot_general(left, right, (((0,), (0,)), ((), ())), preferred_element_type=f32)


def contract(left, right):
    return jnp.dot(left, right, preferred_element_type=f32)


def combine_stats(former, latter):
    highest = jnp.maximum(former[0], latter[0])
    summed = former[1] * jnp.exp(former[0] - highest) + latter[1] * jnp.exp(latter[0] - highest)
    return jnp.stack([highest, summed, former[2] + latter[2]])


def contract_ft(weights, places):
    return lax.dot_general(weights, places, (((0,), (1,)), ((), ())), preferred_element_type=f32)


def contract_tf(features, weights):
    return lax.dot_general(features, weights, (((0,), (1,)), ((), ())), preferred_element_type=f32)


def heads_on_lanes(features):
    return jnp.concatenate([features[h * HD : (h + 1) * HD] for h in range(4)], axis=1)


def heads_on_rows(features):
    return jnp.concatenate(jnp.split(features, 4, axis=1))


VMEM_LIMIT = 50 * 1024 * 1024


GROUP = 4
KEYS = 128 * GROUP
STEPS = TOKENS // KEYS


def key_places(core_bit, spans):
    line = lax.broadcasted_iota(jnp.int32, (128, 1), 0)
    x = (spans[N_CTX] + line // SHARD) % N_X
    place = (x * 2 + (spans[N_CTX + 1] ^ core_bit)) * SHARD + line % SHARD
    return place >= 128, place % 128


def visible_keys(spans, places, step, own, start):
    lines = []
    for block in range(step * GROUP, (step + 1) * GROUP):
        span = spans[block % N_CTX]
        second, within = places[block // N_CTX]
        lines.append(jnp.where(second, (2 * N_CTX - 1 - span) * 128, span * 128) + within)
    at = jnp.concatenate(lines, axis=0)
    return (at >= start) & (at <= own)


def key_columns(kv_ref, step, at):
    return jnp.concatenate(
        [kv_ref[step * GROUP + i, at : at + HD] for i in range(GROUP)], axis=1
    )


def attend_kernel(spans, own_ref, q_ref, kv_ref, o_ref, total_ref, s_ref):
    q = q_ref[...]
    own, start = (own_ref[0:1], own_ref[1:2])
    places = [key_places(core_bit, spans) for core_bit in range(2)]
    top = None
    for step in range(STEPS):
        scores = contract_first(key_columns(kv_ref, step, 0), q)
        scores = jnp.where(visible_keys(spans, places, step, own, start), scores, -1e30)
        s_ref[step * KEYS : (step + 1) * KEYS] = scores
        highest = jnp.max(scores, axis=0, keepdims=True)
        top = highest if top is None else jnp.maximum(top, highest)
    total = jnp.zeros(top.shape, f32)
    for step in range(STEPS):
        powers = jnp.exp(s_ref[step * KEYS : (step + 1) * KEYS] - top)
        s_ref[step * KEYS : (step + 1) * KEYS] = powers
        total = total + jnp.sum(powers, axis=0, keepdims=True)
    share = 1.0 / total
    out = jnp.zeros(q.shape, f32)
    for step in range(STEPS):
        weights = (s_ref[step * KEYS : (step + 1) * KEYS] * share).astype(bf16)
        out = out + contract(key_columns(kv_ref, step, HD), weights)
    o_ref[...] = out.astype(bf16)
    total_ref[...] = top + jnp.log(total)


SPLIT = 2


def attend(spans, own, q, kv):
    lanes = q.shape[1] // SPLIT
    column = lambda rows: pl.BlockSpec((rows, lanes), lambda i: (0, i))
    return pl.pallas_call(
        attend_kernel,
        grid=(SPLIT,),
        in_specs=[
            pl.BlockSpec(memory_space=pltpu.SMEM),
            column(2),
            column(HD),
            pl.BlockSpec(kv.shape, lambda i: (0, 0, 0)),
        ],
        out_specs=[column(HD), column(1)],
        out_shape=[
            jax.ShapeDtypeStruct(q.shape, bf16),
            jax.ShapeDtypeStruct((1, q.shape[1]), f32),
        ],
        scratch_shapes=[pltpu.VMEM((TOKENS, lanes), f32)],
        compiler_params=pltpu.CompilerParams(vmem_limit_bytes=VMEM_LIMIT),
        cost_estimate=pl.CostEstimate(
            flops=16 * TOKENS * q.shape[1] * HD, bytes_accessed=2 << 20, transcendentals=0
        ),
    )(spans, own, q, kv)


def attend_back_kernel(
    spans, own_ref, q_ref, do_ref, total_ref, kv_ref, dq_ref, dkv_ref, p_ref, dp_ref
):
    q, do = (q_ref[...], do_ref[...])
    own, start = (own_ref[0:1], own_ref[1:2])
    total = total_ref[...]
    places = [key_places(core_bit, spans) for core_bit in range(2)]
    rowsum = jnp.zeros(total.shape, f32)
    for step in range(STEPS):
        scores = contract_first(key_columns(kv_ref, step, 0), q)
        scores = jnp.where(visible_keys(spans, places, step, own, start), scores, -1e30)
        probs = jnp.exp(scores - total)
        probs_grad = contract_first(key_columns(kv_ref, step, HD), do)
        p_ref[step * KEYS : (step + 1) * KEYS] = probs
        dp_ref[step * KEYS : (step + 1) * KEYS] = probs_grad
        rowsum = rowsum + jnp.sum(probs * probs_grad, axis=0, keepdims=True)

    @pl.when(pl.program_id(0) == 0)
    def _():
        dkv_ref[...] = jnp.zeros(dkv_ref.shape, f32)

    dq = jnp.zeros(q.shape, f32)
    for step in range(STEPS):
        rows = slice(step * KEYS, (step + 1) * KEYS)
        probs = p_ref[rows]
        score_grad = (probs * (dp_ref[rows] - rowsum)).astype(bf16)
        dkv_ref[rows] += jnp.concatenate(
            [contract_last(score_grad, q), contract_last(probs.astype(bf16), do)], axis=1
        )
        dq = dq + contract(key_columns(kv_ref, step, 0), score_grad)
    dq_ref[...] = dq * (1.0 / math.sqrt(HD))


def attend_back(spans, own, q, do, total, kv):
    lanes = q.shape[1] // SPLIT
    column = lambda rows: pl.BlockSpec((rows, lanes), lambda i: (0, i))
    return pl.pallas_call(
        attend_back_kernel,
        grid=(SPLIT,),
        in_specs=[
            pl.BlockSpec(memory_space=pltpu.SMEM),
            column(2),
            column(HD),
            column(HD),
            column(1),
            pl.BlockSpec(kv.shape, lambda i: (0, 0, 0)),
        ],
        out_specs=[column(HD), pl.BlockSpec((TOKENS, 2 * HD), lambda i: (0, 0))],
        out_shape=[
            jax.ShapeDtypeStruct(q.shape, f32),
            jax.ShapeDtypeStruct((TOKENS, 2 * HD), f32),
        ],
        scratch_shapes=[pltpu.VMEM((TOKENS, lanes), f32), pltpu.VMEM((TOKENS, lanes), f32)],
        compiler_params=pltpu.CompilerParams(vmem_limit_bytes=VMEM_LIMIT),
        cost_estimate=pl.CostEstimate(
            flops=40 * TOKENS * q.shape[1] * HD, bytes_accessed=4 << 20, transcendentals=0
        ),
    )(spans, own, q, do, total, kv)


def moments(old, sums, count):
    return MOMENT_DECAY * old + (1.0 - MOMENT_DECAY) * (sums / count + MOMENT_EPS)


def params():
    return pltpu.CompilerParams(vmem_limit_bytes=VMEM_LIMIT)


def whole(array):
    zeros = (0,) * array.ndim
    return pl.BlockSpec(array.shape, lambda *i: zeros)


def cost(flops, moved):
    return pl.CostEstimate(flops=flops, bytes_accessed=moved, transcendentals=0)


ID_STEP = 2048


def look_kernel(ids_ref, table_ref, out_ref, low_ref):
    @pl.when(pl.program_id(0) == 0)
    def _():
        low_ref[...] = table_ref[0].astype(bf16)

    width = low_ref.shape[0]
    ids = jnp.transpose(jnp.broadcast_to(ids_ref[...], (8, ID_STEP)))[:, :1]
    hits = ids == lax.broadcasted_iota(jnp.int32, (ID_STEP, width), 1)
    out_ref[...] = contract(jnp.where(hits, 1.0, 0.0).astype(bf16), low_ref[...]).astype(bf16)


def look_up(ids, tables):
    width, lines = tables.shape[1:]
    count = ids.shape[1]
    return pl.pallas_call(
        look_kernel,
        grid=(count // ID_STEP,),
        in_specs=[
            pl.BlockSpec((1, ID_STEP), lambda i: (0, i)),
            pl.BlockSpec((1, width, lines), lambda i: (1, 0, 0)),
        ],
        out_specs=pl.BlockSpec((ID_STEP, lines), lambda i: (i, 0)),
        out_shape=jax.ShapeDtypeStruct((count, lines), bf16),
        scratch_shapes=[pltpu.VMEM((width, lines), bf16)],
        compiler_params=params(),
        cost_estimate=cost(4 * count * width * lines, 4 * lines * width),
    )(ids, tables)


def add_kernel(ids_ref, grads_ref, out_ref):
    hits = lax.broadcasted_iota(jnp.int32, (out_ref.shape[0], ID_STEP), 0) == ids_ref[...]
    added = contract(jnp.where(hits, 1.0, 0.0).astype(bf16), grads_ref[...])

    @pl.when(pl.program_id(0) == 0)
    def _():
        out_ref[...] = added

    @pl.when(pl.program_id(0) > 0)
    def _():
        out_ref[...] += added


def add_up(ids, grads, width):
    count, lines = grads.shape
    return pl.pallas_call(
        add_kernel,
        grid=(count // ID_STEP,),
        in_specs=[
            pl.BlockSpec((1, ID_STEP), lambda i: (0, i)),
            pl.BlockSpec((ID_STEP, lines), lambda i: (i, 0)),
        ],
        out_specs=pl.BlockSpec((width, lines), lambda i: (0, 0)),
        out_shape=jax.ShapeDtypeStruct((width, lines), f32),
        compiler_params=params(),
        cost_estimate=cost(4 * count * width * lines, 4 * lines * width),
    )(ids, grads)


LOGIT_STEP = 800


def logits_kernel(c_ref, w_ref, target_ref, out_ref, stats_ref):
    step = pl.program_id(0)
    logits = contract_last(w_ref[...], c_ref[...])
    out_ref[...] = logits
    row = lax.broadcasted_iota(jnp.int32, logits.shape, 0) + step * LOGIT_STEP
    here = jnp.max(logits, axis=0, keepdims=True)
    pick = jnp.sum(jnp.where(row == target_ref[...], logits, 0.0), axis=0, keepdims=True)

    @pl.when(step == 0)
    def _():
        stats_ref[...] = jnp.zeros(stats_ref.shape, f32)
        stats_ref[0:1] = here

    old = stats_ref[0:1]
    top = jnp.maximum(old, here)
    powers = jnp.sum(jnp.exp(logits - top), axis=0, keepdims=True)
    stats_ref[1:2] = stats_ref[1:2] * jnp.exp(old - top) + powers
    stats_ref[2:3] += pick
    stats_ref[0:1] = top


def logits_and_stats(c, head, width, targets):
    places, rows = c.shape
    return pl.pallas_call(
        logits_kernel,
        grid=(width // LOGIT_STEP,),
        in_specs=[whole(c), pl.BlockSpec((LOGIT_STEP, rows), lambda i: (i, 0)), whole(targets)],
        out_specs=[
            pl.BlockSpec((LOGIT_STEP, places), lambda i: (i, 0)),
            pl.BlockSpec((8, places), lambda i: (0, 0)),
        ],
        out_shape=[
            jax.ShapeDtypeStruct((width, places), f32),
            jax.ShapeDtypeStruct((8, places), f32),
        ],
        compiler_params=params(),
        cost_estimate=cost(2 * places * rows * width, 2 * rows * width),
    )(c, head, targets)


def head_grad_kernel(logits_ref, c_ref, place_ref, target_ref, dw_ref, low_ref):
    step = pl.program_id(0)
    logits = logits_ref[...]
    row = lax.broadcasted_iota(jnp.int32, logits.shape, 0) + step * LOGIT_STEP
    hit = row == target_ref[...]
    shares = jnp.exp(logits - place_ref[0:1]) - jnp.where(hit, 1.0, 0.0)
    low = (place_ref[1:2] * shares).astype(bf16)
    low_ref[...] = low
    grad = contract(low, c_ref[...]).astype(bf16)
    for k in range(N_CTX):
        dw_ref[k] = grad[:, k * 128 : (k + 1) * 128]


def head_grads(logits, c, place, targets):
    places, rows = c.shape
    width = logits.shape[0]
    block = pl.BlockSpec((LOGIT_STEP, places), lambda i: (i, 0))
    return pl.pallas_call(
        head_grad_kernel,
        grid=(width // LOGIT_STEP,),
        in_specs=[block, whole(c), whole(place), whole(targets)],
        out_specs=[pl.BlockSpec((N_CTX, LOGIT_STEP, 128), lambda i: (0, i, 0)), block],
        out_shape=[
            jax.ShapeDtypeStruct((N_CTX, width, 128), bf16),
            jax.ShapeDtypeStruct((width, places), bf16),
        ],
        compiler_params=params(),
        cost_estimate=cost(2 * places * rows * width, 2 * rows * width),
    )(logits, c, place, targets)


TURNED = (1, 3)


def products_kernel(count, offsets, *refs):
    lefts, rights = (refs[:count], refs[count : 2 * count])
    out_ref, turned_ref = refs[2 * count :]

    @pl.when(pl.program_id(0) == 0)
    def _():
        for k, (right, (at, width)) in enumerate(zip(rights, offsets)):
            values = right[...]
            turned_ref[at : at + width] = values if k in TURNED else jnp.transpose(values)

    for left, (at, width) in zip(lefts, offsets):
        grad = contract(turned_ref[at : at + width], left[...]).astype(bf16)
        for k in range(2):
            out_ref[k, at : at + width] = grad[:, k * 128 : (k + 1) * 128]


def row_products(lefts, rights):
    places, rows = lefts[0].shape
    offsets, at = ([], 0)
    for k, right in enumerate(rights):
        width = right.shape[0 if k in TURNED else 1]
        offsets.append((at, width))
        at += width
    return pl.pallas_call(
        functools.partial(products_kernel, len(lefts), tuple(offsets)),
        grid=(N_CTX // 2,),
        in_specs=[pl.BlockSpec((places, 256), lambda i: (0, i)) for _ in lefts]
        + [whole(right) for right in rights],
        out_specs=pl.BlockSpec((2, at, 128), lambda i: (i, 0, 0)),
        out_shape=jax.ShapeDtypeStruct((N_CTX, at, rows // N_CTX), bf16),
        scratch_shapes=[pltpu.VMEM((at, places), bf16)],
        compiler_params=params(),
        cost_estimate=cost(2 * places * rows * at, 2 * rows * at),
    )(*lefts, *rights)


MATRICES = 8
WIDTHS = (HQ, HQ, FF, FF, FF, VOCAB, VOCAB, KVW)
EARLY_LANES = 8320
COLUMN_LANES = 11008
COLUMN_AT = {5: (0, 4000), 6: (4096, 4000), 7: (8192, 128), 2: (8320, 704), 3: (9024, 704)}
COLUMN_AT.update({1: (9728, 256), 4: (9984, 704), 0: (10688, 256)})
LAYER = {2: (0, 704), 3: (704, 704), 1: (1408, 256), 4: (1664, 704), 0: (2368, 256)}
S_LANE, T_LANE, OLD_LANE, W_LANE, WG_LANE, UG_LANE, LOSS_LANE = (0, 8, 16, 24, 32, 35, 38)


def lane_is(shape, lane):
    return lax.broadcasted_iota(jnp.int32, shape, 1) == lane


def line_sum(values):
    return jnp.sum(values, axis=0, keepdims=True)


def total_of(values):
    return jnp.sum(line_sum(values), axis=1, keepdims=True)


def column_sums(squares):
    ones = jnp.ones((8, squares.shape[1]), f32)
    return lax.dot_general(
        ones,
        squares,
        (((1,), (1,)), ((), ())),
        precision=lax.Precision.HIGHEST,
        preferred_element_type=f32,
    )


def weights_kernel(tables_ref, feed_ref, attention_ref, kv_master_ref, gain_ref, scalars_ref):
    scalars = jnp.zeros(scalars_ref.shape, f32)
    for number, weights in (
        (0, attention_ref[0]),
        (1, attention_ref[1]),
        (2, feed_ref[0]),
        (3, feed_ref[1]),
        (4, feed_ref[2]),
        (5, tables_ref[0]),
        (6, tables_ref[1]),
        (7, kv_master_ref[...]),
        (8, gain_ref[0:1]),
        (9, gain_ref[1:2]),
        (10, gain_ref[2:3]),
    ):
        scalars += jnp.where(
            lane_is(scalars.shape, W_LANE + number), total_of(weights * weights), 0.0
        )
    scalars_ref[...] = scalars


def weight_squares(*masters):
    return pl.pallas_call(
        weights_kernel,
        out_shape=jax.ShapeDtypeStruct((1, 128), f32),
        compiler_params=params(),
        cost_estimate=cost(0, 6 << 20),
    )(*masters)


def early_kernel(
    head_ref, embed_ref, kv_ref, gains_ref, kv_old_ref, vocab_grad_ref, lines_ref, columns_ref
):
    columns_ref[...] = jnp.zeros(columns_ref.shape, f32)
    lines_ref[...] = jnp.zeros(lines_ref.shape, f32)
    lines_ref[8:11] = gains_ref[...]
    lines_ref[11:12] = kv_old_ref[...]
    for number, ref in ((5, head_ref), (6, embed_ref), (7, kv_ref)):
        grad = ref[...].astype(f32)
        if number in (5, 6):
            vocab_grad_ref[number - 5] = grad
        squares = grad * grad
        lines_ref[number : number + 1] = (0.5 if number == 7 else 1.0) * line_sum(squares)
        at, width = COLUMN_AT[number]
        columns_ref[:, at : at + width] = column_sums(squares)[:1]


def early_figures(*arrays):
    shapes = ((2, *arrays[1].shape), (16, 128), (1, EARLY_LANES))
    return pl.pallas_call(
        early_kernel,
        out_shape=[jax.ShapeDtypeStruct(shape, f32) for shape in shapes],
        compiler_params=params(),
        cost_estimate=cost(0, 12 << 20),
    )(*arrays)


def late_kernel(
    layer_ref, early_lines_ref, early_columns_ref,
    feed_grad_ref, attention_grad_ref, lines_ref, columns_ref,
):
    layer = layer_ref[...].astype(f32)
    squares = layer * layer
    lines_ref[...] = early_lines_ref[...]
    columns_ref[:, :EARLY_LANES] = early_columns_ref[...]
    columns_ref[:, EARLY_LANES:] = jnp.zeros((1, COLUMN_LANES - EARLY_LANES), f32)
    columns_ref[:, EARLY_LANES : EARLY_LANES + layer.shape[0]] = column_sums(squares)[:1]
    for number in range(5):
        at, width = LAYER[number]
        lines_ref[number : number + 1] = line_sum(squares[at : at + width])
        if number > 1:
            feed_grad_ref[number - 2] = layer[at : at + width]
    attention_grad_ref[0] = jnp.transpose(layer[2368:2624])
    attention_grad_ref[1] = jnp.transpose(layer[1408:1664])


def late_figures(*arrays):
    shapes = ((3, 704, 128), (2, 128, 256), (16, 128), (1, COLUMN_LANES))
    return pl.pallas_call(
        late_kernel,
        out_shape=[jax.ShapeDtypeStruct(shape, f32) for shape in shapes],
        compiler_params=params(),
        cost_estimate=cost(0, 4 << 20),
    )(*arrays)


def per_column(figures, number):
    at, width = COLUMN_AT[number]
    return figures[at : at + width, :1]


def on_rows(columns):
    spare = 8 - columns.shape[0]
    return jnp.transpose(
        jnp.concatenate([columns, jnp.ones((spare, columns.shape[1]), f32)], axis=0)
    )


def squares_kernel(
    vocab_ref, layer_ref, kv_ref, lines_ref, columns_ref, old_ref, old_columns_ref, base_ref,
    row_ref, column_ref, scalars_ref, vocab_unit_ref, feed_unit_ref, attention_unit_ref,
):
    lines = lines_ref[...]
    number = lax.broadcasted_iota(jnp.int32, lines.shape, 0)
    old = jnp.where(number == 7, lines_ref[11:12], old_ref[...])
    widths = jnp.full(lines.shape, 1.0, f32)
    for k, width in enumerate(WIDTHS):
        widths = jnp.where(number == k, float(width), widths)
    row_new = moments(old, lines / widths, 1.0)
    row_ref[...] = row_new
    column_new = moments(old_columns_ref[...], jnp.sum(columns_ref[...], axis=0), float(D))
    column_ref[...] = column_new
    row_scale = lax.rsqrt(row_new)
    column_scale = on_rows(lax.rsqrt(column_new))
    scalars = base_ref[...]
    had = jnp.sum(old, axis=1, keepdims=True) * (1.0 / N_TP)
    got = jnp.sum(lines, axis=1, keepdims=True) * (1.0 / N_TP)
    for k in range(MATRICES):
        if k < 5:
            at, width = LAYER[k]
            grad = layer_ref[at : at + width].astype(f32)
        else:
            grad = kv_ref[...] if k == 7 else vocab_ref[k - 5]
        unit = grad * row_scale[k : k + 1] * per_column(column_scale, k)
        if k < 2:
            attention_unit_ref[k] = jnp.transpose(unit)
        elif k < 5:
            feed_unit_ref[k - 2] = unit
        elif k < 7:
            vocab_unit_ref[k - 5] = unit
        part = total_of(unit * unit) * (0.5 if k == 7 else 1.0)
        scalars += jnp.where(lane_is(scalars.shape, S_LANE + k), part, 0.0)
        scalars += jnp.where(lane_is(scalars.shape, T_LANE + k), got[k : k + 1], 0.0)
        scalars += jnp.where(lane_is(scalars.shape, OLD_LANE + k), had[k : k + 1], 0.0)
    scalars_ref[...] = scalars


def step_squares(vocab, layer, kv, lines, columns, old, old_columns, base, units):
    shapes = [a.shape for a in (lines, old_columns, base)] + list(units)
    return pl.pallas_call(
        squares_kernel,
        out_shape=[jax.ShapeDtypeStruct(shape, f32) for shape in shapes],
        compiler_params=params(),
        cost_estimate=cost(0, 16 << 20),
    )(vocab, layer, kv, lines, columns, old, old_columns, base)


UPDATE_STEP = 800


def update_kernel(
    all_ref, vocab_ref, vocab_unit_ref, feed_ref, feed_unit_ref, attention_ref,
    attention_unit_ref, gain_ref, gain_step_ref,
    vocab_new_ref, feed_new_ref, attention_new_ref, gain_new_ref, figures_ref,
):
    sums = jnp.sum(all_ref[...], axis=0, keepdims=True)
    sums = jnp.broadcast_to(sums, (8, 128))

    def lanes_from(at):
        return pltpu.roll(sums, (128 - at) % 128, 1)[0:1]

    lane = lax.broadcasted_iota(jnp.int32, (1, 128), 1)
    counts = jnp.full((1, 128), float(D), f32)
    for k, width in enumerate(WIDTHS):
        counts = jnp.where(lane == k, float(D * width), counts)
    mean = MOMENT_DECAY * lanes_from(OLD_LANE) / D + (1.0 - MOMENT_DECAY) * (
        lanes_from(T_LANE) / counts + MOMENT_EPS
    )
    mean = jnp.where(lane < MATRICES, mean, 1.0)
    rms = jnp.sqrt(mean * lanes_from(S_LANE) / counts)
    factor = (
        STEP_SCALE
        * jnp.sqrt(lanes_from(W_LANE) / counts)
        / jnp.maximum(1.0, rms / CLIP_LIMIT)
        * jnp.sqrt(mean)
    )

    @pl.when(pl.program_id(0) == 0)
    def _():
        for k in range(2):
            attention_new_ref[k] = attention_ref[k] - attention_unit_ref[k] * factor[:, k : k + 1]
        for k in range(3):
            feed_new_ref[k] = feed_ref[k] - feed_unit_ref[k] * factor[:, 2 + k : 3 + k]
        gain_rms = jnp.sqrt(lanes_from(UG_LANE) / D)
        gain_factor = (
            STEP_SCALE
            * jnp.sqrt(lanes_from(WG_LANE) / D)
            / jnp.maximum(1.0, gain_rms / CLIP_LIMIT)
        )
        for k in range(3):
            gain_new_ref[k : k + 1] = (
                gain_ref[k : k + 1] - gain_factor[:, k : k + 1] * gain_step_ref[k : k + 1]
            )
        after = pltpu.roll(jnp.broadcast_to(gain_rms, (8, 128)), MATRICES, 1)[0:1]
        figures_ref[0:1] = jnp.where(lane < MATRICES, rms, after)
        figures_ref[1:2] = factor
        figures_ref[2:3] = lanes_from(LOSS_LANE)
        figures_ref[3:8] = jnp.zeros((5, 128), f32)

    for k in range(2):
        vocab_new_ref[k] = vocab_ref[k] - vocab_unit_ref[k] * factor[:, 5 + k : 6 + k]


def update(gathered, vocab, vocab_unit, feed, feed_unit, attention, attention_unit, gain, gain_step):
    stack = pl.BlockSpec((2, UPDATE_STEP, vocab.shape[2]), lambda i: (0, i, 0))
    others = (feed, feed_unit, attention, attention_unit, gain, gain_step)
    outs = (vocab, feed, attention, gain)
    return pl.pallas_call(
        update_kernel,
        grid=(vocab.shape[1] // UPDATE_STEP,),
        in_specs=[whole(gathered), stack, stack] + [whole(a) for a in others],
        out_specs=[stack]
        + [whole(a) for a in outs[1:]]
        + [pl.BlockSpec((8, 128), lambda i: (0, 0))],
        out_shape=[jax.ShapeDtypeStruct(a.shape, f32) for a in outs]
        + [jax.ShapeDtypeStruct((8, 128), f32)],
        compiler_params=params(),
        cost_estimate=cost(0, 24 << 20),
    )(gathered, vocab, vocab_unit, *others)


def body(
    token_ids,
    target_ids,
    loss_mask,
    segment_ids,
    span_pairs,
    attention_master,
    feed_master,
    vocab_master,
    key_value_master,
    gain_master,
    attention_row_moment,
    attention_column_moment,
    feed_row_moment,
    feed_column_moment,
    vocab_row_moment,
    vocab_column_moment,
    key_value_row_moment,
    key_value_column_moment,
    gain_moment,
):
    ctx_index = lax.axis_index(CTX)
    xs = lax.axis_index("tp_0")
    cs = lax.axis_index("tp_1")
    tp_index = xs * 2 + cs
    vocab_here = vocab_master.shape[2]
    ff_here = feed_master.shape[2]
    first_id = tp_index * vocab_here

    attention_low = attention_master.astype(bf16)
    feed_low = feed_master.astype(bf16)
    layer_all = lax.all_gather(
        jnp.concatenate(
            [attention_low[0], attention_low[1], feed_low[0], feed_low[1], feed_low[2]], axis=1
        ),
        CTX,
        axis=0,
        tiled=True,
    ).T
    head = lax.all_gather(vocab_master[0].astype(bf16), CTX, axis=0, tiled=True).T
    w_query = layer_all[:256]
    w_out = layer_all[256:512]
    gate_up = layer_all[512 : 512 + 2 * ff_here]
    down = layer_all[512 + 2 * ff_here :]

    kv_low = key_value_master.astype(bf16).reshape(16, 2, KV_HEADS, HD).transpose(2, 0, 1, 3)
    gain_low = jnp.pad(gain_master.astype(bf16), ((0, 0), (0, 125)))
    blocks = jnp.concatenate(
        [
            kv_low.reshape(KV_HEADS, 16, 2 * HD),
            jnp.broadcast_to(gain_low, (KV_HEADS, *gain_low.shape)),
        ],
        axis=2,
    )
    ids_here = own_order(token_ids, xs, cs).reshape(1, 256)
    line_block = both_cores(swapped_x(blocks, xs), cs)
    half = LINES // 2
    early = sent_to_all(
        jnp.concatenate(
            [
                lax.dynamic_slice_in_dim(line_block[:, : 2 * HD], cs * half, half, 0),
                line_block[:, 2 * HD : 2 * HD + 3].T,
                (ids_here // 256).astype(bf16).reshape(2, 128),
                (ids_here % 256).astype(bf16).reshape(2, 128),
                jnp.zeros((9, 128), bf16),
            ]
        ),
        CTX,
    )
    own_half = early[:, :half]
    other_half = core_swap(own_half)
    w_pair = jnp.where(
        cs == 0,
        jnp.concatenate([own_half, other_half], axis=1),
        jnp.concatenate([other_half, own_half], axis=1),
    ).reshape(D, 2 * HD)
    gains = early[:, half : half + 3].astype(f32).transpose(1, 0, 2).reshape(3, D)
    parts = early[:, half + 3 : half + 7].astype(jnp.int32).reshape(N_CTX, 2, 256)
    all_ids = parts[:, 0] * 256 + parts[:, 1]
    all_ids = all_ids.reshape(N_CTX, 8, SHARD).transpose(1, 0, 2).reshape(1, TOKENS) - first_id

    order = (
        ((xs + jnp.arange(N_X, dtype=jnp.int32)) % N_X * 2)[None, :]
        + (cs ^ jnp.arange(2, dtype=jnp.int32))[:, None]
    )[:, :, None] * SHARD + jnp.arange(SHARD, dtype=jnp.int32)
    second_span = order >= 128
    within = order % 128
    own_pair = lax.dynamic_slice_in_dim(span_pairs, ctx_index, 1)[0]
    last_span = 2 * N_CTX - 1
    own_pos = (jnp.where(second_span, last_span - own_pair, own_pair) * 128 + within).reshape(-1)
    doc_start = jnp.zeros_like(own_pos)
    for k in range(1, DOCS):
        start = jnp.sum((segment_ids < k).astype(jnp.int32))
        doc_start = jnp.where(own_pos >= start, start, doc_start)
    cosine, sine = rope_tables(own_pos - doc_start)
    cosine_4, sine_4 = (jnp.tile(cosine, (1, 4)), jnp.tile(sine, (1, 4)))
    own_places = jnp.tile(jnp.stack([own_pos, doc_start]), (1, 4))
    spans = jnp.concatenate([span_pairs, jnp.stack([xs, cs]).astype(jnp.int32)])

    tables = vocab_master.transpose(0, 2, 1)
    looked = look_up(all_ids, tables).reshape(2, N_X, N_CTX, SHARD, LINES)
    half = looked[0] + core_swap(looked[1])
    mine = half[0]
    for d in range(1, N_X):
        mine = mine + x_to(half[d], d)
    rows_in = lax.all_to_all(mine, CTX, 0, 0, tiled=True)
    stream_in = rows_in.transpose(1, 0, 2).reshape(SHARD, D).astype(f32)

    normed_low = gather_tp(rms_norm(stream_in, gains[0]).astype(bf16))
    normed_half = normed_low[:128]
    keyval_linear = contract_ft(w_pair, normed_half)
    own_keyvals = jnp.concatenate(
        [rotate_rows(keyval_linear[:HD], cosine[:, :128], sine[:, :128]), keyval_linear[HD:]]
    ).astype(bf16)
    half_keyvals = sent_to_all(own_keyvals, CTX)
    row_keyvals = jnp.concatenate([half_keyvals, core_swap(half_keyvals)])
    query_linear = heads_on_lanes(contract_last(w_query, normed_low))
    queries = rotate_rows(query_linear, cosine_4, sine_4).astype(bf16) * jnp.asarray(
        1.0 / math.sqrt(HD), bf16
    )
    attended, log_total = attend(spans, own_places, queries, row_keyvals)
    attended_rows = heads_on_rows(attended)
    stream_mid = stream_in + scatter_tp(
        contract_first(attended_rows, w_out).reshape(2, N_X, SHARD, D)
    )

    inner_low = gather_tp(rms_norm(stream_mid, gains[1]).astype(bf16))
    both = contract_last(inner_low, gate_up)
    gate, upward = (both[:, :ff_here], both[:, ff_here:])
    sigmoid_gate = jax.nn.sigmoid(gate)
    silu_gate = gate * sigmoid_gate
    hidden_low = (silu_gate * upward).astype(bf16)
    stream_out = stream_mid + scatter_tp(
        contract(hidden_low, down).reshape(2, N_X, SHARD, D)
    )

    feed_tables = feed_master.transpose(0, 2, 1)
    masters = (tables, feed_tables, attention_master, key_value_master, gain_master.T)
    masters, inner_low = lax.optimization_barrier((masters, inner_low))
    weight_sums = weight_squares(*masters)
    finals_low = gather_tp(rms_norm(stream_out, gains[2]).astype(bf16))
    weight_sums, finals_low = lax.optimization_barrier((weight_sums, finals_low))
    local_targets = own_order(target_ids, xs, cs).reshape(1, -1) - first_id
    logits, stats = logits_and_stats(finals_low, head, vocab_here, local_targets)
    stats = stats[:3].reshape(3, 2, N_X, SHARD)
    stats = combine_stats(stats, core_swap(stats)[:, ::-1])
    others = [jnp.roll(x_from(stats, d), d, axis=2) for d in range(1, N_X)]
    stats = combine_stats(combine_stats(stats, others[0]), combine_stats(others[1], others[2]))
    stats = stats.reshape(3, -1)
    vocab_total = stats[0] + jnp.log(stats[1])
    keep = own_order(loss_mask, xs, cs).reshape(-1).astype(f32)
    loss_part = jnp.sum((keep * (vocab_total - stats[2]))[:SHARD]) / TOKENS

    place = jnp.stack([vocab_total, keep / TOKENS])
    head_low, dlogits_low = head_grads(logits, finals_low, place, local_targets)
    head_low = lax.psum_scatter(head_low, CTX, scatter_dimension=0, tiled=True)[0]
    final_part = contract_first(dlogits_low, head)
    final_grad = scatter_tp(final_part.reshape(2, N_X, SHARD, D))
    out_grad, final_gain_grad = jax.vjp(rms_norm, stream_out, gains[2])[1](final_grad)
    branch_low = gather_tp(out_grad.astype(bf16))
    hidden_grad = contract_last(branch_low, down)
    gate_grad_low = (
        hidden_grad * upward * sigmoid_gate * (1.0 + gate * (1.0 - sigmoid_gate))
    ).astype(bf16)
    upward_grad_low = (hidden_grad * silu_gate).astype(bf16)
    both_grad_low = jnp.concatenate([gate_grad_low, upward_grad_low], axis=1)
    inner_grad = scatter_tp(contract(both_grad_low, gate_up).reshape(2, N_X, SHARD, D))
    mid_part, middle_gain_grad = jax.vjp(rms_norm, stream_mid, gains[1])[1](inner_grad)
    mid_grad = out_grad + mid_part
    attend_low = gather_tp(mid_grad.astype(bf16))
    attended_grad = heads_on_lanes(contract_last(w_out, attend_low).astype(bf16))
    dq, pair_grads = attend_back(
        spans, own_places, queries, attended_grad, log_total, row_keyvals
    )
    pair_grads = pair_grads.reshape(2, N_CTX, 128, 2 * HD)
    half_grads = (pair_grads[0] + core_swap(pair_grads[1].astype(bf16)).astype(f32)).astype(bf16)
    query_linear_low = heads_on_rows(rotate_rows(dq, cosine_4, -sine_4).astype(bf16))
    half_grads, both_low = lax.optimization_barrier((half_grads, both_grad_low))
    came = lax.all_to_all(half_grads, CTX, 0, 0, tiled=True)
    layer_low = row_products(
        [inner_low, attend_low, branch_low, normed_low],
        [both_low, attended_rows, hidden_low, query_linear_low],
    )
    own_grads = jnp.sum(came.astype(f32), axis=0)
    keyval_low = jnp.concatenate(
        [
            rotate_lanes(own_grads[:, :HD], cosine[:, :128].T, -sine[:, :128].T),
            own_grads[:, HD:],
        ],
        axis=1,
    ).astype(bf16)
    normed_part = contract_first(query_linear_low, w_query).reshape(2, 128, D)
    normed_part = jnp.stack([normed_part[0] + contract_last(keyval_low, w_pair), normed_part[1]])
    layer_low, head_low, normed_part = lax.optimization_barrier((layer_low, head_low, normed_part))
    layer_low = lax.psum_scatter(layer_low, CTX, scatter_dimension=0, tiled=True)[0]
    normed_grad = scatter_tp(normed_part.reshape(2, N_X, SHARD, D))
    pair_low = contract_first(keyval_low, normed_half).astype(bf16)
    pair_low = pair_low.reshape(2 * HD, N_CTX, LINES).transpose(1, 0, 2)
    first_part, first_gain_grad = jax.vjp(rms_norm, stream_in, gains[0])[1](normed_grad)
    input_low = (mid_grad + first_part).astype(bf16)

    gain_parts = jnp.stack([first_gain_grad, middle_gain_grad, final_gain_grad]).astype(bf16)
    sent = jnp.concatenate(
        [
            input_low.reshape(SHARD, N_CTX, LINES).transpose(1, 0, 2),
            jnp.pad(gain_parts.reshape(3, N_CTX, LINES).transpose(1, 0, 2), ((0, 0), (0, 13), (0, 0))),
            pair_low,
        ],
        axis=1,
    )
    arrived = lax.all_to_all(sent, CTX, 0, 0, tiled=True)
    kv_part = jnp.sum(arrived[:, 48:].astype(f32), axis=0)
    gain_sums = jnp.sum(arrived[:, SHARD : SHARD + 3].astype(f32), axis=0)
    place_grads = gather_tp(arrived[:, :SHARD].reshape(N_CTX * SHARD, LINES))
    embed_grad = add_up(all_ids, place_grads, vocab_here)

    kv_full = kv_part + core_swap(kv_part)
    kv_split, embed_grad = lax.optimization_barrier(
        (kv_full.T.reshape(N_X, 2, 16, 2 * HD), embed_grad)
    )
    kv_owned = swapped_x(jnp.where(cs == 0, kv_split[:, 0], kv_split[:, 1]), xs)
    key_value_grad = (
        kv_owned.reshape(KV_HEADS, 16, 2, HD).transpose(1, 2, 0, 3).reshape(16, KVW)
    )

    old_rows = jnp.concatenate(
        [attention_row_moment, feed_row_moment, vocab_row_moment, jnp.ones((9, LINES), f32)]
    )
    kv_old_columns = lax.dynamic_index_in_dim(
        key_value_column_moment.reshape(2, KV_HEADS, HD), xs, 1, keepdims=False
    ).reshape(-1)
    gap = jnp.ones((96,), f32)
    old_columns = jnp.concatenate(
        [
            vocab_column_moment[0],
            gap,
            vocab_column_moment[1],
            gap,
            kv_old_columns,
            feed_column_moment[0],
            feed_column_moment[1],
            attention_column_moment[1],
            feed_column_moment[2],
            attention_column_moment[0],
            gap[:64],
        ]
    )[None]
    kv_old_line = lax.dynamic_update_slice_in_dim(
        jnp.zeros((1, LINES), f32), key_value_row_moment[None], tp_index * 16, 1
    )
    vocab_grad, line_parts, column_parts = early_figures(
        head_low, embed_grad, kv_full, gain_sums, kv_old_line
    )
    feed_grad, attention_grad, line_parts, column_parts = late_figures(
        layer_low, line_parts, column_parts
    )
    columns = sent_to_all(column_parts, CTX)
    lines = sum_tp(line_parts)
    gain_grad = lax.dynamic_slice_in_dim(lines[8:11], tp_index * 16, 16, 1)
    gain_second = moments(gain_moment.T, gain_grad * gain_grad, 1.0)
    gain_step = gain_grad * lax.rsqrt(gain_second)
    gain_squares = jnp.sum(gain_step * gain_step, axis=1)
    base = weight_sums + jnp.concatenate(
        [
            jnp.zeros((UG_LANE,), f32),
            gain_squares,
            loss_part.reshape(1),
            jnp.zeros((127 - LOSS_LANE,), f32),
        ]
    )
    row_new, column_new, scalars, vocab_unit, feed_unit, attention_unit = step_squares(
        vocab_grad,
        layer_low,
        kv_full,
        lines,
        columns,
        old_rows,
        old_columns,
        base,
        [vocab_grad.shape, feed_grad.shape, attention_grad.shape],
    )
    kv_columns_here = column_new[:, 8192:8320]
    gathered = sent_to_all(jnp.concatenate([scalars, kv_columns_here]), CTX_TP)
    vocab_new, feed_new, attention_new, gain_new, figures = update(
        gathered[:, 0],
        tables,
        vocab_unit,
        feed_tables,
        feed_unit,
        attention_master,
        attention_unit,
        gain_master.T,
        gain_step,
    )
    token_loss = figures[2, 0]
    update_rms = figures[0, :11]
    kv_row_new = lax.dynamic_slice_in_dim(row_new[7], tp_index * 16, 16, 0)
    kv_column_new = (
        gathered[0:8:2, 1].reshape(KV_HEADS, 2, HD).transpose(1, 0, 2).reshape(KVW)
    )
    kv_step = key_value_grad * lax.rsqrt(kv_row_new)[:, None] * lax.rsqrt(kv_column_new)[None]
    kv_new = key_value_master - figures[1, 7] * kv_step
    def columns_of(k):
        at, width = COLUMN_AT[k]
        return column_new[0, at : at + width]

    attention_columns = jnp.stack([columns_of(0), columns_of(1)])
    feed_columns = jnp.stack([columns_of(2), columns_of(3), columns_of(4)])
    return (
        token_loss,
        update_rms,
        attention_grad,
        row_new[0:2],
        attention_columns,
        attention_new,
        feed_grad.transpose(0, 2, 1),
        row_new[2:5],
        feed_columns,
        feed_new.transpose(0, 2, 1),
        vocab_grad.transpose(0, 2, 1),
        row_new[5:7],
        columns_of(5),
        columns_of(6),
        vocab_new.transpose(0, 2, 1),
        key_value_grad,
        kv_row_new,
        kv_column_new,
        kv_new,
        gain_grad.T,
        gain_second.T,
        gain_new.T,
    )


def solution(mesh):
    finer = Mesh(mesh.devices.reshape(4, 4, 4, 2), ("ctx_0", "ctx_1", "tp_0", "tp_1"))
    in_specs = (
        P(CTX),
        P(CTX),
        P(CTX),
        P(),
        P(),
        P(None, CTX, TP),
        P(None, CTX, TP),
        P(None, CTX, TP),
        P(CTX_TP, None),
        P(CTX_TP, None),
        P(None, CTX),
        P(None, TP),
        P(None, CTX),
        P(None, TP),
        P(None, CTX),
        P(None, TP),
        P(CTX_TP),
        P(),
        P(CTX_TP, None),
    )
    out_specs = (
        P(),
        P(),
        P(None, CTX, TP),
        P(None, CTX),
        P(None, TP),
        P(None, CTX, TP),
        P(None, CTX, TP),
        P(None, CTX),
        P(None, TP),
        P(None, CTX, TP),
        P(None, CTX, TP),
        P(None, CTX),
        P(TP),
        P(TP),
        P(None, CTX, TP),
        P(CTX_TP, None),
        P(CTX_TP),
        P(),
        P(CTX_TP, None),
        P(CTX_TP, None),
        P(CTX_TP, None),
        P(CTX_TP, None),
    )
    return jax.shard_map(body, mesh=finer, in_specs=in_specs, out_specs=out_specs, check_vma=False)
```

```python
import functools
import math

import jax
import jax.numpy as jnp
from jax import lax
from jax.experimental import pallas as pl
from jax.experimental.pallas import tpu as pltpu
from jax.sharding import Mesh
from jax.sharding import PartitionSpec as P

D = 2048
HEADS = 32
KV_HEADS = 4
HD = 64
FF = 5632
VOCAB = 32000
ORIG_CTX = 2048
HQ = 2048
KVW = 512
TOKENS = 4096
TP = ("tp_0", "tp_1")
CTX = ("ctx_0", "ctx_1")
CTX_TP = ("ctx_0", "ctx_1", "tp_0", "tp_1")
N_CTX = 16
N_X = 4
N_TP = 8
SHARD = 32
LINES = 128
DOCS = 5

NORM_EPS = 1e-05
MOMENT_DECAY = 0.5
MOMENT_EPS = 1e-30
CLIP_LIMIT = 0.5
STEP_SCALE = 1.0
ROPE_BASE = 10000.0
YARN_SCALE = 4.0
YARN_ALPHA = 1.0
YARN_BETA = 32.0

bf16 = jnp.bfloat16
f32 = jnp.float32


def x_from(values, step):
    return lax.ppermute(values, "tp_0", [((i + step) % N_X, i) for i in range(N_X)])


def x_to(values, step):
    return lax.ppermute(values, "tp_0", [(i, (i + step) % N_X) for i in range(N_X)])


def core_swap(values):
    return lax.ppermute(values, "tp_1", [(0, 1), (1, 0)])


def turned(stack, start):
    return lax.dynamic_slice_in_dim(jnp.concatenate([stack, stack]), start, N_X, 0)


def to_absolute(stack, xs):
    return turned(stack, (N_X - xs) % N_X)


def gather_tp(shard):
    column = jnp.concatenate([shard] + [x_from(shard, d) for d in range(1, N_X)])
    return jnp.concatenate([column, core_swap(column)])


def scatter_tp(partial):
    half = partial[0] + core_swap(partial[1].astype(bf16)).astype(f32)
    low = half.astype(bf16)
    total = half[0]
    for d in range(1, N_X):
        total = total + x_to(low[d], d).astype(f32)
    return total


def both_cores(column, cs):
    other = core_swap(column)
    both = jnp.where(
        cs == 0, jnp.stack([column, other], axis=1), jnp.stack([other, column], axis=1)
    )
    return both.reshape(-1, *column.shape[2:])


def swapped_x(blocks, xs):
    ours = turned(blocks, xs)
    came = [ours[0]] + [x_to(ours[d], d) for d in range(1, N_X)]
    return to_absolute(jnp.stack([came[0], came[3], came[2], came[1]]), xs)


def partner(values, axis, mask):
    size = 2 if axis == "tp_1" else 4
    return lax.ppermute(values, axis, [(i, i ^ mask) for i in range(size)])


def sum_over_four(values, axis):
    return (values + partner(values, axis, 1)) + (
        partner(values, axis, 2) + partner(values, axis, 3)
    )


def sum_tp(values):
    return sum_over_four(values + partner(values, "tp_1", 1), "tp_0")


def sum_ctx(values):
    return sum_over_four(sum_over_four(values, "ctx_1"), "ctx_0")


def own_order(values, xs, cs):
    blocks = turned(values.reshape(N_X, 2, SHARD), xs)
    blocks = jnp.where(cs == 0, blocks, blocks[:, ::-1])
    return blocks.transpose(1, 0, 2)


def sent_to_all(array, axis):
    copies = jnp.broadcast_to(array, (lax.axis_size(axis), *array.shape))
    return lax.all_to_all(copies, axis, split_axis=0, concat_axis=0, tiled=True)


def rope_tables(positions):
    ladder = jnp.arange(HD // 2, dtype=f32)
    freqs = ROPE_BASE ** (-2.0 * ladder / HD)
    ratio = ORIG_CTX * freqs / (2.0 * math.pi)
    ramped = jnp.clip((ratio - YARN_ALPHA) / (YARN_BETA - YARN_ALPHA), 0.0, 1.0)
    inverse = freqs * (1.0 - ramped) / YARN_SCALE + freqs * ramped
    angles = inverse[:, None] * positions.astype(f32)[None, :]
    mscale = 0.1 * math.log(YARN_SCALE) + 1.0
    return (jnp.cos(angles) * mscale, jnp.sin(angles) * mscale)


def rotate_rows(values, cosine, sine):
    half = values.shape[0] // 2
    first, second = (values[:half], values[half:])
    return jnp.concatenate([first * cosine - second * sine, second * cosine + first * sine])


def rotate_lanes(values, cosine, sine):
    half = values.shape[1] // 2
    first, second = (values[:, :half], values[:, half:])
    return jnp.concatenate([first * cosine - second * sine, second * cosine + first * sine], axis=1)


def rms_norm(values, gain):
    return values * lax.rsqrt(jnp.mean(values * values, axis=-1, keepdims=True) + NORM_EPS) * gain


def contract_last(left, right):
    return lax.dot_general(left, right, (((1,), (1,)), ((), ())), preferred_element_type=f32)


def contract_first(left, right):
    return lax.dot_general(left, right, (((0,), (0,)), ((), ())), preferred_element_type=f32)


def contract(left, right):
    return jnp.dot(left, right, preferred_element_type=f32)


def combine_stats(former, latter):
    highest = jnp.maximum(former[0], latter[0])
    summed = former[1] * jnp.exp(former[0] - highest) + latter[1] * jnp.exp(latter[0] - highest)
    return jnp.stack([highest, summed, former[2] + latter[2]])


def contract_ft(weights, places):
    return lax.dot_general(weights, places, (((0,), (1,)), ((), ())), preferred_element_type=f32)


def contract_tf(features, weights):
    return lax.dot_general(features, weights, (((0,), (1,)), ((), ())), preferred_element_type=f32)


def heads_on_lanes(features):
    return jnp.concatenate([features[h * HD : (h + 1) * HD] for h in range(4)], axis=1)


def heads_on_rows(features):
    return jnp.concatenate(jnp.split(features, 4, axis=1))


VMEM_LIMIT = 50 * 1024 * 1024


GROUP = 4
KEYS = 128 * GROUP
STEPS = TOKENS // KEYS


def key_places(core_bit, spans):
    line = lax.broadcasted_iota(jnp.int32, (128, 1), 0)
    x = (spans[N_CTX] + line // SHARD) % N_X
    place = (x * 2 + (spans[N_CTX + 1] ^ core_bit)) * SHARD + line % SHARD
    return place >= 128, place % 128


def visible_keys(spans, places, step, own, start):
    lines = []
    for block in range(step * GROUP, (step + 1) * GROUP):
        span = spans[block % N_CTX]
        second, within = places[block // N_CTX]
        lines.append(jnp.where(second, (2 * N_CTX - 1 - span) * 128, span * 128) + within)
    at = jnp.concatenate(lines, axis=0)
    return (at >= start) & (at <= own)


def key_columns(kv_ref, step, at):
    return jnp.concatenate(
        [kv_ref[step * GROUP + i, at : at + HD] for i in range(GROUP)], axis=1
    )


def attend_kernel(spans, own_ref, q_ref, kv_ref, o_ref, total_ref, s_ref):
    q = q_ref[...]
    own, start = (own_ref[0:1], own_ref[1:2])
    places = [key_places(core_bit, spans) for core_bit in range(2)]
    top = None
    for step in range(STEPS):
        scores = contract_first(key_columns(kv_ref, step, 0), q)
        scores = jnp.where(visible_keys(spans, places, step, own, start), scores, -1e30)
        s_ref[step * KEYS : (step + 1) * KEYS] = scores
        highest = jnp.max(scores, axis=0, keepdims=True)
        top = highest if top is None else jnp.maximum(top, highest)
    total = jnp.zeros(top.shape, f32)
    for step in range(STEPS):
        powers = jnp.exp(s_ref[step * KEYS : (step + 1) * KEYS] - top)
        s_ref[step * KEYS : (step + 1) * KEYS] = powers
        total = total + jnp.sum(powers, axis=0, keepdims=True)
    share = 1.0 / total
    out = jnp.zeros(q.shape, f32)
    for step in range(STEPS):
        weights = (s_ref[step * KEYS : (step + 1) * KEYS] * share).astype(bf16)
        out = out + contract(key_columns(kv_ref, step, HD), weights)
    o_ref[...] = out.astype(bf16)
    total_ref[...] = top + jnp.log(total)


SPLIT = 2


def attend(spans, own, q, kv):
    lanes = q.shape[1] // SPLIT
    column = lambda rows: pl.BlockSpec((rows, lanes), lambda i: (0, i))
    return pl.pallas_call(
        attend_kernel,
        grid=(SPLIT,),
        in_specs=[
            pl.BlockSpec(memory_space=pltpu.SMEM),
            column(2),
            column(HD),
            pl.BlockSpec(kv.shape, lambda i: (0, 0, 0)),
        ],
        out_specs=[column(HD), column(1)],
        out_shape=[
            jax.ShapeDtypeStruct(q.shape, bf16),
            jax.ShapeDtypeStruct((1, q.shape[1]), f32),
        ],
        scratch_shapes=[pltpu.VMEM((TOKENS, lanes), f32)],
        compiler_params=pltpu.CompilerParams(vmem_limit_bytes=VMEM_LIMIT),
        cost_estimate=pl.CostEstimate(
            flops=16 * TOKENS * q.shape[1] * HD, bytes_accessed=2 << 20, transcendentals=0
        ),
    )(spans, own, q, kv)


def attend_back_kernel(
    spans, own_ref, q_ref, do_ref, total_ref, kv_ref, dq_ref, dkv_ref, p_ref, dp_ref
):
    q, do = (q_ref[...], do_ref[...])
    own, start = (own_ref[0:1], own_ref[1:2])
    total = total_ref[...]
    places = [key_places(core_bit, spans) for core_bit in range(2)]
    rowsum = jnp.zeros(total.shape, f32)
    for step in range(STEPS):
        scores = contract_first(key_columns(kv_ref, step, 0), q)
        scores = jnp.where(visible_keys(spans, places, step, own, start), scores, -1e30)
        probs = jnp.exp(scores - total)
        probs_grad = contract_first(key_columns(kv_ref, step, HD), do)
        p_ref[step * KEYS : (step + 1) * KEYS] = probs
        dp_ref[step * KEYS : (step + 1) * KEYS] = probs_grad
        rowsum = rowsum + jnp.sum(probs * probs_grad, axis=0, keepdims=True)

    @pl.when(pl.program_id(0) == 0)
    def _():
        dkv_ref[...] = jnp.zeros(dkv_ref.shape, f32)

    dq = jnp.zeros(q.shape, f32)
    for step in range(STEPS):
        rows = slice(step * KEYS, (step + 1) * KEYS)
        probs = p_ref[rows]
        score_grad = (probs * (dp_ref[rows] - rowsum)).astype(bf16)
        dkv_ref[rows] += jnp.concatenate(
            [contract_last(score_grad, q), contract_last(probs.astype(bf16), do)], axis=1
        )
        dq = dq + contract(key_columns(kv_ref, step, 0), score_grad)
    dq_ref[...] = dq * (1.0 / math.sqrt(HD))


def attend_back(spans, own, q, do, total, kv):
    lanes = q.shape[1] // SPLIT
    column = lambda rows: pl.BlockSpec((rows, lanes), lambda i: (0, i))
    return pl.pallas_call(
        attend_back_kernel,
        grid=(SPLIT,),
        in_specs=[
            pl.BlockSpec(memory_space=pltpu.SMEM),
            column(2),
            column(HD),
            column(HD),
            column(1),
            pl.BlockSpec(kv.shape, lambda i: (0, 0, 0)),
        ],
        out_specs=[column(HD), pl.BlockSpec((TOKENS, 2 * HD), lambda i: (0, 0))],
        out_shape=[
            jax.ShapeDtypeStruct(q.shape, f32),
            jax.ShapeDtypeStruct((TOKENS, 2 * HD), f32),
        ],
        scratch_shapes=[pltpu.VMEM((TOKENS, lanes), f32), pltpu.VMEM((TOKENS, lanes), f32)],
        compiler_params=pltpu.CompilerParams(vmem_limit_bytes=VMEM_LIMIT),
        cost_estimate=pl.CostEstimate(
            flops=40 * TOKENS * q.shape[1] * HD, bytes_accessed=4 << 20, transcendentals=0
        ),
    )(spans, own, q, do, total, kv)


def moments(old, sums, count):
    return MOMENT_DECAY * old + (1.0 - MOMENT_DECAY) * (sums / count + MOMENT_EPS)


def params():
    return pltpu.CompilerParams(vmem_limit_bytes=VMEM_LIMIT)


def whole(array):
    zeros = (0,) * array.ndim
    return pl.BlockSpec(array.shape, lambda *i: zeros)


def cost(flops, moved):
    return pl.CostEstimate(flops=flops, bytes_accessed=moved, transcendentals=0)


ID_STEP = 2048


def look_kernel(ids_ref, table_ref, out_ref, low_ref):
    @pl.when(pl.program_id(0) == 0)
    def _():
        low_ref[...] = table_ref[0].astype(bf16)

    width = low_ref.shape[0]
    ids = jnp.transpose(jnp.broadcast_to(ids_ref[...], (8, ID_STEP)))[:, :1]
    hits = ids == lax.broadcasted_iota(jnp.int32, (ID_STEP, width), 1)
    out_ref[...] = contract(jnp.where(hits, 1.0, 0.0).astype(bf16), low_ref[...]).astype(bf16)


def look_up(ids, tables):
    width, lines = tables.shape[1:]
    count = ids.shape[1]
    return pl.pallas_call(
        look_kernel,
        grid=(count // ID_STEP,),
        in_specs=[
            pl.BlockSpec((1, ID_STEP), lambda i: (0, i)),
            pl.BlockSpec((1, width, lines), lambda i: (1, 0, 0)),
        ],
        out_specs=pl.BlockSpec((ID_STEP, lines), lambda i: (i, 0)),
        out_shape=jax.ShapeDtypeStruct((count, lines), bf16),
        scratch_shapes=[pltpu.VMEM((width, lines), bf16)],
        compiler_params=params(),
        cost_estimate=cost(4 * count * width * lines, 4 * lines * width),
    )(ids, tables)


def add_kernel(ids_ref, grads_ref, out_ref):
    hits = lax.broadcasted_iota(jnp.int32, (out_ref.shape[0], ID_STEP), 0) == ids_ref[...]
    added = contract(jnp.where(hits, 1.0, 0.0).astype(bf16), grads_ref[...])

    @pl.when(pl.program_id(0) == 0)
    def _():
        out_ref[...] = added

    @pl.when(pl.program_id(0) > 0)
    def _():
        out_ref[...] += added


def add_up(ids, grads, width):
    count, lines = grads.shape
    return pl.pallas_call(
        add_kernel,
        grid=(count // ID_STEP,),
        in_specs=[
            pl.BlockSpec((1, ID_STEP), lambda i: (0, i)),
            pl.BlockSpec((ID_STEP, lines), lambda i: (i, 0)),
        ],
        out_specs=pl.BlockSpec((width, lines), lambda i: (0, 0)),
        out_shape=jax.ShapeDtypeStruct((width, lines), f32),
        compiler_params=params(),
        cost_estimate=cost(4 * count * width * lines, 4 * lines * width),
    )(ids, grads)


LOGIT_STEP = 800


def logits_kernel(c_ref, w_ref, target_ref, out_ref, stats_ref):
    step = pl.program_id(0)
    logits = contract_last(w_ref[...], c_ref[...])
    out_ref[...] = logits
    row = lax.broadcasted_iota(jnp.int32, logits.shape, 0) + step * LOGIT_STEP
    here = jnp.max(logits, axis=0, keepdims=True)
    pick = jnp.sum(jnp.where(row == target_ref[...], logits, 0.0), axis=0, keepdims=True)

    @pl.when(step == 0)
    def _():
        stats_ref[...] = jnp.zeros(stats_ref.shape, f32)
        stats_ref[0:1] = here

    old = stats_ref[0:1]
    top = jnp.maximum(old, here)
    powers = jnp.sum(jnp.exp(logits - top), axis=0, keepdims=True)
    stats_ref[1:2] = stats_ref[1:2] * jnp.exp(old - top) + powers
    stats_ref[2:3] += pick
    stats_ref[0:1] = top


def logits_and_stats(c, head, width, targets):
    places, rows = c.shape
    return pl.pallas_call(
        logits_kernel,
        grid=(width // LOGIT_STEP,),
        in_specs=[whole(c), pl.BlockSpec((LOGIT_STEP, rows), lambda i: (i, 0)), whole(targets)],
        out_specs=[
            pl.BlockSpec((LOGIT_STEP, places), lambda i: (i, 0)),
            pl.BlockSpec((8, places), lambda i: (0, 0)),
        ],
        out_shape=[
            jax.ShapeDtypeStruct((width, places), f32),
            jax.ShapeDtypeStruct((8, places), f32),
        ],
        compiler_params=params(),
        cost_estimate=cost(2 * places * rows * width, 2 * rows * width),
    )(c, head, targets)


def head_grad_kernel(logits_ref, c_ref, place_ref, target_ref, dw_ref, low_ref):
    step = pl.program_id(0)
    logits = logits_ref[...]
    row = lax.broadcasted_iota(jnp.int32, logits.shape, 0) + step * LOGIT_STEP
    hit = row == target_ref[...]
    shares = jnp.exp(logits - place_ref[0:1]) - jnp.where(hit, 1.0, 0.0)
    low = (place_ref[1:2] * shares).astype(bf16)
    low_ref[...] = low
    grad = contract(low, c_ref[...]).astype(bf16)
    for k in range(N_CTX):
        dw_ref[k] = grad[:, k * 128 : (k + 1) * 128]


def head_grads(logits, c, place, targets):
    places, rows = c.shape
    width = logits.shape[0]
    block = pl.BlockSpec((LOGIT_STEP, places), lambda i: (i, 0))
    return pl.pallas_call(
        head_grad_kernel,
        grid=(width // LOGIT_STEP,),
        in_specs=[block, whole(c), whole(place), whole(targets)],
        out_specs=[pl.BlockSpec((N_CTX, LOGIT_STEP, 128), lambda i: (0, i, 0)), block],
        out_shape=[
            jax.ShapeDtypeStruct((N_CTX, width, 128), bf16),
            jax.ShapeDtypeStruct((width, places), bf16),
        ],
        compiler_params=params(),
        cost_estimate=cost(2 * places * rows * width, 2 * rows * width),
    )(logits, c, place, targets)


TURNED = (1, 3)


def products_kernel(count, offsets, *refs):
    lefts, rights = (refs[:count], refs[count : 2 * count])
    out_ref, turned_ref = refs[2 * count :]

    @pl.when(pl.program_id(0) == 0)
    def _():
        for k, (right, (at, width)) in enumerate(zip(rights, offsets)):
            values = right[...]
            turned_ref[at : at + width] = values if k in TURNED else jnp.transpose(values)

    for left, (at, width) in zip(lefts, offsets):
        grad = contract(turned_ref[at : at + width], left[...]).astype(bf16)
        for k in range(2):
            out_ref[k, at : at + width] = grad[:, k * 128 : (k + 1) * 128]


def row_products(lefts, rights):
    places, rows = lefts[0].shape
    offsets, at = ([], 0)
    for k, right in enumerate(rights):
        width = right.shape[0 if k in TURNED else 1]
        offsets.append((at, width))
        at += width
    return pl.pallas_call(
        functools.partial(products_kernel, len(lefts), tuple(offsets)),
        grid=(N_CTX // 2,),
        in_specs=[pl.BlockSpec((places, 256), lambda i: (0, i)) for _ in lefts]
        + [whole(right) for right in rights],
        out_specs=pl.BlockSpec((2, at, 128), lambda i: (i, 0, 0)),
        out_shape=jax.ShapeDtypeStruct((N_CTX, at, rows // N_CTX), bf16),
        scratch_shapes=[pltpu.VMEM((at, places), bf16)],
        compiler_params=params(),
        cost_estimate=cost(2 * places * rows * at, 2 * rows * at),
    )(*lefts, *rights)


MATRICES = 8
WIDTHS = (HQ, HQ, FF, FF, FF, VOCAB, VOCAB, KVW)
EARLY_LANES = 8320
LATE_LANES = 2688
COLUMN_AT = {5: (0, 4000), 6: (4096, 4000), 7: (8192, 128)}
COLUMN_AT.update({2: (0, 704), 3: (704, 704), 1: (1408, 256), 4: (1664, 704), 0: (2368, 256)})
S_LANE, T_LANE, OLD_LANE, W_LANE, WG_LANE, UG_LANE, LOSS_LANE = (0, 8, 16, 24, 32, 35, 38)


def lane_is(shape, lane):
    return lax.broadcasted_iota(jnp.int32, shape, 1) == lane


def line_sum(values):
    return jnp.sum(values, axis=0, keepdims=True)


def total_of(values):
    return jnp.sum(line_sum(values), axis=1, keepdims=True)


def column_sums(squares):
    ones = jnp.ones((8, squares.shape[1]), f32)
    return lax.dot_general(
        ones,
        squares,
        (((1,), (1,)), ((), ())),
        precision=lax.Precision.HIGHEST,
        preferred_element_type=f32,
    )


def weights_kernel(tables_ref, feed_ref, attention_ref, kv_master_ref, gain_ref, scalars_ref):
    scalars = jnp.zeros(scalars_ref.shape, f32)
    for number, weights in (
        (0, attention_ref[0]),
        (1, attention_ref[1]),
        (2, feed_ref[0]),
        (3, feed_ref[1]),
        (4, feed_ref[2]),
        (5, tables_ref[0]),
        (6, tables_ref[1]),
        (7, kv_master_ref[...]),
        (8, gain_ref[0:1]),
        (9, gain_ref[1:2]),
        (10, gain_ref[2:3]),
    ):
        scalars += jnp.where(
            lane_is(scalars.shape, W_LANE + number), total_of(weights * weights), 0.0
        )
    scalars_ref[...] = scalars


def weight_squares(*masters):
    return pl.pallas_call(
        weights_kernel,
        out_shape=jax.ShapeDtypeStruct((1, 128), f32),
        compiler_params=params(),
        cost_estimate=cost(0, 6 << 20),
    )(*masters)


def early_kernel(
    head_ref, embed_ref, kv_ref, gains_ref, kv_old_ref, vocab_grad_ref, lines_ref, columns_ref
):
    lines_ref[...] = jnp.zeros(lines_ref.shape, f32)
    lines_ref[8:11] = gains_ref[...]
    lines_ref[11:12] = kv_old_ref[...]
    sums = []
    for number, ref in ((5, head_ref), (6, embed_ref), (7, kv_ref)):
        grad = ref[...].astype(f32)
        if number in (5, 6):
            vocab_grad_ref[number - 5] = grad
        squares = grad * grad
        lines_ref[number : number + 1] = (0.5 if number == 7 else 1.0) * line_sum(squares)
        sums.append(column_sums(squares)[:1])
        if number in (5, 6):
            sums.append(jnp.zeros((1, 96), f32))
    columns_ref[...] = jnp.broadcast_to(
        jnp.concatenate(sums, axis=1)[None], columns_ref.shape
    )


def early_figures(*arrays):
    shapes = ((2, *arrays[1].shape), (16, 128), (N_CTX, 1, EARLY_LANES))
    return pl.pallas_call(
        early_kernel,
        out_shape=[jax.ShapeDtypeStruct(shape, f32) for shape in shapes],
        compiler_params=params(),
        cost_estimate=cost(0, 12 << 20),
    )(*arrays)


def late_kernel(layer_ref, feed_grad_ref, attention_grad_ref, lines_ref, columns_ref):
    layer = layer_ref[...].astype(f32)
    squares = layer * layer
    sums = jnp.concatenate(
        [column_sums(squares)[:1], jnp.zeros((1, LATE_LANES - layer.shape[0]), f32)], axis=1
    )
    columns_ref[...] = jnp.broadcast_to(sums[None], columns_ref.shape)
    lines_ref[...] = jnp.zeros(lines_ref.shape, f32)
    for number in range(5):
        at, width = COLUMN_AT[number]
        lines_ref[number : number + 1] = line_sum(squares[at : at + width])
        if number > 1:
            feed_grad_ref[number - 2] = layer[at : at + width]
    attention_grad_ref[0] = jnp.transpose(layer[2368:2624])
    attention_grad_ref[1] = jnp.transpose(layer[1408:1664])


def late_figures(layer):
    shapes = ((3, 704, 128), (2, 128, 256), (8, 128), (N_CTX, 1, LATE_LANES))
    return pl.pallas_call(
        late_kernel,
        out_shape=[jax.ShapeDtypeStruct(shape, f32) for shape in shapes],
        compiler_params=params(),
        cost_estimate=cost(0, 4 << 20),
    )(layer)


def per_column(figures, number):
    at, width = COLUMN_AT[number]
    return figures[at : at + width, :1]


def on_rows(columns):
    spare = 8 - columns.shape[0]
    return jnp.transpose(
        jnp.concatenate([columns, jnp.ones((spare, columns.shape[1]), f32)], axis=0)
    )


def squares_of(sources, lines, old, columns, old_columns, scalars, row_ref, column_ref):
    number = lax.broadcasted_iota(jnp.int32, lines.shape, 0)
    widths = jnp.full(lines.shape, 1.0, f32)
    for k, width in enumerate(WIDTHS):
        widths = jnp.where(number == k, float(width), widths)
    row_new = moments(old, lines / widths, 1.0)
    row_ref[...] = row_new
    column_new = moments(old_columns, jnp.sum(columns, axis=0), float(D))
    column_ref[...] = column_new
    row_scale = lax.rsqrt(row_new)
    column_scale = on_rows(lax.rsqrt(column_new))
    had = jnp.sum(old, axis=1, keepdims=True) * (1.0 / N_TP)
    got = jnp.sum(lines, axis=1, keepdims=True) * (1.0 / N_TP)
    for k, grad, keep in sources:
        unit = grad * row_scale[k : k + 1] * per_column(column_scale, k)
        if keep is not None:
            keep[0][keep[1]] = jnp.transpose(unit) if k < 2 else unit
        part = total_of(unit * unit) * (0.5 if k == 7 else 1.0)
        scalars += jnp.where(lane_is(scalars.shape, S_LANE + k), part, 0.0)
        scalars += jnp.where(lane_is(scalars.shape, T_LANE + k), got[k : k + 1], 0.0)
        scalars += jnp.where(lane_is(scalars.shape, OLD_LANE + k), had[k : k + 1], 0.0)
    return scalars


def early_squares_kernel(
    vocab_ref, kv_ref, lines_ref, columns_ref, old_ref, old_columns_ref, base_ref,
    row_ref, column_ref, unit_ref, scalars_ref,
):
    lines = lines_ref[...]
    number = lax.broadcasted_iota(jnp.int32, lines.shape, 0)
    old = jnp.where(number == 7, lines_ref[11:12], old_ref[...])
    sources = (
        (5, vocab_ref[0], (unit_ref, 0)),
        (6, vocab_ref[1], (unit_ref, 1)),
        (7, kv_ref[...], None),
    )
    scalars_ref[...] = squares_of(
        sources, lines, old, columns_ref[...], old_columns_ref[...], base_ref[...],
        row_ref, column_ref,
    )


def late_squares_kernel(
    layer_ref, lines_ref, columns_ref, old_ref, old_columns_ref, base_ref, kv_columns_ref,
    row_ref, column_ref, feed_unit_ref, attention_unit_ref, packed_ref,
):
    sources = []
    for number in range(5):
        at, width = COLUMN_AT[number]
        keep = (attention_unit_ref, number) if number < 2 else (feed_unit_ref, number - 2)
        sources.append((number, layer_ref[at : at + width].astype(f32), keep))
    scalars = squares_of(
        sources, lines_ref[...], old_ref[0:8], columns_ref[...], old_columns_ref[...],
        base_ref[...], row_ref, column_ref,
    )
    packed = jnp.concatenate([scalars, kv_columns_ref[...]], axis=0)
    packed_ref[...] = jnp.broadcast_to(packed[None], packed_ref.shape)


def step_squares(kernel, shapes, *arrays):
    return pl.pallas_call(
        kernel,
        out_shape=[jax.ShapeDtypeStruct(shape, f32) for shape in shapes],
        compiler_params=params(),
        cost_estimate=cost(0, 12 << 20),
    )(*arrays)


UPDATE_STEP = 800


def update_kernel(
    all_ref, vocab_ref, vocab_unit_ref, feed_ref, feed_unit_ref, attention_ref,
    attention_unit_ref, gain_ref, gain_step_ref,
    vocab_new_ref, feed_new_ref, attention_new_ref, gain_new_ref, figures_ref,
):
    sums = jnp.sum(all_ref[...], axis=0, keepdims=True)
    sums = jnp.broadcast_to(sums, (8, 128))

    def lanes_from(at):
        return pltpu.roll(sums, (128 - at) % 128, 1)[0:1]

    lane = lax.broadcasted_iota(jnp.int32, (1, 128), 1)
    counts = jnp.full((1, 128), float(D), f32)
    for k, width in enumerate(WIDTHS):
        counts = jnp.where(lane == k, float(D * width), counts)
    mean = MOMENT_DECAY * lanes_from(OLD_LANE) / D + (1.0 - MOMENT_DECAY) * (
        lanes_from(T_LANE) / counts + MOMENT_EPS
    )
    mean = jnp.where(lane < MATRICES, mean, 1.0)
    rms = jnp.sqrt(mean * lanes_from(S_LANE) / counts)
    factor = (
        STEP_SCALE
        * jnp.sqrt(lanes_from(W_LANE) / counts)
        / jnp.maximum(1.0, rms / CLIP_LIMIT)
        * jnp.sqrt(mean)
    )

    @pl.when(pl.program_id(0) == 0)
    def _():
        for k in range(2):
            attention_new_ref[k] = attention_ref[k] - attention_unit_ref[k] * factor[:, k : k + 1]
        for k in range(3):
            feed_new_ref[k] = feed_ref[k] - feed_unit_ref[k] * factor[:, 2 + k : 3 + k]
        gain_rms = jnp.sqrt(lanes_from(UG_LANE) / D)
        gain_factor = (
            STEP_SCALE
            * jnp.sqrt(lanes_from(WG_LANE) / D)
            / jnp.maximum(1.0, gain_rms / CLIP_LIMIT)
        )
        for k in range(3):
            gain_new_ref[k : k + 1] = (
                gain_ref[k : k + 1] - gain_factor[:, k : k + 1] * gain_step_ref[k : k + 1]
            )
        after = pltpu.roll(jnp.broadcast_to(gain_rms, (8, 128)), MATRICES, 1)[0:1]
        figures_ref[0:1] = jnp.where(lane < MATRICES, rms, after)
        figures_ref[1:2] = factor
        figures_ref[2:3] = lanes_from(LOSS_LANE)
        figures_ref[3:8] = jnp.zeros((5, 128), f32)

    for k in range(2):
        vocab_new_ref[k] = vocab_ref[k] - vocab_unit_ref[k] * factor[:, 5 + k : 6 + k]


def update(gathered, vocab, vocab_unit, feed, feed_unit, attention, attention_unit, gain, gain_step):
    stack = pl.BlockSpec((2, UPDATE_STEP, vocab.shape[2]), lambda i: (0, i, 0))
    others = (feed, feed_unit, attention, attention_unit, gain, gain_step)
    outs = (vocab, feed, attention, gain)
    return pl.pallas_call(
        update_kernel,
        grid=(vocab.shape[1] // UPDATE_STEP,),
        in_specs=[whole(gathered), stack, stack] + [whole(a) for a in others],
        out_specs=[stack]
        + [whole(a) for a in outs[1:]]
        + [pl.BlockSpec((8, 128), lambda i: (0, 0))],
        out_shape=[jax.ShapeDtypeStruct(a.shape, f32) for a in outs]
        + [jax.ShapeDtypeStruct((8, 128), f32)],
        compiler_params=params(),
        cost_estimate=cost(0, 24 << 20),
    )(gathered, vocab, vocab_unit, *others)


def body(
    token_ids,
    target_ids,
    loss_mask,
    segment_ids,
    span_pairs,
    attention_master,
    feed_master,
    vocab_master,
    key_value_master,
    gain_master,
    attention_row_moment,
    attention_column_moment,
    feed_row_moment,
    feed_column_moment,
    vocab_row_moment,
    vocab_column_moment,
    key_value_row_moment,
    key_value_column_moment,
    gain_moment,
):
    ctx_index = lax.axis_index(CTX)
    xs = lax.axis_index("tp_0")
    cs = lax.axis_index("tp_1")
    tp_index = xs * 2 + cs
    vocab_here = vocab_master.shape[2]
    ff_here = feed_master.shape[2]
    first_id = tp_index * vocab_here

    attention_low = attention_master.astype(bf16)
    feed_low = feed_master.astype(bf16)
    layer_all = lax.all_gather(
        jnp.concatenate(
            [attention_low[0], attention_low[1], feed_low[0], feed_low[1], feed_low[2]], axis=1
        ),
        CTX,
        axis=0,
        tiled=True,
    ).T
    head = lax.all_gather(vocab_master[0].astype(bf16), CTX, axis=0, tiled=True).T
    w_query = layer_all[:256]
    w_out = layer_all[256:512]
    gate_up = layer_all[512 : 512 + 2 * ff_here]
    down = layer_all[512 + 2 * ff_here :]

    kv_low = key_value_master.astype(bf16).reshape(16, 2, KV_HEADS, HD).transpose(2, 0, 1, 3)
    gain_low = jnp.pad(gain_master.astype(bf16), ((0, 0), (0, 125)))
    blocks = jnp.concatenate(
        [
            kv_low.reshape(KV_HEADS, 16, 2 * HD),
            jnp.broadcast_to(gain_low, (KV_HEADS, *gain_low.shape)),
        ],
        axis=2,
    )
    ids_here = own_order(token_ids, xs, cs).reshape(1, 256)
    line_block = both_cores(swapped_x(blocks, xs), cs)
    half = LINES // 2
    early = sent_to_all(
        jnp.concatenate(
            [
                lax.dynamic_slice_in_dim(line_block[:, : 2 * HD], cs * half, half, 0),
                line_block[:, 2 * HD : 2 * HD + 3].T,
                (ids_here // 256).astype(bf16).reshape(2, 128),
                (ids_here % 256).astype(bf16).reshape(2, 128),
                jnp.zeros((9, 128), bf16),
            ]
        ),
        CTX,
    )
    own_half = early[:, :half]
    other_half = core_swap(own_half)
    w_pair = jnp.where(
        cs == 0,
        jnp.concatenate([own_half, other_half], axis=1),
        jnp.concatenate([other_half, own_half], axis=1),
    ).reshape(D, 2 * HD)
    gains = early[:, half : half + 3].astype(f32).transpose(1, 0, 2).reshape(3, D)
    parts = early[:, half + 3 : half + 7].astype(jnp.int32).reshape(N_CTX, 2, 256)
    all_ids = parts[:, 0] * 256 + parts[:, 1]
    all_ids = all_ids.reshape(N_CTX, 8, SHARD).transpose(1, 0, 2).reshape(1, TOKENS) - first_id

    order = (
        ((xs + jnp.arange(N_X, dtype=jnp.int32)) % N_X * 2)[None, :]
        + (cs ^ jnp.arange(2, dtype=jnp.int32))[:, None]
    )[:, :, None] * SHARD + jnp.arange(SHARD, dtype=jnp.int32)
    second_span = order >= 128
    within = order % 128
    own_pair = lax.dynamic_slice_in_dim(span_pairs, ctx_index, 1)[0]
    last_span = 2 * N_CTX - 1
    own_pos = (jnp.where(second_span, last_span - own_pair, own_pair) * 128 + within).reshape(-1)
    doc_start = jnp.zeros_like(own_pos)
    for k in range(1, DOCS):
        start = jnp.sum((segment_ids < k).astype(jnp.int32))
        doc_start = jnp.where(own_pos >= start, start, doc_start)
    cosine, sine = rope_tables(own_pos - doc_start)
    cosine_4, sine_4 = (jnp.tile(cosine, (1, 4)), jnp.tile(sine, (1, 4)))
    own_places = jnp.tile(jnp.stack([own_pos, doc_start]), (1, 4))
    spans = jnp.concatenate([span_pairs, jnp.stack([xs, cs]).astype(jnp.int32)])

    tables = vocab_master.transpose(0, 2, 1)
    looked = look_up(all_ids, tables).reshape(2, N_X, N_CTX, SHARD, LINES)
    half = looked[0] + core_swap(looked[1])
    mine = half[0]
    for d in range(1, N_X):
        mine = mine + x_to(half[d], d)
    rows_in = lax.all_to_all(mine, CTX, 0, 0, tiled=True)
    stream_in = rows_in.transpose(1, 0, 2).reshape(SHARD, D).astype(f32)

    normed_low = gather_tp(rms_norm(stream_in, gains[0]).astype(bf16))
    normed_half = normed_low[:128]
    keyval_linear = contract_ft(w_pair, normed_half)
    own_keyvals = jnp.concatenate(
        [rotate_rows(keyval_linear[:HD], cosine[:, :128], sine[:, :128]), keyval_linear[HD:]]
    ).astype(bf16)
    half_keyvals = sent_to_all(own_keyvals, CTX)
    row_keyvals = jnp.concatenate([half_keyvals, core_swap(half_keyvals)])
    query_linear = heads_on_lanes(contract_last(w_query, normed_low))
    queries = rotate_rows(query_linear, cosine_4, sine_4).astype(bf16) * jnp.asarray(
        1.0 / math.sqrt(HD), bf16
    )
    attended, log_total = attend(spans, own_places, queries, row_keyvals)
    attended_rows = heads_on_rows(attended)
    stream_mid = stream_in + scatter_tp(
        contract_first(attended_rows, w_out).reshape(2, N_X, SHARD, D)
    )

    inner_low = gather_tp(rms_norm(stream_mid, gains[1]).astype(bf16))
    both = contract_last(inner_low, gate_up)
    gate, upward = (both[:, :ff_here], both[:, ff_here:])
    sigmoid_gate = jax.nn.sigmoid(gate)
    silu_gate = gate * sigmoid_gate
    hidden_low = (silu_gate * upward).astype(bf16)
    stream_out = stream_mid + scatter_tp(
        contract(hidden_low, down).reshape(2, N_X, SHARD, D)
    )

    feed_tables = feed_master.transpose(0, 2, 1)
    masters = (tables, feed_tables, attention_master, key_value_master, gain_master.T)
    masters, inner_low = lax.optimization_barrier((masters, inner_low))
    weight_sums = weight_squares(*masters)
    finals_low = gather_tp(rms_norm(stream_out, gains[2]).astype(bf16))
    weight_sums, finals_low = lax.optimization_barrier((weight_sums, finals_low))
    local_targets = own_order(target_ids, xs, cs).reshape(1, -1) - first_id
    logits, stats = logits_and_stats(finals_low, head, vocab_here, local_targets)
    stats = stats[:3].reshape(3, 2, N_X, SHARD)
    stats = combine_stats(stats, core_swap(stats)[:, ::-1])
    others = [jnp.roll(x_from(stats, d), d, axis=2) for d in range(1, N_X)]
    stats = combine_stats(combine_stats(stats, others[0]), combine_stats(others[1], others[2]))
    stats = stats.reshape(3, -1)
    vocab_total = stats[0] + jnp.log(stats[1])
    keep = own_order(loss_mask, xs, cs).reshape(-1).astype(f32)
    loss_part = jnp.sum((keep * (vocab_total - stats[2]))[:SHARD]) / TOKENS

    place = jnp.stack([vocab_total, keep / TOKENS])
    head_low, dlogits_low = head_grads(logits, finals_low, place, local_targets)
    head_low = lax.psum_scatter(head_low, CTX, scatter_dimension=0, tiled=True)[0]
    final_part = contract_first(dlogits_low, head)
    final_grad = scatter_tp(final_part.reshape(2, N_X, SHARD, D))
    out_grad, final_gain_grad = jax.vjp(rms_norm, stream_out, gains[2])[1](final_grad)
    branch_low = gather_tp(out_grad.astype(bf16))
    hidden_grad = contract_last(branch_low, down)
    gate_grad_low = (
        hidden_grad * upward * sigmoid_gate * (1.0 + gate * (1.0 - sigmoid_gate))
    ).astype(bf16)
    upward_grad_low = (hidden_grad * silu_gate).astype(bf16)
    both_grad_low = jnp.concatenate([gate_grad_low, upward_grad_low], axis=1)
    inner_grad = scatter_tp(contract(both_grad_low, gate_up).reshape(2, N_X, SHARD, D))
    mid_part, middle_gain_grad = jax.vjp(rms_norm, stream_mid, gains[1])[1](inner_grad)
    mid_grad = out_grad + mid_part
    attend_low = gather_tp(mid_grad.astype(bf16))
    attended_grad = heads_on_lanes(contract_last(w_out, attend_low).astype(bf16))
    dq, pair_grads = attend_back(
        spans, own_places, queries, attended_grad, log_total, row_keyvals
    )
    pair_grads = pair_grads.reshape(2, N_CTX, 128, 2 * HD)
    half_grads = (pair_grads[0] + core_swap(pair_grads[1].astype(bf16)).astype(f32)).astype(bf16)
    query_linear_low = heads_on_rows(rotate_rows(dq, cosine_4, -sine_4).astype(bf16))
    half_grads, both_low = lax.optimization_barrier((half_grads, both_grad_low))
    came = lax.all_to_all(half_grads, CTX, 0, 0, tiled=True)
    layer_low = row_products(
        [inner_low, attend_low, branch_low, normed_low],
        [both_low, attended_rows, hidden_low, query_linear_low],
    )
    own_grads = jnp.sum(came.astype(f32), axis=0)
    keyval_low = jnp.concatenate(
        [
            rotate_lanes(own_grads[:, :HD], cosine[:, :128].T, -sine[:, :128].T),
            own_grads[:, HD:],
        ],
        axis=1,
    ).astype(bf16)
    normed_part = contract_first(query_linear_low, w_query).reshape(2, 128, D)
    normed_part = jnp.stack([normed_part[0] + contract_last(keyval_low, w_pair), normed_part[1]])
    layer_low, head_low, normed_part = lax.optimization_barrier((layer_low, head_low, normed_part))
    layer_low = lax.psum_scatter(layer_low, CTX, scatter_dimension=0, tiled=True)[0]
    normed_grad = scatter_tp(normed_part.reshape(2, N_X, SHARD, D))
    pair_low = contract_first(keyval_low, normed_half).astype(bf16)
    pair_low = pair_low.reshape(2 * HD, N_CTX, LINES).transpose(1, 0, 2)
    first_part, first_gain_grad = jax.vjp(rms_norm, stream_in, gains[0])[1](normed_grad)
    input_low = (mid_grad + first_part).astype(bf16)

    gain_parts = jnp.stack([first_gain_grad, middle_gain_grad, final_gain_grad]).astype(bf16)
    sent = jnp.concatenate(
        [
            input_low.reshape(SHARD, N_CTX, LINES).transpose(1, 0, 2),
            jnp.pad(gain_parts.reshape(3, N_CTX, LINES).transpose(1, 0, 2), ((0, 0), (0, 13), (0, 0))),
            pair_low,
        ],
        axis=1,
    )
    arrived = lax.all_to_all(sent, CTX, 0, 0, tiled=True)
    kv_part = jnp.sum(arrived[:, 48:].astype(f32), axis=0)
    gain_sums = jnp.sum(arrived[:, SHARD : SHARD + 3].astype(f32), axis=0)
    place_grads = gather_tp(arrived[:, :SHARD].reshape(N_CTX * SHARD, LINES))
    embed_grad = add_up(all_ids, place_grads, vocab_here)

    kv_full = kv_part + core_swap(kv_part)
    kv_split, embed_grad = lax.optimization_barrier(
        (kv_full.T.reshape(N_X, 2, 16, 2 * HD), embed_grad)
    )
    kv_owned = swapped_x(jnp.where(cs == 0, kv_split[:, 0], kv_split[:, 1]), xs)
    key_value_grad = (
        kv_owned.reshape(KV_HEADS, 16, 2, HD).transpose(1, 2, 0, 3).reshape(16, KVW)
    )

    old_rows = jnp.concatenate(
        [attention_row_moment, feed_row_moment, vocab_row_moment, jnp.ones((9, LINES), f32)]
    )
    kv_old_columns = lax.dynamic_index_in_dim(
        key_value_column_moment.reshape(2, KV_HEADS, HD), xs, 1, keepdims=False
    ).reshape(-1)
    gap = jnp.ones((96,), f32)
    early_old = jnp.concatenate(
        [vocab_column_moment[0], gap, vocab_column_moment[1], gap, kv_old_columns]
    )[None]
    late_old = jnp.concatenate(
        [
            feed_column_moment[0],
            feed_column_moment[1],
            attention_column_moment[1],
            feed_column_moment[2],
            attention_column_moment[0],
            gap[:64],
        ]
    )[None]
    kv_old_line = lax.dynamic_update_slice_in_dim(
        jnp.zeros((1, LINES), f32), key_value_row_moment[None], tp_index * 16, 1
    )
    vocab_grad, line_parts, column_parts = early_figures(
        head_low, embed_grad, kv_full, gain_sums, kv_old_line
    )
    columns = lax.all_to_all(column_parts, CTX, 0, 0, tiled=True)
    lines = sum_tp(line_parts)
    gain_grad = lax.dynamic_slice_in_dim(lines[8:11], tp_index * 16, 16, 1)
    gain_second = moments(gain_moment.T, gain_grad * gain_grad, 1.0)
    gain_step = gain_grad * lax.rsqrt(gain_second)
    gain_squares = jnp.sum(gain_step * gain_step, axis=1)
    base = weight_sums + jnp.concatenate(
        [
            jnp.zeros((UG_LANE,), f32),
            gain_squares,
            loss_part.reshape(1),
            jnp.zeros((127 - LOSS_LANE,), f32),
        ]
    )
    early_rows, early_columns, vocab_unit, base = step_squares(
        early_squares_kernel,
        [(16, LINES), (1, EARLY_LANES), vocab_grad.shape, (1, 128)],
        vocab_grad,
        kv_full,
        lines,
        columns,
        old_rows,
        early_old,
        base,
    )
    feed_grad, attention_grad, line_parts, column_parts = late_figures(layer_low)
    columns = lax.all_to_all(column_parts, CTX, 0, 0, tiled=True)
    lines = sum_tp(line_parts)
    late_rows, late_columns, feed_unit, attention_unit, packed = step_squares(
        late_squares_kernel,
        [(8, LINES), (1, LATE_LANES), feed_grad.shape, attention_grad.shape, (128, 2, 128)],
        layer_low,
        lines,
        columns,
        old_rows,
        late_old,
        base,
        early_columns[:, 8192:],
    )
    gathered = lax.all_to_all(packed, CTX_TP, 0, 0, tiled=True)
    vocab_new, feed_new, attention_new, gain_new, figures = update(
        gathered[:, 0],
        tables,
        vocab_unit,
        feed_tables,
        feed_unit,
        attention_master,
        attention_unit,
        gain_master.T,
        gain_step,
    )
    token_loss = figures[2, 0]
    update_rms = figures[0, :11]
    kv_row_new = lax.dynamic_slice_in_dim(early_rows[7], tp_index * 16, 16, 0)
    kv_column_new = (
        gathered[0:8:2, 1].reshape(KV_HEADS, 2, HD).transpose(1, 0, 2).reshape(KVW)
    )
    kv_step = key_value_grad * lax.rsqrt(kv_row_new)[:, None] * lax.rsqrt(kv_column_new)[None]
    kv_new = key_value_master - figures[1, 7] * kv_step
    def columns_of(k):
        at, width = COLUMN_AT[k]
        return (early_columns if k > 4 else late_columns)[0, at : at + width]

    attention_columns = jnp.stack([columns_of(0), columns_of(1)])
    feed_columns = jnp.stack([columns_of(2), columns_of(3), columns_of(4)])
    return (
        token_loss,
        update_rms,
        attention_grad,
        late_rows[0:2],
        attention_columns,
        attention_new,
        feed_grad.transpose(0, 2, 1),
        late_rows[2:5],
        feed_columns,
        feed_new.transpose(0, 2, 1),
        vocab_grad.transpose(0, 2, 1),
        early_rows[5:7],
        columns_of(5),
        columns_of(6),
        vocab_new.transpose(0, 2, 1),
        key_value_grad,
        kv_row_new,
        kv_column_new,
        kv_new,
        gain_grad.T,
        gain_second.T,
        gain_new.T,
    )


def solution(mesh):
    finer = Mesh(mesh.devices.reshape(4, 4, 4, 2), ("ctx_0", "ctx_1", "tp_0", "tp_1"))
    in_specs = (
        P(CTX),
        P(CTX),
        P(CTX),
        P(),
        P(),
        P(None, CTX, TP),
        P(None, CTX, TP),
        P(None, CTX, TP),
        P(CTX_TP, None),
        P(CTX_TP, None),
        P(None, CTX),
        P(None, TP),
        P(None, CTX),
        P(None, TP),
        P(None, CTX),
        P(None, TP),
        P(CTX_TP),
        P(),
        P(CTX_TP, None),
    )
    out_specs = (
        P(),
        P(),
        P(None, CTX, TP),
        P(None, CTX),
        P(None, TP),
        P(None, CTX, TP),
        P(None, CTX, TP),
        P(None, CTX),
        P(None, TP),
        P(None, CTX, TP),
        P(None, CTX, TP),
        P(None, CTX),
        P(TP),
        P(TP),
        P(None, CTX, TP),
        P(CTX_TP, None),
        P(CTX_TP),
        P(),
        P(CTX_TP, None),
        P(CTX_TP, None),
        P(CTX_TP, None),
        P(CTX_TP, None),
    )
    return jax.shard_map(body, mesh=finer, in_specs=in_specs, out_specs=out_specs, check_vma=False)
```

```python
import functools
import math

import jax
import jax.numpy as jnp
from jax import lax
from jax.experimental import pallas as pl
from jax.experimental.pallas import tpu as pltpu
from jax.sharding import Mesh
from jax.sharding import PartitionSpec as P

D = 2048
HEADS = 32
KV_HEADS = 4
HD = 64
FF = 5632
VOCAB = 32000
ORIG_CTX = 2048
HQ = 2048
KVW = 512
TOKENS = 4096
TP = ("tp_0", "tp_1")
CTX = ("ctx_0", "ctx_1")
CTX_TP = ("ctx_0", "ctx_1", "tp_0", "tp_1")
N_CTX = 16
N_X = 4
N_TP = 8
SHARD = 32
LINES = 128
DOCS = 5

NORM_EPS = 1e-05
MOMENT_DECAY = 0.5
MOMENT_EPS = 1e-30
CLIP_LIMIT = 0.5
STEP_SCALE = 1.0
ROPE_BASE = 10000.0
YARN_SCALE = 4.0
YARN_ALPHA = 1.0
YARN_BETA = 32.0

bf16 = jnp.bfloat16
f32 = jnp.float32


def x_from(values, step):
    return lax.ppermute(values, "tp_0", [((i + step) % N_X, i) for i in range(N_X)])


def x_to(values, step):
    return lax.ppermute(values, "tp_0", [(i, (i + step) % N_X) for i in range(N_X)])


def core_swap(values):
    return lax.ppermute(values, "tp_1", [(0, 1), (1, 0)])


def turned(stack, start):
    return lax.dynamic_slice_in_dim(jnp.concatenate([stack, stack]), start, N_X, 0)


def to_absolute(stack, xs):
    return turned(stack, (N_X - xs) % N_X)


def gather_tp(shard):
    column = jnp.concatenate([shard] + [x_from(shard, d) for d in range(1, N_X)])
    return jnp.concatenate([column, core_swap(column)])


def scatter_tp(partial):
    half = partial[0] + core_swap(partial[1].astype(bf16)).astype(f32)
    low = half.astype(bf16)
    total = half[0]
    for d in range(1, N_X):
        total = total + x_to(low[d], d).astype(f32)
    return total


def both_cores(column, cs):
    other = core_swap(column)
    both = jnp.where(
        cs == 0, jnp.stack([column, other], axis=1), jnp.stack([other, column], axis=1)
    )
    return both.reshape(-1, *column.shape[2:])


def swapped_x(blocks, xs):
    ours = turned(blocks, xs)
    came = [ours[0]] + [x_to(ours[d], d) for d in range(1, N_X)]
    return to_absolute(jnp.stack([came[0], came[3], came[2], came[1]]), xs)


def partner(values, axis, mask):
    size = 2 if axis == "tp_1" else 4
    return lax.ppermute(values, axis, [(i, i ^ mask) for i in range(size)])


def sum_over_four(values, axis):
    return (values + partner(values, axis, 1)) + (
        partner(values, axis, 2) + partner(values, axis, 3)
    )


def sum_tp(values):
    return sum_over_four(values + partner(values, "tp_1", 1), "tp_0")


def sum_ctx(values):
    return sum_over_four(sum_over_four(values, "ctx_1"), "ctx_0")


def own_order(values, xs, cs):
    blocks = turned(values.reshape(N_X, 2, SHARD), xs)
    blocks = jnp.where(cs == 0, blocks, blocks[:, ::-1])
    return blocks.transpose(1, 0, 2)


def sent_to_all(array, axis):
    copies = jnp.broadcast_to(array, (lax.axis_size(axis), *array.shape))
    return lax.all_to_all(copies, axis, split_axis=0, concat_axis=0, tiled=True)


def rope_tables(positions):
    ladder = jnp.arange(HD // 2, dtype=f32)
    freqs = ROPE_BASE ** (-2.0 * ladder / HD)
    ratio = ORIG_CTX * freqs / (2.0 * math.pi)
    ramped = jnp.clip((ratio - YARN_ALPHA) / (YARN_BETA - YARN_ALPHA), 0.0, 1.0)
    inverse = freqs * (1.0 - ramped) / YARN_SCALE + freqs * ramped
    angles = inverse[:, None] * positions.astype(f32)[None, :]
    mscale = 0.1 * math.log(YARN_SCALE) + 1.0
    return (jnp.cos(angles) * mscale, jnp.sin(angles) * mscale)


def rotate_rows(values, cosine, sine):
    half = values.shape[0] // 2
    first, second = (values[:half], values[half:])
    return jnp.concatenate([first * cosine - second * sine, second * cosine + first * sine])


def rotate_lanes(values, cosine, sine):
    half = values.shape[1] // 2
    first, second = (values[:, :half], values[:, half:])
    return jnp.concatenate([first * cosine - second * sine, second * cosine + first * sine], axis=1)


def rms_norm(values, gain):
    return values * lax.rsqrt(jnp.mean(values * values, axis=-1, keepdims=True) + NORM_EPS) * gain


def contract_last(left, right):
    return lax.dot_general(left, right, (((1,), (1,)), ((), ())), preferred_element_type=f32)


def contract_first(left, right):
    return lax.dot_general(left, right, (((0,), (0,)), ((), ())), preferred_element_type=f32)


def contract(left, right):
    return jnp.dot(left, right, preferred_element_type=f32)


def combine_stats(former, latter):
    highest = jnp.maximum(former[0], latter[0])
    summed = former[1] * jnp.exp(former[0] - highest) + latter[1] * jnp.exp(latter[0] - highest)
    return jnp.stack([highest, summed, former[2] + latter[2]])


def contract_ft(weights, places):
    return lax.dot_general(weights, places, (((0,), (1,)), ((), ())), preferred_element_type=f32)


def contract_tf(features, weights):
    return lax.dot_general(features, weights, (((0,), (1,)), ((), ())), preferred_element_type=f32)


def heads_on_lanes(features):
    return jnp.concatenate([features[h * HD : (h + 1) * HD] for h in range(4)], axis=1)


def heads_on_rows(features):
    return jnp.concatenate(jnp.split(features, 4, axis=1))


VMEM_LIMIT = 50 * 1024 * 1024


GROUP = 4
KEYS = 128 * GROUP
STEPS = TOKENS // KEYS


def key_places(core_bit, spans):
    line = lax.broadcasted_iota(jnp.int32, (128, 1), 0)
    x = (spans[N_CTX] + line // SHARD) % N_X
    place = (x * 2 + (spans[N_CTX + 1] ^ core_bit)) * SHARD + line % SHARD
    return place >= 128, place % 128


def visible_keys(spans, places, step, own, start):
    lines = []
    for block in range(step * GROUP, (step + 1) * GROUP):
        span = spans[block % N_CTX]
        second, within = places[block // N_CTX]
        lines.append(jnp.where(second, (2 * N_CTX - 1 - span) * 128, span * 128) + within)
    at = jnp.concatenate(lines, axis=0)
    return (at >= start) & (at <= own)


def key_columns(kv_ref, step, at):
    return jnp.concatenate(
        [kv_ref[step * GROUP + i, at : at + HD] for i in range(GROUP)], axis=1
    )


def attend_kernel(spans, own_ref, q_ref, kv_ref, o_ref, total_ref, s_ref):
    q = q_ref[...]
    own, start = (own_ref[0:1], own_ref[1:2])
    places = [key_places(core_bit, spans) for core_bit in range(2)]
    top = None
    for step in range(STEPS):
        scores = contract_first(key_columns(kv_ref, step, 0), q)
        scores = jnp.where(visible_keys(spans, places, step, own, start), scores, -1e30)
        s_ref[step * KEYS : (step + 1) * KEYS] = scores
        highest = jnp.max(scores, axis=0, keepdims=True)
        top = highest if top is None else jnp.maximum(top, highest)
    total = jnp.zeros(top.shape, f32)
    for step in range(STEPS):
        powers = jnp.exp(s_ref[step * KEYS : (step + 1) * KEYS] - top)
        s_ref[step * KEYS : (step + 1) * KEYS] = powers
        total = total + jnp.sum(powers, axis=0, keepdims=True)
    share = 1.0 / total
    out = jnp.zeros(q.shape, f32)
    for step in range(STEPS):
        weights = (s_ref[step * KEYS : (step + 1) * KEYS] * share).astype(bf16)
        out = out + contract(key_columns(kv_ref, step, HD), weights)
    o_ref[...] = out.astype(bf16)
    total_ref[...] = top + jnp.log(total)


SPLIT = 2


def attend(spans, own, q, kv):
    lanes = q.shape[1] // SPLIT
    column = lambda rows: pl.BlockSpec((rows, lanes), lambda i: (0, i))
    return pl.pallas_call(
        attend_kernel,
        grid=(SPLIT,),
        in_specs=[
            pl.BlockSpec(memory_space=pltpu.SMEM),
            column(2),
            column(HD),
            pl.BlockSpec(kv.shape, lambda i: (0, 0, 0)),
        ],
        out_specs=[column(HD), column(1)],
        out_shape=[
            jax.ShapeDtypeStruct(q.shape, bf16),
            jax.ShapeDtypeStruct((1, q.shape[1]), f32),
        ],
        scratch_shapes=[pltpu.VMEM((TOKENS, lanes), f32)],
        compiler_params=pltpu.CompilerParams(vmem_limit_bytes=VMEM_LIMIT),
        cost_estimate=pl.CostEstimate(
            flops=16 * TOKENS * q.shape[1] * HD, bytes_accessed=2 << 20, transcendentals=0
        ),
    )(spans, own, q, kv)


def attend_back_kernel(
    spans, own_ref, q_ref, do_ref, total_ref, kv_ref, dq_ref, dkv_ref, p_ref, dp_ref
):
    q, do = (q_ref[...], do_ref[...])
    own, start = (own_ref[0:1], own_ref[1:2])
    total = total_ref[...]
    places = [key_places(core_bit, spans) for core_bit in range(2)]
    rowsum = jnp.zeros(total.shape, f32)
    for step in range(STEPS):
        scores = contract_first(key_columns(kv_ref, step, 0), q)
        scores = jnp.where(visible_keys(spans, places, step, own, start), scores, -1e30)
        probs = jnp.exp(scores - total)
        probs_grad = contract_first(key_columns(kv_ref, step, HD), do)
        p_ref[step * KEYS : (step + 1) * KEYS] = probs
        dp_ref[step * KEYS : (step + 1) * KEYS] = probs_grad
        rowsum = rowsum + jnp.sum(probs * probs_grad, axis=0, keepdims=True)

    @pl.when(pl.program_id(0) == 0)
    def _():
        dkv_ref[...] = jnp.zeros(dkv_ref.shape, f32)

    dq = jnp.zeros(q.shape, f32)
    for step in range(STEPS):
        rows = slice(step * KEYS, (step + 1) * KEYS)
        probs = p_ref[rows]
        score_grad = (probs * (dp_ref[rows] - rowsum)).astype(bf16)
        dkv_ref[rows] += jnp.concatenate(
            [contract_last(score_grad, q), contract_last(probs.astype(bf16), do)], axis=1
        )
        dq = dq + contract(key_columns(kv_ref, step, 0), score_grad)
    dq_ref[...] = dq * (1.0 / math.sqrt(HD))


def attend_back(spans, own, q, do, total, kv):
    lanes = q.shape[1] // SPLIT
    column = lambda rows: pl.BlockSpec((rows, lanes), lambda i: (0, i))
    return pl.pallas_call(
        attend_back_kernel,
        grid=(SPLIT,),
        in_specs=[
            pl.BlockSpec(memory_space=pltpu.SMEM),
            column(2),
            column(HD),
            column(HD),
            column(1),
            pl.BlockSpec(kv.shape, lambda i: (0, 0, 0)),
        ],
        out_specs=[column(HD), pl.BlockSpec((TOKENS, 2 * HD), lambda i: (0, 0))],
        out_shape=[
            jax.ShapeDtypeStruct(q.shape, f32),
            jax.ShapeDtypeStruct((TOKENS, 2 * HD), f32),
        ],
        scratch_shapes=[pltpu.VMEM((TOKENS, lanes), f32), pltpu.VMEM((TOKENS, lanes), f32)],
        compiler_params=pltpu.CompilerParams(vmem_limit_bytes=VMEM_LIMIT),
        cost_estimate=pl.CostEstimate(
            flops=40 * TOKENS * q.shape[1] * HD, bytes_accessed=4 << 20, transcendentals=0
        ),
    )(spans, own, q, do, total, kv)


def moments(old, sums, count):
    return MOMENT_DECAY * old + (1.0 - MOMENT_DECAY) * (sums / count + MOMENT_EPS)


def params():
    return pltpu.CompilerParams(vmem_limit_bytes=VMEM_LIMIT)


def whole(array):
    zeros = (0,) * array.ndim
    return pl.BlockSpec(array.shape, lambda *i: zeros)


def cost(flops, moved):
    return pl.CostEstimate(flops=flops, bytes_accessed=moved, transcendentals=0)


ID_STEP = 2048


def look_kernel(ids_ref, table_ref, out_ref, low_ref):
    @pl.when(pl.program_id(0) == 0)
    def _():
        low_ref[...] = table_ref[0].astype(bf16)

    width = low_ref.shape[0]
    ids = jnp.transpose(jnp.broadcast_to(ids_ref[...], (8, ID_STEP)))[:, :1]
    hits = ids == lax.broadcasted_iota(jnp.int32, (ID_STEP, width), 1)
    out_ref[...] = contract(jnp.where(hits, 1.0, 0.0).astype(bf16), low_ref[...]).astype(bf16)


def look_up(ids, tables):
    width, lines = tables.shape[1:]
    count = ids.shape[1]
    return pl.pallas_call(
        look_kernel,
        grid=(count // ID_STEP,),
        in_specs=[
            pl.BlockSpec((1, ID_STEP), lambda i: (0, i)),
            pl.BlockSpec((1, width, lines), lambda i: (1, 0, 0)),
        ],
        out_specs=pl.BlockSpec((ID_STEP, lines), lambda i: (i, 0)),
        out_shape=jax.ShapeDtypeStruct((count, lines), bf16),
        scratch_shapes=[pltpu.VMEM((width, lines), bf16)],
        compiler_params=params(),
        cost_estimate=cost(4 * count * width * lines, 4 * lines * width),
    )(ids, tables)


def add_kernel(ids_ref, grads_ref, out_ref):
    hits = lax.broadcasted_iota(jnp.int32, (out_ref.shape[0], ID_STEP), 0) == ids_ref[...]
    added = contract(jnp.where(hits, 1.0, 0.0).astype(bf16), grads_ref[...])

    @pl.when(pl.program_id(0) == 0)
    def _():
        out_ref[...] = added

    @pl.when(pl.program_id(0) > 0)
    def _():
        out_ref[...] += added


def add_up(ids, grads, width):
    count, lines = grads.shape
    return pl.pallas_call(
        add_kernel,
        grid=(count // ID_STEP,),
        in_specs=[
            pl.BlockSpec((1, ID_STEP), lambda i: (0, i)),
            pl.BlockSpec((ID_STEP, lines), lambda i: (i, 0)),
        ],
        out_specs=pl.BlockSpec((width, lines), lambda i: (0, 0)),
        out_shape=jax.ShapeDtypeStruct((width, lines), f32),
        compiler_params=params(),
        cost_estimate=cost(4 * count * width * lines, 4 * lines * width),
    )(ids, grads)


LOGIT_STEP = 800


def joined(ref):
    return jnp.concatenate([ref[k] for k in range(N_CTX)], axis=1)


def logits_kernel(c_ref, w_ref, target_ref, out_ref, stats_ref):
    step = pl.program_id(0)
    logits = contract_last(joined(w_ref), c_ref[...])
    out_ref[...] = logits
    row = lax.broadcasted_iota(jnp.int32, logits.shape, 0) + step * LOGIT_STEP
    here = jnp.max(logits, axis=0, keepdims=True)
    pick = jnp.sum(jnp.where(row == target_ref[...], logits, 0.0), axis=0, keepdims=True)

    @pl.when(step == 0)
    def _():
        stats_ref[...] = jnp.zeros(stats_ref.shape, f32)
        stats_ref[0:1] = here

    old = stats_ref[0:1]
    top = jnp.maximum(old, here)
    powers = jnp.sum(jnp.exp(logits - top), axis=0, keepdims=True)
    stats_ref[1:2] = stats_ref[1:2] * jnp.exp(old - top) + powers
    stats_ref[2:3] += pick
    stats_ref[0:1] = top


def logits_and_stats(c, head, targets):
    places, rows = c.shape
    width = head.shape[1]
    return pl.pallas_call(
        logits_kernel,
        grid=(width // LOGIT_STEP,),
        in_specs=[
            whole(c),
            pl.BlockSpec((N_CTX, LOGIT_STEP, 128), lambda i: (0, i, 0)),
            whole(targets),
        ],
        out_specs=[
            pl.BlockSpec((LOGIT_STEP, places), lambda i: (i, 0)),
            pl.BlockSpec((8, places), lambda i: (0, 0)),
        ],
        out_shape=[
            jax.ShapeDtypeStruct((width, places), f32),
            jax.ShapeDtypeStruct((8, places), f32),
        ],
        compiler_params=params(),
        cost_estimate=cost(2 * places * rows * width, 2 * rows * width),
    )(c, head, targets)


def head_grad_kernel(logits_ref, c_ref, place_ref, target_ref, dw_ref, low_ref):
    step = pl.program_id(0)
    logits = logits_ref[...]
    row = lax.broadcasted_iota(jnp.int32, logits.shape, 0) + step * LOGIT_STEP
    hit = row == target_ref[...]
    shares = jnp.exp(logits - place_ref[0:1]) - jnp.where(hit, 1.0, 0.0)
    low = (place_ref[1:2] * shares).astype(bf16)
    low_ref[...] = low
    grad = contract(low, c_ref[...]).astype(bf16)
    for k in range(N_CTX):
        dw_ref[k] = grad[:, k * 128 : (k + 1) * 128]


def head_grads(logits, c, place, targets):
    places, rows = c.shape
    width = logits.shape[0]
    block = pl.BlockSpec((LOGIT_STEP, places), lambda i: (i, 0))
    return pl.pallas_call(
        head_grad_kernel,
        grid=(width // LOGIT_STEP,),
        in_specs=[block, whole(c), whole(place), whole(targets)],
        out_specs=[pl.BlockSpec((N_CTX, LOGIT_STEP, 128), lambda i: (0, i, 0)), block],
        out_shape=[
            jax.ShapeDtypeStruct((N_CTX, width, 128), bf16),
            jax.ShapeDtypeStruct((width, places), bf16),
        ],
        compiler_params=params(),
        cost_estimate=cost(2 * places * rows * width, 2 * rows * width),
    )(logits, c, place, targets)


def place_grad_kernel(low_ref, w_ref, out_ref):
    part = contract_first(low_ref[...], joined(w_ref))

    @pl.when(pl.program_id(0) == 0)
    def _():
        out_ref[...] = part

    @pl.when(pl.program_id(0) > 0)
    def _():
        out_ref[...] += part


def place_grads_of(low, head):
    width, places = low.shape
    return pl.pallas_call(
        place_grad_kernel,
        grid=(width // LOGIT_STEP,),
        in_specs=[
            pl.BlockSpec((LOGIT_STEP, places), lambda i: (i, 0)),
            pl.BlockSpec((N_CTX, LOGIT_STEP, 128), lambda i: (0, i, 0)),
        ],
        out_specs=pl.BlockSpec((places, D), lambda i: (0, 0)),
        out_shape=jax.ShapeDtypeStruct((places, D), f32),
        compiler_params=params(),
        cost_estimate=cost(2 * places * D * width, 2 * D * width),
    )(low, head)


TURNED = (1, 3)


def products_kernel(count, offsets, *refs):
    lefts, rights = (refs[:count], refs[count : 2 * count])
    out_ref, turned_ref = refs[2 * count :]

    @pl.when(pl.program_id(0) == 0)
    def _():
        for k, (right, (at, width)) in enumerate(zip(rights, offsets)):
            values = right[...]
            turned_ref[at : at + width] = values if k in TURNED else jnp.transpose(values)

    for left, (at, width) in zip(lefts, offsets):
        grad = contract(turned_ref[at : at + width], left[...]).astype(bf16)
        for k in range(2):
            out_ref[k, at : at + width] = grad[:, k * 128 : (k + 1) * 128]


def row_products(lefts, rights):
    places, rows = lefts[0].shape
    offsets, at = ([], 0)
    for k, right in enumerate(rights):
        width = right.shape[0 if k in TURNED else 1]
        offsets.append((at, width))
        at += width
    return pl.pallas_call(
        functools.partial(products_kernel, len(lefts), tuple(offsets)),
        grid=(N_CTX // 2,),
        in_specs=[pl.BlockSpec((places, 256), lambda i: (0, i)) for _ in lefts]
        + [whole(right) for right in rights],
        out_specs=pl.BlockSpec((2, at, 128), lambda i: (i, 0, 0)),
        out_shape=jax.ShapeDtypeStruct((N_CTX, at, rows // N_CTX), bf16),
        scratch_shapes=[pltpu.VMEM((at, places), bf16)],
        compiler_params=params(),
        cost_estimate=cost(2 * places * rows * at, 2 * rows * at),
    )(*lefts, *rights)


MATRICES = 8
WIDTHS = (HQ, HQ, FF, FF, FF, VOCAB, VOCAB, KVW)
EARLY_LANES = 8320
LATE_LANES = 2688
COLUMN_AT = {5: (0, 4000), 6: (4096, 4000), 7: (8192, 128)}
COLUMN_AT.update({2: (0, 704), 3: (704, 704), 1: (1408, 256), 4: (1664, 704), 0: (2368, 256)})
S_LANE, T_LANE, OLD_LANE, W_LANE, WG_LANE, UG_LANE, LOSS_LANE = (0, 8, 16, 24, 32, 35, 38)


def lane_is(shape, lane):
    return lax.broadcasted_iota(jnp.int32, shape, 1) == lane


def line_sum(values):
    return jnp.sum(values, axis=0, keepdims=True)


def total_of(values):
    return jnp.sum(line_sum(values), axis=1, keepdims=True)


def column_sums(squares):
    ones = jnp.ones((8, squares.shape[1]), f32)
    return lax.dot_general(
        ones,
        squares,
        (((1,), (1,)), ((), ())),
        precision=lax.Precision.HIGHEST,
        preferred_element_type=f32,
    )


def weights_kernel(tables_ref, feed_ref, attention_ref, kv_master_ref, gain_ref, scalars_ref):
    scalars = jnp.zeros(scalars_ref.shape, f32)
    for number, weights in (
        (0, attention_ref[0]),
        (1, attention_ref[1]),
        (2, feed_ref[0]),
        (3, feed_ref[1]),
        (4, feed_ref[2]),
        (5, tables_ref[0]),
        (6, tables_ref[1]),
        (7, kv_master_ref[...]),
        (8, gain_ref[0:1]),
        (9, gain_ref[1:2]),
        (10, gain_ref[2:3]),
    ):
        scalars += jnp.where(
            lane_is(scalars.shape, W_LANE + number), total_of(weights * weights), 0.0
        )
    scalars_ref[...] = scalars


def weight_squares(*masters):
    return pl.pallas_call(
        weights_kernel,
        out_shape=jax.ShapeDtypeStruct((1, 128), f32),
        compiler_params=params(),
        cost_estimate=cost(0, 6 << 20),
    )(*masters)


def early_kernel(
    head_ref, embed_ref, kv_ref, gains_ref, kv_old_ref, vocab_grad_ref, lines_ref, columns_ref
):
    lines_ref[...] = jnp.zeros(lines_ref.shape, f32)
    lines_ref[8:11] = gains_ref[...]
    lines_ref[11:12] = kv_old_ref[...]
    sums = []
    for number, ref in ((5, head_ref), (6, embed_ref), (7, kv_ref)):
        grad = ref[...].astype(f32)
        if number in (5, 6):
            vocab_grad_ref[number - 5] = grad
        squares = grad * grad
        lines_ref[number : number + 1] = (0.5 if number == 7 else 1.0) * line_sum(squares)
        sums.append(column_sums(squares)[:1])
        if number in (5, 6):
            sums.append(jnp.zeros((1, 96), f32))
    columns_ref[...] = jnp.broadcast_to(
        jnp.concatenate(sums, axis=1)[None], columns_ref.shape
    )


def early_figures(*arrays):
    shapes = ((2, *arrays[1].shape), (16, 128), (N_CTX, 1, EARLY_LANES))
    return pl.pallas_call(
        early_kernel,
        out_shape=[jax.ShapeDtypeStruct(shape, f32) for shape in shapes],
        compiler_params=params(),
        cost_estimate=cost(0, 12 << 20),
    )(*arrays)


def late_kernel(layer_ref, feed_grad_ref, attention_grad_ref, lines_ref, columns_ref):
    layer = layer_ref[...].astype(f32)
    squares = layer * layer
    sums = jnp.concatenate(
        [column_sums(squares)[:1], jnp.zeros((1, LATE_LANES - layer.shape[0]), f32)], axis=1
    )
    columns_ref[...] = jnp.broadcast_to(sums[None], columns_ref.shape)
    lines_ref[...] = jnp.zeros(lines_ref.shape, f32)
    for number in range(5):
        at, width = COLUMN_AT[number]
        lines_ref[number : number + 1] = line_sum(squares[at : at + width])
        if number > 1:
            feed_grad_ref[number - 2] = layer[at : at + width]
    attention_grad_ref[0] = jnp.transpose(layer[2368:2624])
    attention_grad_ref[1] = jnp.transpose(layer[1408:1664])


def late_figures(layer):
    shapes = ((3, 704, 128), (2, 128, 256), (8, 128), (N_CTX, 1, LATE_LANES))
    return pl.pallas_call(
        late_kernel,
        out_shape=[jax.ShapeDtypeStruct(shape, f32) for shape in shapes],
        compiler_params=params(),
        cost_estimate=cost(0, 4 << 20),
    )(layer)


def per_column(figures, number):
    at, width = COLUMN_AT[number]
    return figures[at : at + width, :1]


def on_rows(columns):
    spare = 8 - columns.shape[0]
    return jnp.transpose(
        jnp.concatenate([columns, jnp.ones((spare, columns.shape[1]), f32)], axis=0)
    )


def squares_of(sources, lines, old, columns, old_columns, scalars, row_ref, column_ref):
    number = lax.broadcasted_iota(jnp.int32, lines.shape, 0)
    widths = jnp.full(lines.shape, 1.0, f32)
    for k, width in enumerate(WIDTHS):
        widths = jnp.where(number == k, float(width), widths)
    row_new = moments(old, lines / widths, 1.0)
    row_ref[...] = row_new
    column_new = moments(old_columns, jnp.sum(columns, axis=0), float(D))
    column_ref[...] = column_new
    row_scale = lax.rsqrt(row_new)
    column_scale = on_rows(lax.rsqrt(column_new))
    had = jnp.sum(old, axis=1, keepdims=True) * (1.0 / N_TP)
    got = jnp.sum(lines, axis=1, keepdims=True) * (1.0 / N_TP)
    for k, grad, keep in sources:
        unit = grad * row_scale[k : k + 1] * per_column(column_scale, k)
        if keep is not None:
            keep[0][keep[1]] = jnp.transpose(unit) if k < 2 else unit
        part = total_of(unit * unit) * (0.5 if k == 7 else 1.0)
        scalars += jnp.where(lane_is(scalars.shape, S_LANE + k), part, 0.0)
        scalars += jnp.where(lane_is(scalars.shape, T_LANE + k), got[k : k + 1], 0.0)
        scalars += jnp.where(lane_is(scalars.shape, OLD_LANE + k), had[k : k + 1], 0.0)
    return scalars


def early_squares_kernel(
    vocab_ref, kv_ref, lines_ref, columns_ref, old_ref, old_columns_ref, base_ref,
    row_ref, column_ref, unit_ref, scalars_ref,
):
    lines = lines_ref[...]
    number = lax.broadcasted_iota(jnp.int32, lines.shape, 0)
    old = jnp.where(number == 7, lines_ref[11:12], old_ref[...])
    sources = (
        (5, vocab_ref[0], (unit_ref, 0)),
        (6, vocab_ref[1], (unit_ref, 1)),
        (7, kv_ref[...], None),
    )
    scalars_ref[...] = squares_of(
        sources, lines, old, columns_ref[...], old_columns_ref[...], base_ref[...],
        row_ref, column_ref,
    )


def late_squares_kernel(
    layer_ref, lines_ref, columns_ref, old_ref, old_columns_ref, base_ref, kv_columns_ref,
    row_ref, column_ref, feed_unit_ref, attention_unit_ref, packed_ref,
):
    sources = []
    for number in range(5):
        at, width = COLUMN_AT[number]
        keep = (attention_unit_ref, number) if number < 2 else (feed_unit_ref, number - 2)
        sources.append((number, layer_ref[at : at + width].astype(f32), keep))
    scalars = squares_of(
        sources, lines_ref[...], old_ref[0:8], columns_ref[...], old_columns_ref[...],
        base_ref[...], row_ref, column_ref,
    )
    packed = jnp.concatenate([scalars, kv_columns_ref[...]], axis=0)
    packed_ref[...] = jnp.broadcast_to(packed[None], packed_ref.shape)


def step_squares(kernel, shapes, *arrays):
    return pl.pallas_call(
        kernel,
        out_shape=[jax.ShapeDtypeStruct(shape, f32) for shape in shapes],
        compiler_params=params(),
        cost_estimate=cost(0, 12 << 20),
    )(*arrays)


UPDATE_STEP = 800


def update_kernel(
    all_ref, vocab_ref, vocab_unit_ref, feed_ref, feed_unit_ref, attention_ref,
    attention_unit_ref, gain_ref, gain_step_ref,
    vocab_new_ref, feed_new_ref, attention_new_ref, gain_new_ref, figures_ref,
):
    sums = jnp.sum(all_ref[...], axis=0, keepdims=True)
    sums = jnp.broadcast_to(sums, (8, 128))

    def lanes_from(at):
        return pltpu.roll(sums, (128 - at) % 128, 1)[0:1]

    lane = lax.broadcasted_iota(jnp.int32, (1, 128), 1)
    counts = jnp.full((1, 128), float(D), f32)
    for k, width in enumerate(WIDTHS):
        counts = jnp.where(lane == k, float(D * width), counts)
    mean = MOMENT_DECAY * lanes_from(OLD_LANE) / D + (1.0 - MOMENT_DECAY) * (
        lanes_from(T_LANE) / counts + MOMENT_EPS
    )
    mean = jnp.where(lane < MATRICES, mean, 1.0)
    rms = jnp.sqrt(mean * lanes_from(S_LANE) / counts)
    factor = (
        STEP_SCALE
        * jnp.sqrt(lanes_from(W_LANE) / counts)
        / jnp.maximum(1.0, rms / CLIP_LIMIT)
        * jnp.sqrt(mean)
    )

    @pl.when(pl.program_id(0) == 0)
    def _():
        for k in range(2):
            attention_new_ref[k] = attention_ref[k] - attention_unit_ref[k] * factor[:, k : k + 1]
        for k in range(3):
            feed_new_ref[k] = feed_ref[k] - feed_unit_ref[k] * factor[:, 2 + k : 3 + k]
        gain_rms = jnp.sqrt(lanes_from(UG_LANE) / D)
        gain_factor = (
            STEP_SCALE
            * jnp.sqrt(lanes_from(WG_LANE) / D)
            / jnp.maximum(1.0, gain_rms / CLIP_LIMIT)
        )
        for k in range(3):
            gain_new_ref[k : k + 1] = (
                gain_ref[k : k + 1] - gain_factor[:, k : k + 1] * gain_step_ref[k : k + 1]
            )
        after = pltpu.roll(jnp.broadcast_to(gain_rms, (8, 128)), MATRICES, 1)[0:1]
        figures_ref[0:1] = jnp.where(lane < MATRICES, rms, after)
        figures_ref[1:2] = factor
        figures_ref[2:3] = lanes_from(LOSS_LANE)
        figures_ref[3:8] = jnp.zeros((5, 128), f32)

    for k in range(2):
        vocab_new_ref[k] = vocab_ref[k] - vocab_unit_ref[k] * factor[:, 5 + k : 6 + k]


def update(gathered, vocab, vocab_unit, feed, feed_unit, attention, attention_unit, gain, gain_step):
    stack = pl.BlockSpec((2, UPDATE_STEP, vocab.shape[2]), lambda i: (0, i, 0))
    others = (feed, feed_unit, attention, attention_unit, gain, gain_step)
    outs = (vocab, feed, attention, gain)
    return pl.pallas_call(
        update_kernel,
        grid=(vocab.shape[1] // UPDATE_STEP,),
        in_specs=[whole(gathered), stack, stack] + [whole(a) for a in others],
        out_specs=[stack]
        + [whole(a) for a in outs[1:]]
        + [pl.BlockSpec((8, 128), lambda i: (0, 0))],
        out_shape=[jax.ShapeDtypeStruct(a.shape, f32) for a in outs]
        + [jax.ShapeDtypeStruct((8, 128), f32)],
        compiler_params=params(),
        cost_estimate=cost(0, 24 << 20),
    )(gathered, vocab, vocab_unit, *others)


def body(
    token_ids,
    target_ids,
    loss_mask,
    segment_ids,
    span_pairs,
    attention_master,
    feed_master,
    vocab_master,
    key_value_master,
    gain_master,
    attention_row_moment,
    attention_column_moment,
    feed_row_moment,
    feed_column_moment,
    vocab_row_moment,
    vocab_column_moment,
    key_value_row_moment,
    key_value_column_moment,
    gain_moment,
):
    ctx_index = lax.axis_index(CTX)
    xs = lax.axis_index("tp_0")
    cs = lax.axis_index("tp_1")
    tp_index = xs * 2 + cs
    vocab_here = vocab_master.shape[2]
    ff_here = feed_master.shape[2]
    first_id = tp_index * vocab_here

    attention_low = attention_master.astype(bf16)
    feed_low = feed_master.astype(bf16)
    layer_all = lax.all_gather(
        jnp.concatenate(
            [
                attention_low[0].T,
                attention_low[1].T,
                feed_low[0].T,
                feed_low[1].T,
                feed_low[2].T,
            ]
        )[None],
        CTX,
        axis=0,
        tiled=True,
    )
    head = lax.all_gather(vocab_master[0].astype(bf16).T[None], CTX, axis=0, tiled=True)

    def on_lanes(at, width):
        return layer_all[:, at : at + width].transpose(1, 0, 2).reshape(width, D)

    w_query = on_lanes(0, 256)
    w_out = on_lanes(256, 256)
    gate_up = on_lanes(512, 2 * ff_here)
    down = on_lanes(512 + 2 * ff_here, ff_here)

    kv_low = key_value_master.astype(bf16).reshape(16, 2, KV_HEADS, HD).transpose(2, 0, 1, 3)
    gain_low = jnp.pad(gain_master.astype(bf16), ((0, 0), (0, 125)))
    blocks = jnp.concatenate(
        [
            kv_low.reshape(KV_HEADS, 16, 2 * HD),
            jnp.broadcast_to(gain_low, (KV_HEADS, *gain_low.shape)),
        ],
        axis=2,
    )
    ids_here = own_order(token_ids, xs, cs).reshape(1, 256)
    line_block = both_cores(swapped_x(blocks, xs), cs)
    half = LINES // 2
    early = sent_to_all(
        jnp.concatenate(
            [
                lax.dynamic_slice_in_dim(line_block[:, : 2 * HD], cs * half, half, 0),
                line_block[:, 2 * HD : 2 * HD + 3].T,
                (ids_here // 256).astype(bf16).reshape(2, 128),
                (ids_here % 256).astype(bf16).reshape(2, 128),
                jnp.zeros((9, 128), bf16),
            ]
        ),
        CTX,
    )
    own_half = early[:, :half]
    other_half = core_swap(own_half)
    w_pair = jnp.where(
        cs == 0,
        jnp.concatenate([own_half, other_half], axis=1),
        jnp.concatenate([other_half, own_half], axis=1),
    ).reshape(D, 2 * HD)
    gains = early[:, half : half + 3].astype(f32).transpose(1, 0, 2).reshape(3, D)
    parts = early[:, half + 3 : half + 7].astype(jnp.int32).reshape(N_CTX, 2, 256)
    all_ids = parts[:, 0] * 256 + parts[:, 1]
    all_ids = all_ids.reshape(N_CTX, 8, SHARD).transpose(1, 0, 2).reshape(1, TOKENS) - first_id

    order = (
        ((xs + jnp.arange(N_X, dtype=jnp.int32)) % N_X * 2)[None, :]
        + (cs ^ jnp.arange(2, dtype=jnp.int32))[:, None]
    )[:, :, None] * SHARD + jnp.arange(SHARD, dtype=jnp.int32)
    second_span = order >= 128
    within = order % 128
    own_pair = lax.dynamic_slice_in_dim(span_pairs, ctx_index, 1)[0]
    last_span = 2 * N_CTX - 1
    own_pos = (jnp.where(second_span, last_span - own_pair, own_pair) * 128 + within).reshape(-1)
    doc_start = jnp.zeros_like(own_pos)
    for k in range(1, DOCS):
        start = jnp.sum((segment_ids < k).astype(jnp.int32))
        doc_start = jnp.where(own_pos >= start, start, doc_start)
    cosine, sine = rope_tables(own_pos - doc_start)
    cosine_4, sine_4 = (jnp.tile(cosine, (1, 4)), jnp.tile(sine, (1, 4)))
    own_places = jnp.tile(jnp.stack([own_pos, doc_start]), (1, 4))
    spans = jnp.concatenate([span_pairs, jnp.stack([xs, cs]).astype(jnp.int32)])

    tables = vocab_master.transpose(0, 2, 1)
    looked = look_up(all_ids, tables).reshape(2, N_X, N_CTX, SHARD, LINES)
    half = looked[0] + core_swap(looked[1])
    mine = half[0]
    for d in range(1, N_X):
        mine = mine + x_to(half[d], d)
    rows_in = lax.all_to_all(mine, CTX, 0, 0, tiled=True)
    stream_in = rows_in.transpose(1, 0, 2).reshape(SHARD, D).astype(f32)

    normed_low = gather_tp(rms_norm(stream_in, gains[0]).astype(bf16))
    normed_half = normed_low[:128]
    keyval_linear = contract_ft(w_pair, normed_half)
    own_keyvals = jnp.concatenate(
        [rotate_rows(keyval_linear[:HD], cosine[:, :128], sine[:, :128]), keyval_linear[HD:]]
    ).astype(bf16)
    half_keyvals = sent_to_all(own_keyvals, CTX)
    row_keyvals = jnp.concatenate([half_keyvals, core_swap(half_keyvals)])
    query_linear = heads_on_lanes(contract_last(w_query, normed_low))
    queries = rotate_rows(query_linear, cosine_4, sine_4).astype(bf16) * jnp.asarray(
        1.0 / math.sqrt(HD), bf16
    )
    attended, log_total = attend(spans, own_places, queries, row_keyvals)
    attended_rows = heads_on_rows(attended)
    stream_mid = stream_in + scatter_tp(
        contract_first(attended_rows, w_out).reshape(2, N_X, SHARD, D)
    )

    inner_low = gather_tp(rms_norm(stream_mid, gains[1]).astype(bf16))
    both = contract_last(inner_low, gate_up)
    gate, upward = (both[:, :ff_here], both[:, ff_here:])
    sigmoid_gate = jax.nn.sigmoid(gate)
    silu_gate = gate * sigmoid_gate
    hidden_low = (silu_gate * upward).astype(bf16)
    stream_out = stream_mid + scatter_tp(
        contract(hidden_low, down).reshape(2, N_X, SHARD, D)
    )

    feed_tables = feed_master.transpose(0, 2, 1)
    masters = (tables, feed_tables, attention_master, key_value_master, gain_master.T)
    masters, inner_low = lax.optimization_barrier((masters, inner_low))
    weight_sums = weight_squares(*masters)
    finals_low = gather_tp(rms_norm(stream_out, gains[2]).astype(bf16))
    weight_sums, finals_low = lax.optimization_barrier((weight_sums, finals_low))
    local_targets = own_order(target_ids, xs, cs).reshape(1, -1) - first_id
    logits, stats = logits_and_stats(finals_low, head, local_targets)
    stats = stats[:3].reshape(3, 2, N_X, SHARD)
    stats = combine_stats(stats, core_swap(stats)[:, ::-1])
    others = [jnp.roll(x_from(stats, d), d, axis=2) for d in range(1, N_X)]
    stats = combine_stats(combine_stats(stats, others[0]), combine_stats(others[1], others[2]))
    stats = stats.reshape(3, -1)
    vocab_total = stats[0] + jnp.log(stats[1])
    keep = own_order(loss_mask, xs, cs).reshape(-1).astype(f32)
    loss_part = jnp.sum((keep * (vocab_total - stats[2]))[:SHARD]) / TOKENS

    place = jnp.stack([vocab_total, keep / TOKENS])
    head_low, dlogits_low = head_grads(logits, finals_low, place, local_targets)
    head_low = lax.psum_scatter(head_low, CTX, scatter_dimension=0, tiled=True)[0]
    final_part = place_grads_of(dlogits_low, head)
    final_grad = scatter_tp(final_part.reshape(2, N_X, SHARD, D))
    out_grad, final_gain_grad = jax.vjp(rms_norm, stream_out, gains[2])[1](final_grad)
    branch_low = gather_tp(out_grad.astype(bf16))
    hidden_grad = contract_last(branch_low, down)
    gate_grad_low = (
        hidden_grad * upward * sigmoid_gate * (1.0 + gate * (1.0 - sigmoid_gate))
    ).astype(bf16)
    upward_grad_low = (hidden_grad * silu_gate).astype(bf16)
    both_grad_low = jnp.concatenate([gate_grad_low, upward_grad_low], axis=1)
    inner_grad = scatter_tp(contract(both_grad_low, gate_up).reshape(2, N_X, SHARD, D))
    mid_part, middle_gain_grad = jax.vjp(rms_norm, stream_mid, gains[1])[1](inner_grad)
    mid_grad = out_grad + mid_part
    attend_low = gather_tp(mid_grad.astype(bf16))
    attended_grad = heads_on_lanes(contract_last(w_out, attend_low).astype(bf16))
    dq, pair_grads = attend_back(
        spans, own_places, queries, attended_grad, log_total, row_keyvals
    )
    pair_grads = pair_grads.reshape(2, N_CTX, 128, 2 * HD)
    half_grads = (pair_grads[0] + core_swap(pair_grads[1].astype(bf16)).astype(f32)).astype(bf16)
    query_linear_low = heads_on_rows(rotate_rows(dq, cosine_4, -sine_4).astype(bf16))
    half_grads, both_low = lax.optimization_barrier((half_grads, both_grad_low))
    came = lax.all_to_all(half_grads, CTX, 0, 0, tiled=True)
    layer_low = row_products(
        [inner_low, attend_low, branch_low, normed_low],
        [both_low, attended_rows, hidden_low, query_linear_low],
    )
    own_grads = jnp.sum(came.astype(f32), axis=0)
    keyval_low = jnp.concatenate(
        [
            rotate_lanes(own_grads[:, :HD], cosine[:, :128].T, -sine[:, :128].T),
            own_grads[:, HD:],
        ],
        axis=1,
    ).astype(bf16)
    normed_part = contract_first(query_linear_low, w_query).reshape(2, 128, D)
    normed_part = jnp.stack([normed_part[0] + contract_last(keyval_low, w_pair), normed_part[1]])
    layer_low, head_low, normed_part = lax.optimization_barrier((layer_low, head_low, normed_part))
    layer_low = lax.psum_scatter(layer_low, CTX, scatter_dimension=0, tiled=True)[0]
    normed_grad = scatter_tp(normed_part.reshape(2, N_X, SHARD, D))
    pair_low = contract_first(keyval_low, normed_half).astype(bf16)
    pair_low = pair_low.reshape(2 * HD, N_CTX, LINES).transpose(1, 0, 2)
    first_part, first_gain_grad = jax.vjp(rms_norm, stream_in, gains[0])[1](normed_grad)
    input_low = (mid_grad + first_part).astype(bf16)

    gain_parts = jnp.stack([first_gain_grad, middle_gain_grad, final_gain_grad]).astype(bf16)
    sent = jnp.concatenate(
        [
            input_low.reshape(SHARD, N_CTX, LINES).transpose(1, 0, 2),
            jnp.pad(gain_parts.reshape(3, N_CTX, LINES).transpose(1, 0, 2), ((0, 0), (0, 13), (0, 0))),
            pair_low,
        ],
        axis=1,
    )
    arrived = lax.all_to_all(sent, CTX, 0, 0, tiled=True)
    kv_part = jnp.sum(arrived[:, 48:].astype(f32), axis=0)
    gain_sums = jnp.sum(arrived[:, SHARD : SHARD + 3].astype(f32), axis=0)
    place_grads = gather_tp(arrived[:, :SHARD].reshape(N_CTX * SHARD, LINES))
    embed_grad = add_up(all_ids, place_grads, vocab_here)

    kv_full = kv_part + core_swap(kv_part)
    kv_split, embed_grad = lax.optimization_barrier(
        (kv_full.T.reshape(N_X, 2, 16, 2 * HD), embed_grad)
    )
    kv_owned = swapped_x(jnp.where(cs == 0, kv_split[:, 0], kv_split[:, 1]), xs)
    key_value_grad = (
        kv_owned.reshape(KV_HEADS, 16, 2, HD).transpose(1, 2, 0, 3).reshape(16, KVW)
    )

    old_rows = jnp.concatenate(
        [attention_row_moment, feed_row_moment, vocab_row_moment, jnp.ones((9, LINES), f32)]
    )
    kv_old_columns = lax.dynamic_index_in_dim(
        key_value_column_moment.reshape(2, KV_HEADS, HD), xs, 1, keepdims=False
    ).reshape(-1)
    gap = jnp.ones((96,), f32)
    early_old = jnp.concatenate(
        [vocab_column_moment[0], gap, vocab_column_moment[1], gap, kv_old_columns]
    )[None]
    late_old = jnp.concatenate(
        [
            feed_column_moment[0],
            feed_column_moment[1],
            attention_column_moment[1],
            feed_column_moment[2],
            attention_column_moment[0],
            gap[:64],
        ]
    )[None]
    kv_old_line = lax.dynamic_update_slice_in_dim(
        jnp.zeros((1, LINES), f32), key_value_row_moment[None], tp_index * 16, 1
    )
    vocab_grad, line_parts, column_parts = early_figures(
        head_low, embed_grad, kv_full, gain_sums, kv_old_line
    )
    columns = lax.all_to_all(column_parts, CTX, 0, 0, tiled=True)
    lines = sum_tp(line_parts)
    gain_grad = lax.dynamic_slice_in_dim(lines[8:11], tp_index * 16, 16, 1)
    gain_second = moments(gain_moment.T, gain_grad * gain_grad, 1.0)
    gain_step = gain_grad * lax.rsqrt(gain_second)
    gain_squares = jnp.sum(gain_step * gain_step, axis=1)
    base = weight_sums + jnp.concatenate(
        [
            jnp.zeros((UG_LANE,), f32),
            gain_squares,
            loss_part.reshape(1),
            jnp.zeros((127 - LOSS_LANE,), f32),
        ]
    )
    early_rows, early_columns, vocab_unit, base = step_squares(
        early_squares_kernel,
        [(16, LINES), (1, EARLY_LANES), vocab_grad.shape, (1, 128)],
        vocab_grad,
        kv_full,
        lines,
        columns,
        old_rows,
        early_old,
        base,
    )
    feed_grad, attention_grad, line_parts, column_parts = late_figures(layer_low)
    columns = lax.all_to_all(column_parts, CTX, 0, 0, tiled=True)
    lines = sum_tp(line_parts)
    late_rows, late_columns, feed_unit, attention_unit, packed = step_squares(
        late_squares_kernel,
        [(8, LINES), (1, LATE_LANES), feed_grad.shape, attention_grad.shape, (128, 2, 128)],
        layer_low,
        lines,
        columns,
        old_rows,
        late_old,
        base,
        early_columns[:, 8192:],
    )
    gathered = lax.all_to_all(packed, CTX_TP, 0, 0, tiled=True)
    vocab_new, feed_new, attention_new, gain_new, figures = update(
        gathered[:, 0],
        tables,
        vocab_unit,
        feed_tables,
        feed_unit,
        attention_master,
        attention_unit,
        gain_master.T,
        gain_step,
    )
    token_loss = figures[2, 0]
    update_rms = figures[0, :11]
    kv_row_new = lax.dynamic_slice_in_dim(early_rows[7], tp_index * 16, 16, 0)
    kv_column_new = (
        gathered[0:8:2, 1].reshape(KV_HEADS, 2, HD).transpose(1, 0, 2).reshape(KVW)
    )
    kv_step = key_value_grad * lax.rsqrt(kv_row_new)[:, None] * lax.rsqrt(kv_column_new)[None]
    kv_new = key_value_master - figures[1, 7] * kv_step
    def columns_of(k):
        at, width = COLUMN_AT[k]
        return (early_columns if k > 4 else late_columns)[0, at : at + width]

    attention_columns = jnp.stack([columns_of(0), columns_of(1)])
    feed_columns = jnp.stack([columns_of(2), columns_of(3), columns_of(4)])
    return (
        token_loss,
        update_rms,
        attention_grad,
        late_rows[0:2],
        attention_columns,
        attention_new,
        feed_grad.transpose(0, 2, 1),
        late_rows[2:5],
        feed_columns,
        feed_new.transpose(0, 2, 1),
        vocab_grad.transpose(0, 2, 1),
        early_rows[5:7],
        columns_of(5),
        columns_of(6),
        vocab_new.transpose(0, 2, 1),
        key_value_grad,
        kv_row_new,
        kv_column_new,
        kv_new,
        gain_grad.T,
        gain_second.T,
        gain_new.T,
    )


def solution(mesh):
    finer = Mesh(mesh.devices.reshape(4, 4, 4, 2), ("ctx_0", "ctx_1", "tp_0", "tp_1"))
    in_specs = (
        P(CTX),
        P(CTX),
        P(CTX),
        P(),
        P(),
        P(None, CTX, TP),
        P(None, CTX, TP),
        P(None, CTX, TP),
        P(CTX_TP, None),
        P(CTX_TP, None),
        P(None, CTX),
        P(None, TP),
        P(None, CTX),
        P(None, TP),
        P(None, CTX),
        P(None, TP),
        P(CTX_TP),
        P(),
        P(CTX_TP, None),
    )
    out_specs = (
        P(),
        P(),
        P(None, CTX, TP),
        P(None, CTX),
        P(None, TP),
        P(None, CTX, TP),
        P(None, CTX, TP),
        P(None, CTX),
        P(None, TP),
        P(None, CTX, TP),
        P(None, CTX, TP),
        P(None, CTX),
        P(TP),
        P(TP),
        P(None, CTX, TP),
        P(CTX_TP, None),
        P(CTX_TP),
        P(),
        P(CTX_TP, None),
        P(CTX_TP, None),
        P(CTX_TP, None),
        P(CTX_TP, None),
    )
    return jax.shard_map(body, mesh=finer, in_specs=in_specs, out_specs=out_specs, check_vma=False)
```

```python
import functools
import math

import jax
import jax.numpy as jnp
from jax import lax
from jax.experimental import pallas as pl
from jax.experimental.pallas import tpu as pltpu
from jax.sharding import Mesh
from jax.sharding import PartitionSpec as P

D = 2048
HEADS = 32
KV_HEADS = 4
HD = 64
FF = 5632
VOCAB = 32000
ORIG_CTX = 2048
HQ = 2048
KVW = 512
TOKENS = 4096
TP = ("tp_0", "tp_1")
CTX = ("ctx_0", "ctx_1")
CTX_TP = ("ctx_0", "ctx_1", "tp_0", "tp_1")
N_CTX = 16
N_X = 4
N_TP = 8
SHARD = 32
LINES = 128
DOCS = 5

NORM_EPS = 1e-05
MOMENT_DECAY = 0.5
MOMENT_EPS = 1e-30
CLIP_LIMIT = 0.5
STEP_SCALE = 1.0
ROPE_BASE = 10000.0
YARN_SCALE = 4.0
YARN_ALPHA = 1.0
YARN_BETA = 32.0

bf16 = jnp.bfloat16
f32 = jnp.float32


def x_from(values, step):
    return lax.ppermute(values, "tp_0", [((i + step) % N_X, i) for i in range(N_X)])


def x_to(values, step):
    return lax.ppermute(values, "tp_0", [(i, (i + step) % N_X) for i in range(N_X)])


def core_swap(values):
    return lax.ppermute(values, "tp_1", [(0, 1), (1, 0)])


def turned(stack, start):
    return lax.dynamic_slice_in_dim(jnp.concatenate([stack, stack]), start, N_X, 0)


def to_absolute(stack, xs):
    return turned(stack, (N_X - xs) % N_X)


def tp_column(shard):
    return jnp.concatenate([shard] + [x_from(shard, d) for d in range(1, N_X)])


def gather_tp(shard):
    column = tp_column(shard)
    return jnp.concatenate([column, core_swap(column)])


def scatter_tp(partial):
    half = partial[0] + core_swap(partial[1].astype(bf16)).astype(f32)
    low = half.astype(bf16)
    total = half[0]
    for d in range(1, N_X):
        total = total + x_to(low[d], d).astype(f32)
    return total


def both_cores(column, cs):
    other = core_swap(column)
    both = jnp.where(
        cs == 0, jnp.stack([column, other], axis=1), jnp.stack([other, column], axis=1)
    )
    return both.reshape(-1, *column.shape[2:])


def swapped_x(blocks, xs):
    ours = turned(blocks, xs)
    came = [ours[0]] + [x_to(ours[d], d) for d in range(1, N_X)]
    return to_absolute(jnp.stack([came[0], came[3], came[2], came[1]]), xs)


def partner(values, axis, mask):
    size = 2 if axis == "tp_1" else 4
    return lax.ppermute(values, axis, [(i, i ^ mask) for i in range(size)])


def sum_over_four(values, axis):
    return (values + partner(values, axis, 1)) + (
        partner(values, axis, 2) + partner(values, axis, 3)
    )


def sum_tp(values):
    return sum_over_four(values + partner(values, "tp_1", 1), "tp_0")


def sum_ctx(values):
    return sum_over_four(sum_over_four(values, "ctx_1"), "ctx_0")


def own_order(values, xs, cs):
    blocks = turned(values.reshape(N_X, 2, SHARD), xs)
    blocks = jnp.where(cs == 0, blocks, blocks[:, ::-1])
    return blocks.transpose(1, 0, 2)


def sent_to_all(array, axis):
    copies = jnp.broadcast_to(array, (lax.axis_size(axis), *array.shape))
    return lax.all_to_all(copies, axis, split_axis=0, concat_axis=0, tiled=True)


def rope_tables(positions):
    ladder = jnp.arange(HD // 2, dtype=f32)
    freqs = ROPE_BASE ** (-2.0 * ladder / HD)
    ratio = ORIG_CTX * freqs / (2.0 * math.pi)
    ramped = jnp.clip((ratio - YARN_ALPHA) / (YARN_BETA - YARN_ALPHA), 0.0, 1.0)
    inverse = freqs * (1.0 - ramped) / YARN_SCALE + freqs * ramped
    angles = inverse[:, None] * positions.astype(f32)[None, :]
    mscale = 0.1 * math.log(YARN_SCALE) + 1.0
    return (jnp.cos(angles) * mscale, jnp.sin(angles) * mscale)


def rotate_rows(values, cosine, sine):
    half = values.shape[0] // 2
    first, second = (values[:half], values[half:])
    return jnp.concatenate([first * cosine - second * sine, second * cosine + first * sine])


def rotate_lanes(values, cosine, sine):
    half = values.shape[1] // 2
    first, second = (values[:, :half], values[:, half:])
    return jnp.concatenate([first * cosine - second * sine, second * cosine + first * sine], axis=1)


def rms_norm(values, gain):
    return values * lax.rsqrt(jnp.mean(values * values, axis=-1, keepdims=True) + NORM_EPS) * gain


def contract_last(left, right):
    return lax.dot_general(left, right, (((1,), (1,)), ((), ())), preferred_element_type=f32)


def contract_first(left, right):
    return lax.dot_general(left, right, (((0,), (0,)), ((), ())), preferred_element_type=f32)


def contract(left, right):
    return jnp.dot(left, right, preferred_element_type=f32)


def combine_stats(former, latter):
    highest = jnp.maximum(former[0], latter[0])
    summed = former[1] * jnp.exp(former[0] - highest) + latter[1] * jnp.exp(latter[0] - highest)
    return jnp.stack([highest, summed, former[2] + latter[2]])


def contract_ft(weights, places):
    return lax.dot_general(weights, places, (((0,), (1,)), ((), ())), preferred_element_type=f32)


def contract_tf(features, weights):
    return lax.dot_general(features, weights, (((0,), (1,)), ((), ())), preferred_element_type=f32)


def heads_on_lanes(features):
    return jnp.concatenate([features[h * HD : (h + 1) * HD] for h in range(4)], axis=1)


def heads_on_rows(features):
    return jnp.concatenate(jnp.split(features, 4, axis=1))


VMEM_LIMIT = 50 * 1024 * 1024


GROUP = 4
KEYS = 128 * GROUP
STEPS = TOKENS // KEYS


def key_places(core_bit, spans):
    line = lax.broadcasted_iota(jnp.int32, (128, 1), 0)
    x = (spans[N_CTX] + line // SHARD) % N_X
    place = (x * 2 + (spans[N_CTX + 1] ^ core_bit)) * SHARD + line % SHARD
    return place >= 128, place % 128


def visible_keys(spans, places, step, own, start):
    lines = []
    for block in range(step * GROUP, (step + 1) * GROUP):
        span = spans[block % N_CTX]
        second, within = places[block // N_CTX]
        lines.append(jnp.where(second, (2 * N_CTX - 1 - span) * 128, span * 128) + within)
    at = jnp.concatenate(lines, axis=0)
    return (at >= start) & (at <= own)


def key_columns(kv_ref, step, at):
    return jnp.concatenate(
        [kv_ref[step * GROUP + i, at : at + HD] for i in range(GROUP)], axis=1
    )


def attend_kernel(spans, own_ref, q_ref, kv_ref, o_ref, total_ref, s_ref):
    q = q_ref[...]
    own, start = (own_ref[0:1], own_ref[1:2])
    places = [key_places(core_bit, spans) for core_bit in range(2)]
    top = None
    for step in range(STEPS):
        scores = contract_first(key_columns(kv_ref, step, 0), q)
        scores = jnp.where(visible_keys(spans, places, step, own, start), scores, -1e30)
        s_ref[step * KEYS : (step + 1) * KEYS] = scores
        highest = jnp.max(scores, axis=0, keepdims=True)
        top = highest if top is None else jnp.maximum(top, highest)
    total = jnp.zeros(top.shape, f32)
    for step in range(STEPS):
        powers = jnp.exp(s_ref[step * KEYS : (step + 1) * KEYS] - top)
        s_ref[step * KEYS : (step + 1) * KEYS] = powers
        total = total + jnp.sum(powers, axis=0, keepdims=True)
    share = 1.0 / total
    out = jnp.zeros(q.shape, f32)
    for step in range(STEPS):
        weights = (s_ref[step * KEYS : (step + 1) * KEYS] * share).astype(bf16)
        out = out + contract(key_columns(kv_ref, step, HD), weights)
    o_ref[...] = out.astype(bf16)
    total_ref[...] = top + jnp.log(total)


SPLIT = 2


def attend(spans, own, q, kv):
    lanes = q.shape[1] // SPLIT
    column = lambda rows: pl.BlockSpec((rows, lanes), lambda i: (0, i))
    return pl.pallas_call(
        attend_kernel,
        grid=(SPLIT,),
        in_specs=[
            pl.BlockSpec(memory_space=pltpu.SMEM),
            column(2),
            column(HD),
            pl.BlockSpec(kv.shape, lambda i: (0, 0, 0)),
        ],
        out_specs=[column(HD), column(1)],
        out_shape=[
            jax.ShapeDtypeStruct(q.shape, bf16),
            jax.ShapeDtypeStruct((1, q.shape[1]), f32),
        ],
        scratch_shapes=[pltpu.VMEM((TOKENS, lanes), f32)],
        compiler_params=pltpu.CompilerParams(vmem_limit_bytes=VMEM_LIMIT),
        cost_estimate=pl.CostEstimate(
            flops=16 * TOKENS * q.shape[1] * HD, bytes_accessed=2 << 20, transcendentals=0
        ),
    )(spans, own, q, kv)


def attend_back_kernel(
    spans, own_ref, q_ref, do_ref, total_ref, kv_ref, dq_ref, dkv_ref, p_ref, dp_ref
):
    q, do = (q_ref[...], do_ref[...])
    own, start = (own_ref[0:1], own_ref[1:2])
    total = total_ref[...]
    places = [key_places(core_bit, spans) for core_bit in range(2)]
    rowsum = jnp.zeros(total.shape, f32)
    for step in range(STEPS):
        scores = contract_first(key_columns(kv_ref, step, 0), q)
        scores = jnp.where(visible_keys(spans, places, step, own, start), scores, -1e30)
        probs = jnp.exp(scores - total)
        probs_grad = contract_first(key_columns(kv_ref, step, HD), do)
        p_ref[step * KEYS : (step + 1) * KEYS] = probs
        dp_ref[step * KEYS : (step + 1) * KEYS] = probs_grad
        rowsum = rowsum + jnp.sum(probs * probs_grad, axis=0, keepdims=True)

    @pl.when(pl.program_id(0) == 0)
    def _():
        dkv_ref[...] = jnp.zeros(dkv_ref.shape, f32)

    dq = jnp.zeros(q.shape, f32)
    for step in range(STEPS):
        rows = slice(step * KEYS, (step + 1) * KEYS)
        probs = p_ref[rows]
        score_grad = (probs * (dp_ref[rows] - rowsum)).astype(bf16)
        dkv_ref[rows] += jnp.concatenate(
            [contract_last(score_grad, q), contract_last(probs.astype(bf16), do)], axis=1
        )
        dq = dq + contract(key_columns(kv_ref, step, 0), score_grad)
    dq_ref[...] = dq * (1.0 / math.sqrt(HD))


def attend_back(spans, own, q, do, total, kv):
    lanes = q.shape[1] // SPLIT
    column = lambda rows: pl.BlockSpec((rows, lanes), lambda i: (0, i))
    return pl.pallas_call(
        attend_back_kernel,
        grid=(SPLIT,),
        in_specs=[
            pl.BlockSpec(memory_space=pltpu.SMEM),
            column(2),
            column(HD),
            column(HD),
            column(1),
            pl.BlockSpec(kv.shape, lambda i: (0, 0, 0)),
        ],
        out_specs=[column(HD), pl.BlockSpec((TOKENS, 2 * HD), lambda i: (0, 0))],
        out_shape=[
            jax.ShapeDtypeStruct(q.shape, f32),
            jax.ShapeDtypeStruct((TOKENS, 2 * HD), f32),
        ],
        scratch_shapes=[pltpu.VMEM((TOKENS, lanes), f32), pltpu.VMEM((TOKENS, lanes), f32)],
        compiler_params=pltpu.CompilerParams(vmem_limit_bytes=VMEM_LIMIT),
        cost_estimate=pl.CostEstimate(
            flops=40 * TOKENS * q.shape[1] * HD, bytes_accessed=4 << 20, transcendentals=0
        ),
    )(spans, own, q, do, total, kv)


def moments(old, sums, count):
    return MOMENT_DECAY * old + (1.0 - MOMENT_DECAY) * (sums / count + MOMENT_EPS)


def params():
    return pltpu.CompilerParams(vmem_limit_bytes=VMEM_LIMIT)


def whole(array):
    zeros = (0,) * array.ndim
    return pl.BlockSpec(array.shape, lambda *i: zeros)


def cost(flops, moved):
    return pl.CostEstimate(flops=flops, bytes_accessed=moved, transcendentals=0)


ID_STEP = 2048


def look_kernel(ids_ref, table_ref, out_ref, low_ref):
    @pl.when(pl.program_id(0) == 0)
    def _():
        low_ref[...] = table_ref[0].astype(bf16)

    width = low_ref.shape[0]
    ids = jnp.transpose(jnp.broadcast_to(ids_ref[...], (8, ID_STEP)))[:, :1]
    hits = ids == lax.broadcasted_iota(jnp.int32, (ID_STEP, width), 1)
    out_ref[...] = contract(jnp.where(hits, 1.0, 0.0).astype(bf16), low_ref[...]).astype(bf16)


def look_up(ids, tables):
    width, lines = tables.shape[1:]
    count = ids.shape[1]
    return pl.pallas_call(
        look_kernel,
        grid=(count // ID_STEP,),
        in_specs=[
            pl.BlockSpec((1, ID_STEP), lambda i: (0, i)),
            pl.BlockSpec((1, width, lines), lambda i: (1, 0, 0)),
        ],
        out_specs=pl.BlockSpec((ID_STEP, lines), lambda i: (i, 0)),
        out_shape=jax.ShapeDtypeStruct((count, lines), bf16),
        scratch_shapes=[pltpu.VMEM((width, lines), bf16)],
        compiler_params=params(),
        cost_estimate=cost(4 * count * width * lines, 4 * lines * width),
    )(ids, tables)


def add_kernel(ids_ref, own_ref, other_ref, out_ref):
    hits = lax.broadcasted_iota(jnp.int32, (out_ref.shape[0], ID_STEP), 0) == ids_ref[...]
    first = pl.program_id(0) == 0
    grads = jnp.where(first, own_ref[...], other_ref[...])
    added = contract(jnp.where(hits, 1.0, 0.0).astype(bf16), grads)

    @pl.when(first)
    def _():
        out_ref[...] = added

    @pl.when(jnp.logical_not(first))
    def _():
        out_ref[...] += added


def add_up(ids, own, other, width):
    lines = own.shape[1]
    return pl.pallas_call(
        add_kernel,
        grid=(2,),
        in_specs=[pl.BlockSpec((1, ID_STEP), lambda i: (0, i)), whole(own), whole(other)],
        out_specs=pl.BlockSpec((width, lines), lambda i: (0, 0)),
        out_shape=jax.ShapeDtypeStruct((width, lines), f32),
        compiler_params=params(),
        cost_estimate=cost(8 * ID_STEP * width * lines, 4 * lines * width),
    )(ids, own, other)


LOGIT_STEP = 800
TABLE_STEP = 2000


def joined(ref):
    return jnp.concatenate([ref[k] for k in range(N_CTX)], axis=1)


def logits_kernel(c_ref, w_ref, target_ref, out_ref, stats_ref):
    step = pl.program_id(0)
    logits = contract_last(joined(w_ref), c_ref[...])
    out_ref[...] = logits
    row = lax.broadcasted_iota(jnp.int32, logits.shape, 0) + step * TABLE_STEP
    here = jnp.max(logits, axis=0, keepdims=True)
    pick = jnp.sum(jnp.where(row == target_ref[...], logits, 0.0), axis=0, keepdims=True)

    @pl.when(step == 0)
    def _():
        stats_ref[...] = jnp.zeros(stats_ref.shape, f32)
        stats_ref[0:1] = here

    old = stats_ref[0:1]
    top = jnp.maximum(old, here)
    powers = jnp.sum(jnp.exp(logits - top), axis=0, keepdims=True)
    stats_ref[1:2] = stats_ref[1:2] * jnp.exp(old - top) + powers
    stats_ref[2:3] += pick
    stats_ref[0:1] = top


def logits_and_stats(c, head, targets):
    places, rows = c.shape
    width = head.shape[1]
    return pl.pallas_call(
        logits_kernel,
        grid=(width // TABLE_STEP,),
        in_specs=[
            whole(c),
            pl.BlockSpec((N_CTX, TABLE_STEP, 128), lambda i: (0, i, 0)),
            whole(targets),
        ],
        out_specs=[
            pl.BlockSpec((TABLE_STEP, places), lambda i: (i, 0)),
            pl.BlockSpec((8, places), lambda i: (0, 0)),
        ],
        out_shape=[
            jax.ShapeDtypeStruct((width, places), f32),
            jax.ShapeDtypeStruct((8, places), f32),
        ],
        compiler_params=params(),
        cost_estimate=cost(2 * places * rows * width, 2 * rows * width),
    )(c, head, targets)


def head_grad_kernel(logits_ref, c_ref, place_ref, target_ref, dw_ref, low_ref):
    step = pl.program_id(0)
    logits = logits_ref[...]
    row = lax.broadcasted_iota(jnp.int32, logits.shape, 0) + step * LOGIT_STEP
    hit = row == target_ref[...]
    shares = jnp.exp(logits - place_ref[0:1]) - jnp.where(hit, 1.0, 0.0)
    low = (place_ref[1:2] * shares).astype(bf16)
    low_ref[...] = low
    grad = contract(low, c_ref[...]).astype(bf16)
    for k in range(N_CTX):
        dw_ref[k] = grad[:, k * 128 : (k + 1) * 128]


def head_grads(logits, c, place, targets):
    places, rows = c.shape
    width = logits.shape[0]
    block = pl.BlockSpec((LOGIT_STEP, places), lambda i: (i, 0))
    return pl.pallas_call(
        head_grad_kernel,
        grid=(width // LOGIT_STEP,),
        in_specs=[block, whole(c), whole(place), whole(targets)],
        out_specs=[pl.BlockSpec((N_CTX, LOGIT_STEP, 128), lambda i: (0, i, 0)), block],
        out_shape=[
            jax.ShapeDtypeStruct((N_CTX, width, 128), bf16),
            jax.ShapeDtypeStruct((width, places), bf16),
        ],
        compiler_params=params(),
        cost_estimate=cost(2 * places * rows * width, 2 * rows * width),
    )(logits, c, place, targets)


def place_grad_kernel(low_ref, w_ref, out_ref):
    part = contract_first(low_ref[...], joined(w_ref))

    @pl.when(pl.program_id(0) == 0)
    def _():
        out_ref[...] = part

    @pl.when(pl.program_id(0) > 0)
    def _():
        out_ref[...] += part


def place_grads_of(low, head):
    width, places = low.shape
    return pl.pallas_call(
        place_grad_kernel,
        grid=(width // TABLE_STEP,),
        in_specs=[
            pl.BlockSpec((TABLE_STEP, places), lambda i: (i, 0)),
            pl.BlockSpec((N_CTX, TABLE_STEP, 128), lambda i: (0, i, 0)),
        ],
        out_specs=pl.BlockSpec((places, D), lambda i: (0, 0)),
        out_shape=jax.ShapeDtypeStruct((places, D), f32),
        compiler_params=params(),
        cost_estimate=cost(2 * places * D * width, 2 * D * width),
    )(low, head)


TURNED = (1, 3)


def products_kernel(count, offsets, *refs):
    lefts, rights = (refs[:count], refs[count : 2 * count])
    out_ref, turned_ref = refs[2 * count :]

    @pl.when(pl.program_id(0) == 0)
    def _():
        for k, (right, (at, width)) in enumerate(zip(rights, offsets)):
            values = right[...]
            turned_ref[at : at + width] = values if k in TURNED else jnp.transpose(values)

    for left, (at, width) in zip(lefts, offsets):
        grad = contract(turned_ref[at : at + width], left[...]).astype(bf16)
        for k in range(2):
            out_ref[k, at : at + width] = grad[:, k * 128 : (k + 1) * 128]


def row_products(lefts, rights):
    places, rows = lefts[0].shape
    offsets, at = ([], 0)
    for k, right in enumerate(rights):
        width = right.shape[0 if k in TURNED else 1]
        offsets.append((at, width))
        at += width
    return pl.pallas_call(
        functools.partial(products_kernel, len(lefts), tuple(offsets)),
        grid=(N_CTX // 2,),
        in_specs=[pl.BlockSpec((places, 256), lambda i: (0, i)) for _ in lefts]
        + [whole(right) for right in rights],
        out_specs=pl.BlockSpec((2, at, 128), lambda i: (i, 0, 0)),
        out_shape=jax.ShapeDtypeStruct((N_CTX, at, rows // N_CTX), bf16),
        scratch_shapes=[pltpu.VMEM((at, places), bf16)],
        compiler_params=params(),
        cost_estimate=cost(2 * places * rows * at, 2 * rows * at),
    )(*lefts, *rights)


MATRICES = 8
WIDTHS = (HQ, HQ, FF, FF, FF, VOCAB, VOCAB, KVW)
EARLY_LANES = 8320
LATE_LANES = 2688
COLUMN_AT = {5: (0, 4000), 6: (4096, 4000), 7: (8192, 128)}
COLUMN_AT.update({2: (0, 704), 3: (704, 704), 1: (1408, 256), 4: (1664, 704), 0: (2368, 256)})
S_LANE, T_LANE, OLD_LANE, W_LANE, WG_LANE, UG_LANE, LOSS_LANE = (0, 8, 16, 24, 32, 35, 38)


def lane_is(shape, lane):
    return lax.broadcasted_iota(jnp.int32, shape, 1) == lane


def line_sum(values):
    return jnp.sum(values, axis=0, keepdims=True)


def total_of(values):
    return jnp.sum(line_sum(values), axis=1, keepdims=True)


def column_sums(squares):
    ones = jnp.ones((8, squares.shape[1]), f32)
    return lax.dot_general(
        ones,
        squares,
        (((1,), (1,)), ((), ())),
        precision=lax.Precision.HIGHEST,
        preferred_element_type=f32,
    )


def weights_kernel(tables_ref, feed_ref, attention_ref, kv_master_ref, gain_ref, scalars_ref):
    scalars = jnp.zeros(scalars_ref.shape, f32)
    for number, weights in (
        (0, attention_ref[0]),
        (1, attention_ref[1]),
        (2, feed_ref[0]),
        (3, feed_ref[1]),
        (4, feed_ref[2]),
        (5, tables_ref[0]),
        (6, tables_ref[1]),
        (7, kv_master_ref[...]),
        (8, gain_ref[0:1]),
        (9, gain_ref[1:2]),
        (10, gain_ref[2:3]),
    ):
        scalars += jnp.where(
            lane_is(scalars.shape, W_LANE + number), total_of(weights * weights), 0.0
        )
    scalars_ref[...] = scalars


def weight_squares(*masters):
    return pl.pallas_call(
        weights_kernel,
        out_shape=jax.ShapeDtypeStruct((1, 128), f32),
        compiler_params=params(),
        cost_estimate=cost(0, 6 << 20),
    )(*masters)


def head_kernel(head_ref, grad_ref, line_ref, columns_ref):
    grad = head_ref[...].astype(f32)
    grad_ref[0] = grad
    squares = grad * grad
    line_ref[...] = line_sum(squares)
    columns_ref[...] = jnp.concatenate(
        [column_sums(squares)[:1], jnp.zeros((1, 96), f32)], axis=1
    )


def head_figures(head_low):
    width, lines = head_low.shape
    return pl.pallas_call(
        head_kernel,
        grid=(1,),
        in_specs=[whole(head_low)],
        out_specs=[
            pl.BlockSpec((1, width, lines), lambda i: (0, 0, 0)),
            pl.BlockSpec((1, lines), lambda i: (0, 0)),
            pl.BlockSpec((1, width + 96), lambda i: (0, 0)),
        ],
        out_shape=[
            jax.ShapeDtypeStruct((2, width, lines), f32),
            jax.ShapeDtypeStruct((1, lines), f32),
            jax.ShapeDtypeStruct((1, width + 96), f32),
        ],
        compiler_params=params(),
        cost_estimate=cost(0, 4 << 20),
    )(head_low)


def early_kernel(
    grads_ref, embed_ref, kv_ref, gains_ref, kv_old_ref, head_line_ref, head_columns_ref,
    vocab_grad_ref, lines_ref, columns_ref,
):
    lines_ref[...] = jnp.zeros(lines_ref.shape, f32)
    lines_ref[5:6] = head_line_ref[...]
    lines_ref[8:11] = gains_ref[...]
    lines_ref[11:12] = kv_old_ref[...]
    grad = embed_ref[...]
    vocab_grad_ref[0] = grad
    embed_squares = grad * grad
    lines_ref[6:7] = line_sum(embed_squares)
    kv_squares = kv_ref[...] * kv_ref[...]
    lines_ref[7:8] = 0.5 * line_sum(kv_squares)
    sums = jnp.concatenate(
        [
            head_columns_ref[...],
            column_sums(embed_squares)[:1],
            jnp.zeros((1, 96), f32),
            column_sums(kv_squares)[:1],
        ],
        axis=1,
    )
    columns_ref[...] = jnp.broadcast_to(sums[None], columns_ref.shape)


def early_figures(grads, *arrays):
    block = (1, *grads.shape[1:])
    columns = (N_CTX, 1, EARLY_LANES)
    return pl.pallas_call(
        early_kernel,
        grid=(1,),
        in_specs=[pl.BlockSpec(memory_space=pl.ANY)] + [whole(a) for a in arrays],
        out_specs=[
            pl.BlockSpec(block, lambda i: (1, 0, 0)),
            pl.BlockSpec((16, 128), lambda i: (0, 0)),
            pl.BlockSpec(columns, lambda i: (0, 0, 0)),
        ],
        out_shape=[
            jax.ShapeDtypeStruct(grads.shape, f32),
            jax.ShapeDtypeStruct((16, 128), f32),
            jax.ShapeDtypeStruct(columns, f32),
        ],
        input_output_aliases={0: 0},
        compiler_params=params(),
        cost_estimate=cost(0, 6 << 20),
    )(grads, *arrays)


def late_kernel(layer_ref, feed_grad_ref, attention_grad_ref, lines_ref, columns_ref):
    layer = layer_ref[...].astype(f32)
    squares = layer * layer
    sums = jnp.concatenate(
        [column_sums(squares)[:1], jnp.zeros((1, LATE_LANES - layer.shape[0]), f32)], axis=1
    )
    columns_ref[...] = jnp.broadcast_to(sums[None], columns_ref.shape)
    lines_ref[...] = jnp.zeros(lines_ref.shape, f32)
    for number in range(5):
        at, width = COLUMN_AT[number]
        lines_ref[number : number + 1] = line_sum(squares[at : at + width])
        if number > 1:
            feed_grad_ref[number - 2] = layer[at : at + width]
    attention_grad_ref[0] = jnp.transpose(layer[2368:2624])
    attention_grad_ref[1] = jnp.transpose(layer[1408:1664])


def late_figures(layer):
    shapes = ((3, 704, 128), (2, 128, 256), (8, 128), (N_CTX, 1, LATE_LANES))
    return pl.pallas_call(
        late_kernel,
        out_shape=[jax.ShapeDtypeStruct(shape, f32) for shape in shapes],
        compiler_params=params(),
        cost_estimate=cost(0, 4 << 20),
    )(layer)


def per_column(figures, number):
    at, width = COLUMN_AT[number]
    return figures[at : at + width, :1]


def on_rows(columns):
    spare = 8 - columns.shape[0]
    return jnp.transpose(
        jnp.concatenate([columns, jnp.ones((spare, columns.shape[1]), f32)], axis=0)
    )


def squares_of(sources, lines, old, columns, old_columns, scalars, row_ref, column_ref):
    number = lax.broadcasted_iota(jnp.int32, lines.shape, 0)
    widths = jnp.full(lines.shape, 1.0, f32)
    for k, width in enumerate(WIDTHS):
        widths = jnp.where(number == k, float(width), widths)
    row_new = moments(old, lines / widths, 1.0)
    row_ref[...] = row_new
    column_new = moments(old_columns, jnp.sum(columns, axis=0), float(D))
    column_ref[...] = column_new
    row_scale = lax.rsqrt(row_new)
    column_scale = on_rows(lax.rsqrt(column_new))
    had = jnp.sum(old, axis=1, keepdims=True) * (1.0 / N_TP)
    got = jnp.sum(lines, axis=1, keepdims=True) * (1.0 / N_TP)
    for k, grad, keep in sources:
        unit = grad * row_scale[k : k + 1] * per_column(column_scale, k)
        if keep is not None:
            keep[0][keep[1]] = jnp.transpose(unit) if k < 2 else unit
        part = total_of(unit * unit) * (0.5 if k == 7 else 1.0)
        scalars += jnp.where(lane_is(scalars.shape, S_LANE + k), part, 0.0)
        scalars += jnp.where(lane_is(scalars.shape, T_LANE + k), got[k : k + 1], 0.0)
        scalars += jnp.where(lane_is(scalars.shape, OLD_LANE + k), had[k : k + 1], 0.0)
    return scalars


def early_squares_kernel(
    vocab_ref, kv_ref, lines_ref, columns_ref, old_ref, old_columns_ref, base_ref,
    row_ref, column_ref, unit_ref, scalars_ref,
):
    lines = lines_ref[...]
    number = lax.broadcasted_iota(jnp.int32, lines.shape, 0)
    old = jnp.where(number == 7, lines_ref[11:12], old_ref[...])
    sources = (
        (5, vocab_ref[0], (unit_ref, 0)),
        (6, vocab_ref[1], (unit_ref, 1)),
        (7, kv_ref[...], None),
    )
    scalars_ref[...] = squares_of(
        sources, lines, old, columns_ref[...], old_columns_ref[...], base_ref[...],
        row_ref, column_ref,
    )


def late_squares_kernel(
    layer_ref, lines_ref, columns_ref, old_ref, old_columns_ref, base_ref, kv_columns_ref,
    row_ref, column_ref, feed_unit_ref, attention_unit_ref, packed_ref,
):
    sources = []
    for number in range(5):
        at, width = COLUMN_AT[number]
        keep = (attention_unit_ref, number) if number < 2 else (feed_unit_ref, number - 2)
        sources.append((number, layer_ref[at : at + width].astype(f32), keep))
    scalars = squares_of(
        sources, lines_ref[...], old_ref[0:8], columns_ref[...], old_columns_ref[...],
        base_ref[...], row_ref, column_ref,
    )
    packed = jnp.concatenate([scalars, kv_columns_ref[...]], axis=0)
    packed_ref[...] = jnp.broadcast_to(packed[None], packed_ref.shape)


def step_squares(kernel, shapes, *arrays):
    return pl.pallas_call(
        kernel,
        out_shape=[jax.ShapeDtypeStruct(shape, f32) for shape in shapes],
        compiler_params=params(),
        cost_estimate=cost(0, 12 << 20),
    )(*arrays)


UPDATE_STEP = 2000


def update_kernel(
    all_ref, vocab_ref, vocab_unit_ref, feed_ref, feed_unit_ref, attention_ref,
    attention_unit_ref, gain_ref, gain_step_ref,
    vocab_new_ref, feed_new_ref, attention_new_ref, gain_new_ref, figures_ref,
):
    sums = jnp.sum(all_ref[...], axis=0, keepdims=True)
    sums = jnp.broadcast_to(sums, (8, 128))

    def lanes_from(at):
        return pltpu.roll(sums, (128 - at) % 128, 1)[0:1]

    lane = lax.broadcasted_iota(jnp.int32, (1, 128), 1)
    counts = jnp.full((1, 128), float(D), f32)
    for k, width in enumerate(WIDTHS):
        counts = jnp.where(lane == k, float(D * width), counts)
    mean = MOMENT_DECAY * lanes_from(OLD_LANE) / D + (1.0 - MOMENT_DECAY) * (
        lanes_from(T_LANE) / counts + MOMENT_EPS
    )
    mean = jnp.where(lane < MATRICES, mean, 1.0)
    rms = jnp.sqrt(mean * lanes_from(S_LANE) / counts)
    factor = (
        STEP_SCALE
        * jnp.sqrt(lanes_from(W_LANE) / counts)
        / jnp.maximum(1.0, rms / CLIP_LIMIT)
        * jnp.sqrt(mean)
    )

    @pl.when(pl.program_id(0) == 0)
    def _():
        for k in range(2):
            attention_new_ref[k] = attention_ref[k] - attention_unit_ref[k] * factor[:, k : k + 1]
        for k in range(3):
            feed_new_ref[k] = feed_ref[k] - feed_unit_ref[k] * factor[:, 2 + k : 3 + k]
        gain_rms = jnp.sqrt(lanes_from(UG_LANE) / D)
        gain_factor = (
            STEP_SCALE
            * jnp.sqrt(lanes_from(WG_LANE) / D)
            / jnp.maximum(1.0, gain_rms / CLIP_LIMIT)
        )
        for k in range(3):
            gain_new_ref[k : k + 1] = (
                gain_ref[k : k + 1] - gain_factor[:, k : k + 1] * gain_step_ref[k : k + 1]
            )
        after = pltpu.roll(jnp.broadcast_to(gain_rms, (8, 128)), MATRICES, 1)[0:1]
        figures_ref[0:1] = jnp.where(lane < MATRICES, rms, after)
        figures_ref[1:2] = factor
        figures_ref[2:3] = lanes_from(LOSS_LANE)
        figures_ref[3:8] = jnp.zeros((5, 128), f32)

    for k in range(2):
        vocab_new_ref[k] = vocab_ref[k] - vocab_unit_ref[k] * factor[:, 5 + k : 6 + k]


def update(gathered, vocab, vocab_unit, feed, feed_unit, attention, attention_unit, gain, gain_step):
    stack = pl.BlockSpec((2, UPDATE_STEP, vocab.shape[2]), lambda i: (0, i, 0))
    others = (feed, feed_unit, attention, attention_unit, gain, gain_step)
    outs = (vocab, feed, attention, gain)
    return pl.pallas_call(
        update_kernel,
        grid=(vocab.shape[1] // UPDATE_STEP,),
        in_specs=[whole(gathered), stack, stack] + [whole(a) for a in others],
        out_specs=[stack]
        + [whole(a) for a in outs[1:]]
        + [pl.BlockSpec((8, 128), lambda i: (0, 0))],
        out_shape=[jax.ShapeDtypeStruct(a.shape, f32) for a in outs]
        + [jax.ShapeDtypeStruct((8, 128), f32)],
        compiler_params=params(),
        cost_estimate=cost(0, 24 << 20),
    )(gathered, vocab, vocab_unit, *others)


def body(
    token_ids,
    target_ids,
    loss_mask,
    segment_ids,
    span_pairs,
    attention_master,
    feed_master,
    vocab_master,
    key_value_master,
    gain_master,
    attention_row_moment,
    attention_column_moment,
    feed_row_moment,
    feed_column_moment,
    vocab_row_moment,
    vocab_column_moment,
    key_value_row_moment,
    key_value_column_moment,
    gain_moment,
):
    ctx_index = lax.axis_index(CTX)
    xs = lax.axis_index("tp_0")
    cs = lax.axis_index("tp_1")
    tp_index = xs * 2 + cs
    vocab_here = vocab_master.shape[2]
    ff_here = feed_master.shape[2]
    first_id = tp_index * vocab_here

    attention_low = attention_master.astype(bf16)
    feed_low = feed_master.astype(bf16)
    layer_all = lax.all_gather(
        jnp.concatenate(
            [
                attention_low[0].T,
                attention_low[1].T,
                feed_low[0].T,
                feed_low[1].T,
                feed_low[2].T,
            ]
        )[None],
        CTX,
        axis=0,
        tiled=True,
    )
    head = lax.all_gather(vocab_master[0].astype(bf16).T[None], CTX, axis=0, tiled=True)

    def on_lanes(at, width):
        return layer_all[:, at : at + width].transpose(1, 0, 2).reshape(width, D)

    w_query = on_lanes(0, 256)
    w_out = on_lanes(256, 256)
    gate_up = on_lanes(512, 2 * ff_here)
    down = on_lanes(512 + 2 * ff_here, ff_here)

    kv_low = key_value_master.astype(bf16).reshape(16, 2, KV_HEADS, HD).transpose(2, 0, 1, 3)
    gain_low = jnp.pad(gain_master.astype(bf16), ((0, 0), (0, 125)))
    blocks = jnp.concatenate(
        [
            kv_low.reshape(KV_HEADS, 16, 2 * HD),
            jnp.broadcast_to(gain_low, (KV_HEADS, *gain_low.shape)),
        ],
        axis=2,
    )
    ids_here = own_order(token_ids, xs, cs).reshape(1, 256)
    line_block = both_cores(swapped_x(blocks, xs), cs)
    half = LINES // 2
    early = sent_to_all(
        jnp.concatenate(
            [
                lax.dynamic_slice_in_dim(line_block[:, : 2 * HD], cs * half, half, 0),
                line_block[:, 2 * HD : 2 * HD + 3].T,
                (ids_here // 256).astype(bf16).reshape(2, 128),
                (ids_here % 256).astype(bf16).reshape(2, 128),
                jnp.zeros((9, 128), bf16),
            ]
        ),
        CTX,
    )
    own_half = early[:, :half]
    other_half = core_swap(own_half)
    w_pair = jnp.where(
        cs == 0,
        jnp.concatenate([own_half, other_half], axis=1),
        jnp.concatenate([other_half, own_half], axis=1),
    ).reshape(D, 2 * HD)
    gains = early[:, half : half + 3].astype(f32).transpose(1, 0, 2).reshape(3, D)
    parts = early[:, half + 3 : half + 7].astype(jnp.int32).reshape(N_CTX, 2, 256)
    all_ids = parts[:, 0] * 256 + parts[:, 1]
    all_ids = all_ids.reshape(N_CTX, 8, SHARD).transpose(1, 0, 2).reshape(1, TOKENS) - first_id

    order = (
        ((xs + jnp.arange(N_X, dtype=jnp.int32)) % N_X * 2)[None, :]
        + (cs ^ jnp.arange(2, dtype=jnp.int32))[:, None]
    )[:, :, None] * SHARD + jnp.arange(SHARD, dtype=jnp.int32)
    second_span = order >= 128
    within = order % 128
    own_pair = lax.dynamic_slice_in_dim(span_pairs, ctx_index, 1)[0]
    last_span = 2 * N_CTX - 1
    own_pos = (jnp.where(second_span, last_span - own_pair, own_pair) * 128 + within).reshape(-1)
    doc_start = jnp.zeros_like(own_pos)
    for k in range(1, DOCS):
        start = jnp.sum((segment_ids < k).astype(jnp.int32))
        doc_start = jnp.where(own_pos >= start, start, doc_start)
    cosine, sine = rope_tables(own_pos - doc_start)
    cosine_4, sine_4 = (jnp.tile(cosine, (1, 4)), jnp.tile(sine, (1, 4)))
    own_places = jnp.tile(jnp.stack([own_pos, doc_start]), (1, 4))
    spans = jnp.concatenate([span_pairs, jnp.stack([xs, cs]).astype(jnp.int32)])

    tables = vocab_master.transpose(0, 2, 1)
    looked = look_up(all_ids, tables).reshape(2, N_X, N_CTX, SHARD, LINES)
    half = looked[0] + core_swap(looked[1])
    mine = half[0]
    for d in range(1, N_X):
        mine = mine + x_to(half[d], d)
    rows_in = lax.all_to_all(mine, CTX, 0, 0, tiled=True)
    stream_in = rows_in.transpose(1, 0, 2).reshape(SHARD, D).astype(f32)

    normed_low = gather_tp(rms_norm(stream_in, gains[0]).astype(bf16))
    normed_half = normed_low[:128]
    keyval_linear = contract_ft(w_pair, normed_half)
    own_keyvals = jnp.concatenate(
        [rotate_rows(keyval_linear[:HD], cosine[:, :128], sine[:, :128]), keyval_linear[HD:]]
    ).astype(bf16)
    half_keyvals = sent_to_all(own_keyvals, CTX)
    row_keyvals = jnp.concatenate([half_keyvals, core_swap(half_keyvals)])
    query_linear = heads_on_lanes(contract_last(w_query, normed_low))
    queries = rotate_rows(query_linear, cosine_4, sine_4).astype(bf16) * jnp.asarray(
        1.0 / math.sqrt(HD), bf16
    )
    attended, log_total = attend(spans, own_places, queries, row_keyvals)
    attended_rows = heads_on_rows(attended)
    stream_mid = stream_in + scatter_tp(
        contract_first(attended_rows, w_out).reshape(2, N_X, SHARD, D)
    )

    inner_low = gather_tp(rms_norm(stream_mid, gains[1]).astype(bf16))
    both = contract_last(inner_low, gate_up)
    gate, upward = (both[:, :ff_here], both[:, ff_here:])
    sigmoid_gate = jax.nn.sigmoid(gate)
    silu_gate = gate * sigmoid_gate
    hidden_low = (silu_gate * upward).astype(bf16)
    stream_out = stream_mid + scatter_tp(
        contract(hidden_low, down).reshape(2, N_X, SHARD, D)
    )

    feed_tables = feed_master.transpose(0, 2, 1)
    masters = (tables, feed_tables, attention_master, key_value_master, gain_master.T)
    masters, inner_low = lax.optimization_barrier((masters, inner_low))
    weight_sums = weight_squares(*masters)
    finals_low = gather_tp(rms_norm(stream_out, gains[2]).astype(bf16))
    weight_sums, finals_low = lax.optimization_barrier((weight_sums, finals_low))
    local_targets = own_order(target_ids, xs, cs).reshape(1, -1) - first_id
    logits, stats = logits_and_stats(finals_low, head, local_targets)
    stats = stats[:3].reshape(3, 2, N_X, SHARD)
    stats = combine_stats(stats, core_swap(stats)[:, ::-1])
    others = [jnp.roll(x_from(stats, d), d, axis=2) for d in range(1, N_X)]
    stats = combine_stats(combine_stats(stats, others[0]), combine_stats(others[1], others[2]))
    stats = stats.reshape(3, -1)
    vocab_total = stats[0] + jnp.log(stats[1])
    keep = own_order(loss_mask, xs, cs).reshape(-1).astype(f32)
    loss_part = jnp.sum((keep * (vocab_total - stats[2]))[:SHARD]) / TOKENS

    place = jnp.stack([vocab_total, keep / TOKENS])
    head_low, dlogits_low = head_grads(logits, finals_low, place, local_targets)
    head_low = lax.psum_scatter(head_low, CTX, scatter_dimension=0, tiled=True)[0]
    final_part = place_grads_of(dlogits_low, head)
    final_grad = scatter_tp(final_part.reshape(2, N_X, SHARD, D))
    out_grad, final_gain_grad = jax.vjp(rms_norm, stream_out, gains[2])[1](final_grad)
    branch_low = gather_tp(out_grad.astype(bf16))
    hidden_grad = contract_last(branch_low, down)
    gate_grad_low = (
        hidden_grad * upward * sigmoid_gate * (1.0 + gate * (1.0 - sigmoid_gate))
    ).astype(bf16)
    upward_grad_low = (hidden_grad * silu_gate).astype(bf16)
    both_grad_low = jnp.concatenate([gate_grad_low, upward_grad_low], axis=1)
    inner_grad = scatter_tp(contract(both_grad_low, gate_up).reshape(2, N_X, SHARD, D))
    mid_part, middle_gain_grad = jax.vjp(rms_norm, stream_mid, gains[1])[1](inner_grad)
    mid_grad = out_grad + mid_part
    attend_low = gather_tp(mid_grad.astype(bf16))
    attended_grad = heads_on_lanes(contract_last(w_out, attend_low).astype(bf16))
    dq, pair_grads = attend_back(
        spans, own_places, queries, attended_grad, log_total, row_keyvals
    )
    pair_grads = pair_grads.reshape(2, N_CTX, 128, 2 * HD)
    half_grads = (pair_grads[0] + core_swap(pair_grads[1].astype(bf16)).astype(f32)).astype(bf16)
    query_linear_low = heads_on_rows(rotate_rows(dq, cosine_4, -sine_4).astype(bf16))
    half_grads, both_low = lax.optimization_barrier((half_grads, both_grad_low))
    came = lax.all_to_all(half_grads, CTX, 0, 0, tiled=True)
    layer_low = row_products(
        [inner_low, attend_low, branch_low, normed_low],
        [both_low, attended_rows, hidden_low, query_linear_low],
    )
    own_grads = jnp.sum(came.astype(f32), axis=0)
    keyval_low = jnp.concatenate(
        [
            rotate_lanes(own_grads[:, :HD], cosine[:, :128].T, -sine[:, :128].T),
            own_grads[:, HD:],
        ],
        axis=1,
    ).astype(bf16)
    normed_part = contract_first(query_linear_low, w_query).reshape(2, 128, D)
    normed_part = jnp.stack([normed_part[0] + contract_last(keyval_low, w_pair), normed_part[1]])
    layer_low, head_low = lax.optimization_barrier((layer_low, head_low))
    layer_low = lax.psum_scatter(layer_low, CTX, scatter_dimension=0, tiled=True)[0]
    normed_grad = scatter_tp(normed_part.reshape(2, N_X, SHARD, D))
    pair_low = contract_first(keyval_low, normed_half).astype(bf16)
    pair_low = pair_low.reshape(2 * HD, N_CTX, LINES).transpose(1, 0, 2)
    first_part, first_gain_grad = jax.vjp(rms_norm, stream_in, gains[0])[1](normed_grad)
    input_low = (mid_grad + first_part).astype(bf16)

    gain_parts = jnp.stack([first_gain_grad, middle_gain_grad, final_gain_grad]).astype(bf16)
    sent = jnp.concatenate(
        [
            input_low.reshape(SHARD, N_CTX, LINES).transpose(1, 0, 2),
            jnp.pad(gain_parts.reshape(3, N_CTX, LINES).transpose(1, 0, 2), ((0, 0), (0, 13), (0, 0))),
            pair_low,
        ],
        axis=1,
    )
    arrived = lax.all_to_all(sent, CTX, 0, 0, tiled=True)
    head_part, head_line, head_columns = head_figures(head_low)
    arrived, head_part = lax.optimization_barrier((arrived, head_part))
    kv_part = jnp.sum(arrived[:, 48:].astype(f32), axis=0)
    gain_sums = jnp.sum(arrived[:, SHARD : SHARD + 3].astype(f32), axis=0)
    own_column = tp_column(arrived[:, :SHARD].reshape(N_CTX * SHARD, LINES))
    embed_grad = add_up(all_ids, own_column, core_swap(own_column), vocab_here)

    kv_full = kv_part + core_swap(kv_part)
    kv_split, embed_grad = lax.optimization_barrier(
        (kv_full.T.reshape(N_X, 2, 16, 2 * HD), embed_grad)
    )
    kv_owned = swapped_x(jnp.where(cs == 0, kv_split[:, 0], kv_split[:, 1]), xs)
    key_value_grad = (
        kv_owned.reshape(KV_HEADS, 16, 2, HD).transpose(1, 2, 0, 3).reshape(16, KVW)
    )

    old_rows = jnp.concatenate(
        [attention_row_moment, feed_row_moment, vocab_row_moment, jnp.ones((9, LINES), f32)]
    )
    kv_old_columns = lax.dynamic_index_in_dim(
        key_value_column_moment.reshape(2, KV_HEADS, HD), xs, 1, keepdims=False
    ).reshape(-1)
    gap = jnp.ones((96,), f32)
    early_old = jnp.concatenate(
        [vocab_column_moment[0], gap, vocab_column_moment[1], gap, kv_old_columns]
    )[None]
    late_old = jnp.concatenate(
        [
            feed_column_moment[0],
            feed_column_moment[1],
            attention_column_moment[1],
            feed_column_moment[2],
            attention_column_moment[0],
            gap[:64],
        ]
    )[None]
    kv_old_line = lax.dynamic_update_slice_in_dim(
        jnp.zeros((1, LINES), f32), key_value_row_moment[None], tp_index * 16, 1
    )
    vocab_grad, line_parts, column_parts = early_figures(
        head_part, embed_grad, kv_full, gain_sums, kv_old_line, head_line, head_columns
    )
    columns = lax.all_to_all(column_parts, CTX, 0, 0, tiled=True)
    lines = sum_tp(line_parts)
    gain_grad = lax.dynamic_slice_in_dim(lines[8:11], tp_index * 16, 16, 1)
    gain_second = moments(gain_moment.T, gain_grad * gain_grad, 1.0)
    gain_step = gain_grad * lax.rsqrt(gain_second)
    gain_squares = jnp.sum(gain_step * gain_step, axis=1)
    base = weight_sums + jnp.concatenate(
        [
            jnp.zeros((UG_LANE,), f32),
            gain_squares,
            loss_part.reshape(1),
            jnp.zeros((127 - LOSS_LANE,), f32),
        ]
    )
    early_rows, early_columns, vocab_unit, base = step_squares(
        early_squares_kernel,
        [(16, LINES), (1, EARLY_LANES), vocab_grad.shape, (1, 128)],
        vocab_grad,
        kv_full,
        lines,
        columns,
        old_rows,
        early_old,
        base,
    )
    feed_grad, attention_grad, line_parts, column_parts = late_figures(layer_low)
    columns = lax.all_to_all(column_parts, CTX, 0, 0, tiled=True)
    lines = sum_tp(line_parts)
    late_rows, late_columns, feed_unit, attention_unit, packed = step_squares(
        late_squares_kernel,
        [(8, LINES), (1, LATE_LANES), feed_grad.shape, attention_grad.shape, (128, 2, 128)],
        layer_low,
        lines,
        columns,
        old_rows,
        late_old,
        base,
        early_columns[:, 8192:],
    )
    gathered = lax.all_to_all(packed, CTX_TP, 0, 0, tiled=True)
    vocab_new, feed_new, attention_new, gain_new, figures = update(
        gathered[:, 0],
        tables,
        vocab_unit,
        feed_tables,
        feed_unit,
        attention_master,
        attention_unit,
        gain_master.T,
        gain_step,
    )
    token_loss = figures[2, 0]
    update_rms = figures[0, :11]
    kv_row_new = lax.dynamic_slice_in_dim(early_rows[7], tp_index * 16, 16, 0)
    kv_column_new = (
        gathered[0:8:2, 1].reshape(KV_HEADS, 2, HD).transpose(1, 0, 2).reshape(KVW)
    )
    kv_step = key_value_grad * lax.rsqrt(kv_row_new)[:, None] * lax.rsqrt(kv_column_new)[None]
    kv_new = key_value_master - figures[1, 7] * kv_step
    def columns_of(k):
        at, width = COLUMN_AT[k]
        return (early_columns if k > 4 else late_columns)[0, at : at + width]

    attention_columns = jnp.stack([columns_of(0), columns_of(1)])
    feed_columns = jnp.stack([columns_of(2), columns_of(3), columns_of(4)])
    return (
        token_loss,
        update_rms,
        attention_grad,
        late_rows[0:2],
        attention_columns,
        attention_new,
        feed_grad.transpose(0, 2, 1),
        late_rows[2:5],
        feed_columns,
        feed_new.transpose(0, 2, 1),
        vocab_grad.transpose(0, 2, 1),
        early_rows[5:7],
        columns_of(5),
        columns_of(6),
        vocab_new.transpose(0, 2, 1),
        key_value_grad,
        kv_row_new,
        kv_column_new,
        kv_new,
        gain_grad.T,
        gain_second.T,
        gain_new.T,
    )


def solution(mesh):
    finer = Mesh(mesh.devices.reshape(4, 4, 4, 2), ("ctx_0", "ctx_1", "tp_0", "tp_1"))
    in_specs = (
        P(CTX),
        P(CTX),
        P(CTX),
        P(),
        P(),
        P(None, CTX, TP),
        P(None, CTX, TP),
        P(None, CTX, TP),
        P(CTX_TP, None),
        P(CTX_TP, None),
        P(None, CTX),
        P(None, TP),
        P(None, CTX),
        P(None, TP),
        P(None, CTX),
        P(None, TP),
        P(CTX_TP),
        P(),
        P(CTX_TP, None),
    )
    out_specs = (
        P(),
        P(),
        P(None, CTX, TP),
        P(None, CTX),
        P(None, TP),
        P(None, CTX, TP),
        P(None, CTX, TP),
        P(None, CTX),
        P(None, TP),
        P(None, CTX, TP),
        P(None, CTX, TP),
        P(None, CTX),
        P(TP),
        P(TP),
        P(None, CTX, TP),
        P(CTX_TP, None),
        P(CTX_TP),
        P(),
        P(CTX_TP, None),
        P(CTX_TP, None),
        P(CTX_TP, None),
        P(CTX_TP, None),
    )
    return jax.shard_map(body, mesh=finer, in_specs=in_specs, out_specs=out_specs, check_vma=False)
```

```python
import functools
import math

import jax
import jax.numpy as jnp
from jax import lax
from jax.experimental import pallas as pl
from jax.experimental.pallas import tpu as pltpu
from jax.sharding import Mesh
from jax.sharding import PartitionSpec as P

D = 2048
HEADS = 32
KV_HEADS = 4
HD = 64
FF = 5632
VOCAB = 32000
ORIG_CTX = 2048
HQ = 2048
KVW = 512
TOKENS = 4096
TP = ("tp_0", "tp_1")
CTX = ("ctx_0", "ctx_1")
CTX_TP = ("ctx_0", "ctx_1", "tp_0", "tp_1")
N_CTX = 16
N_X = 4
N_TP = 8
SHARD = 32
LINES = 128
DOCS = 5

NORM_EPS = 1e-05
MOMENT_DECAY = 0.5
MOMENT_EPS = 1e-30
CLIP_LIMIT = 0.5
STEP_SCALE = 1.0
ROPE_BASE = 10000.0
YARN_SCALE = 4.0
YARN_ALPHA = 1.0
YARN_BETA = 32.0

bf16 = jnp.bfloat16
f32 = jnp.float32


def x_from(values, step):
    return lax.ppermute(values, "tp_0", [((i + step) % N_X, i) for i in range(N_X)])


def x_to(values, step):
    return lax.ppermute(values, "tp_0", [(i, (i + step) % N_X) for i in range(N_X)])


def core_swap(values):
    return lax.ppermute(values, "tp_1", [(0, 1), (1, 0)])


def turned(stack, start):
    return lax.dynamic_slice_in_dim(jnp.concatenate([stack, stack]), start, N_X, 0)


def to_absolute(stack, xs):
    return turned(stack, (N_X - xs) % N_X)


def tp_column(shard):
    return jnp.concatenate([shard] + [x_from(shard, d) for d in range(1, N_X)])


def gather_tp(shard):
    column = tp_column(shard)
    return jnp.concatenate([column, core_swap(column)])


def scatter_tp(partial):
    half = partial[0] + core_swap(partial[1].astype(bf16)).astype(f32)
    low = half.astype(bf16)
    total = half[0]
    for d in range(1, N_X):
        total = total + x_to(low[d], d).astype(f32)
    return total


def both_cores(column, cs):
    other = core_swap(column)
    both = jnp.where(
        cs == 0, jnp.stack([column, other], axis=1), jnp.stack([other, column], axis=1)
    )
    return both.reshape(-1, *column.shape[2:])


def swapped_x(blocks, xs):
    ours = turned(blocks, xs)
    came = [ours[0]] + [x_to(ours[d], d) for d in range(1, N_X)]
    return to_absolute(jnp.stack([came[0], came[3], came[2], came[1]]), xs)


def partner(values, axis, mask):
    size = 2 if axis == "tp_1" else 4
    return lax.ppermute(values, axis, [(i, i ^ mask) for i in range(size)])


def sum_over_four(values, axis):
    return (values + partner(values, axis, 1)) + (
        partner(values, axis, 2) + partner(values, axis, 3)
    )


def sum_tp(values):
    return sum_over_four(values + partner(values, "tp_1", 1), "tp_0")


def sum_ctx(values):
    return sum_over_four(sum_over_four(values, "ctx_1"), "ctx_0")


def own_order(values, xs, cs):
    blocks = turned(values.reshape(N_X, 2, SHARD), xs)
    blocks = jnp.where(cs == 0, blocks, blocks[:, ::-1])
    return blocks.transpose(1, 0, 2)


def sent_to_all(array, axis):
    copies = jnp.broadcast_to(array, (lax.axis_size(axis), *array.shape))
    return lax.all_to_all(copies, axis, split_axis=0, concat_axis=0, tiled=True)


def rope_tables(positions):
    ladder = jnp.arange(HD // 2, dtype=f32)
    freqs = ROPE_BASE ** (-2.0 * ladder / HD)
    ratio = ORIG_CTX * freqs / (2.0 * math.pi)
    ramped = jnp.clip((ratio - YARN_ALPHA) / (YARN_BETA - YARN_ALPHA), 0.0, 1.0)
    inverse = freqs * (1.0 - ramped) / YARN_SCALE + freqs * ramped
    angles = inverse[:, None] * positions.astype(f32)[None, :]
    mscale = 0.1 * math.log(YARN_SCALE) + 1.0
    return (jnp.cos(angles) * mscale, jnp.sin(angles) * mscale)


def rotate_rows(values, cosine, sine):
    half = values.shape[0] // 2
    first, second = (values[:half], values[half:])
    return jnp.concatenate([first * cosine - second * sine, second * cosine + first * sine])


def rotate_lanes(values, cosine, sine):
    half = values.shape[1] // 2
    first, second = (values[:, :half], values[:, half:])
    return jnp.concatenate([first * cosine - second * sine, second * cosine + first * sine], axis=1)


def rms_norm(values, gain):
    return values * lax.rsqrt(jnp.mean(values * values, axis=-1, keepdims=True) + NORM_EPS) * gain


def contract_last(left, right):
    return lax.dot_general(left, right, (((1,), (1,)), ((), ())), preferred_element_type=f32)


def contract_first(left, right):
    return lax.dot_general(left, right, (((0,), (0,)), ((), ())), preferred_element_type=f32)


def contract(left, right):
    return jnp.dot(left, right, preferred_element_type=f32)


def combine_stats(former, latter):
    highest = jnp.maximum(former[0], latter[0])
    summed = former[1] * jnp.exp(former[0] - highest) + latter[1] * jnp.exp(latter[0] - highest)
    return jnp.stack([highest, summed, former[2] + latter[2]])


def contract_ft(weights, places):
    return lax.dot_general(weights, places, (((0,), (1,)), ((), ())), preferred_element_type=f32)


def contract_tf(features, weights):
    return lax.dot_general(features, weights, (((0,), (1,)), ((), ())), preferred_element_type=f32)


def heads_on_lanes(features):
    return jnp.concatenate([features[h * HD : (h + 1) * HD] for h in range(4)], axis=1)


def heads_on_rows(features):
    return jnp.concatenate(jnp.split(features, 4, axis=1))


VMEM_LIMIT = 50 * 1024 * 1024


GROUP = 4
KEYS = 128 * GROUP
STEPS = TOKENS // KEYS


def key_places(core_bit, spans):
    line = lax.broadcasted_iota(jnp.int32, (128, 1), 0)
    x = (spans[N_CTX] + line // SHARD) % N_X
    place = (x * 2 + (spans[N_CTX + 1] ^ core_bit)) * SHARD + line % SHARD
    return place >= 128, place % 128


def visible_keys(spans, places, step, own, start):
    lines = []
    for block in range(step * GROUP, (step + 1) * GROUP):
        span = spans[block % N_CTX]
        second, within = places[block // N_CTX]
        lines.append(jnp.where(second, (2 * N_CTX - 1 - span) * 128, span * 128) + within)
    at = jnp.concatenate(lines, axis=0)
    return (at >= start) & (at <= own)


def key_columns(kv_ref, step, at):
    return jnp.concatenate(
        [kv_ref[step * GROUP + i, at : at + HD] for i in range(GROUP)], axis=1
    )


def attend_kernel(spans, own_ref, q_ref, kv_ref, o_ref, total_ref, s_ref):
    q = q_ref[...]
    own, start = (own_ref[0:1], own_ref[1:2])
    places = [key_places(core_bit, spans) for core_bit in range(2)]
    top = None
    for step in range(STEPS):
        scores = contract_first(key_columns(kv_ref, step, 0), q)
        scores = jnp.where(visible_keys(spans, places, step, own, start), scores, -1e30)
        s_ref[step * KEYS : (step + 1) * KEYS] = scores
        highest = jnp.max(scores, axis=0, keepdims=True)
        top = highest if top is None else jnp.maximum(top, highest)
    total = jnp.zeros(top.shape, f32)
    for step in range(STEPS):
        powers = jnp.exp(s_ref[step * KEYS : (step + 1) * KEYS] - top)
        s_ref[step * KEYS : (step + 1) * KEYS] = powers
        total = total + jnp.sum(powers, axis=0, keepdims=True)
    share = 1.0 / total
    out = jnp.zeros(q.shape, f32)
    for step in range(STEPS):
        weights = (s_ref[step * KEYS : (step + 1) * KEYS] * share).astype(bf16)
        out = out + contract(key_columns(kv_ref, step, HD), weights)
    o_ref[...] = out.astype(bf16)
    total_ref[...] = top + jnp.log(total)


SPLIT = 2


def attend(spans, own, q, kv):
    lanes = q.shape[1] // SPLIT
    column = lambda rows: pl.BlockSpec((rows, lanes), lambda i: (0, i))
    return pl.pallas_call(
        attend_kernel,
        grid=(SPLIT,),
        in_specs=[
            pl.BlockSpec(memory_space=pltpu.SMEM),
            column(2),
            column(HD),
            pl.BlockSpec(kv.shape, lambda i: (0, 0, 0)),
        ],
        out_specs=[column(HD), column(1)],
        out_shape=[
            jax.ShapeDtypeStruct(q.shape, bf16),
            jax.ShapeDtypeStruct((1, q.shape[1]), f32),
        ],
        scratch_shapes=[pltpu.VMEM((TOKENS, lanes), f32)],
        compiler_params=pltpu.CompilerParams(vmem_limit_bytes=VMEM_LIMIT),
        cost_estimate=pl.CostEstimate(
            flops=16 * TOKENS * q.shape[1] * HD, bytes_accessed=2 << 20, transcendentals=0
        ),
    )(spans, own, q, kv)


def attend_back_kernel(
    spans, own_ref, q_ref, do_ref, total_ref, kv_ref, dq_ref, dkv_ref, p_ref, dp_ref
):
    q, do = (q_ref[...], do_ref[...])
    own, start = (own_ref[0:1], own_ref[1:2])
    total = total_ref[...]
    places = [key_places(core_bit, spans) for core_bit in range(2)]
    rowsum = jnp.zeros(total.shape, f32)
    for step in range(STEPS):
        scores = contract_first(key_columns(kv_ref, step, 0), q)
        scores = jnp.where(visible_keys(spans, places, step, own, start), scores, -1e30)
        probs = jnp.exp(scores - total)
        probs_grad = contract_first(key_columns(kv_ref, step, HD), do)
        p_ref[step * KEYS : (step + 1) * KEYS] = probs
        dp_ref[step * KEYS : (step + 1) * KEYS] = probs_grad
        rowsum = rowsum + jnp.sum(probs * probs_grad, axis=0, keepdims=True)

    @pl.when(pl.program_id(0) == 0)
    def _():
        dkv_ref[...] = jnp.zeros(dkv_ref.shape, f32)

    dq = jnp.zeros(q.shape, f32)
    for step in range(STEPS):
        rows = slice(step * KEYS, (step + 1) * KEYS)
        probs = p_ref[rows]
        score_grad = (probs * (dp_ref[rows] - rowsum)).astype(bf16)
        dkv_ref[rows] += jnp.concatenate(
            [contract_last(score_grad, q), contract_last(probs.astype(bf16), do)], axis=1
        )
        dq = dq + contract(key_columns(kv_ref, step, 0), score_grad)
    dq_ref[...] = dq * (1.0 / math.sqrt(HD))


def attend_back(spans, own, q, do, total, kv):
    lanes = q.shape[1] // SPLIT
    column = lambda rows: pl.BlockSpec((rows, lanes), lambda i: (0, i))
    return pl.pallas_call(
        attend_back_kernel,
        grid=(SPLIT,),
        in_specs=[
            pl.BlockSpec(memory_space=pltpu.SMEM),
            column(2),
            column(HD),
            column(HD),
            column(1),
            pl.BlockSpec(kv.shape, lambda i: (0, 0, 0)),
        ],
        out_specs=[column(HD), pl.BlockSpec((TOKENS, 2 * HD), lambda i: (0, 0))],
        out_shape=[
            jax.ShapeDtypeStruct(q.shape, f32),
            jax.ShapeDtypeStruct((TOKENS, 2 * HD), f32),
        ],
        scratch_shapes=[pltpu.VMEM((TOKENS, lanes), f32), pltpu.VMEM((TOKENS, lanes), f32)],
        compiler_params=pltpu.CompilerParams(vmem_limit_bytes=VMEM_LIMIT),
        cost_estimate=pl.CostEstimate(
            flops=40 * TOKENS * q.shape[1] * HD, bytes_accessed=4 << 20, transcendentals=0
        ),
    )(spans, own, q, do, total, kv)


def moments(old, sums, count):
    return MOMENT_DECAY * old + (1.0 - MOMENT_DECAY) * (sums / count + MOMENT_EPS)


def params():
    return pltpu.CompilerParams(vmem_limit_bytes=VMEM_LIMIT)


def whole(array):
    zeros = (0,) * array.ndim
    return pl.BlockSpec(array.shape, lambda *i: zeros)


def cost(flops, moved):
    return pl.CostEstimate(flops=flops, bytes_accessed=moved, transcendentals=0)


ID_STEP = 2048


def look_kernel(ids_ref, table_ref, out_ref, low_ref):
    @pl.when(pl.program_id(0) == 0)
    def _():
        low_ref[...] = table_ref[0].astype(bf16)

    width = low_ref.shape[0]
    ids = jnp.transpose(jnp.broadcast_to(ids_ref[...], (8, ID_STEP)))[:, :1]
    hits = ids == lax.broadcasted_iota(jnp.int32, (ID_STEP, width), 1)
    out_ref[...] = contract(jnp.where(hits, 1.0, 0.0).astype(bf16), low_ref[...]).astype(bf16)


def look_up(ids, tables):
    width, lines = tables.shape[1:]
    count = ids.shape[1]
    return pl.pallas_call(
        look_kernel,
        grid=(count // ID_STEP,),
        in_specs=[
            pl.BlockSpec((1, ID_STEP), lambda i: (0, i)),
            pl.BlockSpec((1, width, lines), lambda i: (1, 0, 0)),
        ],
        out_specs=pl.BlockSpec((ID_STEP, lines), lambda i: (i, 0)),
        out_shape=jax.ShapeDtypeStruct((count, lines), bf16),
        scratch_shapes=[pltpu.VMEM((width, lines), bf16)],
        compiler_params=params(),
        cost_estimate=cost(4 * count * width * lines, 4 * lines * width),
    )(ids, tables)


def add_kernel(ids_ref, own_ref, other_ref, out_ref):
    hits = lax.broadcasted_iota(jnp.int32, (out_ref.shape[0], ID_STEP), 0) == ids_ref[...]
    first = pl.program_id(0) == 0
    grads = jnp.where(first, own_ref[...], other_ref[...])
    added = contract(jnp.where(hits, 1.0, 0.0).astype(bf16), grads)

    @pl.when(first)
    def _():
        out_ref[...] = added

    @pl.when(jnp.logical_not(first))
    def _():
        out_ref[...] += added


def add_up(ids, own, other, width):
    lines = own.shape[1]
    return pl.pallas_call(
        add_kernel,
        grid=(2,),
        in_specs=[pl.BlockSpec((1, ID_STEP), lambda i: (0, i)), whole(own), whole(other)],
        out_specs=pl.BlockSpec((width, lines), lambda i: (0, 0)),
        out_shape=jax.ShapeDtypeStruct((width, lines), f32),
        compiler_params=params(),
        cost_estimate=cost(8 * ID_STEP * width * lines, 4 * lines * width),
    )(ids, own, other)


LOGIT_STEP = 800
TABLE_STEP = 2000


def joined(ref):
    return jnp.concatenate([ref[k] for k in range(N_CTX)], axis=1)


def logits_kernel(c_ref, w_ref, target_ref, out_ref, stats_ref):
    step = pl.program_id(0)
    logits = contract_last(joined(w_ref), c_ref[...])
    out_ref[...] = logits
    row = lax.broadcasted_iota(jnp.int32, logits.shape, 0) + step * TABLE_STEP
    here = jnp.max(logits, axis=0, keepdims=True)
    pick = jnp.sum(jnp.where(row == target_ref[...], logits, 0.0), axis=0, keepdims=True)

    @pl.when(step == 0)
    def _():
        stats_ref[...] = jnp.zeros(stats_ref.shape, f32)
        stats_ref[0:1] = here

    old = stats_ref[0:1]
    top = jnp.maximum(old, here)
    powers = jnp.sum(jnp.exp(logits - top), axis=0, keepdims=True)
    stats_ref[1:2] = stats_ref[1:2] * jnp.exp(old - top) + powers
    stats_ref[2:3] += pick
    stats_ref[0:1] = top


def logits_and_stats(c, head, targets):
    places, rows = c.shape
    width = head.shape[1]
    return pl.pallas_call(
        logits_kernel,
        grid=(width // TABLE_STEP,),
        in_specs=[
            whole(c),
            pl.BlockSpec((N_CTX, TABLE_STEP, 128), lambda i: (0, i, 0)),
            whole(targets),
        ],
        out_specs=[
            pl.BlockSpec((TABLE_STEP, places), lambda i: (i, 0)),
            pl.BlockSpec((8, places), lambda i: (0, 0)),
        ],
        out_shape=[
            jax.ShapeDtypeStruct((width, places), f32),
            jax.ShapeDtypeStruct((8, places), f32),
        ],
        compiler_params=params(),
        cost_estimate=cost(2 * places * rows * width, 2 * rows * width),
    )(c, head, targets)


def head_grad_kernel(logits_ref, c_ref, place_ref, target_ref, dw_ref, low_ref):
    step = pl.program_id(0)
    logits = logits_ref[...]
    row = lax.broadcasted_iota(jnp.int32, logits.shape, 0) + step * LOGIT_STEP
    hit = row == target_ref[...]
    shares = jnp.exp(logits - place_ref[0:1]) - jnp.where(hit, 1.0, 0.0)
    low = (place_ref[1:2] * shares).astype(bf16)
    low_ref[...] = low
    grad = contract(low, c_ref[...]).astype(bf16)
    for k in range(N_CTX):
        dw_ref[k] = grad[:, k * 128 : (k + 1) * 128]


def head_grads(logits, c, place, targets):
    places, rows = c.shape
    width = logits.shape[0]
    block = pl.BlockSpec((LOGIT_STEP, places), lambda i: (i, 0))
    return pl.pallas_call(
        head_grad_kernel,
        grid=(width // LOGIT_STEP,),
        in_specs=[block, whole(c), whole(place), whole(targets)],
        out_specs=[pl.BlockSpec((N_CTX, LOGIT_STEP, 128), lambda i: (0, i, 0)), block],
        out_shape=[
            jax.ShapeDtypeStruct((N_CTX, width, 128), bf16),
            jax.ShapeDtypeStruct((width, places), bf16),
        ],
        compiler_params=params(),
        cost_estimate=cost(2 * places * rows * width, 2 * rows * width),
    )(logits, c, place, targets)


def place_grad_kernel(low_ref, w_ref, out_ref):
    part = contract_first(low_ref[...], joined(w_ref))

    @pl.when(pl.program_id(0) == 0)
    def _():
        out_ref[...] = part

    @pl.when(pl.program_id(0) > 0)
    def _():
        out_ref[...] += part


def place_grads_of(low, head):
    width, places = low.shape
    return pl.pallas_call(
        place_grad_kernel,
        grid=(width // TABLE_STEP,),
        in_specs=[
            pl.BlockSpec((TABLE_STEP, places), lambda i: (i, 0)),
            pl.BlockSpec((N_CTX, TABLE_STEP, 128), lambda i: (0, i, 0)),
        ],
        out_specs=pl.BlockSpec((places, D), lambda i: (0, 0)),
        out_shape=jax.ShapeDtypeStruct((places, D), f32),
        compiler_params=params(),
        cost_estimate=cost(2 * places * D * width, 2 * D * width),
    )(low, head)


TURNED = (1, 3)


def products_kernel(count, offsets, *refs):
    lefts, rights = (refs[:count], refs[count : 2 * count])
    out_ref, turned_ref = refs[2 * count :]

    @pl.when(pl.program_id(0) == 0)
    def _():
        for k, (right, (at, width)) in enumerate(zip(rights, offsets)):
            values = right[...]
            turned_ref[at : at + width] = values if k in TURNED else jnp.transpose(values)

    for left, (at, width) in zip(lefts, offsets):
        grad = contract(turned_ref[at : at + width], left[...]).astype(bf16)
        for k in range(2):
            out_ref[k, at : at + width] = grad[:, k * 128 : (k + 1) * 128]


def row_products(lefts, rights):
    places, rows = lefts[0].shape
    offsets, at = ([], 0)
    for k, right in enumerate(rights):
        width = right.shape[0 if k in TURNED else 1]
        offsets.append((at, width))
        at += width
    return pl.pallas_call(
        functools.partial(products_kernel, len(lefts), tuple(offsets)),
        grid=(N_CTX // 2,),
        in_specs=[pl.BlockSpec((places, 256), lambda i: (0, i)) for _ in lefts]
        + [whole(right) for right in rights],
        out_specs=pl.BlockSpec((2, at, 128), lambda i: (i, 0, 0)),
        out_shape=jax.ShapeDtypeStruct((N_CTX, at, rows // N_CTX), bf16),
        scratch_shapes=[pltpu.VMEM((at, places), bf16)],
        compiler_params=params(),
        cost_estimate=cost(2 * places * rows * at, 2 * rows * at),
    )(*lefts, *rights)


MATRICES = 8
WIDTHS = (HQ, HQ, FF, FF, FF, VOCAB, VOCAB, KVW)
EARLY_LANES = 8320
LATE_LANES = 2688
COLUMN_AT = {5: (0, 4000), 6: (4096, 4000), 7: (8192, 128)}
COLUMN_AT.update({2: (0, 704), 3: (704, 704), 1: (1408, 256), 4: (1664, 704), 0: (2368, 256)})
S_LANE, T_LANE, OLD_LANE, W_LANE, WG_LANE, UG_LANE, LOSS_LANE = (0, 8, 16, 24, 32, 35, 38)


def lane_is(shape, lane):
    return lax.broadcasted_iota(jnp.int32, shape, 1) == lane


def line_sum(values):
    return jnp.sum(values, axis=0, keepdims=True)


def total_of(values):
    return jnp.sum(line_sum(values), axis=1, keepdims=True)


def column_sums(squares):
    ones = jnp.ones((8, squares.shape[1]), f32)
    return lax.dot_general(
        ones,
        squares,
        (((1,), (1,)), ((), ())),
        precision=lax.Precision.HIGHEST,
        preferred_element_type=f32,
    )


def weights_kernel(tables_ref, feed_ref, attention_ref, kv_master_ref, gain_ref, scalars_ref):
    scalars = jnp.zeros(scalars_ref.shape, f32)
    for number, weights in (
        (0, attention_ref[0]),
        (1, attention_ref[1]),
        (2, feed_ref[0]),
        (3, feed_ref[1]),
        (4, feed_ref[2]),
        (5, tables_ref[0]),
        (6, tables_ref[1]),
        (7, kv_master_ref[...]),
        (8, gain_ref[0:1]),
        (9, gain_ref[1:2]),
        (10, gain_ref[2:3]),
    ):
        scalars += jnp.where(
            lane_is(scalars.shape, W_LANE + number), total_of(weights * weights), 0.0
        )
    scalars_ref[...] = scalars


def weight_squares(*masters):
    return pl.pallas_call(
        weights_kernel,
        out_shape=jax.ShapeDtypeStruct((1, 128), f32),
        compiler_params=params(),
        cost_estimate=cost(0, 6 << 20),
    )(*masters)


def head_kernel(head_ref, grad_ref, line_ref, columns_ref):
    grad = head_ref[...].astype(f32)
    grad_ref[0] = grad
    squares = grad * grad
    line_ref[...] = line_sum(squares)
    columns_ref[...] = jnp.concatenate(
        [column_sums(squares)[:1], jnp.zeros((1, 96), f32)], axis=1
    )


def head_figures(head_low):
    width, lines = head_low.shape
    return pl.pallas_call(
        head_kernel,
        grid=(1,),
        in_specs=[whole(head_low)],
        out_specs=[
            pl.BlockSpec((1, width, lines), lambda i: (0, 0, 0)),
            pl.BlockSpec((1, lines), lambda i: (0, 0)),
            pl.BlockSpec((1, width + 96), lambda i: (0, 0)),
        ],
        out_shape=[
            jax.ShapeDtypeStruct((2, width, lines), f32),
            jax.ShapeDtypeStruct((1, lines), f32),
            jax.ShapeDtypeStruct((1, width + 96), f32),
        ],
        compiler_params=params(),
        cost_estimate=cost(0, 4 << 20),
    )(head_low)


def early_kernel(
    grads_ref, embed_ref, kv_ref, gains_ref, kv_old_ref, head_line_ref, head_columns_ref,
    vocab_grad_ref, lines_ref, columns_ref,
):
    lines_ref[...] = jnp.zeros(lines_ref.shape, f32)
    lines_ref[5:6] = head_line_ref[...]
    lines_ref[8:11] = gains_ref[...]
    lines_ref[11:12] = kv_old_ref[...]
    grad = embed_ref[...]
    vocab_grad_ref[0] = grad
    embed_squares = grad * grad
    lines_ref[6:7] = line_sum(embed_squares)
    kv_squares = kv_ref[...] * kv_ref[...]
    lines_ref[7:8] = 0.5 * line_sum(kv_squares)
    sums = jnp.concatenate(
        [
            head_columns_ref[...],
            column_sums(embed_squares)[:1],
            jnp.zeros((1, 96), f32),
            column_sums(kv_squares)[:1],
        ],
        axis=1,
    )
    columns_ref[...] = jnp.broadcast_to(sums[None], columns_ref.shape)


def early_figures(grads, *arrays):
    block = (1, *grads.shape[1:])
    columns = (N_CTX, 1, EARLY_LANES)
    return pl.pallas_call(
        early_kernel,
        grid=(1,),
        in_specs=[pl.BlockSpec(memory_space=pl.ANY)] + [whole(a) for a in arrays],
        out_specs=[
            pl.BlockSpec(block, lambda i: (1, 0, 0)),
            pl.BlockSpec((16, 128), lambda i: (0, 0)),
            pl.BlockSpec(columns, lambda i: (0, 0, 0)),
        ],
        out_shape=[
            jax.ShapeDtypeStruct(grads.shape, f32),
            jax.ShapeDtypeStruct((16, 128), f32),
            jax.ShapeDtypeStruct(columns, f32),
        ],
        input_output_aliases={0: 0},
        compiler_params=params(),
        cost_estimate=cost(0, 6 << 20),
    )(grads, *arrays)


def late_kernel(layer_ref, feed_grad_ref, attention_grad_ref, lines_ref, columns_ref):
    layer = layer_ref[...].astype(f32)
    squares = layer * layer
    sums = jnp.concatenate(
        [column_sums(squares)[:1], jnp.zeros((1, LATE_LANES - layer.shape[0]), f32)], axis=1
    )
    columns_ref[...] = jnp.broadcast_to(sums[None], columns_ref.shape)
    lines_ref[...] = jnp.zeros(lines_ref.shape, f32)
    for number in range(5):
        at, width = COLUMN_AT[number]
        lines_ref[number : number + 1] = line_sum(squares[at : at + width])
        if number > 1:
            feed_grad_ref[number - 2] = layer[at : at + width]
    attention_grad_ref[0] = jnp.transpose(layer[2368:2624])
    attention_grad_ref[1] = jnp.transpose(layer[1408:1664])


def late_figures(layer):
    shapes = ((3, 704, 128), (2, 128, 256), (8, 128), (N_CTX, 1, LATE_LANES))
    return pl.pallas_call(
        late_kernel,
        out_shape=[jax.ShapeDtypeStruct(shape, f32) for shape in shapes],
        compiler_params=params(),
        cost_estimate=cost(0, 4 << 20),
    )(layer)


def per_column(figures, number):
    at, width = COLUMN_AT[number]
    return figures[at : at + width, :1]


def on_rows(columns):
    spare = 8 - columns.shape[0]
    return jnp.transpose(
        jnp.concatenate([columns, jnp.ones((spare, columns.shape[1]), f32)], axis=0)
    )


def squares_of(sources, lines, old, columns, old_columns, scalars, row_ref, column_ref):
    number = lax.broadcasted_iota(jnp.int32, lines.shape, 0)
    widths = jnp.full(lines.shape, 1.0, f32)
    for k, width in enumerate(WIDTHS):
        widths = jnp.where(number == k, float(width), widths)
    row_new = moments(old, lines / widths, 1.0)
    row_ref[...] = row_new
    column_new = moments(old_columns, jnp.sum(columns, axis=0), float(D))
    column_ref[...] = column_new
    row_scale = lax.rsqrt(row_new)
    column_scale = on_rows(lax.rsqrt(column_new))
    had = jnp.sum(old, axis=1, keepdims=True) * (1.0 / N_TP)
    got = jnp.sum(lines, axis=1, keepdims=True) * (1.0 / N_TP)
    for k, grad, keep in sources:
        unit = grad * row_scale[k : k + 1] * per_column(column_scale, k)
        if keep is not None:
            keep[0][keep[1]] = jnp.transpose(unit) if k < 2 else unit
        part = total_of(unit * unit) * (0.5 if k == 7 else 1.0)
        scalars += jnp.where(lane_is(scalars.shape, S_LANE + k), part, 0.0)
        scalars += jnp.where(lane_is(scalars.shape, T_LANE + k), got[k : k + 1], 0.0)
        scalars += jnp.where(lane_is(scalars.shape, OLD_LANE + k), had[k : k + 1], 0.0)
    return scalars


def early_squares_kernel(
    vocab_ref, kv_ref, lines_ref, columns_ref, old_ref, old_columns_ref, base_ref,
    row_ref, column_ref, unit_ref, scalars_ref,
):
    lines = lines_ref[...]
    number = lax.broadcasted_iota(jnp.int32, lines.shape, 0)
    old = jnp.where(number == 7, lines_ref[11:12], old_ref[...])
    sources = (
        (5, vocab_ref[0], (unit_ref, 0)),
        (6, vocab_ref[1], (unit_ref, 1)),
        (7, kv_ref[...], None),
    )
    scalars_ref[...] = squares_of(
        sources, lines, old, columns_ref[...], old_columns_ref[...], base_ref[...],
        row_ref, column_ref,
    )


def late_squares_kernel(
    layer_ref, lines_ref, columns_ref, old_ref, old_columns_ref, base_ref, kv_columns_ref,
    row_ref, column_ref, feed_unit_ref, attention_unit_ref, packed_ref,
):
    sources = []
    for number in range(5):
        at, width = COLUMN_AT[number]
        keep = (attention_unit_ref, number) if number < 2 else (feed_unit_ref, number - 2)
        sources.append((number, layer_ref[at : at + width].astype(f32), keep))
    scalars = squares_of(
        sources, lines_ref[...], old_ref[0:8], columns_ref[...], old_columns_ref[...],
        base_ref[...], row_ref, column_ref,
    )
    packed = jnp.concatenate([scalars, kv_columns_ref[...]], axis=0)
    packed_ref[...] = jnp.broadcast_to(packed[None], packed_ref.shape)


def step_squares(kernel, shapes, *arrays):
    return pl.pallas_call(
        kernel,
        out_shape=[jax.ShapeDtypeStruct(shape, f32) for shape in shapes],
        compiler_params=params(),
        cost_estimate=cost(0, 12 << 20),
    )(*arrays)


UPDATE_STEP = 2000


def update_kernel(
    all_ref, vocab_ref, vocab_unit_ref, feed_ref, feed_unit_ref, attention_ref,
    attention_unit_ref, gain_ref, gain_step_ref,
    vocab_new_ref, feed_new_ref, attention_new_ref, gain_new_ref, figures_ref,
):
    sums = jnp.sum(all_ref[...], axis=0, keepdims=True)
    sums = jnp.broadcast_to(sums, (8, 128))

    def lanes_from(at):
        return pltpu.roll(sums, (128 - at) % 128, 1)[0:1]

    lane = lax.broadcasted_iota(jnp.int32, (1, 128), 1)
    counts = jnp.full((1, 128), float(D), f32)
    for k, width in enumerate(WIDTHS):
        counts = jnp.where(lane == k, float(D * width), counts)
    mean = MOMENT_DECAY * lanes_from(OLD_LANE) / D + (1.0 - MOMENT_DECAY) * (
        lanes_from(T_LANE) / counts + MOMENT_EPS
    )
    mean = jnp.where(lane < MATRICES, mean, 1.0)
    rms = jnp.sqrt(mean * lanes_from(S_LANE) / counts)
    factor = (
        STEP_SCALE
        * jnp.sqrt(lanes_from(W_LANE) / counts)
        / jnp.maximum(1.0, rms / CLIP_LIMIT)
        * jnp.sqrt(mean)
    )

    @pl.when(pl.program_id(0) == 0)
    def _():
        for k in range(2):
            attention_new_ref[k] = attention_ref[k] - attention_unit_ref[k] * factor[:, k : k + 1]
        for k in range(3):
            feed_new_ref[k] = feed_ref[k] - feed_unit_ref[k] * factor[:, 2 + k : 3 + k]
        gain_rms = jnp.sqrt(lanes_from(UG_LANE) / D)
        gain_factor = (
            STEP_SCALE
            * jnp.sqrt(lanes_from(WG_LANE) / D)
            / jnp.maximum(1.0, gain_rms / CLIP_LIMIT)
        )
        for k in range(3):
            gain_new_ref[k : k + 1] = (
                gain_ref[k : k + 1] - gain_factor[:, k : k + 1] * gain_step_ref[k : k + 1]
            )
        after = pltpu.roll(jnp.broadcast_to(gain_rms, (8, 128)), MATRICES, 1)[0:1]
        figures_ref[0:1] = jnp.where(lane < MATRICES, rms, after)
        figures_ref[1:2] = factor
        figures_ref[2:3] = lanes_from(LOSS_LANE)
        figures_ref[3:8] = jnp.zeros((5, 128), f32)

    for k in range(2):
        vocab_new_ref[k] = vocab_ref[k] - vocab_unit_ref[k] * factor[:, 5 + k : 6 + k]


def update(gathered, vocab, vocab_unit, feed, feed_unit, attention, attention_unit, gain, gain_step):
    stack = pl.BlockSpec((2, UPDATE_STEP, vocab.shape[2]), lambda i: (0, i, 0))
    others = (feed, feed_unit, attention, attention_unit, gain, gain_step)
    outs = (vocab, feed, attention, gain)
    return pl.pallas_call(
        update_kernel,
        grid=(vocab.shape[1] // UPDATE_STEP,),
        in_specs=[whole(gathered), stack, stack] + [whole(a) for a in others],
        out_specs=[stack]
        + [whole(a) for a in outs[1:]]
        + [pl.BlockSpec((8, 128), lambda i: (0, 0))],
        out_shape=[jax.ShapeDtypeStruct(a.shape, f32) for a in outs]
        + [jax.ShapeDtypeStruct((8, 128), f32)],
        compiler_params=params(),
        cost_estimate=cost(0, 24 << 20),
    )(gathered, vocab, vocab_unit, *others)


def body(
    token_ids,
    target_ids,
    loss_mask,
    segment_ids,
    span_pairs,
    attention_master,
    feed_master,
    vocab_master,
    key_value_master,
    gain_master,
    attention_row_moment,
    attention_column_moment,
    feed_row_moment,
    feed_column_moment,
    vocab_row_moment,
    vocab_column_moment,
    key_value_row_moment,
    key_value_column_moment,
    gain_moment,
):
    ctx_index = lax.axis_index(CTX)
    xs = lax.axis_index("tp_0")
    cs = lax.axis_index("tp_1")
    tp_index = xs * 2 + cs
    vocab_here = vocab_master.shape[2]
    ff_here = feed_master.shape[2]
    first_id = tp_index * vocab_here

    attention_low = attention_master.astype(bf16)
    feed_low = feed_master.astype(bf16)
    layer_all = lax.all_gather(
        jnp.concatenate(
            [
                attention_low[0].T,
                attention_low[1].T,
                feed_low[0].T,
                feed_low[1].T,
                feed_low[2].T,
            ]
        )[None],
        CTX,
        axis=0,
        tiled=True,
    )
    head = lax.all_gather(vocab_master[0].astype(bf16).T[None], CTX, axis=0, tiled=True)

    def on_lanes(at, width):
        return layer_all[:, at : at + width].transpose(1, 0, 2).reshape(width, D)

    w_query = on_lanes(0, 256)
    w_out = on_lanes(256, 256)
    gate_up = on_lanes(512, 2 * ff_here)
    down = on_lanes(512 + 2 * ff_here, ff_here)

    kv_low = key_value_master.astype(bf16).reshape(16, 2, KV_HEADS, HD).transpose(2, 0, 1, 3)
    gain_low = jnp.pad(gain_master.astype(bf16), ((0, 0), (0, 125)))
    blocks = jnp.concatenate(
        [
            kv_low.reshape(KV_HEADS, 16, 2 * HD),
            jnp.broadcast_to(gain_low, (KV_HEADS, *gain_low.shape)),
        ],
        axis=2,
    )
    ids_here = own_order(token_ids, xs, cs).reshape(1, 256)
    line_block = both_cores(swapped_x(blocks, xs), cs)
    half = LINES // 2
    early = sent_to_all(
        jnp.concatenate(
            [
                lax.dynamic_slice_in_dim(line_block[:, : 2 * HD], cs * half, half, 0),
                line_block[:, 2 * HD : 2 * HD + 3].T,
                (ids_here // 256).astype(bf16).reshape(2, 128),
                (ids_here % 256).astype(bf16).reshape(2, 128),
                jnp.zeros((9, 128), bf16),
            ]
        ),
        CTX,
    )
    own_half = early[:, :half]
    other_half = core_swap(own_half)
    w_pair = jnp.where(
        cs == 0,
        jnp.concatenate([own_half, other_half], axis=1),
        jnp.concatenate([other_half, own_half], axis=1),
    ).reshape(D, 2 * HD)
    gains = early[:, half : half + 3].astype(f32).transpose(1, 0, 2).reshape(3, D)
    parts = early[:, half + 3 : half + 7].astype(jnp.int32).reshape(N_CTX, 2, 256)
    all_ids = parts[:, 0] * 256 + parts[:, 1]
    all_ids = all_ids.reshape(N_CTX, 8, SHARD).transpose(1, 0, 2).reshape(1, TOKENS) - first_id

    order = (
        ((xs + jnp.arange(N_X, dtype=jnp.int32)) % N_X * 2)[None, :]
        + (cs ^ jnp.arange(2, dtype=jnp.int32))[:, None]
    )[:, :, None] * SHARD + jnp.arange(SHARD, dtype=jnp.int32)
    second_span = order >= 128
    within = order % 128
    own_pair = lax.dynamic_slice_in_dim(span_pairs, ctx_index, 1)[0]
    last_span = 2 * N_CTX - 1
    own_pos = (jnp.where(second_span, last_span - own_pair, own_pair) * 128 + within).reshape(-1)
    doc_start = jnp.zeros_like(own_pos)
    for k in range(1, DOCS):
        start = jnp.sum((segment_ids < k).astype(jnp.int32))
        doc_start = jnp.where(own_pos >= start, start, doc_start)
    cosine, sine = rope_tables(own_pos - doc_start)
    cosine_4, sine_4 = (jnp.tile(cosine, (1, 4)), jnp.tile(sine, (1, 4)))
    own_places = jnp.tile(jnp.stack([own_pos, doc_start]), (1, 4))
    spans = jnp.concatenate([span_pairs, jnp.stack([xs, cs]).astype(jnp.int32)])

    tables = vocab_master.transpose(0, 2, 1)
    looked = look_up(all_ids, tables).reshape(2, N_X, N_CTX, SHARD, LINES)
    half = looked[0] + core_swap(looked[1])
    mine = half[0]
    for d in range(1, N_X):
        mine = mine + x_to(half[d], d)
    rows_in = lax.all_to_all(mine, CTX, 0, 0, tiled=True)
    stream_in = rows_in.transpose(1, 0, 2).reshape(SHARD, D).astype(f32)

    normed_low = gather_tp(rms_norm(stream_in, gains[0]).astype(bf16))
    normed_half = normed_low[:128]
    keyval_linear = contract_ft(w_pair, normed_half)
    own_keyvals = jnp.concatenate(
        [rotate_rows(keyval_linear[:HD], cosine[:, :128], sine[:, :128]), keyval_linear[HD:]]
    ).astype(bf16)
    half_keyvals = sent_to_all(own_keyvals, CTX)
    row_keyvals = jnp.concatenate([half_keyvals, core_swap(half_keyvals)])
    query_linear = heads_on_lanes(contract_last(w_query, normed_low))
    queries = rotate_rows(query_linear, cosine_4, sine_4).astype(bf16) * jnp.asarray(
        1.0 / math.sqrt(HD), bf16
    )
    attended, log_total = attend(spans, own_places, queries, row_keyvals)
    attended_rows = heads_on_rows(attended)
    stream_mid = stream_in + scatter_tp(
        contract_first(attended_rows, w_out).reshape(2, N_X, SHARD, D)
    )

    inner_low = gather_tp(rms_norm(stream_mid, gains[1]).astype(bf16))
    both = contract_last(inner_low, gate_up)
    gate, upward = (both[:, :ff_here], both[:, ff_here:])
    sigmoid_gate = jax.nn.sigmoid(gate)
    silu_gate = gate * sigmoid_gate
    hidden_low = (silu_gate * upward).astype(bf16)
    stream_out = stream_mid + scatter_tp(
        contract(hidden_low, down).reshape(2, N_X, SHARD, D)
    )

    feed_tables = feed_master.transpose(0, 2, 1)
    masters = (tables, feed_tables, attention_master, key_value_master, gain_master.T)
    masters, inner_low = lax.optimization_barrier((masters, inner_low))
    weight_sums = weight_squares(*masters)
    finals_low = gather_tp(rms_norm(stream_out, gains[2]).astype(bf16))
    weight_sums, finals_low = lax.optimization_barrier((weight_sums, finals_low))
    local_targets = own_order(target_ids, xs, cs).reshape(1, -1) - first_id
    logits, stats = logits_and_stats(finals_low, head, local_targets)
    stats = stats[:3].reshape(3, 2, N_X, SHARD)
    stats = combine_stats(stats, core_swap(stats)[:, ::-1])
    others = [jnp.roll(x_from(stats, d), d, axis=2) for d in range(1, N_X)]
    stats = combine_stats(combine_stats(stats, others[0]), combine_stats(others[1], others[2]))
    stats = stats.reshape(3, -1)
    vocab_total = stats[0] + jnp.log(stats[1])
    keep = own_order(loss_mask, xs, cs).reshape(-1).astype(f32)
    loss_part = jnp.sum((keep * (vocab_total - stats[2]))[:SHARD]) / TOKENS

    place = jnp.stack([vocab_total, keep / TOKENS])
    head_low, dlogits_low = head_grads(logits, finals_low, place, local_targets)
    head_low = lax.psum_scatter(head_low, CTX, scatter_dimension=0, tiled=True)[0]
    final_part = place_grads_of(dlogits_low, head)
    final_grad = scatter_tp(final_part.reshape(2, N_X, SHARD, D))
    out_grad, final_gain_grad = jax.vjp(rms_norm, stream_out, gains[2])[1](final_grad)
    branch_low = gather_tp(out_grad.astype(bf16))
    hidden_grad = contract_last(branch_low, down)
    gate_grad_low = (
        hidden_grad * upward * sigmoid_gate * (1.0 + gate * (1.0 - sigmoid_gate))
    ).astype(bf16)
    upward_grad_low = (hidden_grad * silu_gate).astype(bf16)
    both_grad_low = jnp.concatenate([gate_grad_low, upward_grad_low], axis=1)
    inner_grad = scatter_tp(contract(both_grad_low, gate_up).reshape(2, N_X, SHARD, D))
    mid_part, middle_gain_grad = jax.vjp(rms_norm, stream_mid, gains[1])[1](inner_grad)
    mid_grad = out_grad + mid_part
    attend_low = gather_tp(mid_grad.astype(bf16))
    attended_grad = heads_on_lanes(contract_last(w_out, attend_low).astype(bf16))
    dq, pair_grads = attend_back(
        spans, own_places, queries, attended_grad, log_total, row_keyvals
    )
    pair_grads = pair_grads.reshape(2, N_CTX, 128, 2 * HD)
    half_grads = (pair_grads[0] + core_swap(pair_grads[1].astype(bf16)).astype(f32)).astype(bf16)
    query_linear_low = heads_on_rows(rotate_rows(dq, cosine_4, -sine_4).astype(bf16))
    half_grads, both_low = lax.optimization_barrier((half_grads, both_grad_low))
    came = lax.all_to_all(half_grads, CTX, 0, 0, tiled=True)
    layer_low = row_products(
        [inner_low, attend_low, branch_low, normed_low],
        [both_low, attended_rows, hidden_low, query_linear_low],
    )
    layer_low, head_low, came = lax.optimization_barrier((layer_low, head_low, came))
    layer_low = lax.psum_scatter(layer_low, CTX, scatter_dimension=0, tiled=True)[0]
    own_grads = jnp.sum(came.astype(f32), axis=0)
    keyval_low = jnp.concatenate(
        [
            rotate_lanes(own_grads[:, :HD], cosine[:, :128].T, -sine[:, :128].T),
            own_grads[:, HD:],
        ],
        axis=1,
    ).astype(bf16)
    normed_part = contract_first(query_linear_low, w_query).reshape(2, 128, D)
    normed_part = jnp.stack([normed_part[0] + contract_last(keyval_low, w_pair), normed_part[1]])
    normed_grad = scatter_tp(normed_part.reshape(2, N_X, SHARD, D))
    pair_low = contract_first(keyval_low, normed_half).astype(bf16)
    pair_low = pair_low.reshape(2 * HD, N_CTX, LINES).transpose(1, 0, 2)
    first_part, first_gain_grad = jax.vjp(rms_norm, stream_in, gains[0])[1](normed_grad)
    input_low = (mid_grad + first_part).astype(bf16)

    gain_parts = jnp.stack([first_gain_grad, middle_gain_grad, final_gain_grad]).astype(bf16)
    sent = jnp.concatenate(
        [
            input_low.reshape(SHARD, N_CTX, LINES).transpose(1, 0, 2),
            jnp.pad(gain_parts.reshape(3, N_CTX, LINES).transpose(1, 0, 2), ((0, 0), (0, 13), (0, 0))),
            pair_low,
        ],
        axis=1,
    )
    arrived = lax.all_to_all(sent, CTX, 0, 0, tiled=True)
    head_part, head_line, head_columns = head_figures(head_low)
    arrived, head_part = lax.optimization_barrier((arrived, head_part))
    kv_part = jnp.sum(arrived[:, 48:].astype(f32), axis=0)
    gain_sums = jnp.sum(arrived[:, SHARD : SHARD + 3].astype(f32), axis=0)
    own_column = tp_column(arrived[:, :SHARD].reshape(N_CTX * SHARD, LINES))
    embed_grad = add_up(all_ids, own_column, core_swap(own_column), vocab_here)

    kv_full = kv_part + core_swap(kv_part)
    kv_split, embed_grad = lax.optimization_barrier(
        (kv_full.T.reshape(N_X, 2, 16, 2 * HD), embed_grad)
    )
    kv_owned = swapped_x(jnp.where(cs == 0, kv_split[:, 0], kv_split[:, 1]), xs)
    key_value_grad = (
        kv_owned.reshape(KV_HEADS, 16, 2, HD).transpose(1, 2, 0, 3).reshape(16, KVW)
    )

    old_rows = jnp.concatenate(
        [attention_row_moment, feed_row_moment, vocab_row_moment, jnp.ones((9, LINES), f32)]
    )
    kv_old_columns = lax.dynamic_index_in_dim(
        key_value_column_moment.reshape(2, KV_HEADS, HD), xs, 1, keepdims=False
    ).reshape(-1)
    gap = jnp.ones((96,), f32)
    early_old = jnp.concatenate(
        [vocab_column_moment[0], gap, vocab_column_moment[1], gap, kv_old_columns]
    )[None]
    late_old = jnp.concatenate(
        [
            feed_column_moment[0],
            feed_column_moment[1],
            attention_column_moment[1],
            feed_column_moment[2],
            attention_column_moment[0],
            gap[:64],
        ]
    )[None]
    kv_old_line = lax.dynamic_update_slice_in_dim(
        jnp.zeros((1, LINES), f32), key_value_row_moment[None], tp_index * 16, 1
    )
    vocab_grad, line_parts, column_parts = early_figures(
        head_part, embed_grad, kv_full, gain_sums, kv_old_line, head_line, head_columns
    )
    columns = lax.all_to_all(column_parts, CTX, 0, 0, tiled=True)
    lines = sum_tp(line_parts)
    gain_grad = lax.dynamic_slice_in_dim(lines[8:11], tp_index * 16, 16, 1)
    gain_second = moments(gain_moment.T, gain_grad * gain_grad, 1.0)
    gain_step = gain_grad * lax.rsqrt(gain_second)
    gain_squares = jnp.sum(gain_step * gain_step, axis=1)
    base = weight_sums + jnp.concatenate(
        [
            jnp.zeros((UG_LANE,), f32),
            gain_squares,
            loss_part.reshape(1),
            jnp.zeros((127 - LOSS_LANE,), f32),
        ]
    )
    early_rows, early_columns, vocab_unit, base = step_squares(
        early_squares_kernel,
        [(16, LINES), (1, EARLY_LANES), vocab_grad.shape, (1, 128)],
        vocab_grad,
        kv_full,
        lines,
        columns,
        old_rows,
        early_old,
        base,
    )
    feed_grad, attention_grad, line_parts, column_parts = late_figures(layer_low)
    columns = lax.all_to_all(column_parts, CTX, 0, 0, tiled=True)
    lines = sum_tp(line_parts)
    late_rows, late_columns, feed_unit, attention_unit, packed = step_squares(
        late_squares_kernel,
        [(8, LINES), (1, LATE_LANES), feed_grad.shape, attention_grad.shape, (128, 2, 128)],
        layer_low,
        lines,
        columns,
        old_rows,
        late_old,
        base,
        early_columns[:, 8192:],
    )
    gathered = lax.all_to_all(packed, CTX_TP, 0, 0, tiled=True)
    vocab_new, feed_new, attention_new, gain_new, figures = update(
        gathered[:, 0],
        tables,
        vocab_unit,
        feed_tables,
        feed_unit,
        attention_master,
        attention_unit,
        gain_master.T,
        gain_step,
    )
    token_loss = figures[2, 0]
    update_rms = figures[0, :11]
    kv_row_new = lax.dynamic_slice_in_dim(early_rows[7], tp_index * 16, 16, 0)
    kv_column_new = (
        gathered[0:8:2, 1].reshape(KV_HEADS, 2, HD).transpose(1, 0, 2).reshape(KVW)
    )
    kv_step = key_value_grad * lax.rsqrt(kv_row_new)[:, None] * lax.rsqrt(kv_column_new)[None]
    kv_new = key_value_master - figures[1, 7] * kv_step
    def columns_of(k):
        at, width = COLUMN_AT[k]
        return (early_columns if k > 4 else late_columns)[0, at : at + width]

    attention_columns = jnp.stack([columns_of(0), columns_of(1)])
    feed_columns = jnp.stack([columns_of(2), columns_of(3), columns_of(4)])
    return (
        token_loss,
        update_rms,
        attention_grad,
        late_rows[0:2],
        attention_columns,
        attention_new,
        feed_grad.transpose(0, 2, 1),
        late_rows[2:5],
        feed_columns,
        feed_new.transpose(0, 2, 1),
        vocab_grad.transpose(0, 2, 1),
        early_rows[5:7],
        columns_of(5),
        columns_of(6),
        vocab_new.transpose(0, 2, 1),
        key_value_grad,
        kv_row_new,
        kv_column_new,
        kv_new,
        gain_grad.T,
        gain_second.T,
        gain_new.T,
    )


def solution(mesh):
    finer = Mesh(mesh.devices.reshape(4, 4, 4, 2), ("ctx_0", "ctx_1", "tp_0", "tp_1"))
    in_specs = (
        P(CTX),
        P(CTX),
        P(CTX),
        P(),
        P(),
        P(None, CTX, TP),
        P(None, CTX, TP),
        P(None, CTX, TP),
        P(CTX_TP, None),
        P(CTX_TP, None),
        P(None, CTX),
        P(None, TP),
        P(None, CTX),
        P(None, TP),
        P(None, CTX),
        P(None, TP),
        P(CTX_TP),
        P(),
        P(CTX_TP, None),
    )
    out_specs = (
        P(),
        P(),
        P(None, CTX, TP),
        P(None, CTX),
        P(None, TP),
        P(None, CTX, TP),
        P(None, CTX, TP),
        P(None, CTX),
        P(None, TP),
        P(None, CTX, TP),
        P(None, CTX, TP),
        P(None, CTX),
        P(TP),
        P(TP),
        P(None, CTX, TP),
        P(CTX_TP, None),
        P(CTX_TP),
        P(),
        P(CTX_TP, None),
        P(CTX_TP, None),
        P(CTX_TP, None),
        P(CTX_TP, None),
    )
    return jax.shard_map(body, mesh=finer, in_specs=in_specs, out_specs=out_specs, check_vma=False)
```
